32 devices in a mesh: outer: 4 (over z), inner: 4 (over y, x), head: 2 (over core).
Axes of the slice: x: 2, y: 2, z: 4, core: 2. Of those that a mesh axis runs over, the one named last changes fastest.
Arguments:
- token_ids: int32 [16, 1536], P(('outer', 'inner'), 'head'), may hold values from 0 to 32127
- lengths: int32 [16], P(('outer', 'inner')), may hold values from 768 to 1536, as said below
- query_weight: bfloat16 [768, 768], P(None, 'head'), may hold values from -0.21875 to 0.21875
- key_weight: bfloat16 [768, 768], P(None, 'head'), may hold values from -0.21875 to 0.21875
- value_weight: bfloat16 [768, 768], P(None, 'head'), may hold values from -0.21875 to 0.21875
- output_weight: bfloat16 [768, 768], P('head'), may hold values from -0.875 to 0.875
- expand_weight: bfloat16 [768, 3072], P(None, 'head'), may hold values from -0.21875 to 0.21875
- reduce_weight: bfloat16 [3072, 768], P('head'), may hold values from -0.109375 to 0.109375
- dconv_taps: float32 [3, 3, 768], P(None, None, 'head'), may hold values from -3 to 3
- gain_first: float32 [768], replicated, may hold values from 0.5 to 1.5
- bias_first: float32 [768], replicated, may hold values from -1 to 1
- gain_second: float32 [768], replicated, may hold values from 0.5 to 1.5
- bias_second: float32 [768], replicated, may hold values from -1 to 1
- cotangent: float32 [16, 1536, 768], P(('outer', 'inner'), 'head'), may hold values from -6 to 6
Outputs:
- activations: float32 [16, 1536, 768], P(('outer', 'inner'), 'head')
- grad_input: float32 [16, 1536, 768], P(('outer', 'inner'), 'head')
- grad_query: float32 [768, 768], P('inner', 'head')
- grad_key: float32 [768, 768], P('inner', 'head')
- grad_value: float32 [768, 768], P('inner', 'head')
- grad_output: float32 [768, 768], P('head', 'inner')
- grad_expand: float32 [768, 3072], P('inner', 'head')
- grad_reduce: float32 [3072, 768], P('head', 'inner')
- grad_taps: float32 [3, 3, 768], replicated
- dgain_first: float32 [768], replicated
- dbias_first: float32 [768], replicated
- dgain_second: float32 [768], replicated
- dbias_second: float32 [768], replicated
The draws below stay inside these ranges and needn't reach their ends.
Inputs may be any that keep to these rules, and one draw needn't show every extreme that they name: `lengths`: in every aligned pair of sub-batches (0 and 1, 2 and 3, and so on) one, which one drawn from the seed, is full; slots at or past a sub-batch's length are padding.
All inputs are finite; a program needn't handle non-finite values.
Results may differ from the reference program's by a relative error of at most 0.023.
Values may be sent and summed in bfloat16 or wider, within the bound.
A program may use at most 320 MiB of HBM per device.

```python
import math
import jax
import jax.numpy as jnp
from jax import lax

HEADS = 12
HEAD_DIM = 64
D = 768
FF = 3072
VOCAB = 32128
SLOT = 1536
SUBS = 1
QBLOCK = 512
BATCH = 16
N_HEAD = 2


def draw_lengths(key, part):
    key = jax.random.fold_in(key, 11)
    first_key, second_key = jax.random.split(key)
    pairs = BATCH // 2
    drawn = jax.random.randint(first_key, (pairs, 2), SLOT // 2, SLOT + 1)
    chosen = jax.random.randint(second_key, (pairs, 1), 0, 2)
    filled = jnp.where(jnp.arange(2)[None, :] == chosen, SLOT, drawn)
    return filled.reshape(BATCH).astype(jnp.int32)


def place_ends(values, stream_key, least, high):
    longest = values.shape.index(max(values.shape))
    spots = []
    for shift in (0, 1):
        where = [jax.random.randint(jax.random.fold_in(stream_key, axis), (), 0, length) for axis, length in enumerate(values.shape)]
        where[longest] = (where[longest] + shift) % values.shape[longest]
        spots.append(tuple(where))
    return values.at[spots[0]].set(least).at[spots[1]].set(high)


def spiked(values, own_key, source, target, blocks, factor):
    owner, partner = [(jnp.arange(values.shape[dim]) // (values.shape[dim] // blocks)).reshape([-1 if axis == dim else 1 for axis in range(values.ndim)]) for dim in (source, target)]
    chosen = jax.random.permutation(own_key, blocks)[partner]
    strong = (owner == chosen) | (owner == (partner + blocks // 2) % blocks)
    return jnp.where(strong, factor * values, values)


def shard_levels(stream_key, extent, cuts, least, high):
    level, own = 1.0, jax.random.fold_in(stream_key, 6)
    for axis_at, shards_of in cuts:
        draws = jnp.exp(jax.random.uniform(jax.random.fold_in(own, axis_at), (shards_of,), jnp.float32, least / len(cuts), high / len(cuts)))
        level = level * jnp.repeat(draws, extent[axis_at] // shards_of).reshape([-1 if axis == axis_at else 1 for axis in range(len(extent))])
    return level


def gaussian(stream_key, shape, deviation, bound, shards=(), held_as=jnp.bfloat16):
    entries = deviation * jax.random.normal(stream_key, shape, jnp.float32)
    if shards:
        entries = entries * shard_levels(stream_key, shape, shards, -0.22, 0.18)
    return jnp.clip(entries, -bound, bound).astype(held_as)


def noise_with(key, shape, scale, reach, cuts, heavy, kind=jnp.bfloat16):
    array = scale * jax.random.normal(key, shape, jnp.float32)
    if cuts:
        array = array * shard_levels(key, shape, cuts, -0.22, 0.18)
    return jnp.clip(spiked(array, jax.random.fold_in(key, 3), *heavy), -reach, reach).astype(kind)


def setup_inputs(seed: int = 0) -> dict:
    seeds = jax.random.split(jax.random.key(seed), 15)
    token_ids = place_ends(jax.random.randint(seeds[0], (BATCH, SLOT), 0, VOCAB), jax.random.fold_in(seeds[0], 1), 0, VOCAB - 1).astype(jnp.int32)
    lengths = draw_lengths(jax.random.fold_in(seeds[14], 71), 0)
    query_weight = gaussian(seeds[2], (D, D), D ** -0.5, 0.21875, ((1, 2),))
    key_weight = gaussian(seeds[3], (D, D), D ** -0.5, 0.21875, ((1, 2),))
    value_weight = gaussian(seeds[4], (D, D), D ** -0.5, 0.21875, ((1, 2),))
    output_weight = gaussian(seeds[5], (D, D), (D // 16) ** -0.5, 0.875, ((0, 2),))
    expand_weight = gaussian(seeds[6], (D, FF), D ** -0.5, 0.21875, ((1, 2),))
    reduce_weight = gaussian(seeds[7], (FF, D), FF ** -0.5, 0.109375, ((0, 2),))
    dconv_taps = gaussian(seeds[8], (3, 3, D), 0.7, 3.0, ((2, 2),), jnp.float32)
    gain_first = jnp.clip(1.0 + 0.1 * jax.random.normal(seeds[9], (D,), jnp.float32), 0.5, 1.5)
    bias_first = gaussian(seeds[10], (D,), 0.2, 1.0, (), jnp.float32)
    gain_second = jnp.clip(1.0 + 0.1 * jax.random.normal(seeds[11], (D,), jnp.float32), 0.5, 1.5)
    bias_second = gaussian(seeds[12], (D,), 0.2, 1.0, (), jnp.float32)
    cotangent = noise_with(seeds[13], (BATCH, SLOT, D), 1.0, 6.0, ((0, 16), (1, 2)), (0, 2, 16, 2.0), jnp.float32)
    return dict(token_ids=token_ids, lengths=lengths, query_weight=query_weight, key_weight=key_weight, value_weight=value_weight, output_weight=output_weight, expand_weight=expand_weight, reduce_weight=reduce_weight, dconv_taps=dconv_taps, gain_first=gain_first, bias_first=bias_first, gain_second=gain_second, bias_second=bias_second, cotangent=cotangent)


eps_norm = 1e-05
modulus = 32749
highest = lax.Precision.HIGHEST
negative = -1e+30

@jax.custom_vjp
def low(v):
    return lax.optimization_barrier(v.astype(jnp.bfloat16)).astype(jnp.float32)

@jax.custom_vjp
def low_back(v):
    return v

def low_keep(v):
    return (low(v), None)

def low_pass(kept, grad):
    return (grad,)

def back_keep(v):
    return (v, None)

def back_low(kept, grad):
    return (low(grad),)
low.defvjp(low_keep, low_pass)
low_back.defvjp(back_keep, back_low)

def embed(token_ids):
    columns = jnp.arange(D, dtype=jnp.int32)
    phases = (token_ids.astype(jnp.int32)[..., None] * (columns + 1) + columns * columns) % modulus
    return math.sqrt(2.0) * jnp.sin(phases.astype(jnp.float32) * (2.0 * math.pi / modulus))

def layer_norm(values, gain_vec, bias_vec):
    centre = values - lax.optimization_barrier(jnp.mean(values, axis=-1, keepdims=True))
    spread = lax.optimization_barrier(jnp.mean(centre * centre, axis=-1, keepdims=True))
    return centre * lax.rsqrt(spread + eps_norm) * gain_vec + bias_vec

def causal_taps(values, tap_rows):
    shift_one = jnp.pad(values, ((0, 0), (1, 0), (0, 0)))[:, :-1]
    shift_two = jnp.pad(values, ((0, 0), (2, 0), (0, 0)))[:, :-2]
    return tap_rows[0] * values + tap_rows[1] * shift_one + tap_rows[2] * shift_two

def project(left, right):
    return jnp.einsum('bsd,de->bse', left, right, precision=highest)

def attention(queries, key_rows, value_rows, lengths):
    blocks = SLOT // QBLOCK
    query_blocks = queries.reshape(SUBS, blocks, QBLOCK, HEADS, HEAD_DIM).transpose(1, 0, 2, 3, 4)
    starts = jnp.arange(blocks, dtype=jnp.int32) * QBLOCK
    key_pos = jnp.arange(SLOT, dtype=jnp.int32)

    def one_block(packed):
        block_query, first_row = packed
        scores = jnp.einsum('bqhd,bkhd->bhqk', block_query, key_rows, precision=highest)
        scores = low_back(scores) * HEAD_DIM ** (-0.5)
        query_pos = first_row + jnp.arange(QBLOCK, dtype=jnp.int32)
        allowed = (key_pos[None, None, None, :] <= query_pos[None, None, :, None]) & (key_pos[None, None, None, :] < lengths[:, None, None, None])
        row_max = lax.optimization_barrier(jnp.max(jnp.where(allowed, scores, negative), axis=-1, keepdims=True))
        exp_terms = jnp.where(allowed, jnp.exp(jnp.where(allowed, scores, row_max) - row_max), 0.0)
        prob_low = low(exp_terms / lax.optimization_barrier(jnp.sum(exp_terms, axis=-1, keepdims=True)))
        return jnp.einsum('bhqk,bkhd->bqhd', prob_low, value_rows, precision=highest)
    blocks_out = lax.map(jax.checkpoint(one_block), (query_blocks, starts))
    return blocks_out.transpose(1, 0, 2, 3, 4).reshape(SUBS, SLOT, HEADS * HEAD_DIM)

def forward(params, inputs, lengths):
    query_w, key_w, value_w, output_w, expand_w, reduce_w, tap_rows, gain_a, bias_a, gain_b, bias_b = params
    head_cols = D // N_HEAD
    ffn_cols = FF // N_HEAD
    normed = low(layer_norm(inputs, gain_a, bias_a))
    query_list, key_list, value_list = ([], [], [])
    for group in range(N_HEAD):
        columns = slice(group * head_cols, (group + 1) * head_cols)
        own_rows = low_back(normed)
        query_list.append(project(own_rows, query_w[:, columns]))
        key_list.append(project(own_rows, key_w[:, columns]))
        value_list.append(project(own_rows, value_w[:, columns]))
    query_raw = low_back(jnp.concatenate(query_list, axis=-1))
    key_raw = low_back(jnp.concatenate(key_list, axis=-1))
    value_raw = low_back(jnp.concatenate(value_list, axis=-1))
    shape_heads = (SUBS, SLOT, HEADS, HEAD_DIM)
    queries = low(causal_taps(query_raw, tap_rows[0])).reshape(shape_heads)
    key_rows = low(causal_taps(key_raw, tap_rows[1])).reshape(shape_heads)
    value_rows = low(causal_taps(value_raw, tap_rows[2])).reshape(shape_heads)
    attended = low(low_back(attention(queries, key_rows, value_rows, lengths)))
    attn_total = jnp.zeros_like(inputs)
    for group in range(N_HEAD):
        columns = slice(group * head_cols, (group + 1) * head_cols)
        attn_total = attn_total + low(project(attended[..., columns], output_w[columns]))
    hidden = inputs + low_back(attn_total)
    normed_b = low(layer_norm(hidden, gain_b, bias_b))
    expand_list = []
    for group in range(N_HEAD):
        columns = slice(group * ffn_cols, (group + 1) * ffn_cols)
        expand_list.append(project(low_back(normed_b), expand_w[:, columns]))
    expanded = low_back(jnp.concatenate(expand_list, axis=-1))
    squared = low(jnp.square(jnp.maximum(expanded, 0.0)))
    ffn_total = jnp.zeros_like(inputs)
    for group in range(N_HEAD):
        columns = slice(group * ffn_cols, (group + 1) * ffn_cols)
        ffn_total = ffn_total + low(project(squared[..., columns], reduce_w[columns]))
    return hidden + low_back(ffn_total)

def reference(token_ids, lengths, query_weight, key_weight, value_weight, output_weight, expand_weight, reduce_weight, dconv_taps, gain_first, bias_first, gain_second, bias_second, cotangent):
    params = (query_weight.astype(jnp.float32), key_weight.astype(jnp.float32), value_weight.astype(jnp.float32), output_weight.astype(jnp.float32), expand_weight.astype(jnp.float32), reduce_weight.astype(jnp.float32), dconv_taps.astype(jnp.float32), gain_first.astype(jnp.float32), bias_first.astype(jnp.float32), gain_second.astype(jnp.float32), bias_second.astype(jnp.float32))
    groups = BATCH // SUBS
    group_ids = token_ids.reshape(groups, SUBS, SLOT)
    group_lengths = lengths.astype(jnp.int32).reshape(groups, SUBS)
    group_cots = cotangent.reshape(groups, SUBS, SLOT, D)

    def one_group(running, packed):
        ids_group, lengths_group, cot_group = packed
        inputs = embed(ids_group)
        result, pullback = jax.vjp(lambda weights, values: forward(weights, values, lengths_group), params, inputs)
        valid = (jnp.arange(SLOT, dtype=jnp.int32)[None, :] < lengths_group[:, None]).astype(jnp.float32)
        weight_grads, input_grad = pullback(cot_group.astype(jnp.float32) * valid[..., None])
        running = jax.tree.map(jnp.add, running, weight_grads)
        return (running, (result, input_grad))
    start_sums = jax.tree.map(jnp.zeros_like, params)
    final, (results, input_grads) = lax.scan(one_group, start_sums, (group_ids, group_lengths, group_cots))
    return (results.reshape(BATCH, SLOT, D), input_grads.reshape(BATCH, SLOT, D), final[0], final[1], final[2], final[3], final[4], final[5], final[6], final[7], final[8], final[9], final[10])
```

```python
import functools
import math

import jax
import jax.numpy as jnp
from jax import lax
from jax.experimental import pallas as pl
from jax.experimental.pallas import tpu as pltpu
from jax.sharding import PartitionSpec as P

HEAD_DIM = 64
D = 768
BLOCK = 256
LANES = 128
EPS = 1e-05
MODULUS = 32749
NEGATIVE = -1e30
SCALE = HEAD_DIM ** (-0.5)
F32 = jnp.float32
BF16 = jnp.bfloat16
MIB = 1024 * 1024

SINE = (
    4.442882913726386,
    -7.308248583654593,
    3.606466623722958,
    -0.8474403474577161,
    0.11605422299047748,
    -0.010267162611370253,
    0.0005523348366953617,
)


def dot(a, b):
    return lax.dot_general(a, b, (((1,), (0,)), ((), ())), preferred_element_type=F32)


def dot_nt(a, b):
    return lax.dot_general(a, b, (((1,), (1,)), ((), ())), preferred_element_type=F32)


def whole(shape):
    return pl.BlockSpec(shape, lambda *_: (0,) * len(shape))


def normalise(values):
    centre = values - jnp.mean(values, axis=-1, keepdims=True)
    spread = jnp.mean(centre * centre, axis=-1, keepdims=True)
    scale = lax.rsqrt(spread + EPS)
    return centre * scale, scale


def norm_back(grad, hat, scale, gain):
    q = grad * gain
    mean_q = jnp.mean(q, axis=-1, keepdims=True)
    mean_qh = jnp.mean(q * hat, axis=-1, keepdims=True)
    return scale * (q - mean_q - hat * mean_qh)


def embed_kernel(tok_ref, gain_ref, bias_ref, emb_ref, normed_ref):
    rows = emb_ref.shape[0]

    def step(i, _):
        first = pl.multiple_of(i * LANES, LANES)
        tokens = jnp.broadcast_to(tok_ref[:, pl.ds(first, LANES)], (LANES, LANES)).T
        parts = []
        for c in range(D // LANES):
            column = lax.broadcasted_iota(jnp.int32, (1, LANES), 1) + c * LANES
            product = tokens * (column + 1) + column * column
            turns = jnp.floor(product.astype(F32) * (1.0 / MODULUS) + 0.5)
            left = product - turns.astype(jnp.int32) * MODULUS
            u = left.astype(F32) * (2.0 / MODULUS)
            z = u * u
            value = jnp.full_like(u, SINE[-1])
            for coefficient in SINE[-2::-1]:
                value = value * z + coefficient
            parts.append(value * u)
        embedded = jnp.concatenate(parts, axis=1)
        emb_ref[pl.ds(first, LANES), :] = embedded
        hat, _ = normalise(embedded)
        normed_ref[pl.ds(first, LANES), :] = (hat * gain_ref[...] + bias_ref[...]).astype(BF16)
        return 0

    lax.fori_loop(0, rows // LANES, step, 0)


def lane_ids(rows):
    return lax.broadcasted_iota(jnp.int32, (rows, LANES), 1)


def split_three(column):
    high = column.astype(BF16).astype(F32)
    rest = column - high
    middle = rest.astype(BF16).astype(F32)
    return high, middle, rest - middle


def with_parts(base, lane, offset, column):
    high, middle, small = split_three(column)
    base = jnp.where(lane == offset + 1, high, base)
    base = jnp.where(lane == offset + 2, middle, base)
    return jnp.where(lane == offset + 3, small, base)


def forward_kernel(
    place_ref, own_ref, oth_ref, wq_ref, wk_ref, wv_ref, taps_ref,
    att_ref, qa_ref, ka_ref, va_ref, raw_ref,
    normed_ref, shift_ref,
):
    slot = att_ref.shape[0]
    half = slot // 2
    head, length = place_ref[0], place_ref[1]

    @pl.when(pl.program_id(0) == 0)
    def _():
        normed_ref[pl.ds(pl.multiple_of(head * half, half), half), :] = own_ref[...]
        normed_ref[pl.ds(pl.multiple_of((1 - head) * half, half), half), :] = oth_ref[...]
        shift_ref[0:8, :] = jnp.zeros((8, LANES), F32)

    lane = lane_ids(slot)
    mixed = []
    for j, w_ref in enumerate((wq_ref, wk_ref, wv_ref)):
        raw = dot(normed_ref[...], w_ref[...])
        raw_ref[:, j * LANES : (j + 1) * LANES] = raw.astype(BF16)
        shift_ref[8 : 8 + slot, :] = raw
        one = shift_ref[7 : 7 + slot, :]
        two = shift_ref[6 : 6 + slot, :]
        value = taps_ref[j, 0:1, :] * raw + taps_ref[j, 1:2, :] * one + taps_ref[j, 2:3, :] * two
        mixed.append(value * SCALE if j == 0 else value)
    row = lax.broadcasted_iota(jnp.int32, (slot, 1), 0)
    key_bias = jnp.where(row < length, 0.0, NEGATIVE)
    for e in range(2):
        mine = (lane // HEAD_DIM) == e
        other = HEAD_DIM * (1 - e)
        ones = jnp.where((lane > other) & (lane < other + 4), 1.0, 0.0)
        qa_ref[e] = jnp.where(mine, mixed[0], jnp.where(lane == other, 1.0, 0.0)).astype(BF16)
        ka_ref[e] = jnp.where(mine, mixed[1], jnp.where(lane == other, key_bias, ones)).astype(BF16)
        va_ref[e] = jnp.where(mine, mixed[2], ones).astype(BF16)
    block_lane = lane_ids(BLOCK)
    causal = lax.broadcasted_iota(jnp.int32, (BLOCK, BLOCK), 1) <= lax.broadcasted_iota(
        jnp.int32, (BLOCK, BLOCK), 0
    )
    for i in range(slot // BLOCK):
        rows = slice(i * BLOCK, (i + 1) * BLOCK)
        before = i * BLOCK
        heads = []
        for e in range(2):
            other = HEAD_DIM * (1 - e)
            query = qa_ref[e, rows, :]
            diagonal = jnp.where(causal, dot_nt(query, ka_ref[e, rows, :]), NEGATIVE)
            row_max = jnp.max(diagonal, axis=1, keepdims=True)
            if before:
                scores = dot_nt(query, ka_ref[e, :before, :])
                row_max = jnp.maximum(row_max, jnp.max(scores, axis=1, keepdims=True))
            out = dot(jnp.exp(diagonal - row_max).astype(BF16), va_ref[e, rows, :])
            if before:
                out += dot(jnp.exp(scores - row_max).astype(BF16), va_ref[e, :before, :])
            total = out[:, other + 1 : other + 2]
            heads.append(out / total)
            log_norm = -(row_max + jnp.log(total))
            qa_ref[e, rows, :] = with_parts(query.astype(F32), block_lane, other, log_norm).astype(BF16)
        att_ref[rows, :] = jnp.where(block_lane < HEAD_DIM, heads[0], heads[1]).astype(BF16)


def ffn_kernel(
    place_ref, att_own_ref, att_oth_ref, emb_ref, cot_ref, gain_ref, bias_ref,
    wo_own_ref, wo_oth_ref, we_own_ref, we_oth_ref, wr_own_ref, wr_oth_ref,
    act_ref, gh_ref, gatt_own_ref, gatt_oth_ref, go_own_ref, go_oth_ref,
    ge_own_ref, ge_oth_ref, gr_own_ref, gr_oth_ref, small_ref,
    n2_ref, n2t_ref, gl_ref, glt_ref, hid_ref, ffn_ref, gn_ref,
):
    half = emb_ref.shape[0]
    step = pl.program_id(0)
    head, length = place_ref[0], place_ref[1]
    row = lax.broadcasted_iota(jnp.int32, (half, 1), 0) + head * half
    valid = row < length

    @pl.when(step == 0)
    def _():
        hidden = emb_ref[...] + dot(att_own_ref[...], wo_own_ref[...]) + dot(att_oth_ref[...], wo_oth_ref[...])
        hid_ref[...] = hidden
        hat, _ = normalise(hidden)
        normed = hat * gain_ref[...] + bias_ref[...]
        n2_ref[...] = normed.astype(BF16)
        n2t_ref[...] = normed.astype(BF16).T
        grad = jnp.where(valid, cot_ref[...], 0.0)
        gl_ref[...] = grad.astype(BF16)
        glt_ref[...] = grad.astype(BF16).T
        ffn_ref[...] = jnp.zeros_like(ffn_ref)
        gn_ref[...] = jnp.zeros_like(gn_ref)

    for we_ref, wr_ref, ge_ref, gr_ref in (
        (we_oth_ref, wr_oth_ref, ge_oth_ref, gr_oth_ref),
        (we_own_ref, wr_own_ref, ge_own_ref, gr_own_ref),
    ):
        relu = jnp.maximum(dot(n2_ref[...], we_ref[...]), 0.0)
        squared = (relu * relu).astype(BF16)
        gr_ref[...] = dot(glt_ref[...], squared).astype(BF16)
        grad_e = (dot_nt(gl_ref[...], wr_ref[...]) * (2.0 * relu)).astype(BF16)
        ge_ref[...] = dot(n2t_ref[...], grad_e).astype(BF16)
        gn_ref[...] += dot_nt(grad_e, we_ref[...])
        ffn_ref[...] += dot(squared, wr_ref[...])

    @pl.when(step == pl.num_programs(0) - 1)
    def _():
        hidden = hid_ref[...]
        act_ref[...] = hidden + ffn_ref[...]
        hat, scale = normalise(hidden)
        grad_n = gn_ref[...]
        small_ref[0:1, :] = jnp.sum(grad_n * hat, axis=0, keepdims=True)
        small_ref[1:2, :] = jnp.sum(grad_n, axis=0, keepdims=True)
        grad_h = jnp.where(valid, cot_ref[...], 0.0) + norm_back(grad_n, hat, scale, gain_ref[...])
        gh_ref[...] = grad_h
        low = grad_h.astype(BF16)
        gatt_oth_ref[...] = dot_nt(low, wo_oth_ref[...]).astype(BF16)
        gatt_own_ref[...] = dot_nt(low, wo_own_ref[...]).astype(BF16)
        low_t = low.T
        go_oth_ref[...] = dot(low_t, att_oth_ref[...]).astype(BF16)
        go_own_ref[...] = dot(low_t, att_own_ref[...]).astype(BF16)


def backward_kernel(
    place_ref, own_ref, oth_ref, gown_ref, goth_ref, wq_ref, wk_ref, wv_ref, taps_ref,
    att_ref, qa_ref, ka_ref, va_ref, raw_ref,
    gq_ref, gk_ref, gv_ref, gtaps_ref, first_own_ref, first_oth_ref,
    nt_ref, do_ref, doa_ref, dqt_ref, mix_ref, all_ref, first_ref,
):
    slot = att_ref.shape[0]
    half = slot // 2
    head = place_ref[0]
    step = pl.program_id(0)

    def put(dst, own, oth):
        dst[pl.ds(pl.multiple_of(head * half, half), half), :] = own
        dst[pl.ds(pl.multiple_of((1 - head) * half, half), half), :] = oth

    @pl.when(step == 0)
    def _():
        nt_ref[:, pl.ds(pl.multiple_of(head * half, half), half)] = own_ref[...].T
        nt_ref[:, pl.ds(pl.multiple_of((1 - head) * half, half), half)] = oth_ref[...].T
        mix_ref[:, slot : slot + 8, :] = jnp.zeros((3, 8, LANES), F32)
        first_ref[...] = jnp.zeros_like(first_ref)

    put(do_ref, gown_ref[...], goth_ref[...])
    lane = lane_ids(slot)
    grad_out = do_ref[...].astype(F32)
    product = grad_out * att_ref[...].astype(F32)
    for e in range(2):
        mine = (lane // HEAD_DIM) == e
        delta = -jnp.sum(jnp.where(mine, product, 0.0), axis=1, keepdims=True)
        other = HEAD_DIM * (1 - e)
        doa_ref[e] = with_parts(jnp.where(mine, grad_out, 0.0), lane, other, delta).astype(BF16)
    causal = lax.broadcasted_iota(jnp.int32, (BLOCK, BLOCK), 0) <= lax.broadcasted_iota(
        jnp.int32, (BLOCK, BLOCK), 1
    )
    block_lane = lane_ids(BLOCK)
    dqt_ref[...] = jnp.zeros_like(dqt_ref)
    for j in range(slot // BLOCK):
        keys = slice(j * BLOCK, (j + 1) * BLOCK)
        first = j * BLOCK
        after = first + BLOCK
        dks, dvs = [], []
        for e in range(2):
            ka = ka_ref[e, keys, :]
            va = va_ref[e, keys, :]
            kat = ka.T
            spans = [(first, after, True)] + ([(after, slot, False)] if after < slot else [])
            dk = dv = None
            for lo, hi, masked in spans:
                scores = dot_nt(ka, qa_ref[e, lo:hi, :])
                if masked:
                    scores = jnp.where(causal, scores, NEGATIVE)
                probs = jnp.exp(scores)
                grads = (probs * dot_nt(va, doa_ref[e, lo:hi, :])).astype(BF16)
                dv_part = dot(probs.astype(BF16), doa_ref[e, lo:hi, :])
                dk_part = dot(grads, qa_ref[e, lo:hi, :])
                dv = dv_part if dv is None else dv + dv_part
                dk = dk_part if dk is None else dk + dk_part
                dqt_ref[e, :, lo:hi] += dot(kat, grads)
            dks.append(dk)
            dvs.append(dv)
        mix_ref[1, keys, :] = jnp.where(block_lane < HEAD_DIM, dks[0], dks[1])
        mix_ref[2, keys, :] = jnp.where(block_lane < HEAD_DIM, dvs[0], dvs[1])
    sub = lax.broadcasted_iota(jnp.int32, (LANES, slot), 0)
    mix_ref[0, 0:slot, :] = (jnp.where(sub < HEAD_DIM, dqt_ref[0], dqt_ref[1]) * SCALE).T
    for j, out_ref in enumerate((gq_ref, gk_ref, gv_ref)):
        zero = mix_ref[j, 0:slot, :]
        one = mix_ref[j, 1 : 1 + slot, :]
        two = mix_ref[j, 2 : 2 + slot, :]
        raw = raw_ref[:, j * LANES : (j + 1) * LANES].astype(F32)
        for s, moved in enumerate((zero, one, two)):
            gtaps_ref[j, s : s + 1, :] = jnp.sum(moved * raw, axis=0, keepdims=True)
        value = taps_ref[j, 0:1, :] * zero + taps_ref[j, 1:2, :] * one + taps_ref[j, 2:3, :] * two
        all_ref[:, j * LANES : (j + 1) * LANES] = value.astype(BF16)
    grads = dot(nt_ref[...], all_ref[...]).astype(BF16)
    for j, out_ref in enumerate((gq_ref, gk_ref, gv_ref)):
        out_ref[...] = grads[:, j * LANES : (j + 1) * LANES]
    joined = jnp.concatenate([wq_ref[...], wk_ref[...], wv_ref[...]], axis=1)
    first_ref[...] += dot_nt(all_ref[...], joined)

    @pl.when(step == pl.num_programs(0) - 1)
    def _():
        first_own_ref[...] = first_ref[pl.ds(pl.multiple_of(head * half, half), half), :]
        first_oth_ref[...] = first_ref[pl.ds(pl.multiple_of((1 - head) * half, half), half), :].astype(BF16)


def last_kernel(own_ref, got_ref, emb_ref, gh_ref, gain_ref, out_ref, small_ref):
    grad_n = own_ref[...] + got_ref[...].astype(F32)
    hat, scale = normalise(emb_ref[...])
    small_ref[0:1, :] = jnp.sum(grad_n * hat, axis=0, keepdims=True)
    small_ref[1:2, :] = jnp.sum(grad_n, axis=0, keepdims=True)
    out_ref[...] = gh_ref[...] + norm_back(grad_n, hat, scale, gain_ref[...])


def params(vmem, **kw):
    return pltpu.CompilerParams(vmem_limit_bytes=vmem * MIB, **kw)


def body(
    token_ids, lengths, query_weight, key_weight, value_weight, output_weight,
    expand_weight, reduce_weight, dconv_taps, gain_first, bias_first,
    gain_second, bias_second, cotangent,
):
    half = token_ids.shape[1]
    slot = 2 * half
    local = query_weight.shape[1]
    units = expand_weight.shape[1]
    pairs = local // LANES
    head = lax.axis_index("head").astype(jnp.int32)
    place = jnp.stack([head, lengths[0]])

    def swap(value):
        return lax.ppermute(value, "head", [(0, 1), (1, 0)])

    shape = jax.ShapeDtypeStruct
    row_vec = lambda v: v.reshape(1, D)
    smem = pl.BlockSpec(memory_space=pltpu.SMEM)
    embedded, normed = pl.pallas_call(
        embed_kernel,
        out_shape=(shape((half, D), F32), shape((half, D), BF16)),
        compiler_params=params(32),
        name="embed",
    )(token_ids, row_vec(gain_first), row_vec(bias_first))
    normed_oth = swap(normed)
    we_oth, wr_oth, wo_oth = swap(expand_weight), swap(reduce_weight), swap(output_weight)

    column = pl.BlockSpec((D, LANES), lambda p: (0, p))
    taps_spec = pl.BlockSpec((3, 3, LANES), lambda p: (0, 0, p))
    pair_rows = pl.BlockSpec((slot, LANES), lambda p: (0, p))
    pair_heads = pl.BlockSpec((2, slot, LANES), lambda p: (p, 0, 0))
    raw_spec = pl.BlockSpec((slot, 3 * LANES), lambda p: (0, p))
    attended, qa, ka, va, raw = pl.pallas_call(
        forward_kernel,
        grid=(pairs,),
        in_specs=[smem, whole((half, D)), whole((half, D)), column, column, column, taps_spec],
        out_specs=[pair_rows, pair_heads, pair_heads, pair_heads, raw_spec],
        out_shape=[shape((slot, local), BF16)]
        + [shape((2 * pairs, slot, LANES), BF16)] * 3
        + [shape((slot, 3 * local), BF16)],
        scratch_shapes=[pltpu.VMEM((slot, D), BF16), pltpu.VMEM((slot + 8, LANES), F32)],
        compiler_params=params(56),
        name="attention_forward",
    )(place, normed, normed_oth, query_weight, key_weight, value_weight, dconv_taps)

    att_own = lax.dynamic_slice(attended, (head * half, 0), (half, local))
    att_send = lax.dynamic_slice(attended, ((1 - head) * half, 0), (half, local))
    att_oth = swap(att_send)
    chunk = D
    wide = pl.BlockSpec((D, chunk), lambda c: (0, c))
    tall = pl.BlockSpec((chunk, D), lambda c: (c, 0))
    hd = whole((half, D))
    hl = whole((half, local))
    dl = whole((D, local))
    ld = whole((local, D))
    vec = whole((1, D))
    (
        activations, grad_hidden, gatt_own, gatt_oth, go_own, go_oth,
        ge_own, ge_oth, gr_own, gr_oth, small_second,
    ) = pl.pallas_call(
        ffn_kernel,
        grid=(units // chunk,),
        in_specs=[smem, hl, hl, hd, hd, vec, vec, ld, ld, wide, wide, tall, tall],
        out_specs=[hd, hd, hl, hl, dl, dl, wide, wide, wide, wide, whole((2, D))],
        out_shape=[
            shape((half, D), F32), shape((half, D), F32),
            shape((half, local), BF16), shape((half, local), BF16),
            shape((D, local), BF16), shape((D, local), BF16),
            shape((D, units), BF16), shape((D, units), BF16),
            shape((D, units), BF16), shape((D, units), BF16),
            shape((2, D), F32),
        ],
        scratch_shapes=[
            pltpu.VMEM((half, D), BF16), pltpu.VMEM((D, half), BF16),
            pltpu.VMEM((half, D), BF16), pltpu.VMEM((D, half), BF16),
            pltpu.VMEM((half, D), F32), pltpu.VMEM((half, D), F32), pltpu.VMEM((half, D), F32),
        ],
        compiler_params=params(60),
        name="feed_forward",
    )(
        place, att_own, att_oth, embedded, cotangent[0], row_vec(gain_second), row_vec(bias_second),
        output_weight, wo_oth, expand_weight, we_oth, reduce_weight, wr_oth,
    )
    gatt_got = swap(gatt_oth)
    rounded = lambda a, b: (a.astype(F32) + b.astype(F32)).astype(BF16)
    ge = rounded(ge_own, swap(ge_oth))
    gr = rounded(gr_own, swap(gr_oth))
    go = rounded(go_own, swap(go_oth))
    ffn_grads = jnp.concatenate([ge, gr, go], axis=1)
    ffn_share = lax.psum_scatter(ffn_grads, "inner", scatter_dimension=0, tiled=True)

    half_pair = pl.BlockSpec((half, LANES), lambda p: (0, p))
    gq, gk, gv, gtaps, first_own, first_oth = pl.pallas_call(
        backward_kernel,
        grid=(pairs,),
        in_specs=[
            smem, hd, hd, half_pair, half_pair, column, column, column, taps_spec,
            pair_rows, pair_heads, pair_heads, pair_heads, raw_spec,
        ],
        out_specs=[column, column, column, taps_spec, hd, hd],
        out_shape=[shape((D, local), BF16)] * 3
        + [shape((3, 3, local), F32), shape((half, D), F32), shape((half, D), BF16)],
        scratch_shapes=[
            pltpu.VMEM((D, slot), BF16),
            pltpu.VMEM((slot, LANES), BF16),
            pltpu.VMEM((2, slot, LANES), BF16),
            pltpu.VMEM((2, LANES, slot), F32),
            pltpu.VMEM((3, slot + 8, LANES), F32),
            pltpu.VMEM((slot, 3 * LANES), BF16),
            pltpu.VMEM((slot, D), F32),
        ],
        compiler_params=params(60),
        name="attention_backward",
    )(
        place, normed, normed_oth, gatt_own, gatt_got, query_weight, key_weight, value_weight,
        dconv_taps, attended, qa, ka, va, raw,
    )
    grad_input, small_first = pl.pallas_call(
        last_kernel,
        out_shape=(shape((half, D), F32), shape((2, D), F32)),
        compiler_params=params(48),
        name="first_norm_back",
    )(first_own, swap(first_oth), embedded, grad_hidden, row_vec(gain_first))
    qkv_share = lax.psum_scatter(
        jnp.concatenate([gq, gk, gv], axis=1), "inner", scatter_dimension=0, tiled=True
    )
    ffn_sum = lax.psum(ffn_share, "outer").astype(F32)
    qkv_sum = lax.psum(qkv_share, "outer").astype(F32)
    tap_full = lax.dynamic_update_slice(jnp.zeros((9, D), F32), gtaps.reshape(9, local), (0, head * local))
    small = jnp.concatenate([small_first, small_second, tap_full], axis=0)
    small = lax.psum(small, ("outer", "inner", "head"))
    return (
        activations[None],
        grad_input[None],
        qkv_sum[:, :local],
        qkv_sum[:, local : 2 * local],
        qkv_sum[:, 2 * local :],
        ffn_sum[:, 2 * units :].T,
        ffn_sum[:, :units],
        ffn_sum[:, units : 2 * units].T,
        small[4:13].reshape(3, 3, D),
        small[0],
        small[1],
        small[2],
        small[3],
    )


def solution(mesh):
    return jax.shard_map(
        body,
        mesh=mesh,
        in_specs=(
            P(("outer", "inner"), "head"),
            P(("outer", "inner")),
            P(None, "head"),
            P(None, "head"),
            P(None, "head"),
            P("head", None),
            P(None, "head"),
            P("head", None),
            P(None, None, "head"),
            P(),
            P(),
            P(),
            P(),
            P(("outer", "inner"), "head", None),
        ),
        out_specs=(
            P(("outer", "inner"), "head", None),
            P(("outer", "inner"), "head", None),
            P("inner", "head"),
            P("inner", "head"),
            P("inner", "head"),
            P("head", "inner"),
            P("inner", "head"),
            P("head", "inner"),
            P(),
            P(),
            P(),
            P(),
            P(),
        ),
        check_vma=False,
    )
```

```python
import functools
import math

import jax
import jax.numpy as jnp
from jax import lax
from jax.experimental import pallas as pl
from jax.experimental.pallas import tpu as pltpu
from jax.sharding import PartitionSpec as P

HEAD_DIM = 64
D = 768
BLOCK = 256
LANES = 128
EPS = 1e-05
MODULUS = 32749
NEGATIVE = -1e30
SCALE = HEAD_DIM ** (-0.5)
F32 = jnp.float32
BF16 = jnp.bfloat16
MIB = 1024 * 1024

SINE = (
    4.442882913726386,
    -7.308248583654593,
    3.606466623722958,
    -0.8474403474577161,
    0.11605422299047748,
    -0.010267162611370253,
    0.0005523348366953617,
)


def dot(a, b):
    return lax.dot_general(a, b, (((1,), (0,)), ((), ())), preferred_element_type=F32)


def dot_nt(a, b):
    return lax.dot_general(a, b, (((1,), (1,)), ((), ())), preferred_element_type=F32)


def whole(shape):
    return pl.BlockSpec(shape, lambda *_: (0,) * len(shape))


def normalise(values):
    centre = values - jnp.mean(values, axis=-1, keepdims=True)
    spread = jnp.mean(centre * centre, axis=-1, keepdims=True)
    scale = lax.rsqrt(spread + EPS)
    return centre * scale, scale


def norm_back(grad, hat, scale, gain):
    q = grad * gain
    mean_q = jnp.mean(q, axis=-1, keepdims=True)
    mean_qh = jnp.mean(q * hat, axis=-1, keepdims=True)
    return scale * (q - mean_q - hat * mean_qh)


def lane_ids(rows):
    return lax.broadcasted_iota(jnp.int32, (rows, LANES), 1)


def split_three(column):
    high = column.astype(BF16).astype(F32)
    rest = column - high
    middle = rest.astype(BF16).astype(F32)
    return high, middle, rest - middle


def with_parts(base, lane, offset, column):
    high, middle, small = split_three(column)
    base = jnp.where(lane == offset + 1, high, base)
    base = jnp.where(lane == offset + 2, middle, base)
    return jnp.where(lane == offset + 3, small, base)


def remote(src, dst, send, recv, **place):
    return pltpu.make_async_remote_copy(
        src_ref=src, dst_ref=dst, send_sem=send, recv_sem=recv,
        device_id=place, device_id_type=pl.DeviceIdType.MESH,
    )


def greet(*places):
    barrier = pltpu.get_barrier_semaphore()
    for place in places:
        pl.semaphore_signal(barrier, inc=1, device_id=place, device_id_type=pl.DeviceIdType.MESH)
    pl.semaphore_wait(barrier, len(places))


def rows_of(which, half):
    return pl.ds(pl.multiple_of(which * half, half), half)


def embed_rows(tok_ref, gain_ref, bias_ref, emb_ref, normed_ref, base, first):
    tokens = jnp.broadcast_to(tok_ref[:, pl.ds(first, LANES)], (LANES, LANES)).T
    parts = []
    for c in range(D // LANES):
        column = lax.broadcasted_iota(jnp.int32, (1, LANES), 1) + c * LANES
        product = tokens * (column + 1) + column * column
        turns = jnp.floor(product.astype(F32) * (1.0 / MODULUS) + 0.5)
        left = product - turns.astype(jnp.int32) * MODULUS
        u = left.astype(F32) * (2.0 / MODULUS)
        z = u * u
        value = jnp.full_like(u, SINE[-1])
        for coefficient in SINE[-2::-1]:
            value = value * z + coefficient
        parts.append(value * u)
    embedded = jnp.concatenate(parts, axis=1)
    emb_ref[pl.ds(first, LANES), :] = embedded
    hat, _ = normalise(embedded)
    rows = pl.ds(pl.multiple_of(base + first, LANES), LANES)
    normed_ref[rows, :] = (hat * gain_ref[...] + bias_ref[...]).astype(BF16)


PIECES = 3


def forward_kernel(
    len_ref, tok_ref, gain_ref, bias_ref, wq_ref, wk_ref, wv_ref, taps_ref,
    att_ref, qa_ref, ka_ref, va_ref, raw_ref, emb_ref, nt_ref, att_own_ref, att_oth_ref,
    normed_ref, shift_ref, give_ref, got_ref, row_send, row_recv, att_send, att_recv,
):
    slot = att_ref.shape[0]
    half = slot // 2
    step = pl.program_id(0)
    head = lax.axis_index("head")
    partner = 1 - head
    piece = half // PIECES

    def row_copy(k):
        rows = pl.ds(pl.multiple_of(head * half + k * piece, piece), piece)
        return remote(normed_ref.at[rows], normed_ref.at[rows], row_send.at[k], row_recv.at[k], head=partner)

    def att_copy(p):
        return remote(give_ref.at[p], got_ref.at[p], att_send.at[p], att_recv.at[p], head=partner)

    @pl.when(step == 0)
    def _():
        greet({"head": partner})
        base = head * half
        for k in range(PIECES):
            def embed_step(i, _):
                first = pl.multiple_of(k * piece + i * LANES, LANES)
                embed_rows(tok_ref, gain_ref, bias_ref, emb_ref, normed_ref, base, first)
                return 0

            lax.fori_loop(0, piece // LANES, embed_step, 0)
            row_copy(k).start()
        nt_ref[:, rows_of(head, half)] = normed_ref[rows_of(head, half), :].T
        shift_ref[0:8, :] = jnp.zeros((8, LANES), F32)
        for k in range(PIECES):
            row_copy(k).wait()
        nt_ref[:, rows_of(partner, half)] = normed_ref[rows_of(partner, half), :].T

    lane = lane_ids(slot)
    mixed = []
    for j, w_ref in enumerate((wq_ref, wk_ref, wv_ref)):
        raw = dot(normed_ref[...], w_ref[...])
        raw_ref[:, j * LANES : (j + 1) * LANES] = raw.astype(BF16)
        shift_ref[8 : 8 + slot, :] = raw
        one = shift_ref[7 : 7 + slot, :]
        two = shift_ref[6 : 6 + slot, :]
        value = taps_ref[j, 0:1, :] * raw + taps_ref[j, 1:2, :] * one + taps_ref[j, 2:3, :] * two
        mixed.append(value * SCALE if j == 0 else value)
    row = lax.broadcasted_iota(jnp.int32, (slot, 1), 0)
    key_bias = jnp.where(row < len_ref[0], 0.0, NEGATIVE)
    for e in range(2):
        mine = (lane // HEAD_DIM) == e
        other = HEAD_DIM * (1 - e)
        ones = jnp.where((lane > other) & (lane < other + 4), 1.0, 0.0)
        qa_ref[e] = jnp.where(mine, mixed[0], jnp.where(lane == other, 1.0, 0.0)).astype(BF16)
        ka_ref[e] = jnp.where(mine, mixed[1], jnp.where(lane == other, key_bias, ones)).astype(BF16)
        va_ref[e] = jnp.where(mine, mixed[2], ones).astype(BF16)
    block_lane = lane_ids(BLOCK)
    causal = lax.broadcasted_iota(jnp.int32, (BLOCK, BLOCK), 1) <= lax.broadcasted_iota(
        jnp.int32, (BLOCK, BLOCK), 0
    )
    for i in range(slot // BLOCK):
        rows = slice(i * BLOCK, (i + 1) * BLOCK)
        before = i * BLOCK
        heads = []
        for e in range(2):
            other = HEAD_DIM * (1 - e)
            query = qa_ref[e, rows, :]
            diagonal = jnp.where(causal, dot_nt(query, ka_ref[e, rows, :]), NEGATIVE)
            row_max = jnp.max(diagonal, axis=1, keepdims=True)
            if before:
                scores = dot_nt(query, ka_ref[e, :before, :])
                row_max = jnp.maximum(row_max, jnp.max(scores, axis=1, keepdims=True))
            out = dot(jnp.exp(diagonal - row_max).astype(BF16), va_ref[e, rows, :])
            if before:
                out += dot(jnp.exp(scores - row_max).astype(BF16), va_ref[e, :before, :])
            total = out[:, other + 1 : other + 2]
            heads.append(out / total)
            log_norm = -(row_max + jnp.log(total))
            qa_ref[e, rows, :] = with_parts(query.astype(F32), block_lane, other, log_norm).astype(BF16)
        att_ref[rows, :] = jnp.where(block_lane < HEAD_DIM, heads[0], heads[1]).astype(BF16)

    for p in range(att_own_ref.shape[1] // LANES):
        @pl.when(step == p)
        def _():
            give_ref[p] = att_ref[rows_of(partner, half), :]
            att_copy(p).start()
            att_own_ref[:, p * LANES : (p + 1) * LANES] = att_ref[rows_of(head, half), :]

    @pl.when(step == pl.num_programs(0) - 1)
    def _():
        for p in range(att_own_ref.shape[1] // LANES):
            att_copy(p).wait()
            att_oth_ref[:, p * LANES : (p + 1) * LANES] = got_ref[p]


def ffn_kernel(
    len_ref, att_own_ref, att_oth_ref, emb_ref, cot_ref, gain_ref, bias_ref,
    wo_own_ref, wo_oth_ref, we_own_ref, we_oth_ref, wr_own_ref, wr_oth_ref,
    act_ref, gh_ref, gatt_own_ref, gatt_oth_ref, go_ref, ge_ref, gr_ref, small_ref,
    n2_ref, n2t_ref, gl_ref, glt_ref, hid_ref, ffn_ref, gn_ref,
    give_ref, got_ref, give_att, got_att, give_go, got_go, send_sem, recv_sem, last_send, last_recv,
):
    half = emb_ref.shape[0]
    step = pl.program_id(0)
    head = lax.axis_index("head")
    partner = 1 - head
    row = lax.broadcasted_iota(jnp.int32, (half, 1), 0) + head * half
    valid = row < len_ref[0]

    @pl.when(step == 0)
    def _():
        greet({"head": partner})
        hidden = emb_ref[...] + dot(att_own_ref[...], wo_own_ref[...]) + dot(att_oth_ref[...], wo_oth_ref[...])
        hid_ref[...] = hidden
        hat, _ = normalise(hidden)
        normed = hat * gain_ref[...] + bias_ref[...]
        n2_ref[...] = normed.astype(BF16)
        n2t_ref[...] = normed.astype(BF16).T
        grad = jnp.where(valid, cot_ref[...], 0.0)
        gl_ref[...] = grad.astype(BF16)
        glt_ref[...] = grad.astype(BF16).T
        ffn_ref[...] = jnp.zeros_like(ffn_ref)
        gn_ref[...] = jnp.zeros_like(gn_ref)

    def grad_copy(c, kind):
        return remote(
            give_ref.at[c, kind], got_ref.at[c, kind], send_sem.at[c, kind], recv_sem.at[c, kind], head=partner
        )

    def ffn_part(we_ref, wr_ref, put_r, put_e):
        relu = jnp.maximum(dot(n2_ref[...], we_ref[...]), 0.0)
        squared = (relu * relu).astype(BF16)
        put_r(dot(glt_ref[...], squared).astype(BF16))
        grad_e = (dot_nt(gl_ref[...], wr_ref[...]) * (2.0 * relu)).astype(BF16)
        put_e(dot(n2t_ref[...], grad_e).astype(BF16))
        gn_ref[...] += dot_nt(grad_e, we_ref[...])
        ffn_ref[...] += dot(squared, wr_ref[...])

    def give(kind):
        def put(value):
            give_ref[step, kind] = value
            grad_copy(step, kind).start()

        return put

    width = ge_ref.shape[2]

    def keep(ref):
        def put(value):
            for k in range(ref.shape[0]):
                ref[k] = value[:, k * width : (k + 1) * width]

        return put

    ffn_part(we_oth_ref, wr_oth_ref, give(0), give(1))
    ffn_part(we_own_ref, wr_own_ref, keep(gr_ref), keep(ge_ref))
    for kind, ref in enumerate((gr_ref, ge_ref)):
        grad_copy(step, kind).wait()
        for k in range(ref.shape[0]):
            ref[k] = ref[k] + got_ref[step, kind, :, k * width : (k + 1) * width]

    @pl.when(step == pl.num_programs(0) - 1)
    def _():
        hidden = hid_ref[...]
        act_ref[...] = hidden + ffn_ref[...]
        hat, scale = normalise(hidden)
        grad_n = gn_ref[...]
        small_ref[0:1, :] = jnp.sum(grad_n * hat, axis=0, keepdims=True)
        small_ref[1:2, :] = jnp.sum(grad_n, axis=0, keepdims=True)
        grad_h = jnp.where(valid, cot_ref[...], 0.0) + norm_back(grad_n, hat, scale, gain_ref[...])
        gh_ref[...] = grad_h
        low = grad_h.astype(BF16)
        give_att[...] = dot_nt(low, wo_oth_ref[...]).astype(BF16)
        att_copy = remote(give_att, got_att, last_send.at[0], last_recv.at[0], head=partner)
        att_copy.start()
        low_t = low.T
        give_go[...] = dot(low_t, att_oth_ref[...]).astype(BF16)
        go_copy = remote(give_go, got_go, last_send.at[1], last_recv.at[1], head=partner)
        go_copy.start()
        gatt_own_ref[...] = dot_nt(low, wo_own_ref[...]).astype(BF16)
        grad_o = dot(low_t, att_own_ref[...]).astype(BF16)
        att_copy.wait()
        gatt_oth_ref[...] = got_att[...]
        go_copy.wait()
        go_ref[0] = grad_o + got_go[...]


def backward_kernel(
    inner_bits, outer,
    gown_ref, goth_ref, wq_ref, wk_ref, wv_ref, taps_ref,
    att_ref, qa_ref, ka_ref, va_ref, raw_ref, second_ref, gain_ref,
    nt_hbm, emb_hbm, gh_hbm, ge_hbm, gr_hbm, go_hbm,
    sum_ref, small_ref, gin_hbm,
    nt_ref, do_ref, doa_ref, dqt_ref, mix_ref, all_ref, wcat_ref, emb_ref, gh_ref,
    give_first, got_first, own_first, g_ref, rz_ref, rc_ref, acc_ref, got_small,
    load_sem, first_sem, send_sem, recv_sem, small_send, small_recv, *halves,
):
    slot = att_ref.shape[0]
    half = slot // 2
    step = pl.program_id(0)
    pairs = sum_ref.shape[0] - ge_hbm.shape[0] - gr_hbm.shape[0] - go_hbm.shape[0]
    blocks = slot // BLOCK
    width = sum_ref.shape[2]
    head = lax.axis_index("head")
    partner = 1 - head
    mine = lax.axis_index("inner")
    line = lax.axis_index("outer")
    centre = outer // 2
    left = line < centre
    depth = jnp.where(left, centre - 1 - line, line - centre)
    inward = jnp.where(left, line + 1, line - 1)
    outward = jnp.where(left, line - 1, line + 1)
    bit = [(mine // (1 << b)) % 2 for b in range(inner_bits)]
    across = [mine + (1 << b) * (1 - 2 * bit[b]) for b in range(inner_bits)]

    sources = [(ref, k) for pair in zip(range(ge_hbm.shape[0]), range(gr_hbm.shape[0])) for ref, k in ((gr_hbm, pair[0]), (ge_hbm, pair[1]))]
    sources.append((go_hbm, 0))
    fed = len(sources)
    entries = [(c, 0, width, c % 2) for c in range(fed + pairs - 1)]
    entries += [(fed + pairs - 1, 0, 256, 0), (fed + pairs - 1, 256, width - 256, 1)]
    order_of = [tuple((b + first) % inner_bits for b in range(inner_bits)) for first in range(2)]
    line_steps = 2 * centre - 1
    stage_count = inner_bits + line_steps + 1

    def index_of(fixed):
        return tuple(fixed.get(b, slice(None)) for b in reversed(range(inner_bits)))

    def lanes(entry):
        return slice(entry[1], entry[1] + entry[2])

    def halving(n, s):
        c, _, _, kind = entries[n]
        order = order_of[kind]
        fixed = {b: bit[b] for b in order[:s]}
        b = order[s]
        give = g_ref.at[(c,) + index_of({**fixed, b: 1 - bit[b]}) + (slice(None), lanes(entries[n]))]
        land = halves[s].at[(c,) + (slice(None),) * (inner_bits - 1 - s) + (slice(None), lanes(entries[n]))]
        return remote(give, land, send_sem.at[n, s], recv_sem.at[n, s], inner=across[b])

    def add_half(n, s):
        c, _, _, kind = entries[n]
        order = order_of[kind]
        index = (c,) + index_of({b: bit[b] for b in order[: s + 1]}) + (slice(None), lanes(entries[n]))
        land = (c,) + (slice(None),) * (inner_bits - 1 - s) + (slice(None), lanes(entries[n]))
        g_ref[index] = g_ref[index] + halves[s][land]

    def own(n):
        return (entries[n][0],) + tuple(bit[b] for b in reversed(range(inner_bits))) + (slice(None), lanes(entries[n]))

    def flat(n):
        return (entries[n][0], slice(None), lanes(entries[n]))

    def line_copy(n, t):
        s = inner_bits + t
        sems = (send_sem.at[n, s], recv_sem.at[n, s])
        if t < centre - 1:
            return remote(g_ref.at[own(n)], rz_ref.at[flat(n)], *sems, outer=inward)
        if t == centre - 1:
            return remote(g_ref.at[own(n)], rc_ref.at[flat(n)], *sems, outer=inward)
        return remote(rc_ref.at[flat(n)], rc_ref.at[flat(n)], *sems, outer=outward)

    def line_start(n, t):
        if t < centre - 1:
            sender = depth == centre - 1 - t
        elif t == centre - 1:
            sender = depth == 0
        else:
            sender = depth == t - centre
        pl.when(sender)(lambda: line_copy(n, t).start())

    def line_finish(n, t):
        if t < centre - 1:
            @pl.when(depth == centre - 2 - t)
            def _():
                line_copy(n, t).wait_recv()
                g_ref[own(n)] = g_ref[own(n)] + rz_ref[flat(n)]
        elif t == centre - 1:
            @pl.when(depth == 0)
            def _():
                line_copy(n, t).wait_recv()
                rc_ref[flat(n)] = g_ref[own(n)] + rc_ref[flat(n)]
        else:
            pl.when(depth == t - centre + 1)(lambda: line_copy(n, t).wait_recv())

    def load_chunk(c):
        ref, k = sources[c]
        return pltpu.make_async_copy(ref.at[k], g_ref.at[c], load_sem.at[3 + c])

    def advance(n, stage):
        if 0 < stage <= inner_bits:
            halving(n, stage - 1).wait_recv()
            add_half(n, stage - 1)
        elif stage > inner_bits:
            line_finish(n, stage - inner_bits - 1)
        if stage == 0 and entries[n][0] < fed:
            load_chunk(entries[n][0]).wait()
        if stage < inner_bits:
            halving(n, stage).start()
        elif stage < stage_count - 1:
            line_start(n, stage - inner_bits)
        else:
            sum_ref[flat(n)] = rc_ref[flat(n)]

    def drain(n):
        for s in range(inner_bits):
            halving(n, s).wait_send()
        for t in range(line_steps):
            if t < centre - 1:
                sender = depth == centre - 1 - t
            elif t == centre - 1:
                sender = depth == 0
            else:
                sender = depth == t - centre
            pl.when(sender)(lambda t=t: line_copy(n, t).wait_send())

    tail_tick = pairs * blocks
    plan = {}
    for n, (c, _, _, _) in enumerate(entries):
        begin = 2 * (c - c % 2) if c < fed else (c - fed + 1) * blocks
        for stage in range(stage_count):
            plan.setdefault(begin + (0 if stage == 0 else 1 + 2 * stage), []).append((n, stage))
    ready = fed + pairs

    def tick(now):
        for n, stage in plan.get(now, ()):
            advance(n, stage)

    def small_copy(k):
        sems = (small_send.at[k], small_recv.at[k])
        if k == 0:
            return remote(acc_ref.at[0], got_small.at[0], *sems, head=partner)
        if k <= inner_bits:
            return remote(acc_ref.at[k], got_small.at[k], *sems, inner=across[k - 1])
        t = k - 1 - inner_bits
        if t <= centre - 1:
            return remote(acc_ref.at[inner_bits + 1], got_small.at[inner_bits + 1 + (t == centre - 1)], *sems, outer=inward)
        last = got_small.at[inner_bits + 2]
        return remote(last, last, *sems, outer=outward)

    def small_step(k):
        if 0 < k <= inner_bits + 1:
            small_copy(k - 1).wait_recv()
            acc_ref[k] = acc_ref[k - 1] + got_small[k - 1]
        elif k > inner_bits + 1:
            t = k - 2 - inner_bits
            if t < centre - 1:
                @pl.when(depth == centre - 2 - t)
                def _():
                    small_copy(k - 1).wait_recv()
                    acc_ref[inner_bits + 1] = acc_ref[inner_bits + 1] + got_small[inner_bits + 1]
            elif t == centre - 1:
                @pl.when(depth == 0)
                def _():
                    small_copy(k - 1).wait_recv()
                    got_small[inner_bits + 2] = acc_ref[inner_bits + 1] + got_small[inner_bits + 2]
            else:
                pl.when(depth == t - centre + 1)(lambda: small_copy(k - 1).wait_recv())
        if k <= inner_bits:
            small_copy(k).start()
        elif k <= inner_bits + line_steps:
            pl.when(small_sender(k))(lambda: small_copy(k).start())
        else:
            small_ref[...] = got_small[inner_bits + 2]

    def small_sender(k):
        t = k - 1 - inner_bits
        if t < centre - 1:
            return depth == centre - 1 - t
        if t == centre - 1:
            return depth == 0
        return depth == t - centre

    small_steps = inner_bits + line_steps + 2

    nt_load = pltpu.make_async_copy(nt_hbm, nt_ref, load_sem.at[0])
    emb_load = pltpu.make_async_copy(emb_hbm, emb_ref, load_sem.at[1])
    gh_load = pltpu.make_async_copy(gh_hbm, gh_ref, load_sem.at[2])

    @pl.when(step == 0)
    def _():
        for c in range(fed):
            load_chunk(c).start()
        nt_load.start()
        emb_load.start()
        gh_load.start()
        barrier = pltpu.get_barrier_semaphore()
        places = [{"head": partner}] + [{"inner": a} for a in across]
        for place in places:
            pl.semaphore_signal(barrier, inc=1, device_id=place, device_id_type=pl.DeviceIdType.MESH)
        for there, away in ((line > 0, line - 1), (line < outer - 1, line + 1)):
            @pl.when(there)
            def _():
                pl.semaphore_signal(
                    barrier, inc=1, device_id={"outer": away}, device_id_type=pl.DeviceIdType.MESH
                )
        beside = jnp.where(line > 0, 1, 0) + jnp.where(line < outer - 1, 1, 0)
        pl.semaphore_wait(barrier, len(places) + beside)
        mix_ref[:, slot : slot + 8, :] = jnp.zeros((3, 8, LANES), F32)
        acc_ref[0] = jnp.zeros(acc_ref.shape[1:], F32)
        acc_ref[0, 2:4, :] = second_ref[...]

    do_ref[rows_of(head, half), :] = gown_ref[...]
    do_ref[rows_of(partner, half), :] = goth_ref[...]
    lane = lane_ids(slot)
    grad_out = do_ref[...].astype(F32)
    product = grad_out * att_ref[...].astype(F32)
    for e in range(2):
        in_head = (lane // HEAD_DIM) == e
        delta = -jnp.sum(jnp.where(in_head, product, 0.0), axis=1, keepdims=True)
        other = HEAD_DIM * (1 - e)
        doa_ref[e] = with_parts(jnp.where(in_head, grad_out, 0.0), lane, other, delta).astype(BF16)
    causal = lax.broadcasted_iota(jnp.int32, (BLOCK, BLOCK), 0) <= lax.broadcasted_iota(
        jnp.int32, (BLOCK, BLOCK), 1
    )
    block_lane = lane_ids(BLOCK)
    dqt_ref[...] = jnp.zeros_like(dqt_ref)
    for j in range(blocks):
        for p in range(pairs):
            pl.when(step == p)(functools.partial(tick, p * blocks + j))
        keys = slice(j * BLOCK, (j + 1) * BLOCK)
        first = j * BLOCK
        after = first + BLOCK
        dks, dvs = [], []
        for e in range(2):
            ka = ka_ref[e, keys, :]
            va = va_ref[e, keys, :]
            kat = ka.T
            spans = [(first, after, True)] + ([(after, slot, False)] if after < slot else [])
            dk = dv = None
            for lo, hi, masked in spans:
                scores = dot_nt(ka, qa_ref[e, lo:hi, :])
                if masked:
                    scores = jnp.where(causal, scores, NEGATIVE)
                probs = jnp.exp(scores)
                grads = (probs * dot_nt(va, doa_ref[e, lo:hi, :])).astype(BF16)
                dv_part = dot(probs.astype(BF16), doa_ref[e, lo:hi, :])
                dk_part = dot(grads, qa_ref[e, lo:hi, :])
                dv = dv_part if dv is None else dv + dv_part
                dk = dk_part if dk is None else dk + dk_part
                dqt_ref[e, :, lo:hi] += dot(kat, grads)
            dks.append(dk)
            dvs.append(dv)
        mix_ref[1, keys, :] = jnp.where(block_lane < HEAD_DIM, dks[0], dks[1])
        mix_ref[2, keys, :] = jnp.where(block_lane < HEAD_DIM, dvs[0], dvs[1])
    sub = lax.broadcasted_iota(jnp.int32, (LANES, slot), 0)
    mix_ref[0, 0:slot, :] = (jnp.where(sub < HEAD_DIM, dqt_ref[0], dqt_ref[1]) * SCALE).T

    local = pairs * LANES
    for p in range(pairs):
        @pl.when(step == p)
        def _():
            base = p * 3 * LANES
            if p == 0:
                nt_load.wait()
            for j, w_ref in enumerate((wq_ref, wk_ref, wv_ref)):
                zero = mix_ref[j, 0:slot, :]
                one = mix_ref[j, 1 : 1 + slot, :]
                two = mix_ref[j, 2 : 2 + slot, :]
                raw = raw_ref[:, j * LANES : (j + 1) * LANES].astype(F32)
                cols = pl.ds(pl.multiple_of(head * local + p * LANES, LANES), LANES)
                for s, moved in enumerate((zero, one, two)):
                    total = jnp.sum(moved * raw, axis=0, keepdims=True)
                    acc_ref[0, 4 + 3 * j + s : 5 + 3 * j + s, cols] = total
                value = taps_ref[j, 0:1, :] * zero + taps_ref[j, 1:2, :] * one + taps_ref[j, 2:3, :] * two
                all_ref[:, base + j * LANES : base + (j + 1) * LANES] = value.astype(BF16)
                wcat_ref[:, base + j * LANES : base + (j + 1) * LANES] = w_ref[...]
            grads = dot(nt_ref[...], all_ref[:, base : base + 3 * LANES]).astype(BF16)
            g_ref[fed + p] = grads.reshape(g_ref.shape[1:])

    @pl.when(step == pairs - 1)
    def _():
        tick(tail_tick)
        give_first[...] = dot_nt(all_ref[rows_of(partner, half), :], wcat_ref[...]).astype(BF16)
        first_copy = remote(give_first, got_first, first_sem.at[0], first_sem.at[1], head=partner)
        first_copy.start()
        tick(tail_tick + 1)
        own_first[...] = dot_nt(all_ref[rows_of(head, half), :], wcat_ref[...])
        tick(tail_tick + 2)
        emb_load.wait()
        gh_load.wait()
        tick(tail_tick + 3)
        first_copy.wait()
        grad_n = own_first[...] + got_first[...].astype(F32)
        hat, scale = normalise(emb_ref[...])
        acc_ref[0, 0:1, :] = jnp.sum(grad_n * hat, axis=0, keepdims=True)
        acc_ref[0, 1:2, :] = jnp.sum(grad_n, axis=0, keepdims=True)
        gh_ref[...] = gh_ref[...] + norm_back(grad_n, hat, scale, gain_ref[...])
        gin_store = pltpu.make_async_copy(gh_ref, gin_hbm, load_sem.at[0])
        gin_store.start()
        small_step(0)
        now, k = tail_tick + 4, 1
        while now <= max(plan) or k < small_steps:
            tick(now)
            if k < small_steps:
                small_step(k)
            now, k = now + 1, k + 1
        gin_store.wait()
        for n in range(len(entries)):
            drain(n)
        for k in range(inner_bits + 1):
            small_copy(k).wait_send()
        for k in range(inner_bits + 1, inner_bits + 1 + line_steps):
            pl.when(small_sender(k))(lambda k=k: small_copy(k).wait_send())


def params(vmem, **kw):
    return pltpu.CompilerParams(vmem_limit_bytes=vmem * MIB, **kw)


def body(
    token_ids, lengths, query_weight, key_weight, value_weight, output_weight,
    expand_weight, reduce_weight, dconv_taps, gain_first, bias_first,
    gain_second, bias_second, cotangent,
):
    half = token_ids.shape[1]
    slot = 2 * half
    local = query_weight.shape[1]
    units = expand_weight.shape[1]
    pairs = local // LANES
    outer = lax.axis_size("outer")
    inner = lax.axis_size("inner")
    inner_bits = inner.bit_length() - 1
    rows = D // inner
    width = 3 * LANES

    def swap(value):
        return lax.ppermute(value, "head", [(0, 1), (1, 0)])

    shape = jax.ShapeDtypeStruct
    row_vec = lambda v: v.reshape(1, D)
    smem = pl.BlockSpec(memory_space=pltpu.SMEM)
    anywhere = pl.BlockSpec(memory_space=pl.ANY)
    dma = pltpu.SemaphoreType.DMA
    hd = whole((half, D))
    hl = whole((half, local))
    ld = whole((local, D))
    vec = whole((1, D))
    we_oth, wr_oth, wo_oth = swap(expand_weight), swap(reduce_weight), swap(output_weight)

    column = pl.BlockSpec((D, LANES), lambda p: (0, p))
    taps_spec = pl.BlockSpec((3, 3, LANES), lambda p: (0, 0, p))
    pair_rows = pl.BlockSpec((slot, LANES), lambda p: (0, p))
    pair_heads = pl.BlockSpec((2, slot, LANES), lambda p: (p, 0, 0))
    raw_spec = pl.BlockSpec((slot, 3 * LANES), lambda p: (0, p))
    attended, qa, ka, va, raw, embedded, normed_t, att_own, att_oth = pl.pallas_call(
        forward_kernel,
        grid=(pairs,),
        in_specs=[smem, whole((1, half)), vec, vec, column, column, column, taps_spec],
        out_specs=[pair_rows, pair_heads, pair_heads, pair_heads, raw_spec, hd, whole((D, slot)), hl, hl],
        out_shape=[shape((slot, local), BF16)]
        + [shape((2 * pairs, slot, LANES), BF16)] * 3
        + [shape((slot, 3 * local), BF16), shape((half, D), F32), shape((D, slot), BF16)]
        + [shape((half, local), BF16)] * 2,
        scratch_shapes=[
            pltpu.VMEM((slot, D), BF16),
            pltpu.VMEM((slot + 8, LANES), F32),
            pltpu.VMEM((pairs, half, LANES), BF16),
            pltpu.VMEM((pairs, half, LANES), BF16),
            dma((PIECES,)), dma((PIECES,)), dma((pairs,)), dma((pairs,)),
        ],
        compiler_params=params(58, collective_id=0, has_side_effects=True),
        name="attention_forward",
    )(
        lengths, token_ids, row_vec(gain_first), row_vec(bias_first),
        query_weight, key_weight, value_weight, dconv_taps,
    )

    chunk = D
    wide = pl.BlockSpec((D, chunk), lambda c: (0, c))
    tall = pl.BlockSpec((chunk, D), lambda c: (c, 0))
    steps = units // chunk
    split = chunk // width
    grad_spec = pl.BlockSpec((split, D, width), lambda c: (c, 0, 0))
    (
        activations, grad_hidden, gatt_own, gatt_oth, go, ge, gr, small_second,
    ) = pl.pallas_call(
        ffn_kernel,
        grid=(steps,),
        in_specs=[smem, hl, hl, hd, hd, vec, vec, ld, ld, wide, wide, tall, tall],
        out_specs=[hd, hd, hl, hl, whole((1, D, local)), grad_spec, grad_spec, whole((2, D))],
        out_shape=[
            shape((half, D), F32), shape((half, D), F32),
            shape((half, local), BF16), shape((half, local), BF16),
            shape((1, D, local), BF16),
            shape((steps * split, D, width), BF16), shape((steps * split, D, width), BF16),
            shape((2, D), F32),
        ],
        scratch_shapes=[
            pltpu.VMEM((half, D), BF16), pltpu.VMEM((D, half), BF16),
            pltpu.VMEM((half, D), BF16), pltpu.VMEM((D, half), BF16),
            pltpu.VMEM((half, D), F32), pltpu.VMEM((half, D), F32), pltpu.VMEM((half, D), F32),
            pltpu.VMEM((steps, 2, D, chunk), BF16), pltpu.VMEM((steps, 2, D, chunk), BF16),
            pltpu.VMEM((half, local), BF16), pltpu.VMEM((half, local), BF16),
            pltpu.VMEM((D, local), BF16), pltpu.VMEM((D, local), BF16),
            dma((steps, 2)), dma((steps, 2)), dma((2,)), dma((2,)),
        ],
        compiler_params=params(62, collective_id=1, has_side_effects=True),
        name="feed_forward",
    )(
        lengths, att_own, att_oth, embedded, cotangent[0], row_vec(gain_second), row_vec(bias_second),
        output_weight, wo_oth, expand_weight, we_oth, reduce_weight, wr_oth,
    )

    half_pair = pl.BlockSpec((half, LANES), lambda p: (0, p))
    fed = 2 * steps * split + 1
    chunks = fed + pairs
    twos = (2,) * inner_bits
    cut = lambda g: g.reshape((g.shape[0],) + twos + (rows, width))
    line_stages = inner_bits + outer
    sums, small, grad_input = pl.pallas_call(
        functools.partial(backward_kernel, inner_bits, outer),
        grid=(pairs,),
        in_specs=[
            half_pair, half_pair, column, column, column, taps_spec,
            pair_rows, pair_heads, pair_heads, pair_heads, raw_spec, whole((2, D)), vec,
        ]
        + [anywhere] * 6,
        out_specs=[whole((chunks, rows, width)), whole((16, D)), anywhere],
        out_shape=[shape((chunks, rows, width), BF16), shape((16, D), F32), shape((half, D), F32)],
        scratch_shapes=[
            pltpu.VMEM((D, slot), BF16),
            pltpu.VMEM((slot, LANES), BF16),
            pltpu.VMEM((2, slot, LANES), BF16),
            pltpu.VMEM((2, LANES, slot), F32),
            pltpu.VMEM((3, slot + 8, LANES), F32),
            pltpu.VMEM((slot, 3 * local), BF16),
            pltpu.VMEM((D, 3 * local), BF16),
            pltpu.VMEM((half, D), F32),
            pltpu.VMEM((half, D), F32),
            pltpu.VMEM((half, D), BF16),
            pltpu.VMEM((half, D), BF16),
            pltpu.VMEM((half, D), F32),
            pltpu.VMEM((chunks,) + twos + (rows, width), BF16),
            pltpu.VMEM((chunks, rows, width), BF16),
            pltpu.VMEM((chunks, rows, width), BF16),
            pltpu.VMEM((inner_bits + 2, 16, D), F32),
            pltpu.VMEM((inner_bits + 3, 16, D), F32),
            dma((3 + fed,)), dma((2,)),
            dma((chunks + 1, line_stages)), dma((chunks + 1, line_stages)),
            dma((line_stages + 1,)), dma((line_stages + 1,)),
        ]
        + [pltpu.VMEM((chunks,) + (2,) * (inner_bits - 1 - s) + (rows, width), BF16) for s in range(inner_bits)],
        compiler_params=params(62, collective_id=2, has_side_effects=True),
        name="attention_backward",
    )(
        gatt_own, gatt_oth, query_weight, key_weight, value_weight, dconv_taps,
        attended, qa, ka, va, raw, small_second, row_vec(gain_first),
        normed_t, embedded, grad_hidden, cut(ge), cut(gr), cut(go),
    )
    sums = sums.astype(F32)
    pieces = lambda picked: jnp.concatenate(picked, axis=1)
    many = steps * split
    gr_sum = pieces([sums[2 * c] for c in range(many)])
    ge_sum = pieces([sums[2 * c + 1] for c in range(many)])
    go_sum = sums[fed - 1]
    qkv = [pieces([sums[fed + p][:, j * LANES : (j + 1) * LANES] for p in range(pairs)]) for j in range(3)]
    return (
        activations[None],
        grad_input[None],
        qkv[0],
        qkv[1],
        qkv[2],
        go_sum.T,
        ge_sum,
        gr_sum.T,
        small[4:13].reshape(3, 3, D),
        small[0],
        small[1],
        small[2],
        small[3],
    )


def solution(mesh):
    return jax.shard_map(
        body,
        mesh=mesh,
        in_specs=(
            P(("outer", "inner"), "head"),
            P(("outer", "inner")),
            P(None, "head"),
            P(None, "head"),
            P(None, "head"),
            P("head", None),
            P(None, "head"),
            P("head", None),
            P(None, None, "head"),
            P(),
            P(),
            P(),
            P(),
            P(("outer", "inner"), "head", None),
        ),
        out_specs=(
            P(("outer", "inner"), "head", None),
            P(("outer", "inner"), "head", None),
            P("inner", "head"),
            P("inner", "head"),
            P("inner", "head"),
            P("head", "inner"),
            P("inner", "head"),
            P("head", "inner"),
            P(),
            P(),
            P(),
            P(),
            P(),
        ),
        check_vma=False,
    )
```

```python
import functools
import math

import jax
import jax.numpy as jnp
from jax import lax
from jax.experimental import pallas as pl
from jax.experimental.pallas import tpu as pltpu
from jax.sharding import PartitionSpec as P

HEAD_DIM = 64
D = 768
BLOCK = 256
LANES = 128
EPS = 1e-05
MODULUS = 32749
NEGATIVE = -1e30
SCALE = HEAD_DIM ** (-0.5)
F32 = jnp.float32
BF16 = jnp.bfloat16
MIB = 1024 * 1024

SINE = (
    4.442882913726386,
    -7.308248583654593,
    3.606466623722958,
    -0.8474403474577161,
    0.11605422299047748,
    -0.010267162611370253,
    0.0005523348366953617,
)


def dot(a, b):
    return lax.dot_general(a, b, (((1,), (0,)), ((), ())), preferred_element_type=F32)


def dot_nt(a, b):
    return lax.dot_general(a, b, (((1,), (1,)), ((), ())), preferred_element_type=F32)


def whole(shape):
    return pl.BlockSpec(shape, lambda *_: (0,) * len(shape))


def normalise(values):
    centre = values - jnp.mean(values, axis=-1, keepdims=True)
    spread = jnp.mean(centre * centre, axis=-1, keepdims=True)
    scale = lax.rsqrt(spread + EPS)
    return centre * scale, scale


def norm_back(grad, hat, scale, gain):
    q = grad * gain
    mean_q = jnp.mean(q, axis=-1, keepdims=True)
    mean_qh = jnp.mean(q * hat, axis=-1, keepdims=True)
    return scale * (q - mean_q - hat * mean_qh)


def lane_ids(rows):
    return lax.broadcasted_iota(jnp.int32, (rows, LANES), 1)


def split_three(column):
    high = column.astype(BF16).astype(F32)
    rest = column - high
    middle = rest.astype(BF16).astype(F32)
    return high, middle, rest - middle


def with_parts(base, lane, offset, column):
    high, middle, small = split_three(column)
    base = jnp.where(lane == offset + 1, high, base)
    base = jnp.where(lane == offset + 2, middle, base)
    return jnp.where(lane == offset + 3, small, base)


def remote(src, dst, send, recv, **place):
    return pltpu.make_async_remote_copy(
        src_ref=src, dst_ref=dst, send_sem=send, recv_sem=recv,
        device_id=place, device_id_type=pl.DeviceIdType.MESH,
    )


def greet(*places):
    barrier = pltpu.get_barrier_semaphore()
    for place in places:
        pl.semaphore_signal(barrier, inc=1, device_id=place, device_id_type=pl.DeviceIdType.MESH)
    pl.semaphore_wait(barrier, len(places))


def rows_of(which, half):
    return pl.ds(pl.multiple_of(which * half, half), half)


def embed_rows(tok_ref, vec_ref, emb_ref, normed_ref, base, first):
    tokens = jnp.broadcast_to(tok_ref[:, pl.ds(first, LANES)], (LANES, LANES)).T
    parts = []
    for c in range(D // LANES):
        column = lax.broadcasted_iota(jnp.int32, (1, LANES), 1) + c * LANES
        product = tokens * (column + 1) + column * column
        turns = jnp.floor(product.astype(F32) * (1.0 / MODULUS) + 0.5)
        left = product - turns.astype(jnp.int32) * MODULUS
        u = left.astype(F32) * (2.0 / MODULUS)
        z = u * u
        value = jnp.full_like(u, SINE[-1])
        for coefficient in SINE[-2::-1]:
            value = value * z + coefficient
        parts.append(value * u)
    embedded = jnp.concatenate(parts, axis=1)
    emb_ref[pl.ds(first, LANES), :] = embedded
    hat, _ = normalise(embedded)
    rows = pl.ds(pl.multiple_of(base + first, LANES), LANES)
    normed_ref[rows, :] = (hat * vec_ref[0:1, :] + vec_ref[1:2, :]).astype(BF16)


PIECES = 3


def forward_kernel(
    len_ref, tok_ref, vec_ref, wq_ref, wk_ref, wv_ref, taps_ref,
    att_ref, qa_ref, ka_ref, va_ref, raw_ref, emb_ref, nt_ref, att_own_ref, att_oth_ref,
    normed_ref, shift_ref, give_ref, got_ref, row_send, row_recv, att_send, att_recv,
):
    slot = att_ref.shape[0]
    half = slot // 2
    step = pl.program_id(0)
    head = lax.axis_index("head")
    partner = 1 - head
    piece = half // PIECES

    def row_copy(k):
        rows = pl.ds(pl.multiple_of(head * half + k * piece, piece), piece)
        return remote(normed_ref.at[rows], normed_ref.at[rows], row_send.at[k], row_recv.at[k], head=partner)

    def att_copy(p):
        return remote(give_ref.at[p], got_ref.at[p], att_send.at[p], att_recv.at[p], head=partner)

    @pl.when(step == 0)
    def _():
        greet({"head": partner})
        base = head * half
        for k in range(PIECES):
            def embed_step(i, _):
                first = pl.multiple_of(k * piece + i * LANES, LANES)
                embed_rows(tok_ref, vec_ref, emb_ref, normed_ref, base, first)
                return 0

            lax.fori_loop(0, piece // LANES, embed_step, 0)
            row_copy(k).start()
        nt_ref[:, rows_of(head, half)] = normed_ref[rows_of(head, half), :].T
        shift_ref[0:8, :] = jnp.zeros((8, LANES), F32)
        for k in range(PIECES):
            row_copy(k).wait()
        nt_ref[:, rows_of(partner, half)] = normed_ref[rows_of(partner, half), :].T

    lane = lane_ids(slot)
    mixed = []
    for j, w_ref in enumerate((wq_ref, wk_ref, wv_ref)):
        raw = dot(normed_ref[...], w_ref[...])
        raw_ref[:, j * LANES : (j + 1) * LANES] = raw.astype(BF16)
        shift_ref[8 : 8 + slot, :] = raw
        one = shift_ref[7 : 7 + slot, :]
        two = shift_ref[6 : 6 + slot, :]
        value = taps_ref[j, 0:1, :] * raw + taps_ref[j, 1:2, :] * one + taps_ref[j, 2:3, :] * two
        mixed.append(value * SCALE if j == 0 else value)
    row = lax.broadcasted_iota(jnp.int32, (slot, 1), 0)
    key_bias = jnp.where(row < len_ref[0], 0.0, NEGATIVE)
    for e in range(2):
        mine = (lane // HEAD_DIM) == e
        other = HEAD_DIM * (1 - e)
        ones = jnp.where((lane > other) & (lane < other + 4), 1.0, 0.0)
        qa_ref[e] = jnp.where(mine, mixed[0], jnp.where(lane == other, 1.0, 0.0)).astype(BF16)
        ka_ref[e] = jnp.where(mine, mixed[1], jnp.where(lane == other, key_bias, ones)).astype(BF16)
        va_ref[e] = jnp.where(mine, mixed[2], ones).astype(BF16)
    block_lane = lane_ids(BLOCK)
    causal = lax.broadcasted_iota(jnp.int32, (BLOCK, BLOCK), 1) <= lax.broadcasted_iota(
        jnp.int32, (BLOCK, BLOCK), 0
    )
    for i in range(slot // BLOCK):
        rows = slice(i * BLOCK, (i + 1) * BLOCK)
        before = i * BLOCK
        heads = []
        for e in range(2):
            other = HEAD_DIM * (1 - e)
            query = qa_ref[e, rows, :]
            diagonal = jnp.where(causal, dot_nt(query, ka_ref[e, rows, :]), NEGATIVE)
            row_max = jnp.max(diagonal, axis=1, keepdims=True)
            if before:
                scores = dot_nt(query, ka_ref[e, :before, :])
                row_max = jnp.maximum(row_max, jnp.max(scores, axis=1, keepdims=True))
            out = dot(jnp.exp(diagonal - row_max).astype(BF16), va_ref[e, rows, :])
            if before:
                out += dot(jnp.exp(scores - row_max).astype(BF16), va_ref[e, :before, :])
            total = out[:, other + 1 : other + 2]
            heads.append(out / total)
            log_norm = -(row_max + jnp.log(total))
            qa_ref[e, rows, :] = with_parts(query.astype(F32), block_lane, other, log_norm).astype(BF16)
        att_ref[rows, :] = jnp.where(block_lane < HEAD_DIM, heads[0], heads[1]).astype(BF16)

    for p in range(att_own_ref.shape[1] // LANES):
        @pl.when(step == p)
        def _():
            give_ref[p] = att_ref[rows_of(partner, half), :]
            att_copy(p).start()
            att_own_ref[:, p * LANES : (p + 1) * LANES] = att_ref[rows_of(head, half), :]

    @pl.when(step == pl.num_programs(0) - 1)
    def _():
        for p in range(att_own_ref.shape[1] // LANES):
            att_copy(p).wait()
            att_oth_ref[:, p * LANES : (p + 1) * LANES] = got_ref[p]


def ffn_kernel(
    len_ref, att_own_ref, att_oth_ref, emb_ref, cot_ref, vec_ref,
    wo_own_ref, wo_oth_ref, we_own_ref, we_oth_ref, wr_own_ref, wr_oth_ref,
    act_ref, gh_ref, gatt_own_ref, gatt_oth_ref, go_ref, ge_ref, gr_ref, small_ref,
    n2_ref, n2t_ref, gl_ref, glt_ref, hid_ref, ffn_ref, gn_ref,
    give_ref, got_ref, give_att, got_att, give_go, got_go, send_sem, recv_sem, last_send, last_recv,
):
    half = emb_ref.shape[0]
    step = pl.program_id(0)
    head = lax.axis_index("head")
    partner = 1 - head
    row = lax.broadcasted_iota(jnp.int32, (half, 1), 0) + head * half
    valid = row < len_ref[0]

    @pl.when(step == 0)
    def _():
        greet({"head": partner})
        hidden = emb_ref[...] + dot(att_own_ref[...], wo_own_ref[...]) + dot(att_oth_ref[...], wo_oth_ref[...])
        hid_ref[...] = hidden
        hat, _ = normalise(hidden)
        normed = hat * vec_ref[2:3, :] + vec_ref[3:4, :]
        n2_ref[...] = normed.astype(BF16)
        n2t_ref[...] = normed.astype(BF16).T
        grad = jnp.where(valid, cot_ref[...], 0.0)
        gl_ref[...] = grad.astype(BF16)
        glt_ref[...] = grad.astype(BF16).T
        ffn_ref[...] = jnp.zeros_like(ffn_ref)
        gn_ref[...] = jnp.zeros_like(gn_ref)

    def grad_copy(c, kind):
        return remote(
            give_ref.at[c, kind], got_ref.at[c, kind], send_sem.at[c, kind], recv_sem.at[c, kind], head=partner
        )

    def ffn_part(we_ref, wr_ref, put_r, put_e):
        relu = jnp.maximum(dot(n2_ref[...], we_ref[...]), 0.0)
        squared = (relu * relu).astype(BF16)
        put_r(dot(glt_ref[...], squared).astype(BF16))
        grad_e = (dot_nt(gl_ref[...], wr_ref[...]) * (2.0 * relu)).astype(BF16)
        put_e(dot(n2t_ref[...], grad_e).astype(BF16))
        gn_ref[...] += dot_nt(grad_e, we_ref[...])
        ffn_ref[...] += dot(squared, wr_ref[...])

    def give(kind):
        def put(value):
            give_ref[step, kind] = value
            grad_copy(step, kind).start()

        return put

    width = ge_ref.shape[2]

    def keep(ref):
        def put(value):
            for k in range(ref.shape[0]):
                ref[k] = value[:, k * width : (k + 1) * width]

        return put

    ffn_part(we_oth_ref, wr_oth_ref, give(0), give(1))
    ffn_part(we_own_ref, wr_own_ref, keep(gr_ref), keep(ge_ref))
    for kind, ref in enumerate((gr_ref, ge_ref)):
        grad_copy(step, kind).wait()
        for k in range(ref.shape[0]):
            ref[k] = ref[k] + got_ref[step, kind, :, k * width : (k + 1) * width]

    @pl.when(step == pl.num_programs(0) - 1)
    def _():
        hidden = hid_ref[...]
        act_ref[...] = hidden + ffn_ref[...]
        hat, scale = normalise(hidden)
        grad_n = gn_ref[...]
        small_ref[0:1, :] = jnp.sum(grad_n * hat, axis=0, keepdims=True)
        small_ref[1:2, :] = jnp.sum(grad_n, axis=0, keepdims=True)
        grad_h = jnp.where(valid, cot_ref[...], 0.0) + norm_back(grad_n, hat, scale, vec_ref[2:3, :])
        gh_ref[...] = grad_h
        low = grad_h.astype(BF16)
        give_att[...] = dot_nt(low, wo_oth_ref[...]).astype(BF16)
        att_copy = remote(give_att, got_att, last_send.at[0], last_recv.at[0], head=partner)
        att_copy.start()
        low_t = low.T
        give_go[...] = dot(low_t, att_oth_ref[...]).astype(BF16)
        go_copy = remote(give_go, got_go, last_send.at[1], last_recv.at[1], head=partner)
        go_copy.start()
        gatt_own_ref[...] = dot_nt(low, wo_own_ref[...]).astype(BF16)
        grad_o = dot(low_t, att_own_ref[...]).astype(BF16)
        att_copy.wait()
        gatt_oth_ref[...] = got_att[...]
        go_copy.wait()
        go_ref[0] = grad_o + got_go[...]


def backward_kernel(
    inner_bits, outer,
    gown_ref, goth_ref, wq_ref, wk_ref, wv_ref, taps_ref,
    att_ref, qa_ref, ka_ref, va_ref, raw_ref, second_ref, vec_ref,
    nt_hbm, emb_hbm, gh_hbm, ge_hbm, gr_hbm, go_hbm,
    sum_ref, small_ref, gin_hbm,
    nt_ref, do_ref, doa_ref, dqt_ref, mix_ref, all_ref, wcat_ref, emb_ref, gh_ref,
    give_first, got_first, own_first, g_ref, rz_ref, rc_ref, acc_ref, got_small,
    load_sem, first_sem, send_sem, recv_sem, small_send, small_recv, *halves,
):
    slot = att_ref.shape[0]
    half = slot // 2
    step = pl.program_id(0)
    pairs = sum_ref.shape[0] - ge_hbm.shape[0] - gr_hbm.shape[0] - go_hbm.shape[0]
    blocks = slot // BLOCK
    width = sum_ref.shape[2]
    head = lax.axis_index("head")
    partner = 1 - head
    mine = lax.axis_index("inner")
    line = lax.axis_index("outer")
    centre = outer // 2
    left = line < centre
    depth = jnp.where(left, centre - 1 - line, line - centre)
    inward = jnp.where(left, line + 1, line - 1)
    outward = jnp.where(left, line - 1, line + 1)
    bit = [(mine // (1 << b)) % 2 for b in range(inner_bits)]
    across = [mine + (1 << b) * (1 - 2 * bit[b]) for b in range(inner_bits)]

    sources = [(ref, k) for pair in zip(range(ge_hbm.shape[0]), range(gr_hbm.shape[0])) for ref, k in ((gr_hbm, pair[0]), (ge_hbm, pair[1]))]
    sources.append((go_hbm, 0))
    fed = len(sources)
    entries = [(c, 0, width, c % 2) for c in range(fed + pairs - 1)]
    entries += [(fed + pairs - 1, 0, 256, 0), (fed + pairs - 1, 256, width - 256, 1)]
    order_of = [tuple((b + first) % inner_bits for b in range(inner_bits)) for first in range(2)]
    line_steps = 2 * centre - 1
    stage_count = inner_bits + line_steps + 1

    def index_of(fixed):
        return tuple(fixed.get(b, slice(None)) for b in reversed(range(inner_bits)))

    def lanes(entry):
        return slice(entry[1], entry[1] + entry[2])

    def halving(n, s):
        c, _, _, kind = entries[n]
        order = order_of[kind]
        fixed = {b: bit[b] for b in order[:s]}
        b = order[s]
        if s == inner_bits - 1:
            give = g_ref.at[(c,) + index_of({**fixed, b: 1 - bit[b]}) + (slice(None), lanes(entries[n]))]
            land = halves[s].at[c, :, lanes(entries[n])]
            return [remote(give, land, send_sem.at[n, s, 0], recv_sem.at[n, s, 0], inner=across[b])]
        free = [d for d in reversed(range(inner_bits)) if d not in order[: s + 1]]
        copies = []
        for half_of in range(2):
            give = g_ref.at[
                (c,) + index_of({**fixed, b: 1 - bit[b], free[0]: half_of}) + (slice(None), lanes(entries[n]))
            ]
            land = halves[s].at[(c, half_of) + (slice(None),) * (inner_bits - 2 - s) + (slice(None), lanes(entries[n]))]
            sems = (send_sem.at[n, s, half_of], recv_sem.at[n, s, half_of])
            copies.append(remote(give, land, *sems, inner=across[b]))
        return copies

    def add_half(n, s):
        c, _, _, kind = entries[n]
        order = order_of[kind]
        index = (c,) + index_of({b: bit[b] for b in order[: s + 1]}) + (slice(None), lanes(entries[n]))
        land = (c,) + (slice(None),) * (inner_bits - 1 - s) + (slice(None), lanes(entries[n]))
        g_ref[index] = g_ref[index] + halves[s][land]

    def own(n):
        return (entries[n][0],) + tuple(bit[b] for b in reversed(range(inner_bits))) + (slice(None), lanes(entries[n]))

    def flat(n):
        return (entries[n][0], slice(None), lanes(entries[n]))

    def line_copy(n, t):
        s = inner_bits + t
        sems = (send_sem.at[n, s, 0], recv_sem.at[n, s, 0])
        if t < centre - 1:
            return remote(g_ref.at[own(n)], rz_ref.at[flat(n)], *sems, outer=inward)
        if t == centre - 1:
            return remote(g_ref.at[own(n)], rc_ref.at[flat(n)], *sems, outer=inward)
        return remote(rc_ref.at[flat(n)], rc_ref.at[flat(n)], *sems, outer=outward)

    def line_start(n, t):
        if t < centre - 1:
            sender = depth == centre - 1 - t
        elif t == centre - 1:
            sender = depth == 0
        else:
            sender = depth == t - centre
        pl.when(sender)(lambda: line_copy(n, t).start())

    def line_finish(n, t):
        if t < centre - 1:
            @pl.when(depth == centre - 2 - t)
            def _():
                line_copy(n, t).wait_recv()
                g_ref[own(n)] = g_ref[own(n)] + rz_ref[flat(n)]
        elif t == centre - 1:
            @pl.when(depth == 0)
            def _():
                line_copy(n, t).wait_recv()
                rc_ref[flat(n)] = g_ref[own(n)] + rc_ref[flat(n)]
        else:
            pl.when(depth == t - centre + 1)(lambda: line_copy(n, t).wait_recv())

    def load_chunk(c):
        ref, k = sources[c]
        return pltpu.make_async_copy(ref.at[k], g_ref.at[c], load_sem.at[3 + c])

    def advance(n, stage):
        if 0 < stage <= inner_bits:
            for copy in halving(n, stage - 1):
                copy.wait_recv()
            add_half(n, stage - 1)
        elif stage > inner_bits:
            line_finish(n, stage - inner_bits - 1)
        if stage == 0 and entries[n][0] < fed:
            load_chunk(entries[n][0]).wait()
        if stage < inner_bits:
            for copy in halving(n, stage):
                copy.start()
        elif stage < stage_count - 1:
            line_start(n, stage - inner_bits)
        else:
            sum_ref[flat(n)] = rc_ref[flat(n)]

    def drain(n):
        for s in range(inner_bits):
            for copy in halving(n, s):
                copy.wait_send()
        for t in range(line_steps):
            if t < centre - 1:
                sender = depth == centre - 1 - t
            elif t == centre - 1:
                sender = depth == 0
            else:
                sender = depth == t - centre
            pl.when(sender)(lambda t=t: line_copy(n, t).wait_send())

    tail_tick = pairs * blocks
    plan = {}
    for n, (c, _, _, _) in enumerate(entries):
        begin = 3 * (c // 2) if c < fed else (c - fed + 1) * blocks
        late = c == fed + pairs - 1
        for stage in range(stage_count):
            wait = 0 if stage == 0 else (1 if late else 2) + 2 * stage
            plan.setdefault(begin + wait, []).append((n, stage))
    ready = fed + pairs

    def tick(now):
        for n, stage in plan.get(now, ()):
            advance(n, stage)

    def small_copy(k):
        sems = (small_send.at[k], small_recv.at[k])
        if k == 0:
            return remote(acc_ref.at[0], got_small.at[0], *sems, head=partner)
        if k <= inner_bits:
            return remote(acc_ref.at[k], got_small.at[k], *sems, inner=across[k - 1])
        t = k - 1 - inner_bits
        if t <= centre - 1:
            return remote(acc_ref.at[inner_bits + 1], got_small.at[inner_bits + 1 + (t == centre - 1)], *sems, outer=inward)
        last = got_small.at[inner_bits + 2]
        return remote(last, last, *sems, outer=outward)

    def small_step(k):
        if 0 < k <= inner_bits + 1:
            small_copy(k - 1).wait_recv()
            acc_ref[k] = acc_ref[k - 1] + got_small[k - 1]
        elif k > inner_bits + 1:
            t = k - 2 - inner_bits
            if t < centre - 1:
                @pl.when(depth == centre - 2 - t)
                def _():
                    small_copy(k - 1).wait_recv()
                    acc_ref[inner_bits + 1] = acc_ref[inner_bits + 1] + got_small[inner_bits + 1]
            elif t == centre - 1:
                @pl.when(depth == 0)
                def _():
                    small_copy(k - 1).wait_recv()
                    got_small[inner_bits + 2] = acc_ref[inner_bits + 1] + got_small[inner_bits + 2]
            else:
                pl.when(depth == t - centre + 1)(lambda: small_copy(k - 1).wait_recv())
        if k <= inner_bits:
            small_copy(k).start()
        elif k <= inner_bits + line_steps:
            pl.when(small_sender(k))(lambda: small_copy(k).start())
        else:
            small_ref[...] = got_small[inner_bits + 2]

    def small_sender(k):
        t = k - 1 - inner_bits
        if t < centre - 1:
            return depth == centre - 1 - t
        if t == centre - 1:
            return depth == 0
        return depth == t - centre

    small_steps = inner_bits + line_steps + 2

    nt_load = pltpu.make_async_copy(nt_hbm, nt_ref, load_sem.at[0])
    emb_load = pltpu.make_async_copy(emb_hbm, emb_ref, load_sem.at[1])
    gh_load = pltpu.make_async_copy(gh_hbm, gh_ref, load_sem.at[2])

    @pl.when(step == 0)
    def _():
        for c in range(fed):
            load_chunk(c).start()
        nt_load.start()
        emb_load.start()
        gh_load.start()
        barrier = pltpu.get_barrier_semaphore()
        places = [{"head": partner}] + [{"inner": a} for a in across]
        for place in places:
            pl.semaphore_signal(barrier, inc=1, device_id=place, device_id_type=pl.DeviceIdType.MESH)
        for there, away in ((line > 0, line - 1), (line < outer - 1, line + 1)):
            @pl.when(there)
            def _():
                pl.semaphore_signal(
                    barrier, inc=1, device_id={"outer": away}, device_id_type=pl.DeviceIdType.MESH
                )
        beside = jnp.where(line > 0, 1, 0) + jnp.where(line < outer - 1, 1, 0)
        pl.semaphore_wait(barrier, len(places) + beside)
        mix_ref[:, slot : slot + 8, :] = jnp.zeros((3, 8, LANES), F32)
        acc_ref[0] = jnp.zeros(acc_ref.shape[1:], F32)
        acc_ref[0, 2:4, :] = second_ref[...]

    do_ref[rows_of(head, half), :] = gown_ref[...]
    do_ref[rows_of(partner, half), :] = goth_ref[...]
    lane = lane_ids(slot)
    grad_out = do_ref[...].astype(F32)
    product = grad_out * att_ref[...].astype(F32)
    for e in range(2):
        in_head = (lane // HEAD_DIM) == e
        delta = -jnp.sum(jnp.where(in_head, product, 0.0), axis=1, keepdims=True)
        other = HEAD_DIM * (1 - e)
        doa_ref[e] = with_parts(jnp.where(in_head, grad_out, 0.0), lane, other, delta).astype(BF16)
    causal = lax.broadcasted_iota(jnp.int32, (BLOCK, BLOCK), 0) <= lax.broadcasted_iota(
        jnp.int32, (BLOCK, BLOCK), 1
    )
    block_lane = lane_ids(BLOCK)
    dqt_ref[...] = jnp.zeros_like(dqt_ref)
    for j in range(blocks):
        for p in range(pairs):
            pl.when(step == p)(functools.partial(tick, p * blocks + j))
        keys = slice(j * BLOCK, (j + 1) * BLOCK)
        first = j * BLOCK
        after = first + BLOCK
        dks, dvs = [], []
        for e in range(2):
            ka = ka_ref[e, keys, :]
            va = va_ref[e, keys, :]
            kat = ka.T
            spans = [(first, after, True)] + ([(after, slot, False)] if after < slot else [])
            dk = dv = None
            for lo, hi, masked in spans:
                scores = dot_nt(ka, qa_ref[e, lo:hi, :])
                if masked:
                    scores = jnp.where(causal, scores, NEGATIVE)
                probs = jnp.exp(scores)
                grads = (probs * dot_nt(va, doa_ref[e, lo:hi, :])).astype(BF16)
                dv_part = dot(probs.astype(BF16), doa_ref[e, lo:hi, :])
                dk_part = dot(grads, qa_ref[e, lo:hi, :])
                dv = dv_part if dv is None else dv + dv_part
                dk = dk_part if dk is None else dk + dk_part
                dqt_ref[e, :, lo:hi] += dot(kat, grads)
            dks.append(dk)
            dvs.append(dv)
        mix_ref[1, keys, :] = jnp.where(block_lane < HEAD_DIM, dks[0], dks[1])
        mix_ref[2, keys, :] = jnp.where(block_lane < HEAD_DIM, dvs[0], dvs[1])
    sub = lax.broadcasted_iota(jnp.int32, (LANES, slot), 0)
    mix_ref[0, 0:slot, :] = (jnp.where(sub < HEAD_DIM, dqt_ref[0], dqt_ref[1]) * SCALE).T

    local = pairs * LANES
    for p in range(pairs):
        @pl.when(step == p)
        def _():
            base = p * 3 * LANES
            if p == 0:
                nt_load.wait()
            for j, w_ref in enumerate((wq_ref, wk_ref, wv_ref)):
                zero = mix_ref[j, 0:slot, :]
                one = mix_ref[j, 1 : 1 + slot, :]
                two = mix_ref[j, 2 : 2 + slot, :]
                raw = raw_ref[:, j * LANES : (j + 1) * LANES].astype(F32)
                cols = pl.ds(pl.multiple_of(head * local + p * LANES, LANES), LANES)
                for s, moved in enumerate((zero, one, two)):
                    total = jnp.sum(moved * raw, axis=0, keepdims=True)
                    acc_ref[0, 4 + 3 * j + s : 5 + 3 * j + s, cols] = total
                value = taps_ref[j, 0:1, :] * zero + taps_ref[j, 1:2, :] * one + taps_ref[j, 2:3, :] * two
                all_ref[:, base + j * LANES : base + (j + 1) * LANES] = value.astype(BF16)
                wcat_ref[:, base + j * LANES : base + (j + 1) * LANES] = w_ref[...]
            grads = dot(nt_ref[...], all_ref[:, base : base + 3 * LANES]).astype(BF16)
            g_ref[fed + p] = grads.reshape(g_ref.shape[1:])

    @pl.when(step == pairs - 1)
    def _():
        tick(tail_tick)
        give_first[...] = dot_nt(all_ref[rows_of(partner, half), :], wcat_ref[...]).astype(BF16)
        first_copy = remote(give_first, got_first, first_sem.at[0], first_sem.at[1], head=partner)
        first_copy.start()
        tick(tail_tick + 1)
        own_first[...] = dot_nt(all_ref[rows_of(head, half), :], wcat_ref[...])
        tick(tail_tick + 2)
        emb_load.wait()
        gh_load.wait()
        tick(tail_tick + 3)
        first_copy.wait()
        grad_n = own_first[...] + got_first[...].astype(F32)
        hat, scale = normalise(emb_ref[...])
        acc_ref[0, 0:1, :] = jnp.sum(grad_n * hat, axis=0, keepdims=True)
        acc_ref[0, 1:2, :] = jnp.sum(grad_n, axis=0, keepdims=True)
        gh_ref[...] = gh_ref[...] + norm_back(grad_n, hat, scale, vec_ref[0:1, :])
        gin_store = pltpu.make_async_copy(gh_ref, gin_hbm, load_sem.at[0])
        gin_store.start()
        small_step(0)
        now, k = tail_tick + 4, 1
        while now <= max(plan) or k < small_steps:
            tick(now)
            if k < small_steps:
                small_step(k)
            now, k = now + 1, k + 1
        gin_store.wait()
        for n in range(len(entries)):
            drain(n)
        for k in range(inner_bits + 1):
            small_copy(k).wait_send()
        for k in range(inner_bits + 1, inner_bits + 1 + line_steps):
            pl.when(small_sender(k))(lambda k=k: small_copy(k).wait_send())


def finish_kernel(
    gr_in, ge_in, go_in, qkv_in, act_in, gin_in,
    act_ref, gin_ref, q_ref, k_ref, v_ref, go_ref, ge_ref, gr_ref,
):
    act_ref[...] = act_in[...]
    gin_ref[...] = gin_in[...]
    for j, ref in enumerate((q_ref, k_ref, v_ref)):
        ref[...] = qkv_in[0, :, j * LANES : (j + 1) * LANES].astype(F32)
    ge_ref[...] = ge_in[0].astype(F32)
    gr_ref[...] = gr_in[0].astype(F32).T

    @pl.when(pl.program_id(0) == 0)
    def _():
        go_ref[...] = go_in[0].astype(F32).T


def params(vmem, **kw):
    return pltpu.CompilerParams(vmem_limit_bytes=vmem * MIB, **kw)


def body(
    token_ids, lengths, query_weight, key_weight, value_weight, output_weight,
    expand_weight, reduce_weight, dconv_taps, gain_first, bias_first,
    gain_second, bias_second, cotangent,
):
    half = token_ids.shape[1]
    slot = 2 * half
    local = query_weight.shape[1]
    units = expand_weight.shape[1]
    pairs = local // LANES
    outer = lax.axis_size("outer")
    inner = lax.axis_size("inner")
    inner_bits = inner.bit_length() - 1
    rows = D // inner
    width = 3 * LANES

    def swap(value):
        return lax.ppermute(value, "head", [(0, 1), (1, 0)])

    shape = jax.ShapeDtypeStruct
    vectors = jnp.stack([gain_first, bias_first, gain_second, bias_second])
    smem = pl.BlockSpec(memory_space=pltpu.SMEM)
    anywhere = pl.BlockSpec(memory_space=pl.ANY)
    dma = pltpu.SemaphoreType.DMA
    hd = whole((half, D))
    hl = whole((half, local))
    ld = whole((local, D))
    vec = whole((4, D))
    we_oth, wr_oth, wo_oth = swap(expand_weight), swap(reduce_weight), swap(output_weight)

    column = pl.BlockSpec((D, LANES), lambda p: (0, p))
    taps_spec = pl.BlockSpec((3, 3, LANES), lambda p: (0, 0, p))
    pair_rows = pl.BlockSpec((slot, LANES), lambda p: (0, p))
    pair_heads = pl.BlockSpec((2, slot, LANES), lambda p: (p, 0, 0))
    raw_spec = pl.BlockSpec((slot, 3 * LANES), lambda p: (0, p))
    attended, qa, ka, va, raw, embedded, normed_t, att_own, att_oth = pl.pallas_call(
        forward_kernel,
        grid=(pairs,),
        in_specs=[smem, whole((1, half)), vec, column, column, column, taps_spec],
        out_specs=[pair_rows, pair_heads, pair_heads, pair_heads, raw_spec, hd, whole((D, slot)), hl, hl],
        out_shape=[shape((slot, local), BF16)]
        + [shape((2 * pairs, slot, LANES), BF16)] * 3
        + [shape((slot, 3 * local), BF16), shape((half, D), F32), shape((D, slot), BF16)]
        + [shape((half, local), BF16)] * 2,
        scratch_shapes=[
            pltpu.VMEM((slot, D), BF16),
            pltpu.VMEM((slot + 8, LANES), F32),
            pltpu.VMEM((pairs, half, LANES), BF16),
            pltpu.VMEM((pairs, half, LANES), BF16),
            dma((PIECES,)), dma((PIECES,)), dma((pairs,)), dma((pairs,)),
        ],
        compiler_params=params(58, collective_id=0, has_side_effects=True),
        name="attention_forward",
    )(
        lengths, token_ids, vectors,
        query_weight, key_weight, value_weight, dconv_taps,
    )

    chunk = D
    wide = pl.BlockSpec((D, chunk), lambda c: (0, c))
    tall = pl.BlockSpec((chunk, D), lambda c: (c, 0))
    steps = units // chunk
    split = chunk // width
    grad_spec = pl.BlockSpec((split, D, width), lambda c: (c, 0, 0))
    (
        activations, grad_hidden, gatt_own, gatt_oth, go, ge, gr, small_second,
    ) = pl.pallas_call(
        ffn_kernel,
        grid=(steps,),
        in_specs=[smem, hl, hl, hd, hd, vec, ld, ld, wide, wide, tall, tall],
        out_specs=[hd, hd, hl, hl, whole((1, D, local)), grad_spec, grad_spec, whole((2, D))],
        out_shape=[
            shape((half, D), F32), shape((half, D), F32),
            shape((half, local), BF16), shape((half, local), BF16),
            shape((1, D, local), BF16),
            shape((steps * split, D, width), BF16), shape((steps * split, D, width), BF16),
            shape((2, D), F32),
        ],
        scratch_shapes=[
            pltpu.VMEM((half, D), BF16), pltpu.VMEM((D, half), BF16),
            pltpu.VMEM((half, D), BF16), pltpu.VMEM((D, half), BF16),
            pltpu.VMEM((half, D), F32), pltpu.VMEM((half, D), F32), pltpu.VMEM((half, D), F32),
            pltpu.VMEM((steps, 2, D, chunk), BF16), pltpu.VMEM((steps, 2, D, chunk), BF16),
            pltpu.VMEM((half, local), BF16), pltpu.VMEM((half, local), BF16),
            pltpu.VMEM((D, local), BF16), pltpu.VMEM((D, local), BF16),
            dma((steps, 2)), dma((steps, 2)), dma((2,)), dma((2,)),
        ],
        compiler_params=params(62, collective_id=1, has_side_effects=True),
        name="feed_forward",
    )(
        lengths, att_own, att_oth, embedded, cotangent[0], vectors,
        output_weight, wo_oth, expand_weight, we_oth, reduce_weight, wr_oth,
    )

    half_pair = pl.BlockSpec((half, LANES), lambda p: (0, p))
    fed = 2 * steps * split + 1
    chunks = fed + pairs
    twos = (2,) * inner_bits
    cut = lambda g: g.reshape((g.shape[0],) + twos + (rows, width))
    line_stages = inner_bits + outer
    sums, small, grad_input = pl.pallas_call(
        functools.partial(backward_kernel, inner_bits, outer),
        grid=(pairs,),
        in_specs=[
            half_pair, half_pair, column, column, column, taps_spec,
            pair_rows, pair_heads, pair_heads, pair_heads, raw_spec, whole((2, D)), vec,
        ]
        + [anywhere] * 6,
        out_specs=[whole((chunks, rows, width)), whole((16, D)), anywhere],
        out_shape=[shape((chunks, rows, width), BF16), shape((16, D), F32), shape((half, D), F32)],
        scratch_shapes=[
            pltpu.VMEM((D, slot), BF16),
            pltpu.VMEM((slot, LANES), BF16),
            pltpu.VMEM((2, slot, LANES), BF16),
            pltpu.VMEM((2, LANES, slot), F32),
            pltpu.VMEM((3, slot + 8, LANES), F32),
            pltpu.VMEM((slot, 3 * local), BF16),
            pltpu.VMEM((D, 3 * local), BF16),
            pltpu.VMEM((half, D), F32),
            pltpu.VMEM((half, D), F32),
            pltpu.VMEM((half, D), BF16),
            pltpu.VMEM((half, D), BF16),
            pltpu.VMEM((half, D), F32),
            pltpu.VMEM((chunks,) + twos + (rows, width), BF16),
            pltpu.VMEM((chunks, rows, width), BF16),
            pltpu.VMEM((chunks, rows, width), BF16),
            pltpu.VMEM((inner_bits + 2, 16, D), F32),
            pltpu.VMEM((inner_bits + 3, 16, D), F32),
            dma((3 + fed,)), dma((2,)),
            dma((chunks + 1, line_stages, 2)), dma((chunks + 1, line_stages, 2)),
            dma((line_stages + 1,)), dma((line_stages + 1,)),
        ]
        + [pltpu.VMEM((chunks,) + (2,) * (inner_bits - 1 - s) + (rows, width), BF16) for s in range(inner_bits)],
        compiler_params=params(62, collective_id=2, has_side_effects=True),
        name="attention_backward",
    )(
        gatt_own, gatt_oth, query_weight, key_weight, value_weight, dconv_taps,
        attended, qa, ka, va, raw, small_second, vectors,
        normed_t, embedded, grad_hidden, cut(ge), cut(gr), cut(go),
    )
    many = steps * split
    part = half // many
    some_rows = pl.BlockSpec((part, D), lambda i: (i, 0))
    pick = lambda index: pl.BlockSpec((1, rows, width), lambda i: (index(i), 0, 0))
    last = lambda i: jnp.minimum(i, pairs - 1)
    out_pair = pl.BlockSpec((rows, LANES), lambda i: (0, last(i)))
    activations, grad_input, gq, gk, gv, go_sum, ge_sum, gr_sum = pl.pallas_call(
        finish_kernel,
        grid=(many,),
        in_specs=[
            pick(lambda i: 2 * i), pick(lambda i: 2 * i + 1), pick(lambda i: fed - 1),
            pick(lambda i: fed + last(i)), some_rows, some_rows,
        ],
        out_specs=[
            some_rows, some_rows, out_pair, out_pair, out_pair, whole((local, rows)),
            pl.BlockSpec((rows, width), lambda i: (0, i)), pl.BlockSpec((width, rows), lambda i: (i, 0)),
        ],
        out_shape=[shape((half, D), F32)] * 2
        + [shape((rows, local), F32)] * 3
        + [shape((local, rows), F32), shape((rows, units), F32), shape((units, rows), F32)],
        compiler_params=params(32),
        name="finish",
    )(sums, sums, sums, sums, activations, grad_input)
    return (
        activations[None],
        grad_input[None],
        gq,
        gk,
        gv,
        go_sum,
        ge_sum,
        gr_sum,
        small[4:13].reshape(3, 3, D),
        small[0],
        small[1],
        small[2],
        small[3],
    )


def solution(mesh):
    return jax.shard_map(
        body,
        mesh=mesh,
        in_specs=(
            P(("outer", "inner"), "head"),
            P(("outer", "inner")),
            P(None, "head"),
            P(None, "head"),
            P(None, "head"),
            P("head", None),
            P(None, "head"),
            P("head", None),
            P(None, None, "head"),
            P(),
            P(),
            P(),
            P(),
            P(("outer", "inner"), "head", None),
        ),
        out_specs=(
            P(("outer", "inner"), "head", None),
            P(("outer", "inner"), "head", None),
            P("inner", "head"),
            P("inner", "head"),
            P("inner", "head"),
            P("head", "inner"),
            P("inner", "head"),
            P("head", "inner"),
            P(),
            P(),
            P(),
            P(),
            P(),
        ),
        check_vma=False,
    )
```

```python
import functools
import math

import jax
import jax.numpy as jnp
from jax import lax
from jax.experimental import pallas as pl
from jax.experimental.pallas import tpu as pltpu
from jax.sharding import PartitionSpec as P

HEAD_DIM = 64
D = 768
BLOCK = 256
LANES = 128
EPS = 1e-05
MODULUS = 32749
NEGATIVE = -1e30
SCALE = HEAD_DIM ** (-0.5)
F32 = jnp.float32
BF16 = jnp.bfloat16
MIB = 1024 * 1024

SINE = (
    4.442882913726386,
    -7.308248583654593,
    3.606466623722958,
    -0.8474403474577161,
    0.11605422299047748,
    -0.010267162611370253,
    0.0005523348366953617,
)


def dot(a, b):
    return lax.dot_general(a, b, (((1,), (0,)), ((), ())), preferred_element_type=F32)


def dot_nt(a, b):
    return lax.dot_general(a, b, (((1,), (1,)), ((), ())), preferred_element_type=F32)


def whole(shape):
    return pl.BlockSpec(shape, lambda *_: (0,) * len(shape))


def normalise(values):
    centre = values - jnp.mean(values, axis=-1, keepdims=True)
    spread = jnp.mean(centre * centre, axis=-1, keepdims=True)
    scale = lax.rsqrt(spread + EPS)
    return centre * scale, scale


def norm_back(grad, hat, scale, gain):
    q = grad * gain
    mean_q = jnp.mean(q, axis=-1, keepdims=True)
    mean_qh = jnp.mean(q * hat, axis=-1, keepdims=True)
    return scale * (q - mean_q - hat * mean_qh)


def lane_ids(rows):
    return lax.broadcasted_iota(jnp.int32, (rows, LANES), 1)


def split_three(column):
    high = column.astype(BF16).astype(F32)
    rest = column - high
    middle = rest.astype(BF16).astype(F32)
    return high, middle, rest - middle


def with_parts(base, lane, offset, column):
    high, middle, small = split_three(column)
    base = jnp.where(lane == offset + 1, high, base)
    base = jnp.where(lane == offset + 2, middle, base)
    return jnp.where(lane == offset + 3, small, base)


def remote(src, dst, send, recv, **place):
    return pltpu.make_async_remote_copy(
        src_ref=src, dst_ref=dst, send_sem=send, recv_sem=recv,
        device_id=place, device_id_type=pl.DeviceIdType.MESH,
    )


def greet(*places):
    barrier = pltpu.get_barrier_semaphore()
    for place in places:
        pl.semaphore_signal(barrier, inc=1, device_id=place, device_id_type=pl.DeviceIdType.MESH)
    pl.semaphore_wait(barrier, len(places))


def rows_of(which, half):
    return pl.ds(pl.multiple_of(which * half, half), half)


def embed_rows(tok_ref, vec_ref, emb_ref, normed_ref, base, first):
    tokens = jnp.broadcast_to(tok_ref[:, pl.ds(first, LANES)], (LANES, LANES)).T
    parts = []
    for c in range(D // LANES):
        column = lax.broadcasted_iota(jnp.int32, (1, LANES), 1) + c * LANES
        product = tokens * (column + 1) + column * column
        turns = jnp.floor(product.astype(F32) * (1.0 / MODULUS) + 0.5)
        left = product - turns.astype(jnp.int32) * MODULUS
        u = left.astype(F32) * (2.0 / MODULUS)
        z = u * u
        value = jnp.full_like(u, SINE[-1])
        for coefficient in SINE[-2::-1]:
            value = value * z + coefficient
        parts.append(value * u)
    embedded = jnp.concatenate(parts, axis=1)
    emb_ref[pl.ds(first, LANES), :] = embedded
    hat, _ = normalise(embedded)
    rows = pl.ds(pl.multiple_of(base + first, LANES), LANES)
    normed_ref[rows, :] = (hat * vec_ref[0:1, :] + vec_ref[1:2, :]).astype(BF16)


PIECES = 3


def forward_kernel(
    len_ref, tok_ref, vec_ref, wq_ref, wk_ref, wv_ref, taps_ref,
    att_ref, qa_ref, ka_ref, va_ref, raw_ref, emb_ref, nt_ref, att_own_ref, att_oth_ref,
    normed_ref, shift_ref, give_ref, got_ref, row_send, row_recv, att_send, att_recv,
):
    slot = att_ref.shape[0]
    half = slot // 2
    step = pl.program_id(0)
    head = lax.axis_index("head")
    partner = 1 - head
    piece = half // PIECES

    def row_copy(k):
        rows = pl.ds(pl.multiple_of(head * half + k * piece, piece), piece)
        return remote(normed_ref.at[rows], normed_ref.at[rows], row_send.at[k], row_recv.at[k], head=partner)

    def att_copy(p):
        return remote(give_ref.at[p], got_ref.at[p], att_send.at[p], att_recv.at[p], head=partner)

    @pl.when(step == 0)
    def _():
        greet({"head": partner})
        base = head * half
        for k in range(PIECES):
            def embed_step(i, _):
                first = pl.multiple_of(k * piece + i * LANES, LANES)
                embed_rows(tok_ref, vec_ref, emb_ref, normed_ref, base, first)
                return 0

            lax.fori_loop(0, piece // LANES, embed_step, 0)
            row_copy(k).start()
        nt_ref[:, rows_of(head, half)] = normed_ref[rows_of(head, half), :].T
        shift_ref[0:8, :] = jnp.zeros((8, LANES), F32)
        for k in range(PIECES):
            row_copy(k).wait()
        nt_ref[:, rows_of(partner, half)] = normed_ref[rows_of(partner, half), :].T

    lane = lane_ids(slot)
    mixed = []
    for j, w_ref in enumerate((wq_ref, wk_ref, wv_ref)):
        raw = dot(normed_ref[...], w_ref[...])
        raw_ref[:, j * LANES : (j + 1) * LANES] = raw.astype(BF16)
        shift_ref[8 : 8 + slot, :] = raw
        one = shift_ref[7 : 7 + slot, :]
        two = shift_ref[6 : 6 + slot, :]
        value = taps_ref[j, 0:1, :] * raw + taps_ref[j, 1:2, :] * one + taps_ref[j, 2:3, :] * two
        mixed.append(value * SCALE if j == 0 else value)
    row = lax.broadcasted_iota(jnp.int32, (slot, 1), 0)
    key_bias = jnp.where(row < len_ref[0], 0.0, NEGATIVE)
    for e in range(2):
        mine = (lane // HEAD_DIM) == e
        other = HEAD_DIM * (1 - e)
        ones = jnp.where((lane > other) & (lane < other + 4), 1.0, 0.0)
        qa_ref[e] = jnp.where(mine, mixed[0], jnp.where(lane == other, 1.0, 0.0)).astype(BF16)
        ka_ref[e] = jnp.where(mine, mixed[1], jnp.where(lane == other, key_bias, ones)).astype(BF16)
        va_ref[e] = jnp.where(mine, mixed[2], ones).astype(BF16)
    block_lane = lane_ids(BLOCK)
    causal = lax.broadcasted_iota(jnp.int32, (BLOCK, BLOCK), 1) <= lax.broadcasted_iota(
        jnp.int32, (BLOCK, BLOCK), 0
    )
    for i in range(slot // BLOCK):
        rows = slice(i * BLOCK, (i + 1) * BLOCK)
        before = i * BLOCK
        heads = []
        for e in range(2):
            other = HEAD_DIM * (1 - e)
            query = qa_ref[e, rows, :]
            diagonal = jnp.where(causal, dot_nt(query, ka_ref[e, rows, :]), NEGATIVE)
            row_max = jnp.max(diagonal, axis=1, keepdims=True)
            if before:
                scores = dot_nt(query, ka_ref[e, :before, :])
                row_max = jnp.maximum(row_max, jnp.max(scores, axis=1, keepdims=True))
            out = dot(jnp.exp(diagonal - row_max).astype(BF16), va_ref[e, rows, :])
            if before:
                out += dot(jnp.exp(scores - row_max).astype(BF16), va_ref[e, :before, :])
            total = out[:, other + 1 : other + 2]
            heads.append(out / total)
            log_norm = -(row_max + jnp.log(total))
            qa_ref[e, rows, :] = with_parts(query.astype(F32), block_lane, other, log_norm).astype(BF16)
        att_ref[rows, :] = jnp.where(block_lane < HEAD_DIM, heads[0], heads[1]).astype(BF16)

    for p in range(att_own_ref.shape[1] // LANES):
        @pl.when(step == p)
        def _():
            give_ref[p] = att_ref[rows_of(partner, half), :]
            att_copy(p).start()
            att_own_ref[:, p * LANES : (p + 1) * LANES] = att_ref[rows_of(head, half), :]

    @pl.when(step == pl.num_programs(0) - 1)
    def _():
        for p in range(att_own_ref.shape[1] // LANES):
            att_copy(p).wait()
            att_oth_ref[:, p * LANES : (p + 1) * LANES] = got_ref[p]


def layer_kernel(
    inner_bits, outer,
    len_ref, vec_ref, taps_ref,
    att_own_hbm, att_oth_hbm, emb_hbm, cot_hbm, wo_own_hbm, wo_oth_hbm,
    we_own_hbm, we_oth_hbm, wr_own_hbm, wr_oth_hbm, wq_hbm, wk_hbm, wv_hbm,
    att_hbm, qa_hbm, ka_hbm, va_hbm, raw_hbm, nt_hbm,
    sum_ref, small_ref, act_hbm, gin_hbm,
    gh_ref, g_ref, rz_ref, rc_ref, do_ref, got_ref, got_go, got_first, acc_ref, got_small,
    load_sem, send_sem, recv_sem, small_send, small_recv, core_send, core_recv, *halves,
):
    half = gh_ref.shape[0]
    slot = 2 * half
    local = att_own_hbm.shape[1]
    units = we_own_hbm.shape[1]
    steps = units // D
    width = sum_ref.shape[2]
    split = D // width
    pairs = local // LANES
    fed = 2 * steps * split + 1
    blocks = slot // BLOCK
    head = lax.axis_index("head")
    partner = 1 - head
    mine = lax.axis_index("inner")
    line = lax.axis_index("outer")
    centre = outer // 2
    left = line < centre
    depth = jnp.where(left, centre - 1 - line, line - centre)
    inward = jnp.where(left, line + 1, line - 1)
    outward = jnp.where(left, line - 1, line + 1)
    bit = [(mine // (1 << b)) % 2 for b in range(inner_bits)]
    across = [mine + (1 << b) * (1 - 2 * bit[b]) for b in range(inner_bits)]

    def chunk_of(c, kind, k):
        return (2 * c + kind) * split + k

    entries = [(c, 0, width, c % 2) for c in range(fed + pairs - 1)]
    entries += [(fed + pairs - 1, 0, 256, 0), (fed + pairs - 1, 256, width - 256, 1)]
    order_of = [tuple((b + first) % inner_bits for b in range(inner_bits)) for first in range(2)]
    line_steps = 2 * centre - 1
    stage_count = inner_bits + line_steps + 1

    def index_of(fixed):
        return tuple(fixed.get(b, slice(None)) for b in reversed(range(inner_bits)))

    def lanes(entry):
        return slice(entry[1], entry[1] + entry[2])

    def halving(n, s):
        c, _, _, kind = entries[n]
        order = order_of[kind]
        fixed = {b: bit[b] for b in order[:s]}
        b = order[s]
        give = g_ref.at[(c,) + index_of({**fixed, b: 1 - bit[b]}) + (slice(None), lanes(entries[n]))]
        land = halves[s].at[(c,) + (slice(None),) * (inner_bits - 1 - s) + (slice(None), lanes(entries[n]))]
        return remote(give, land, send_sem.at[n, s], recv_sem.at[n, s], inner=across[b])

    def add_half(n, s):
        c, _, _, kind = entries[n]
        order = order_of[kind]
        index = (c,) + index_of({b: bit[b] for b in order[: s + 1]}) + (slice(None), lanes(entries[n]))
        land = (c,) + (slice(None),) * (inner_bits - 1 - s) + (slice(None), lanes(entries[n]))
        g_ref[index] = g_ref[index] + halves[s][land]

    def own(n):
        return (entries[n][0],) + tuple(bit[b] for b in reversed(range(inner_bits))) + (slice(None), lanes(entries[n]))

    def flat(n):
        return (entries[n][0], slice(None), lanes(entries[n]))

    def line_sender(t):
        if t < centre - 1:
            return depth == centre - 1 - t
        if t == centre - 1:
            return depth == 0
        return depth == t - centre

    def line_copy(n, t):
        s = inner_bits + t
        sems = (send_sem.at[n, s], recv_sem.at[n, s])
        if t < centre - 1:
            return remote(g_ref.at[own(n)], rz_ref.at[flat(n)], *sems, outer=inward)
        if t == centre - 1:
            return remote(g_ref.at[own(n)], rc_ref.at[flat(n)], *sems, outer=inward)
        return remote(rc_ref.at[flat(n)], rc_ref.at[flat(n)], *sems, outer=outward)

    def line_finish(n, t):
        if t < centre - 1:
            @pl.when(depth == centre - 2 - t)
            def _():
                line_copy(n, t).wait_recv()
                g_ref[own(n)] = g_ref[own(n)] + rz_ref[flat(n)]
        elif t == centre - 1:
            @pl.when(depth == 0)
            def _():
                line_copy(n, t).wait_recv()
                rc_ref[flat(n)] = g_ref[own(n)] + rc_ref[flat(n)]
        else:
            pl.when(depth == t - centre + 1)(lambda: line_copy(n, t).wait_recv())

    def advance(n, stage):
        if 0 < stage <= inner_bits:
            halving(n, stage - 1).wait_recv()
            add_half(n, stage - 1)
        elif stage > inner_bits:
            line_finish(n, stage - inner_bits - 1)
        if stage < inner_bits:
            halving(n, stage).start()
        elif stage < stage_count - 1:
            t = stage - inner_bits
            pl.when(line_sender(t))(lambda: line_copy(n, t).start())
        else:
            sum_ref[flat(n)] = rc_ref[flat(n)]

    def drain(n):
        for s in range(inner_bits):
            halving(n, s).wait_send()
        for t in range(line_steps):
            pl.when(line_sender(t))(lambda t=t: line_copy(n, t).wait_send())

    clock = {}
    now = 3.0
    for c in range(steps):
        for k in range(6):
            now += 3.2
            clock[("feed", c, k)] = now
    for k in range(3):
        now += 1.5
        clock[("norm", k)] = now
    for p in range(pairs):
        for j in range(blocks):
            clock[("pair", p, j)] = now + 2.5 * j
        now += 2.5 * blocks + 2.0
        clock[("taps", p)] = now
    for k in range(2 * stage_count + 8):
        clock[("tail", k)] = now + 2.0 * k
    ready = {}
    for c in range(steps):
        for k in range(split):
            ready[chunk_of(c, 0, k)] = ("feed", c, 2)
            ready[chunk_of(c, 1, k)] = ("feed", c, 5)
    ready[fed - 1] = ("norm", 2)
    for p in range(pairs):
        ready[fed + p] = ("taps", p) if p < pairs - 1 else ("tail", 0)
    plan = {}
    order = list(clock)
    for n, (c, _, _, _) in enumerate(entries):
        last = c == fed + pairs - 1
        spot = order.index(ready[c])
        for stage in range(stage_count):
            if stage:
                lag = 3.0 if last else (11.0 if stage == 1 else 6.5)
                due = clock[order[spot]] + lag
                spot = min(spot + 1, len(order) - 1)
                while spot < len(order) - 1 and (order[spot][0] == "norm" or clock[order[spot]] < due):
                    spot += 1
            plan.setdefault(order[spot], []).append((n, stage))

    def tick(place):
        for n, stage in plan.pop(place, ()):
            advance(n, stage)

    def small_copy(k):
        sems = (small_send.at[k], small_recv.at[k])
        if k == 0:
            return remote(acc_ref.at[0], got_small.at[0], *sems, head=partner)
        if k <= inner_bits:
            return remote(acc_ref.at[k], got_small.at[k], *sems, inner=across[k - 1])
        t = k - 1 - inner_bits
        if t <= centre - 1:
            return remote(acc_ref.at[inner_bits + 1], got_small.at[inner_bits + 1 + (t == centre - 1)], *sems, outer=inward)
        last = got_small.at[inner_bits + 2]
        return remote(last, last, *sems, outer=outward)

    def small_step(k):
        if 0 < k <= inner_bits + 1:
            small_copy(k - 1).wait_recv()
            acc_ref[k] = acc_ref[k - 1] + got_small[k - 1]
        elif k > inner_bits + 1:
            t = k - 2 - inner_bits
            if t < centre - 1:
                @pl.when(depth == centre - 2 - t)
                def _():
                    small_copy(k - 1).wait_recv()
                    acc_ref[inner_bits + 1] = acc_ref[inner_bits + 1] + got_small[inner_bits + 1]
            elif t == centre - 1:
                @pl.when(depth == 0)
                def _():
                    small_copy(k - 1).wait_recv()
                    got_small[inner_bits + 2] = acc_ref[inner_bits + 1] + got_small[inner_bits + 2]
            else:
                pl.when(depth == t - centre + 1)(lambda: small_copy(k - 1).wait_recv())
        if k <= inner_bits:
            small_copy(k).start()
        elif k <= inner_bits + line_steps:
            pl.when(line_sender(k - 1 - inner_bits))(lambda: small_copy(k).start())
        else:
            small_ref[...] = got_small[inner_bits + 2]

    small_steps = inner_bits + line_steps + 2

    load_count = iter(range(load_sem.shape[0]))

    def load(src, dst):
        return pltpu.make_async_copy(src, dst, load_sem.at[next(load_count)])

    row = lax.broadcasted_iota(jnp.int32, (half, 1), 0) + head * half
    valid = row < len_ref[0]

    def greet_all():
        barrier = pltpu.get_barrier_semaphore()
        places = [{"head": partner}] + [{"inner": a} for a in across]
        for place in places:
            pl.semaphore_signal(barrier, inc=1, device_id=place, device_id_type=pl.DeviceIdType.MESH)
        for there, away in ((line > 0, line - 1), (line < outer - 1, line + 1)):
            @pl.when(there)
            def _():
                pl.semaphore_signal(
                    barrier, inc=1, device_id={"outer": away}, device_id_type=pl.DeviceIdType.MESH
                )
        beside = jnp.where(line > 0, 1, 0) + jnp.where(line < outer - 1, 1, 0)
        pl.semaphore_wait(barrier, len(places) + beside)

    def feed_forward(
        att_ref, wo_ref, we_ref, wr_ref, cot_ref, hid_ref, ffn_ref, gn_ref,
        n2_ref, n2t_ref, gl_ref, glt_ref, give_ref, give_att, give_go, relu_ref, sq_ref,
    ):
        loads = {}
        for k, (att, wo) in enumerate(((att_own_hbm, wo_own_hbm), (att_oth_hbm, wo_oth_hbm))):
            loads["att", k] = load(att, att_ref.at[k])
            loads["wo", k] = load(wo, wo_ref.at[k])
        loads["emb"] = load(emb_hbm, hid_ref)
        loads["cot"] = load(cot_hbm, cot_ref)
        for c in range(steps):
            cols = pl.ds(c * D, D)
            for k, we in ((1, we_oth_hbm), (0, we_own_hbm)):
                loads["we", c, k] = load(we.at[:, cols], we_ref.at[c, k])
            for k, wr in ((1, wr_oth_hbm), (0, wr_own_hbm)):
                loads["wr", c, k] = load(wr.at[cols, :], wr_ref.at[c, k])
        for copy in loads.values():
            copy.start()
        greet_all()
        for key in (("att", 0), ("wo", 0), ("att", 1), ("wo", 1), "emb"):
            loads[key].wait()
        hidden = hid_ref[...] + dot(att_ref[0], wo_ref[0]) + dot(att_ref[1], wo_ref[1])
        hid_ref[...] = hidden
        ffn_ref[...] = hidden
        hat, _ = normalise(hidden)
        normed = (hat * vec_ref[2:3, :] + vec_ref[3:4, :]).astype(BF16)
        n2_ref[...] = normed
        n2t_ref[...] = normed.T
        loads["cot"].wait()
        grad = jnp.where(valid, cot_ref[...], 0.0)
        cot_ref[...] = grad
        gl_ref[...] = grad.astype(BF16)
        glt_ref[...] = grad.astype(BF16).T

        def grad_copy(c, kind):
            return remote(
                give_ref.at[kind], got_ref.at[c % 2, kind], core_send.at[c, kind], core_recv.at[c, kind], head=partner
            )

        def put_own(c, kind, value):
            for k in range(split):
                part = value[:, k * width : (k + 1) * width].astype(BF16)
                g_ref[chunk_of(c, kind, k)] = part.reshape(g_ref.shape[1:])

        def add_other(c, kind):
            grad_copy(c, kind).wait_recv()
            for k in range(split):
                got = got_ref[c % 2, kind, :, k * width : (k + 1) * width]
                g_ref[chunk_of(c, kind, k)] += got.reshape(g_ref.shape[1:])

        for c in range(steps):
            for k in (1, 0):
                loads["we", c, k].wait()
                relu = jnp.maximum(dot(n2_ref[...], we_ref[c, k]), 0.0)
                relu_ref[k] = relu.astype(BF16)
                sq_ref[k] = (relu * relu).astype(BF16)
                grad = dot(glt_ref[...], sq_ref[k])
                if k == 1:
                    if c:
                        grad_copy(c - 1, 0).wait_send()
                    give_ref[0] = grad.astype(BF16)
                    grad_copy(c, 0).start()
                    tick(("feed", c, 0))
                else:
                    put_own(c, 0, grad)
                    tick(("feed", c, 1))
            add_other(c, 0)
            tick(("feed", c, 2))
            for k in (1, 0):
                loads["wr", c, k].wait()
                back = dot_nt(gl_ref[...], wr_ref[c, k])
                grad_e = (back * (2.0 * relu_ref[k].astype(F32))).astype(BF16)
                relu_ref[k] = grad_e
                grad = dot(n2t_ref[...], grad_e)
                if k == 1:
                    if c:
                        grad_copy(c - 1, 1).wait_send()
                    give_ref[1] = grad.astype(BF16)
                    grad_copy(c, 1).start()
                    tick(("feed", c, 3))
                else:
                    put_own(c, 1, grad)
                    tick(("feed", c, 4))
            for k in (1, 0):
                gn = dot_nt(relu_ref[k], we_ref[c, k])
                if c == 0 and k == 1:
                    gn_ref[...] = gn
                else:
                    gn_ref[...] += gn
                if k == 1:
                    add_other(c, 1)
                    tick(("feed", c, 5))
                ffn_ref[...] += dot(sq_ref[k], wr_ref[c, k])
        act_store = load(ffn_ref, act_hbm)
        act_store.start()
        hat, scale = normalise(hid_ref[...])
        grad_n = gn_ref[...]
        acc_ref[0] = jnp.zeros(acc_ref.shape[1:], F32)
        acc_ref[0, 2:3, :] = jnp.sum(grad_n * hat, axis=0, keepdims=True)
        acc_ref[0, 3:4, :] = jnp.sum(grad_n, axis=0, keepdims=True)
        grad_h = cot_ref[...] + norm_back(grad_n, hat, scale, vec_ref[2:3, :])
        gh_ref[...] = grad_h
        low = grad_h.astype(BF16)
        give_att[...] = dot_nt(low, wo_ref[1]).astype(BF16)
        rows = rows_of(head, half)
        att_copy = remote(give_att, do_ref.at[rows], core_send.at[steps, 0], core_recv.at[steps, 0], head=partner)
        att_copy.start()
        tick(("norm", 0))
        low_t = low.T
        give_go[...] = dot(low_t, att_ref[1]).astype(BF16)
        go_copy = remote(give_go, got_go, core_send.at[steps, 1], core_recv.at[steps, 1], head=partner)
        go_copy.start()
        do_ref[rows, :] = dot_nt(low, wo_ref[0]).astype(BF16)
        tick(("norm", 1))
        grad_o = dot(low_t, att_ref[0]).astype(BF16)
        go_copy.wait()
        g_ref[fed - 1] = (grad_o + got_go[...]).reshape(g_ref.shape[1:])
        tick(("norm", 2))
        for kind in range(2):
            grad_copy(steps - 1, kind).wait_send()
        act_store.wait()
        att_copy.wait()

    pl.run_scoped(
        feed_forward,
        pltpu.VMEM((2, half, local), BF16), pltpu.VMEM((2, local, D), BF16),
        pltpu.VMEM((steps, 2, D, D), BF16), pltpu.VMEM((steps, 2, D, D), BF16),
        pltpu.VMEM((half, D), F32), pltpu.VMEM((half, D), F32), pltpu.VMEM((half, D), F32), pltpu.VMEM((half, D), F32),
        pltpu.VMEM((half, D), BF16), pltpu.VMEM((D, half), BF16),
        pltpu.VMEM((half, D), BF16), pltpu.VMEM((D, half), BF16),
        pltpu.VMEM((2, D, D), BF16), pltpu.VMEM((half, local), BF16), pltpu.VMEM((D, local), BF16),
        pltpu.VMEM((2, half, D), BF16), pltpu.VMEM((2, half, D), BF16),
    )

    def attention(
        nt_ref, doa_ref, dqt_ref, mix_ref, all_ref, wcat_ref, emb_ref, give_first, own_first,
        att_ref, qa_ref, ka_ref, va_ref, raw_ref, pair_sem,
    ):
        def pair_loads(p, place):
            two = pl.ds(2 * p, 2)
            one = pl.ds(pl.multiple_of(p * LANES, LANES), LANES)
            three = pl.ds(pl.multiple_of(p * 3 * LANES, LANES), 3 * LANES)
            return [
                pltpu.make_async_copy(ka_hbm.at[two], ka_ref.at[place], pair_sem.at[place, 0]),
                pltpu.make_async_copy(qa_hbm.at[two], qa_ref.at[place], pair_sem.at[place, 1]),
                pltpu.make_async_copy(att_hbm.at[:, one], att_ref.at[place], pair_sem.at[place, 2]),
                pltpu.make_async_copy(va_hbm.at[two], va_ref.at[place], pair_sem.at[place, 3]),
                pltpu.make_async_copy(raw_hbm.at[:, three], raw_ref.at[place], pair_sem.at[place, 4]),
            ]

        for copy in pair_loads(0, 0):
            copy.start()
        nt_load = load(nt_hbm, nt_ref)
        nt_load.start()
        late = []
        for p in range(pairs):
            for j, w_hbm in enumerate((wq_hbm, wk_hbm, wv_hbm)):
                base = (3 * p + j) * LANES
                late.append(load(w_hbm.at[:, pl.ds(p * LANES, LANES)], wcat_ref.at[:, pl.ds(base, LANES)]))
        late.append(load(emb_hbm, emb_ref))
        for copy in late:
            copy.start()
        mix_ref[:, slot : slot + 8, :] = jnp.zeros((3, 8, LANES), F32)
        lane = lane_ids(slot)
        causal = lax.broadcasted_iota(jnp.int32, (BLOCK, BLOCK), 0) <= lax.broadcasted_iota(
            jnp.int32, (BLOCK, BLOCK), 1
        )
        block_lane = lane_ids(BLOCK)
        sub = lax.broadcasted_iota(jnp.int32, (LANES, slot), 0)

        def at_pair(p, kind, *rest):
            for q in range(pairs):
                if plan.get((kind, q) + rest):
                    pl.when(p == q)(functools.partial(tick, (kind, q) + rest))

        def one_pair(p, _):
            place = lax.rem(p, 2)
            one = pl.ds(pl.multiple_of(p * LANES, LANES), LANES)

            @pl.when(p + 1 < pairs)
            def _():
                for copy in pair_loads(p + 1, 1 - place):
                    copy.start()

            for copy in pair_loads(p, place):
                copy.wait()
            grad_out = do_ref[:, one].astype(F32)
            product = grad_out * att_ref[place].astype(F32)
            for e in range(2):
                in_head = (lane // HEAD_DIM) == e
                delta = -jnp.sum(jnp.where(in_head, product, 0.0), axis=1, keepdims=True)
                other = HEAD_DIM * (1 - e)
                doa_ref[e] = with_parts(jnp.where(in_head, grad_out, 0.0), lane, other, delta).astype(BF16)
            for j in range(blocks):
                at_pair(p, "pair", j)
                keys = slice(j * BLOCK, (j + 1) * BLOCK)
                first = j * BLOCK
                after = first + BLOCK
                dks, dvs = [], []
                for e in range(2):
                    ka = ka_ref[place, e, keys, :]
                    va = va_ref[place, e, keys, :]
                    kat = ka.T
                    spans = [(first, after, True)] + ([(after, slot, False)] if after < slot else [])
                    dk = dv = None
                    for lo, hi, masked in spans:
                        scores = dot_nt(ka, qa_ref[place, e, lo:hi, :])
                        if masked:
                            scores = jnp.where(causal, scores, NEGATIVE)
                        probs = jnp.exp(scores)
                        grads = (probs * dot_nt(va, doa_ref[e, lo:hi, :])).astype(BF16)
                        dv_part = dot(probs.astype(BF16), doa_ref[e, lo:hi, :])
                        dk_part = dot(grads, qa_ref[place, e, lo:hi, :])
                        dv = dv_part if dv is None else dv + dv_part
                        dk = dk_part if dk is None else dk + dk_part
                        if j:
                            dqt_ref[e, :, lo:hi] += dot(kat, grads)
                        else:
                            dqt_ref[e, :, lo:hi] = dot(kat, grads)
                    dks.append(dk)
                    dvs.append(dv)
                mix_ref[1, keys, :] = jnp.where(block_lane < HEAD_DIM, dks[0], dks[1])
                mix_ref[2, keys, :] = jnp.where(block_lane < HEAD_DIM, dvs[0], dvs[1])
            mix_ref[0, 0:slot, :] = (jnp.where(sub < HEAD_DIM, dqt_ref[0], dqt_ref[1]) * SCALE).T
            base = pl.multiple_of(p * 3 * LANES, LANES)
            for j in range(3):
                zero = mix_ref[j, 0:slot, :]
                one_on = mix_ref[j, 1 : 1 + slot, :]
                two_on = mix_ref[j, 2 : 2 + slot, :]
                raw = raw_ref[place, :, j * LANES : (j + 1) * LANES].astype(F32)
                cols = pl.ds(pl.multiple_of(head * local + p * LANES, LANES), LANES)
                value = 0.0
                for s, moved in enumerate((zero, one_on, two_on)):
                    total = jnp.sum(moved * raw, axis=0, keepdims=True)
                    acc_ref[0, 4 + 3 * j + s : 5 + 3 * j + s, cols] = total
                    value += taps_ref[j, s : s + 1, one] * moved
                all_ref[:, pl.ds(pl.multiple_of(base + j * LANES, LANES), LANES)] = value.astype(BF16)

            @pl.when(p == 0)
            def _():
                nt_load.wait()

            grads = dot(nt_ref[...], all_ref[:, pl.ds(base, 3 * LANES)]).astype(BF16)
            g_ref[fed + p] = grads.reshape(g_ref.shape[1:])
            at_pair(p, "taps")
            return 0

        lax.fori_loop(0, pairs, one_pair, 0)
        tick(("tail", 0))
        for copy in late:
            copy.wait()
        give_first[...] = dot_nt(all_ref[rows_of(partner, half), :], wcat_ref[...]).astype(BF16)
        first_copy = remote(
            give_first, got_first, core_send.at[steps + 1, 0], core_recv.at[steps + 1, 0], head=partner
        )
        first_copy.start()
        tick(("tail", 1))
        own_first[...] = dot_nt(all_ref[rows_of(head, half), :], wcat_ref[...])
        tick(("tail", 2))
        first_copy.wait()
        grad_n = own_first[...] + got_first[...].astype(F32)
        hat, scale = normalise(emb_ref[...])
        acc_ref[0, 0:1, :] = jnp.sum(grad_n * hat, axis=0, keepdims=True)
        acc_ref[0, 1:2, :] = jnp.sum(grad_n, axis=0, keepdims=True)
        small_step(0)
        gh_ref[...] = gh_ref[...] + norm_back(grad_n, hat, scale, vec_ref[0:1, :])
        gin_store = load(gh_ref, gin_hbm)
        gin_store.start()
        now, k = 3, 1
        while plan or k < small_steps:
            assert ("tail", now) in clock or not plan
            tick(("tail", now))
            if k < small_steps:
                small_step(k)
            now, k = now + 1, k + 1
        gin_store.wait()

    pl.run_scoped(
        attention,
        pltpu.VMEM((D, slot), BF16),
        pltpu.VMEM((2, slot, LANES), BF16),
        pltpu.VMEM((2, LANES, slot), F32),
        pltpu.VMEM((3, slot + 8, LANES), F32),
        pltpu.VMEM((slot, 3 * local), BF16),
        pltpu.VMEM((D, 3 * local), BF16),
        pltpu.VMEM((half, D), F32),
        pltpu.VMEM((half, D), BF16),
        pltpu.VMEM((half, D), F32),
        pltpu.VMEM((2, slot, LANES), BF16),
        pltpu.VMEM((2, 2, slot, LANES), BF16),
        pltpu.VMEM((2, 2, slot, LANES), BF16),
        pltpu.VMEM((2, 2, slot, LANES), BF16),
        pltpu.VMEM((2, slot, 3 * LANES), BF16),
        pltpu.SemaphoreType.DMA((2, 5)),
    )
    for n in range(len(entries)):
        drain(n)
    for k in range(inner_bits + 1):
        small_copy(k).wait_send()
    for k in range(inner_bits + 1, inner_bits + 1 + line_steps):
        pl.when(line_sender(k - 1 - inner_bits))(lambda k=k: small_copy(k).wait_send())


def finish_kernel(
    gr_in, ge_in, go_in, qkv_in, act_in, gin_in,
    act_ref, gin_ref, q_ref, k_ref, v_ref, go_ref, ge_ref, gr_ref,
):
    act_ref[...] = act_in[...]
    gin_ref[...] = gin_in[...]
    for j, ref in enumerate((q_ref, k_ref, v_ref)):
        ref[...] = qkv_in[0, :, j * LANES : (j + 1) * LANES].astype(F32)
    ge_ref[...] = ge_in[0].astype(F32)
    gr_ref[...] = gr_in[0].astype(F32).T

    @pl.when(pl.program_id(0) == 0)
    def _():
        go_ref[...] = go_in[0].astype(F32).T


def params(vmem, **kw):
    return pltpu.CompilerParams(vmem_limit_bytes=vmem * MIB, **kw)


def body(
    token_ids, lengths, query_weight, key_weight, value_weight, output_weight,
    expand_weight, reduce_weight, dconv_taps, gain_first, bias_first,
    gain_second, bias_second, cotangent,
):
    half = token_ids.shape[1]
    slot = 2 * half
    local = query_weight.shape[1]
    units = expand_weight.shape[1]
    pairs = local // LANES
    outer = lax.axis_size("outer")
    inner = lax.axis_size("inner")
    inner_bits = inner.bit_length() - 1
    rows = D // inner
    width = 3 * LANES

    def swap(value):
        return lax.ppermute(value, "head", [(0, 1), (1, 0)])

    shape = jax.ShapeDtypeStruct
    vectors = jnp.stack([gain_first, bias_first, gain_second, bias_second])
    smem = pl.BlockSpec(memory_space=pltpu.SMEM)
    anywhere = pl.BlockSpec(memory_space=pl.ANY)
    dma = pltpu.SemaphoreType.DMA
    hd = whole((half, D))
    hl = whole((half, local))
    ld = whole((local, D))
    vec = whole((4, D))
    we_oth, wr_oth, wo_oth = swap(expand_weight), swap(reduce_weight), swap(output_weight)

    column = pl.BlockSpec((D, LANES), lambda p: (0, p))
    taps_spec = pl.BlockSpec((3, 3, LANES), lambda p: (0, 0, p))
    pair_rows = pl.BlockSpec((slot, LANES), lambda p: (0, p))
    pair_heads = pl.BlockSpec((2, slot, LANES), lambda p: (p, 0, 0))
    raw_spec = pl.BlockSpec((slot, 3 * LANES), lambda p: (0, p))
    attended, qa, ka, va, raw, embedded, normed_t, att_own, att_oth = pl.pallas_call(
        forward_kernel,
        grid=(pairs,),
        in_specs=[smem, whole((1, half)), vec, column, column, column, taps_spec],
        out_specs=[pair_rows, pair_heads, pair_heads, pair_heads, raw_spec, hd, whole((D, slot)), hl, hl],
        out_shape=[shape((slot, local), BF16)]
        + [shape((2 * pairs, slot, LANES), BF16)] * 3
        + [shape((slot, 3 * local), BF16), shape((half, D), F32), shape((D, slot), BF16)]
        + [shape((half, local), BF16)] * 2,
        scratch_shapes=[
            pltpu.VMEM((slot, D), BF16),
            pltpu.VMEM((slot + 8, LANES), F32),
            pltpu.VMEM((pairs, half, LANES), BF16),
            pltpu.VMEM((pairs, half, LANES), BF16),
            dma((PIECES,)), dma((PIECES,)), dma((pairs,)), dma((pairs,)),
        ],
        compiler_params=params(58, collective_id=0, has_side_effects=True),
        name="attention_forward",
    )(
        lengths, token_ids, vectors,
        query_weight, key_weight, value_weight, dconv_taps,
    )

    steps = units // D
    split = D // width
    fed = 2 * steps * split + 1
    chunks = fed + pairs
    twos = (2,) * inner_bits
    line_stages = inner_bits + outer
    vmem = lambda dims, kind: pltpu.VMEM(dims, kind)
    sums, small, activations, grad_input = pl.pallas_call(
        functools.partial(layer_kernel, inner_bits, outer),
        in_specs=[smem, vec, whole((3, 3, local))] + [anywhere] * 19,
        out_specs=[whole((chunks, rows, width)), whole((16, D)), anywhere, anywhere],
        out_shape=[
            shape((chunks, rows, width), BF16), shape((16, D), F32), shape((half, D), F32), shape((half, D), F32)
        ],
        scratch_shapes=[
            vmem((half, D), F32),
            vmem((chunks,) + twos + (rows, width), BF16),
            vmem((chunks, rows, width), BF16),
            vmem((chunks, rows, width), BF16),
            vmem((slot, local), BF16),
            vmem((2, 2, D, D), BF16),
            vmem((D, local), BF16),
            vmem((half, D), BF16),
            vmem((inner_bits + 2, 16, D), F32),
            vmem((inner_bits + 3, 16, D), F32),
            dma((10 + 4 * steps + 3 * pairs,)),
            dma((chunks + 1, line_stages)), dma((chunks + 1, line_stages)),
            dma((line_stages + 1,)), dma((line_stages + 1,)),
            dma((steps + 2, 2)), dma((steps + 2, 2)),
        ]
        + [vmem((chunks,) + (2,) * (inner_bits - 1 - s) + (rows, width), BF16) for s in range(inner_bits)],
        compiler_params=params(63, collective_id=1, has_side_effects=True),
        name="layer",
    )(
        lengths, vectors, dconv_taps,
        att_own, att_oth, embedded, cotangent[0], output_weight, wo_oth,
        expand_weight, we_oth, reduce_weight, wr_oth, query_weight, key_weight, value_weight,
        attended, qa, ka, va, raw, normed_t,
    )
    many = steps * split
    part = half // many
    some_rows = pl.BlockSpec((part, D), lambda i: (i, 0))
    pick = lambda index: pl.BlockSpec((1, rows, width), lambda i: (index(i), 0, 0))
    last = lambda i: jnp.minimum(i, pairs - 1)
    chunk_at = lambda i: (i // split) * 2 * split + i % split
    out_pair = pl.BlockSpec((rows, LANES), lambda i: (0, last(i)))
    activations, grad_input, gq, gk, gv, go_sum, ge_sum, gr_sum = pl.pallas_call(
        finish_kernel,
        grid=(many,),
        in_specs=[
            pick(chunk_at), pick(lambda i: chunk_at(i) + split), pick(lambda i: fed - 1),
            pick(lambda i: fed + last(i)), some_rows, some_rows,
        ],
        out_specs=[
            some_rows, some_rows, out_pair, out_pair, out_pair, whole((local, rows)),
            pl.BlockSpec((rows, width), lambda i: (0, i)), pl.BlockSpec((width, rows), lambda i: (i, 0)),
        ],
        out_shape=[shape((half, D), F32)] * 2
        + [shape((rows, local), F32)] * 3
        + [shape((local, rows), F32), shape((rows, units), F32), shape((units, rows), F32)],
        compiler_params=params(32),
        name="finish",
    )(sums, sums, sums, sums, activations, grad_input)
    return (
        activations[None],
        grad_input[None],
        gq,
        gk,
        gv,
        go_sum,
        ge_sum,
        gr_sum,
        small[4:13].reshape(3, 3, D),
        small[0],
        small[1],
        small[2],
        small[3],
    )


def solution(mesh):
    return jax.shard_map(
        body,
        mesh=mesh,
        in_specs=(
            P(("outer", "inner"), "head"),
            P(("outer", "inner")),
            P(None, "head"),
            P(None, "head"),
            P(None, "head"),
            P("head", None),
            P(None, "head"),
            P("head", None),
            P(None, None, "head"),
            P(),
            P(),
            P(),
            P(),
            P(("outer", "inner"), "head", None),
        ),
        out_specs=(
            P(("outer", "inner"), "head", None),
            P(("outer", "inner"), "head", None),
            P("inner", "head"),
            P("inner", "head"),
            P("inner", "head"),
            P("head", "inner"),
            P("inner", "head"),
            P("head", "inner"),
            P(),
            P(),
            P(),
            P(),
            P(),
        ),
        check_vma=False,
    )
```

```python
import functools
import math

import jax
import jax.numpy as jnp
from jax import lax
from jax.experimental import pallas as pl
from jax.experimental.pallas import tpu as pltpu
from jax.sharding import PartitionSpec as P

HEAD_DIM = 64
D = 768
BLOCK = 256
LANES = 128
EPS = 1e-05
MODULUS = 32749
NEGATIVE = -1e30
SCALE = HEAD_DIM ** (-0.5)
F32 = jnp.float32
BF16 = jnp.bfloat16
MIB = 1024 * 1024

SINE = (
    4.442882913726386,
    -7.308248583654593,
    3.606466623722958,
    -0.8474403474577161,
    0.11605422299047748,
    -0.010267162611370253,
    0.0005523348366953617,
)


def dot(a, b):
    return lax.dot_general(a, b, (((1,), (0,)), ((), ())), preferred_element_type=F32)


def dot_nt(a, b):
    return lax.dot_general(a, b, (((1,), (1,)), ((), ())), preferred_element_type=F32)


def whole(shape):
    return pl.BlockSpec(shape, lambda *_: (0,) * len(shape))


def normalise(values):
    centre = values - jnp.mean(values, axis=-1, keepdims=True)
    spread = jnp.mean(centre * centre, axis=-1, keepdims=True)
    scale = lax.rsqrt(spread + EPS)
    return centre * scale, scale


def norm_back(grad, hat, scale, gain):
    q = grad * gain
    mean_q = jnp.mean(q, axis=-1, keepdims=True)
    mean_qh = jnp.mean(q * hat, axis=-1, keepdims=True)
    return scale * (q - mean_q - hat * mean_qh)


def lane_ids(rows):
    return lax.broadcasted_iota(jnp.int32, (rows, LANES), 1)


def split_three(column):
    high = column.astype(BF16).astype(F32)
    rest = column - high
    middle = rest.astype(BF16).astype(F32)
    return high, middle, rest - middle


def with_parts(base, lane, offset, column):
    high, middle, small = split_three(column)
    base = jnp.where(lane == offset + 1, high, base)
    base = jnp.where(lane == offset + 2, middle, base)
    return jnp.where(lane == offset + 3, small, base)


def remote(src, dst, send, recv, **place):
    return pltpu.make_async_remote_copy(
        src_ref=src, dst_ref=dst, send_sem=send, recv_sem=recv,
        device_id=place, device_id_type=pl.DeviceIdType.MESH,
    )


def greet(*places):
    barrier = pltpu.get_barrier_semaphore()
    for place in places:
        pl.semaphore_signal(barrier, inc=1, device_id=place, device_id_type=pl.DeviceIdType.MESH)
    pl.semaphore_wait(barrier, len(places))


def rows_of(which, half):
    return pl.ds(pl.multiple_of(which * half, half), half)


def embed_rows(tok_ref, gain, bias, emb_ref, normed_ref, base, first):
    tokens = jnp.broadcast_to(tok_ref[:, pl.ds(first, LANES)], (LANES, LANES)).T
    parts = []
    for c in range(D // LANES):
        column = lax.broadcasted_iota(jnp.int32, (1, LANES), 1) + c * LANES
        product = tokens * (column + 1) + column * column
        turns = jnp.floor(product.astype(F32) * (1.0 / MODULUS) + 0.5)
        left = product - turns.astype(jnp.int32) * MODULUS
        u = left.astype(F32) * (2.0 / MODULUS)
        z = u * u
        value = jnp.full_like(u, SINE[-1])
        for coefficient in SINE[-2::-1]:
            value = value * z + coefficient
        parts.append(value * u)
    embedded = jnp.concatenate(parts, axis=1)
    emb_ref[pl.ds(first, LANES), :] = embedded
    hat, _ = normalise(embedded)
    rows = pl.ds(pl.multiple_of(base + first, LANES), LANES)
    normed_ref[rows, :] = (hat * gain + bias).astype(BF16)


PIECES = 3


def row_of(ref):
    return ref[...].reshape(1, D)


def forward_kernel(
    len_ref, tok_ref, gain_ref, bias_ref, wq_ref, wk_ref, wv_ref, taps_ref, we_hbm, wr_hbm, wo_hbm,
    att_ref, qa_ref, ka_ref, va_ref, raw_ref, emb_ref, nt_ref, att_own_ref, att_oth_ref,
    we_oth_hbm, wr_oth_hbm, wo_oth_hbm,
    normed_ref, shift_ref, wcat_ref, give_ref, got_ref,
    row_send, row_recv, att_send, att_recv, weight_send, weight_recv,
):
    slot = att_ref.shape[0]
    half = slot // 2
    step = pl.program_id(0)
    head = lax.axis_index("head")
    partner = 1 - head
    piece = half // PIECES

    def row_copy(k):
        rows = pl.ds(pl.multiple_of(head * half + k * piece, piece), piece)
        return remote(normed_ref.at[rows], normed_ref.at[rows], row_send.at[k], row_recv.at[k], head=partner)

    def att_copy(p):
        return remote(give_ref.at[p], got_ref.at[p], att_send.at[p], att_recv.at[p], head=partner)

    def weight_copy(k):
        src, dst = ((wo_hbm, wo_oth_hbm), (we_hbm, we_oth_hbm), (wr_hbm, wr_oth_hbm))[k]
        return remote(src, dst, weight_send.at[k], weight_recv.at[k], head=partner)

    @pl.when(step == 0)
    def _():
        greet({"head": partner})
        base = head * half
        for k in range(PIECES):
            def embed_step(i, _):
                first = pl.multiple_of(k * piece + i * LANES, LANES)
                embed_rows(tok_ref, row_of(gain_ref), row_of(bias_ref), emb_ref, normed_ref, base, first)
                return 0

            lax.fori_loop(0, piece // LANES, embed_step, 0)
            row_copy(k).start()
        for k in range(3):
            weight_copy(k).start()
        nt_ref[:, rows_of(head, half)] = normed_ref[rows_of(head, half), :].T
        for k in range(PIECES):
            row_copy(k).wait()
        nt_ref[:, rows_of(partner, half)] = normed_ref[rows_of(partner, half), :].T

    for j, w_ref in enumerate((wq_ref, wk_ref, wv_ref)):
        wcat_ref[:, j * LANES : (j + 1) * LANES] = w_ref[...]
    shift_ref[:, 0:8, :] = jnp.zeros((3, 8, LANES), F32)
    lane = lane_ids(BLOCK)

    def project(r, _):
        first = pl.multiple_of(r * BLOCK, BLOCK)
        rows = pl.ds(first, BLOCK)
        raws = dot(normed_ref[rows, :], wcat_ref[...])
        raw_ref[rows, :] = raws.astype(BF16)
        mixed = []
        for j in range(3):
            raw = raws[:, j * LANES : (j + 1) * LANES]
            shift_ref[j, 8 : 8 + BLOCK, :] = raw
            one = shift_ref[j, 7 : 7 + BLOCK, :]
            two = shift_ref[j, 6 : 6 + BLOCK, :]
            value = taps_ref[j, 0:1, :] * raw + taps_ref[j, 1:2, :] * one + taps_ref[j, 2:3, :] * two
            mixed.append(value * SCALE if j == 0 else value)
            shift_ref[j, 0:8, :] = raw[BLOCK - 8 :, :]
        row = lax.broadcasted_iota(jnp.int32, (BLOCK, 1), 0) + first
        key_bias = jnp.where(row < len_ref[0], 0.0, NEGATIVE)
        for e in range(2):
            mine = (lane // HEAD_DIM) == e
            other = HEAD_DIM * (1 - e)
            ones = jnp.where((lane > other) & (lane < other + 4), 1.0, 0.0)
            qa_ref[e, rows, :] = jnp.where(mine, mixed[0], jnp.where(lane == other, 1.0, 0.0)).astype(BF16)
            ka_ref[e, rows, :] = jnp.where(mine, mixed[1], jnp.where(lane == other, key_bias, ones)).astype(BF16)
            va_ref[e, rows, :] = jnp.where(mine, mixed[2], ones).astype(BF16)
        return 0

    lax.fori_loop(0, slot // BLOCK, project, 0)
    block_lane = lane_ids(BLOCK)
    causal = lax.broadcasted_iota(jnp.int32, (BLOCK, BLOCK), 1) <= lax.broadcasted_iota(
        jnp.int32, (BLOCK, BLOCK), 0
    )
    for i in range(slot // BLOCK):
        rows = slice(i * BLOCK, (i + 1) * BLOCK)
        before = i * BLOCK
        heads = []
        for e in range(2):
            other = HEAD_DIM * (1 - e)
            query = qa_ref[e, rows, :]
            diagonal = jnp.where(causal, dot_nt(query, ka_ref[e, rows, :]), NEGATIVE)
            row_max = jnp.max(diagonal, axis=1, keepdims=True)
            if before:
                scores = dot_nt(query, ka_ref[e, :before, :])
                row_max = jnp.maximum(row_max, jnp.max(scores, axis=1, keepdims=True))
            out = dot(jnp.exp(diagonal - row_max).astype(BF16), va_ref[e, rows, :])
            if before:
                out += dot(jnp.exp(scores - row_max).astype(BF16), va_ref[e, :before, :])
            total = out[:, other + 1 : other + 2]
            heads.append(out / total)
            log_norm = -(row_max + jnp.log(total))
            qa_ref[e, rows, :] = with_parts(query.astype(F32), block_lane, other, log_norm).astype(BF16)
        att_ref[rows, :] = jnp.where(block_lane < HEAD_DIM, heads[0], heads[1]).astype(BF16)

    for p in range(att_own_ref.shape[1] // LANES):
        @pl.when(step == p)
        def _():
            give_ref[p] = att_ref[rows_of(partner, half), :]
            att_copy(p).start()
            att_own_ref[:, p * LANES : (p + 1) * LANES] = att_ref[rows_of(head, half), :]

    @pl.when(step == pl.num_programs(0) - 1)
    def _():
        for p in range(att_own_ref.shape[1] // LANES):
            att_copy(p).wait()
            att_oth_ref[:, p * LANES : (p + 1) * LANES] = got_ref[p]
        for k in range(3):
            weight_copy(k).wait()


def layer_kernel(
    inner_bits, outer,
    len_ref, gain_first_ref, gain_second_ref, bias_second_ref, taps_ref,
    att_own_hbm, att_oth_hbm, emb_hbm, cot_hbm, wo_own_hbm, wo_oth_hbm,
    we_own_hbm, we_oth_hbm, wr_own_hbm, wr_oth_hbm, wq_hbm, wk_hbm, wv_hbm,
    att_hbm, qa_hbm, ka_hbm, va_hbm, raw_hbm, nt_hbm,
    sum_ref, small_ref, act_hbm, gin_hbm, sq_hbm,
    gh_ref, g_ref, rz_ref, rc_ref, do_ref, got_ref, got_go, got_first, acc_ref, got_small, late_ref, got_group, got_outer,
    load_sem, send_sem, recv_sem, small_send, small_recv, core_send, core_recv,
    group_send, group_recv, outer_send, outer_recv, *halves,
):
    half = gh_ref.shape[0]
    slot = 2 * half
    local = att_own_hbm.shape[1]
    units = we_own_hbm.shape[1]
    steps = units // D
    width = sum_ref.shape[2]
    split = D // width
    pairs = local // LANES
    fed = 2 * steps * split + 1
    blocks = slot // BLOCK
    head = lax.axis_index("head")
    partner = 1 - head
    mine = lax.axis_index("inner")
    line = lax.axis_index("outer")
    centre = outer // 2
    left = line < centre
    depth = jnp.where(left, centre - 1 - line, line - centre)
    inward = jnp.where(left, line + 1, line - 1)
    outward = jnp.where(left, line - 1, line + 1)
    bit = [(mine // (1 << b)) % 2 for b in range(inner_bits)]
    across = [mine + (1 << b) * (1 - 2 * bit[b]) for b in range(inner_bits)]

    def chunk_of(c, kind, k):
        return (2 * c + kind) * split + k

    entries = [(c, 0, width, c % 2) for c in range(fed + pairs - 1)]
    entries += [(fed + pairs - 1, j * LANES, LANES, j % 2) for j in range(3)]
    order_of = [tuple((b + first) % inner_bits for b in range(inner_bits)) for first in range(2)]
    line_steps = 2 * centre - 1
    stage_count = inner_bits + line_steps + 1

    def index_of(fixed):
        return tuple(fixed.get(b, slice(None)) for b in reversed(range(inner_bits)))

    def lanes(entry):
        return slice(entry[1], entry[1] + entry[2])

    def halving(n, s):
        c, _, _, kind = entries[n]
        order = order_of[kind]
        fixed = {b: bit[b] for b in order[:s]}
        b = order[s]
        give = g_ref.at[(c,) + index_of({**fixed, b: 1 - bit[b]}) + (slice(None), lanes(entries[n]))]
        land = halves[s].at[(c,) + (slice(None),) * (inner_bits - 1 - s) + (slice(None), lanes(entries[n]))]
        return remote(give, land, send_sem.at[n, s], recv_sem.at[n, s], inner=across[b])

    def add_half(n, s):
        c, _, _, kind = entries[n]
        order = order_of[kind]
        index = (c,) + index_of({b: bit[b] for b in order[: s + 1]}) + (slice(None), lanes(entries[n]))
        land = (c,) + (slice(None),) * (inner_bits - 1 - s) + (slice(None), lanes(entries[n]))
        g_ref[index] = g_ref[index] + halves[s][land]

    def own(n):
        return (entries[n][0],) + tuple(bit[b] for b in reversed(range(inner_bits))) + (slice(None), lanes(entries[n]))

    def flat(n):
        return (entries[n][0], slice(None), lanes(entries[n]))

    def line_sender(t):
        if t < centre - 1:
            return depth == centre - 1 - t
        if t == centre - 1:
            return depth == 0
        return depth == t - centre

    def line_copy(n, t):
        s = inner_bits + t
        sems = (send_sem.at[n, s], recv_sem.at[n, s])
        if t < centre - 1:
            return remote(g_ref.at[own(n)], rz_ref.at[flat(n)], *sems, outer=inward)
        if t == centre - 1:
            return remote(g_ref.at[own(n)], rc_ref.at[flat(n)], *sems, outer=inward)
        return remote(rc_ref.at[flat(n)], rc_ref.at[flat(n)], *sems, outer=outward)

    def line_finish(n, t):
        if t < centre - 1:
            @pl.when(depth == centre - 2 - t)
            def _():
                line_copy(n, t).wait_recv()
                g_ref[own(n)] = g_ref[own(n)] + rz_ref[flat(n)]
        elif t == centre - 1:
            @pl.when(depth == 0)
            def _():
                line_copy(n, t).wait_recv()
                rc_ref[flat(n)] = g_ref[own(n)] + rc_ref[flat(n)]
        else:
            pl.when(depth == t - centre + 1)(lambda: line_copy(n, t).wait_recv())

    def advance(n, stage):
        if 0 < stage <= inner_bits:
            halving(n, stage - 1).wait_recv()
            add_half(n, stage - 1)
        elif stage > inner_bits:
            line_finish(n, stage - inner_bits - 1)
        if stage < inner_bits:
            halving(n, stage).start()
        elif stage < stage_count - 1:
            t = stage - inner_bits
            pl.when(line_sender(t))(lambda: line_copy(n, t).start())
        else:
            sum_ref[flat(n)] = rc_ref[flat(n)]

    def drain(n):
        for s in range(inner_bits):
            halving(n, s).wait_send()
        for t in range(line_steps):
            pl.when(line_sender(t))(lambda t=t: line_copy(n, t).wait_send())

    clock = {}
    now = 6.0
    for c in range(steps):
        for k, spent in enumerate((2.8, 2.8, 0.3, 2.8, 2.8, 1.5)):
            now += spent
            clock[("feed", c, k)] = now
        now += 1.4
    for k in range(3):
        now += 1.5
        clock[("norm", k)] = now
    for p in range(pairs):
        for j in range(blocks):
            clock[("pair", p, j)] = now + 2.5 * j
        now += 2.5 * blocks + 2.0
        clock[("taps", p)] = now
    for k in range(2 * stage_count + 8):
        clock[("tail", k)] = now + 2.5 * k
    ready = {}
    for c in range(steps):
        for k in range(split):
            ready[chunk_of(c, 0, k)] = ("feed", c, 2)
            ready[chunk_of(c, 1, k)] = ("feed", c, 5)
    ready[fed - 1] = ("norm", 2)
    for p in range(pairs):
        ready[fed + p] = ("taps", p) if p < pairs - 1 else ("tail", 0)
    plan = {}
    order = list(clock)
    for n, (c, _, _, _) in enumerate(entries):
        last = c == fed + pairs - 1
        spot = order.index(ready[c])
        for stage in range(stage_count):
            if stage:
                lag = (4.0 if stage == 1 else 2.0) if last else (9.0 if stage == 1 else 5.0)
                due = clock[order[spot]] + lag
                spot = min(spot + 1, len(order) - 1)
                while spot < len(order) - 1 and (order[spot][0] == "norm" or clock[order[spot]] < due):
                    spot += 1
            plan.setdefault(order[spot], []).append((n, stage))

    def tick(place):
        for n, stage in plan.pop(place, ()):
            advance(n, stage)

    def small_copy(k):
        sems = (small_send.at[k], small_recv.at[k])
        if k == 0:
            return remote(acc_ref.at[0], got_small.at[0], *sems, head=partner)
        if k <= inner_bits:
            return remote(acc_ref.at[k], got_small.at[k], *sems, inner=across[k - 1])
        t = k - 1 - inner_bits
        if t <= centre - 1:
            return remote(acc_ref.at[inner_bits + 1], got_small.at[inner_bits + 1 + (t == centre - 1)], *sems, outer=inward)
        last = got_small.at[inner_bits + 2]
        return remote(last, last, *sems, outer=outward)

    def small_step(k):
        if 0 < k <= inner_bits + 1:
            small_copy(k - 1).wait_recv()
            acc_ref[k] = acc_ref[k - 1] + got_small[k - 1]
        elif k > inner_bits + 1:
            t = k - 2 - inner_bits
            if t < centre - 1:
                @pl.when(depth == centre - 2 - t)
                def _():
                    small_copy(k - 1).wait_recv()
                    acc_ref[inner_bits + 1] = acc_ref[inner_bits + 1] + got_small[inner_bits + 1]
            elif t == centre - 1:
                @pl.when(depth == 0)
                def _():
                    small_copy(k - 1).wait_recv()
                    got_small[inner_bits + 2] = acc_ref[inner_bits + 1] + got_small[inner_bits + 2]
            else:
                pl.when(depth == t - centre + 1)(lambda: small_copy(k - 1).wait_recv())
        if k <= inner_bits:
            small_copy(k).start()
        elif k <= inner_bits + line_steps:
            pl.when(line_sender(k - 1 - inner_bits))(lambda: small_copy(k).start())
        else:
            small_ref[...] = got_small[inner_bits + 2]

    small_steps = inner_bits + line_steps + 2

    inner = 1 << inner_bits
    group = 2 * inner
    seat = mine * 2 + head

    def group_place(k, way):
        other = lax.rem(seat + group + way * k, group)
        return other, {"inner": other // 2, "head": lax.rem(other, 2)}

    def outer_place(k, way):
        other = lax.rem(line + outer + way * k, outer)
        return other, {"outer": other}

    def late_copies(places, count, me, src, land, sends, recvs):
        give = [remote(src, land.at[me], sends.at[k], recvs.at[k], **places(k, 1)[1]) for k in range(1, count)]
        take = [
            remote(src, land.at[places(k, -1)[0]], sends.at[k], recvs.at[k], **places(k, 1)[1]) for k in range(1, count)
        ]
        return give, take

    group_give, group_take = late_copies(
        group_place, group, seat, late_ref.at[0], got_group, group_send, group_recv
    )
    outer_give, outer_take = late_copies(outer_place, outer, line, late_ref.at[1], got_outer, outer_send, outer_recv)

    load_count = iter(range(load_sem.shape[0]))

    def load(src, dst):
        return pltpu.make_async_copy(src, dst, load_sem.at[next(load_count)])

    row = lax.broadcasted_iota(jnp.int32, (half, 1), 0) + head * half
    valid = row < len_ref[0]

    def greet_all():
        barrier = pltpu.get_barrier_semaphore()
        places = [group_place(k, 1)[1] for k in range(1, group)] + [outer_place(k, 1)[1] for k in range(1, outer)]
        for place in places:
            pl.semaphore_signal(barrier, inc=1, device_id=place, device_id_type=pl.DeviceIdType.MESH)
        pl.semaphore_wait(barrier, len(places))

    two_rows = half // 2

    def halves_of(step):
        def run(r, _):
            step(r, pl.ds(pl.multiple_of(r * two_rows, two_rows), two_rows))
            return 0

        lax.fori_loop(0, 2, run, 0)

    def feed_forward(
        att_ref, wo_ref, we_ref, wr_ref, cot_ref, hid_ref, gn_ref,
        n2_ref, n2t_ref, gl_ref, glt_ref, give_ref, relu_ref, sq_ref,
    ):
        give_att = relu_ref.at[0, :, 0:local]
        give_go = relu_ref.at[1, :, 0:local]
        loads = {}
        for k, (att, wo) in enumerate(((att_own_hbm, wo_own_hbm), (att_oth_hbm, wo_oth_hbm))):
            loads["att", k] = load(att, att_ref.at[k])
            loads["wo", k] = load(wo, wo_ref.at[k])
        loads["emb"] = load(emb_hbm, hid_ref)
        loads["cot"] = load(cot_hbm, cot_ref)
        for c in range(steps):
            cols = pl.ds(c * D, D)
            for k, we in ((1, we_oth_hbm), (0, we_own_hbm)):
                loads["we", c, k] = load(we.at[:, cols], we_ref.at[c, k])
            for k, wr in ((1, wr_oth_hbm), (0, wr_own_hbm)):
                loads["wr", c, k] = load(wr.at[cols, :], wr_ref.at[c, k])
        for copy in loads.values():
            copy.start()
        greet_all()
        for key in (("att", 0), ("wo", 0), ("att", 1), ("wo", 1), "emb", "cot"):
            loads[key].wait()
        gain, bias = row_of(gain_second_ref), row_of(bias_second_ref)

        def open_rows(r, rows):
            hidden = hid_ref[rows, :] + dot(att_ref[0, rows, :], wo_ref[0]) + dot(att_ref[1, rows, :], wo_ref[1])
            hid_ref[rows, :] = hidden
            hat, _ = normalise(hidden)
            normed = (hat * gain + bias).astype(BF16)
            n2_ref[rows, :] = normed
            n2t_ref[:, rows] = normed.T
            position = lax.broadcasted_iota(jnp.int32, (two_rows, 1), 0) + head * half + r * two_rows
            grad = jnp.where(position < len_ref[0], cot_ref[rows, :], 0.0)
            cot_ref[rows, :] = grad
            gl_ref[rows, :] = grad.astype(BF16)
            glt_ref[:, rows] = grad.astype(BF16).T

        halves_of(open_rows)
        hid_store = load(hid_ref, act_hbm)
        hid_store.start()

        def grad_copy(c, kind):
            return remote(
                give_ref.at[kind], got_ref.at[c % 2, kind], core_send.at[c, kind], core_recv.at[c, kind], head=partner
            )

        def put_own(c, kind, r, value):
            for k in range(split):
                part = value[:, k * width : (k + 1) * width].astype(BF16)
                g_ref[chunk_of(c, kind, k), r] = part.reshape(g_ref.shape[2:])

        def add_other(c, kind):
            grad_copy(c, kind).wait_recv()
            for k in range(split):
                got = got_ref[c % 2, kind, :, k * width : (k + 1) * width]
                g_ref[chunk_of(c, kind, k)] += got.reshape(g_ref.shape[1:])

        def weight_grad(c, kind, k, left_ref, right_ref):
            def run(r, rows):
                grad = dot(left_ref[rows, :], right_ref[...])
                if k == 1:
                    give_ref[kind, rows, :] = grad.astype(BF16)
                else:
                    put_own(c, kind, r, grad)

            if k == 1 and c:
                grad_copy(c - 1, kind).wait_send()
            halves_of(run)
            if k == 1:
                grad_copy(c, kind).start()

        stores = []
        for c in range(steps):
            for k in (1, 0):
                loads["we", c, k].wait()

                def expand(r, rows):
                    relu = jnp.maximum(dot(n2_ref[rows, :], we_ref[c, k]), 0.0)
                    relu_ref[k, rows, :] = relu.astype(BF16)
                    sq_ref[c, k, rows, :] = (relu * relu).astype(BF16)

                halves_of(expand)
                stores.append(load(sq_ref.at[c, k], sq_hbm.at[c, k]))
                stores[-1].start()
                weight_grad(c, 0, k, glt_ref, sq_ref.at[c, k])
                tick(("feed", c, 1 - k))
            add_other(c, 0)
            tick(("feed", c, 2))
            for k in (1, 0):
                loads["wr", c, k].wait()

                def reduce_back(r, rows):
                    back = dot_nt(gl_ref[rows, :], wr_ref[c, k])
                    relu_ref[k, rows, :] = (back * (2.0 * relu_ref[k, rows, :].astype(F32))).astype(BF16)

                halves_of(reduce_back)
                weight_grad(c, 1, k, n2t_ref, relu_ref.at[k])
                tick(("feed", c, 4 - k))
            for k in (1, 0):
                def expand_back(r, rows):
                    gn = dot_nt(relu_ref[k, rows, :], we_ref[c, k])
                    if c == 0 and k == 1:
                        gn_ref[rows, :] = gn
                    else:
                        gn_ref[rows, :] += gn

                halves_of(expand_back)
                if k == 1:
                    add_other(c, 1)
                    tick(("feed", c, 5))
        acc_ref[0] = jnp.zeros(acc_ref.shape[1:], F32)

        def close_rows(r, rows):
            hat, scale = normalise(hid_ref[rows, :])
            grad_n = gn_ref[rows, :]
            acc_ref[0, 2:3, :] += jnp.sum(grad_n * hat, axis=0, keepdims=True)
            acc_ref[0, 3:4, :] += jnp.sum(grad_n, axis=0, keepdims=True)
            grad_h = cot_ref[rows, :] + norm_back(grad_n, hat, scale, gain)
            gh_ref[rows, :] = grad_h
            low = grad_h.astype(BF16)
            n2_ref[rows, :] = low
            n2t_ref[:, rows] = low.T
            give_att[rows, :] = dot_nt(low, wo_ref[1]).astype(BF16)

        halves_of(close_rows)
        own_rows = rows_of(head, half)
        att_copy = remote(give_att, do_ref.at[own_rows], core_send.at[steps, 0], core_recv.at[steps, 0], head=partner)
        att_copy.start()
        tick(("norm", 0))
        give_go[...] = dot(n2t_ref[...], att_ref[1]).astype(BF16)
        go_copy = remote(give_go, got_go, core_send.at[steps, 1], core_recv.at[steps, 1], head=partner)
        go_copy.start()
        do_ref[own_rows, :] = dot_nt(n2_ref[...], wo_ref[0]).astype(BF16)
        tick(("norm", 1))
        grad_o = dot(n2t_ref[...], att_ref[0]).astype(BF16)
        go_copy.wait()
        g_ref[fed - 1] = (grad_o + got_go[...]).reshape(g_ref.shape[1:])
        tick(("norm", 2))
        for kind in range(2):
            grad_copy(steps - 1, kind).wait_send()
        for copy in [hid_store] + stores:
            copy.wait()
        att_copy.wait()

    pl.run_scoped(
        feed_forward,
        pltpu.VMEM((2, half, local), BF16), pltpu.VMEM((2, local, D), BF16),
        pltpu.VMEM((steps, 2, D, D), BF16), pltpu.VMEM((steps, 2, D, D), BF16),
        pltpu.VMEM((half, D), F32), pltpu.VMEM((half, D), F32), pltpu.VMEM((half, D), F32),
        pltpu.VMEM((half, D), BF16), pltpu.VMEM((D, half), BF16),
        pltpu.VMEM((half, D), BF16), pltpu.VMEM((D, half), BF16),
        pltpu.VMEM((2, D, D), BF16), pltpu.VMEM((2, half, D), BF16), pltpu.VMEM((steps, 2, half, D), BF16),
    )

    def attention(
        all_ref, wcat_ref, nt_ref, doa_ref, dqt_ref, mix_ref, late,
        att_ref, qa_ref, ka_ref, va_ref, raw_ref, pair_sem,
    ):
        def pair_loads(p, place):
            two = pl.ds(2 * p, 2)
            one = pl.ds(pl.multiple_of(p * LANES, LANES), LANES)
            three = pl.ds(pl.multiple_of(p * 3 * LANES, LANES), 3 * LANES)
            return [
                pltpu.make_async_copy(ka_hbm.at[two], ka_ref.at[place], pair_sem.at[place, 0]),
                pltpu.make_async_copy(qa_hbm.at[two], qa_ref.at[place], pair_sem.at[place, 1]),
                pltpu.make_async_copy(att_hbm.at[:, one], att_ref.at[place], pair_sem.at[place, 2]),
                pltpu.make_async_copy(va_hbm.at[two], va_ref.at[place], pair_sem.at[place, 3]),
                pltpu.make_async_copy(raw_hbm.at[:, three], raw_ref.at[place], pair_sem.at[place, 4]),
            ]

        for copy in pair_loads(0, 0):
            copy.start()
        nt_load = load(nt_hbm, nt_ref)
        nt_load.start()
        for copy in late:
            copy.start()
        mix_ref[:, slot : slot + 8, :] = jnp.zeros((3, 8, LANES), F32)
        lane = lane_ids(slot)
        causal = lax.broadcasted_iota(jnp.int32, (BLOCK, BLOCK), 0) <= lax.broadcasted_iota(
            jnp.int32, (BLOCK, BLOCK), 1
        )
        block_lane = lane_ids(BLOCK)
        sub = lax.broadcasted_iota(jnp.int32, (LANES, slot), 0)

        def at_pair(p, kind, *rest):
            for q in range(pairs):
                if plan.get((kind, q) + rest):
                    pl.when(p == q)(functools.partial(tick, (kind, q) + rest))

        def one_pair(p, _):
            place = lax.rem(p, 2)
            one = pl.ds(pl.multiple_of(p * LANES, LANES), LANES)

            @pl.when(p + 1 < pairs)
            def _():
                for copy in pair_loads(p + 1, 1 - place):
                    copy.start()

            for copy in pair_loads(p, place):
                copy.wait()
            grad_out = do_ref[:, one].astype(F32)
            product = grad_out * att_ref[place].astype(F32)
            for e in range(2):
                in_head = (lane // HEAD_DIM) == e
                delta = -jnp.sum(jnp.where(in_head, product, 0.0), axis=1, keepdims=True)
                other = HEAD_DIM * (1 - e)
                doa_ref[e] = with_parts(jnp.where(in_head, grad_out, 0.0), lane, other, delta).astype(BF16)
            for j in range(blocks):
                at_pair(p, "pair", j)
                keys = slice(j * BLOCK, (j + 1) * BLOCK)
                first = j * BLOCK
                after = first + BLOCK
                dks, dvs = [], []
                for e in range(2):
                    ka = ka_ref[place, e, keys, :]
                    va = va_ref[place, e, keys, :]
                    kat = ka.T
                    spans = [(first, after, True)] + ([(after, slot, False)] if after < slot else [])
                    dk = dv = None
                    for lo, hi, masked in spans:
                        scores = dot_nt(ka, qa_ref[place, e, lo:hi, :])
                        if masked:
                            scores = jnp.where(causal, scores, NEGATIVE)
                        probs = jnp.exp(scores)
                        grads = (probs * dot_nt(va, doa_ref[e, lo:hi, :])).astype(BF16)
                        dv_part = dot(probs.astype(BF16), doa_ref[e, lo:hi, :])
                        dk_part = dot(grads, qa_ref[place, e, lo:hi, :])
                        dv = dv_part if dv is None else dv + dv_part
                        dk = dk_part if dk is None else dk + dk_part
                        if j:
                            dqt_ref[e, :, lo:hi] += dot(kat, grads)
                        else:
                            dqt_ref[e, :, lo:hi] = dot(kat, grads)
                    dks.append(dk)
                    dvs.append(dv)
                mix_ref[1, keys, :] = jnp.where(block_lane < HEAD_DIM, dks[0], dks[1])
                mix_ref[2, keys, :] = jnp.where(block_lane < HEAD_DIM, dvs[0], dvs[1])
            mix_ref[0, 0:slot, :] = (jnp.where(sub < HEAD_DIM, dqt_ref[0], dqt_ref[1]) * SCALE).T
            base = pl.multiple_of(p * 3 * LANES, LANES)
            for j in range(3):
                zero = mix_ref[j, 0:slot, :]
                one_on = mix_ref[j, 1 : 1 + slot, :]
                two_on = mix_ref[j, 2 : 2 + slot, :]
                raw = raw_ref[place, :, j * LANES : (j + 1) * LANES].astype(F32)
                cols = pl.ds(pl.multiple_of(head * local + p * LANES, LANES), LANES)
                value = 0.0
                for s, moved in enumerate((zero, one_on, two_on)):
                    total = jnp.sum(moved * raw, axis=0, keepdims=True)
                    acc_ref[0, 4 + 3 * j + s : 5 + 3 * j + s, cols] = total
                    value += taps_ref[j, s : s + 1, one] * moved
                all_ref[:, pl.ds(pl.multiple_of(base + j * LANES, LANES), LANES)] = value.astype(BF16)

            @pl.when(p == 0)
            def _():
                nt_load.wait()

            grads = dot(nt_ref[...], all_ref[:, pl.ds(base, 3 * LANES)]).astype(BF16)
            g_ref[fed + p] = grads.reshape(g_ref.shape[1:])
            at_pair(p, "taps")
            return 0

        lax.fori_loop(0, pairs, one_pair, 0)

    def tail(all_ref, wcat_ref, late, emb_ref, give_first, own_first, hid_ref, sq_ref, wr_ref):
        emb_load = load(emb_hbm, emb_ref)
        emb_load.start()
        tick(("tail", 0))
        hid_load = load(act_hbm, hid_ref)
        hid_load.start()
        ffn_loads = []
        for c in range(steps):
            for k, wr in ((1, wr_oth_hbm), (0, wr_own_hbm)):
                ffn_loads.append(load(sq_hbm.at[c, k], sq_ref.at[c, k]))
                ffn_loads.append(load(wr.at[pl.ds(c * D, D), :], wr_ref.at[c, k]))
        for copy in ffn_loads:
            copy.start()
        small_step(0)
        for copy in late:
            copy.wait()

        def other_rows(r, rows):
            there = pl.ds(pl.multiple_of(partner * half + r * two_rows, two_rows), two_rows)
            give_first[rows, :] = dot_nt(all_ref[there, :], wcat_ref[...]).astype(BF16)

        halves_of(other_rows)
        first_copy = remote(
            give_first, got_first, core_send.at[steps + 1, 0], core_recv.at[steps + 1, 0], head=partner
        )
        first_copy.start()
        tick(("tail", 1))
        small_step(1)

        def own_rows(r, rows):
            here = pl.ds(pl.multiple_of(head * half + r * two_rows, two_rows), two_rows)
            own_first[rows, :] = dot_nt(all_ref[here, :], wcat_ref[...])

        halves_of(own_rows)
        tick(("tail", 2))
        small_step(2)
        emb_load.wait()
        first_copy.wait()
        gain = row_of(gain_first_ref)
        late_ref[0] = jnp.zeros(late_ref.shape[1:], F32)

        def norm_rows(r, rows):
            grad_n = own_first[rows, :] + got_first[rows, :].astype(F32)
            hat, scale = normalise(emb_ref[rows, :])
            late_ref[0, 0:1, :] += jnp.sum(grad_n * hat, axis=0, keepdims=True)
            late_ref[0, 1:2, :] += jnp.sum(grad_n, axis=0, keepdims=True)
            gh_ref[rows, :] = gh_ref[rows, :] + norm_back(grad_n, hat, scale, gain)

        halves_of(norm_rows)
        for copy in group_give:
            copy.start()
        got_group[seat] = late_ref[0]
        gin_store = load(gh_ref, gin_hbm)
        gin_store.start()
        tick(("tail", 3))
        small_step(3)
        hid_load.wait()
        for copy in ffn_loads:
            copy.wait()

        def ffn_rows(first):
            rows = slice(first, first + two_rows)
            total = hid_ref[rows, :]
            for c in range(steps):
                for k in range(2):
                    total += dot(sq_ref[c, k, rows, :], wr_ref[c, k])
            hid_ref[rows, :] = total

        ffn_rows(0)
        tick(("tail", 4))
        for copy in group_take:
            copy.wait_recv()
        total = got_group[0]
        for k in range(1, group):
            total = total + got_group[k]
        late_ref[1] = total
        for copy in outer_give:
            copy.start()
        got_outer[line] = total
        small_step(4)
        ffn_rows(two_rows)
        act_store = load(hid_ref, act_hbm)
        act_store.start()
        tick(("tail", 5))
        small_step(5)
        for copy in outer_take:
            copy.wait_recv()
        total = got_outer[0]
        for k in range(1, outer):
            total = total + got_outer[k]
        now, k = 6, 6
        while plan or k < small_steps:
            assert ("tail", now) in clock or not plan
            tick(("tail", now))
            if k < small_steps:
                small_step(k)
            now, k = now + 1, k + 1
        small_ref[0:2, :] = total[0:2, :]
        gin_store.wait()
        act_store.wait()
        for copy in group_give + outer_give:
            copy.wait_send()

    def backward(all_ref, wcat_ref):
        late = []
        for p in range(pairs):
            for j, w_hbm in enumerate((wq_hbm, wk_hbm, wv_hbm)):
                base = (3 * p + j) * LANES
                late.append(load(w_hbm.at[:, pl.ds(p * LANES, LANES)], wcat_ref.at[:, pl.ds(base, LANES)]))
        pl.run_scoped(
            lambda nt, doa, dqt, mix, *rest: attention(all_ref, wcat_ref, nt, doa, dqt, mix, late, *rest),
            pltpu.VMEM((D, slot), BF16),
            pltpu.VMEM((2, slot, LANES), BF16),
            pltpu.VMEM((2, LANES, slot), F32),
            pltpu.VMEM((3, slot + 8, LANES), F32),
            pltpu.VMEM((2, slot, LANES), BF16),
            pltpu.VMEM((2, 2, slot, LANES), BF16),
            pltpu.VMEM((2, 2, slot, LANES), BF16),
            pltpu.VMEM((2, 2, slot, LANES), BF16),
            pltpu.VMEM((2, slot, 3 * LANES), BF16),
            pltpu.SemaphoreType.DMA((2, 5)),
        )
        pl.run_scoped(
            functools.partial(tail, all_ref, wcat_ref, late),
            pltpu.VMEM((half, D), F32),
            pltpu.VMEM((half, D), BF16),
            pltpu.VMEM((half, D), F32),
            pltpu.VMEM((half, D), F32),
            pltpu.VMEM((steps, 2, half, D), BF16),
            pltpu.VMEM((steps, 2, D, D), BF16),
        )

    pl.run_scoped(backward, pltpu.VMEM((slot, 3 * local), BF16), pltpu.VMEM((D, 3 * local), BF16))
    for n in range(len(entries)):
        drain(n)
    for k in range(inner_bits + 1):
        small_copy(k).wait_send()
    for k in range(inner_bits + 1, inner_bits + 1 + line_steps):
        pl.when(line_sender(k - 1 - inner_bits))(lambda k=k: small_copy(k).wait_send())


def finish_kernel(
    gr_in, ge_in, go_in, qkv_in, act_in, gin_in, small_in,
    act_ref, gin_ref, q_ref, k_ref, v_ref, go_ref, ge_ref, gr_ref, taps_ref, *vec_refs,
):
    act_ref[...] = act_in[...]
    gin_ref[...] = gin_in[...]
    for j, ref in enumerate((q_ref, k_ref, v_ref)):
        ref[...] = qkv_in[0, :, j * LANES : (j + 1) * LANES].astype(F32)
    ge_ref[...] = ge_in[0].astype(F32)
    gr_ref[...] = gr_in[0].astype(F32)

    @pl.when(pl.program_id(0) == 0)
    def _():
        go_ref[...] = go_in[0].astype(F32)
        for j in range(3):
            taps_ref[j] = small_in[4 + 3 * j : 7 + 3 * j, :]
        for k, ref in enumerate(vec_refs):
            ref[...] = small_in[k, :]


def params(vmem, **kw):
    return pltpu.CompilerParams(vmem_limit_bytes=vmem * MIB, **kw)


def body(
    token_ids, lengths, query_weight, key_weight, value_weight, output_weight,
    expand_weight, reduce_weight, dconv_taps, gain_first, bias_first,
    gain_second, bias_second, cotangent,
):
    half = token_ids.shape[1]
    slot = 2 * half
    local = query_weight.shape[1]
    units = expand_weight.shape[1]
    pairs = local // LANES
    outer = lax.axis_size("outer")
    inner = lax.axis_size("inner")
    inner_bits = inner.bit_length() - 1
    rows = D // inner
    width = 3 * LANES

    shape = jax.ShapeDtypeStruct
    smem = pl.BlockSpec(memory_space=pltpu.SMEM)
    anywhere = pl.BlockSpec(memory_space=pl.ANY)
    dma = pltpu.SemaphoreType.DMA
    hd = whole((half, D))
    hl = whole((half, local))
    ld = whole((local, D))
    vec = whole((D,))

    column = pl.BlockSpec((D, LANES), lambda p: (0, p))
    taps_spec = pl.BlockSpec((3, 3, LANES), lambda p: (0, 0, p))
    pair_rows = pl.BlockSpec((slot, LANES), lambda p: (0, p))
    pair_heads = pl.BlockSpec((2, slot, LANES), lambda p: (p, 0, 0))
    raw_spec = pl.BlockSpec((slot, 3 * LANES), lambda p: (0, p))
    attended, qa, ka, va, raw, embedded, normed_t, att_own, att_oth, we_oth, wr_oth, wo_oth = pl.pallas_call(
        forward_kernel,
        grid=(pairs,),
        in_specs=[smem, whole((1, half)), vec, vec, column, column, column, taps_spec] + [anywhere] * 3,
        out_specs=[pair_rows, pair_heads, pair_heads, pair_heads, raw_spec, hd, whole((D, slot)), hl, hl] + [anywhere] * 3,
        out_shape=[shape((slot, local), BF16)]
        + [shape((2 * pairs, slot, LANES), BF16)] * 3
        + [shape((slot, 3 * local), BF16), shape((half, D), F32), shape((D, slot), BF16)]
        + [shape((half, local), BF16)] * 2
        + [shape(w.shape, BF16) for w in (expand_weight, reduce_weight, output_weight)],
        scratch_shapes=[
            pltpu.VMEM((slot, D), BF16),
            pltpu.VMEM((3, BLOCK + 8, LANES), F32),
            pltpu.VMEM((D, 3 * LANES), BF16),
            pltpu.VMEM((pairs, half, LANES), BF16),
            pltpu.VMEM((pairs, half, LANES), BF16),
            dma((PIECES,)), dma((PIECES,)), dma((pairs,)), dma((pairs,)), dma((3,)), dma((3,)),
        ],
        compiler_params=params(58, collective_id=0, has_side_effects=True),
        name="attention_forward",
    )(
        lengths, token_ids, gain_first, bias_first,
        query_weight, key_weight, value_weight, dconv_taps, expand_weight, reduce_weight, output_weight,
    )

    steps = units // D
    split = D // width
    fed = 2 * steps * split + 1
    chunks = fed + pairs
    twos = (2,) * inner_bits
    line_stages = inner_bits + outer
    vmem = lambda dims, kind: pltpu.VMEM(dims, kind)
    sums, small, activations, grad_input, _ = pl.pallas_call(
        functools.partial(layer_kernel, inner_bits, outer),
        in_specs=[smem, vec, vec, vec, whole((3, 3, local))] + [anywhere] * 19,
        out_specs=[whole((chunks, rows, width)), whole((16, D)), anywhere, anywhere, anywhere],
        out_shape=[
            shape((chunks, rows, width), BF16), shape((16, D), F32), shape((half, D), F32), shape((half, D), F32),
            shape((steps, 2, half, D), BF16),
        ],
        scratch_shapes=[
            vmem((half, D), F32),
            vmem((chunks,) + twos + (rows, width), BF16),
            vmem((chunks, rows, width), BF16),
            vmem((chunks, rows, width), BF16),
            vmem((slot, local), BF16),
            vmem((2, 2, D, D), BF16),
            vmem((D, local), BF16),
            vmem((half, D), BF16),
            vmem((inner_bits + 2, 16, D), F32),
            vmem((inner_bits + 3, 16, D), F32),
            vmem((2, 8, D), F32),
            vmem((2 * inner, 8, D), F32),
            vmem((outer, 8, D), F32),
            dma((12 + 10 * steps + 3 * pairs,)),
            dma((chunks + 2, line_stages)), dma((chunks + 2, line_stages)),
            dma((line_stages + 1,)), dma((line_stages + 1,)),
            dma((steps + 2, 2)), dma((steps + 2, 2)),
            dma((2 * inner,)), dma((2 * inner,)), dma((outer,)), dma((outer,)),
        ]
        + [vmem((chunks,) + (2,) * (inner_bits - 1 - s) + (rows, width), BF16) for s in range(inner_bits)],
        compiler_params=params(63, collective_id=1, has_side_effects=True),
        name="layer",
    )(
        lengths, gain_first, gain_second, bias_second, dconv_taps,
        att_own, att_oth, embedded, cotangent[0], output_weight, wo_oth,
        expand_weight, we_oth, reduce_weight, wr_oth, query_weight, key_weight, value_weight,
        attended, qa, ka, va, raw, normed_t,
    )
    many = steps * split
    part = half // many
    some_rows = pl.BlockSpec((part, D), lambda i: (i, 0))
    pick = lambda index: pl.BlockSpec((1, rows, width), lambda i: (index(i), 0, 0))
    last = lambda i: jnp.minimum(i, pairs - 1)
    chunk_at = lambda i: (i // split) * 2 * split + i % split
    out_pair = pl.BlockSpec((rows, LANES), lambda i: (0, last(i)))
    activations, grad_input, gq, gk, gv, go_sum, ge_sum, gr_sum, tap_sum, *vec_sums = pl.pallas_call(
        finish_kernel,
        grid=(many,),
        in_specs=[
            pick(chunk_at), pick(lambda i: chunk_at(i) + split), pick(lambda i: fed - 1),
            pick(lambda i: fed + last(i)), some_rows, some_rows, whole((16, D)),
        ],
        out_specs=[
            some_rows, some_rows, out_pair, out_pair, out_pair, whole((rows, local)),
            pl.BlockSpec((rows, width), lambda i: (0, i)), pl.BlockSpec((rows, width), lambda i: (0, i)),
            whole((3, 3, D)), vec, vec, vec, vec,
        ],
        out_shape=[shape((half, D), F32)] * 2
        + [shape((rows, local), F32)] * 4
        + [shape((rows, units), F32)] * 2
        + [shape((3, 3, D), F32)]
        + [shape((D,), F32)] * 4,
        compiler_params=params(62),
        name="finish",
    )(sums, sums, sums, sums, activations, grad_input, small)
    return (
        activations[None],
        grad_input[None],
        gq,
        gk,
        gv,
        go_sum.T,
        ge_sum,
        gr_sum.T,
        tap_sum,
        *vec_sums,
    )


def solution(mesh):
    return jax.shard_map(
        body,
        mesh=mesh,
        in_specs=(
            P(("outer", "inner"), "head"),
            P(("outer", "inner")),
            P(None, "head"),
            P(None, "head"),
            P(None, "head"),
            P("head", None),
            P(None, "head"),
            P("head", None),
            P(None, None, "head"),
            P(),
            P(),
            P(),
            P(),
            P(("outer", "inner"), "head", None),
        ),
        out_specs=(
            P(("outer", "inner"), "head", None),
            P(("outer", "inner"), "head", None),
            P("inner", "head"),
            P("inner", "head"),
            P("inner", "head"),
            P("head", "inner"),
            P("inner", "head"),
            P("head", "inner"),
            P(),
            P(),
            P(),
            P(),
            P(),
        ),
        check_vma=False,
    )
```

```python
import functools
import math

import jax
import jax.numpy as jnp
from jax import lax
from jax.experimental import pallas as pl
from jax.experimental.pallas import tpu as pltpu
from jax.sharding import PartitionSpec as P

HEAD_DIM = 64
D = 768
BLOCK = 256
LANES = 128
EPS = 1e-05
MODULUS = 32749
NEGATIVE = -1e30
SCALE = HEAD_DIM ** (-0.5)
F32 = jnp.float32
BF16 = jnp.bfloat16
MIB = 1024 * 1024

SINE = (
    4.442882913726386,
    -7.308248583654593,
    3.606466623722958,
    -0.8474403474577161,
    0.11605422299047748,
    -0.010267162611370253,
    0.0005523348366953617,
)


def dot(a, b):
    return lax.dot_general(a, b, (((1,), (0,)), ((), ())), preferred_element_type=F32)


def dot_nt(a, b):
    return lax.dot_general(a, b, (((1,), (1,)), ((), ())), preferred_element_type=F32)


def whole(shape):
    return pl.BlockSpec(shape, lambda *_: (0,) * len(shape))


def normalise(values):
    centre = values - jnp.mean(values, axis=-1, keepdims=True)
    spread = jnp.mean(centre * centre, axis=-1, keepdims=True)
    scale = lax.rsqrt(spread + EPS)
    return centre * scale, scale


def norm_back(grad, hat, scale, gain):
    q = grad * gain
    mean_q = jnp.mean(q, axis=-1, keepdims=True)
    mean_qh = jnp.mean(q * hat, axis=-1, keepdims=True)
    return scale * (q - mean_q - hat * mean_qh)


def lane_ids(rows):
    return lax.broadcasted_iota(jnp.int32, (rows, LANES), 1)


def split_three(column):
    high = column.astype(BF16).astype(F32)
    rest = column - high
    middle = rest.astype(BF16).astype(F32)
    return high, middle, rest - middle


def with_parts(base, lane, offset, column):
    high, middle, small = split_three(column)
    base = jnp.where(lane == offset + 1, high, base)
    base = jnp.where(lane == offset + 2, middle, base)
    return jnp.where(lane == offset + 3, small, base)


def remote(src, dst, send, recv, **place):
    return pltpu.make_async_remote_copy(
        src_ref=src, dst_ref=dst, send_sem=send, recv_sem=recv,
        device_id=place, device_id_type=pl.DeviceIdType.MESH,
    )


def greet(*places):
    barrier = pltpu.get_barrier_semaphore()
    for place in places:
        pl.semaphore_signal(barrier, inc=1, device_id=place, device_id_type=pl.DeviceIdType.MESH)
    pl.semaphore_wait(barrier, len(places))


def rows_of(which, half):
    return pl.ds(pl.multiple_of(which * half, half), half)


def embed_rows(tok_ref, gain, bias, emb_ref, normed_ref, base, first):
    tokens = jnp.broadcast_to(tok_ref[:, pl.ds(first, LANES)], (LANES, LANES)).T
    parts = []
    for c in range(D // LANES):
        column = lax.broadcasted_iota(jnp.int32, (1, LANES), 1) + c * LANES
        product = tokens * (column + 1) + column * column
        turns = jnp.floor(product.astype(F32) * (1.0 / MODULUS) + 0.5)
        left = product - turns.astype(jnp.int32) * MODULUS
        u = left.astype(F32) * (2.0 / MODULUS)
        z = u * u
        value = jnp.full_like(u, SINE[-1])
        for coefficient in SINE[-2::-1]:
            value = value * z + coefficient
        parts.append(value * u)
    embedded = jnp.concatenate(parts, axis=1)
    emb_ref[pl.ds(first, LANES), :] = embedded
    hat, _ = normalise(embedded)
    rows = pl.ds(pl.multiple_of(base + first, LANES), LANES)
    normed_ref[rows, :] = (hat * gain + bias).astype(BF16)


PIECES = 3


def row_of(ref):
    return ref[...].reshape(1, D)


def forward_kernel(
    len_ref, tok_ref, gain_ref, bias_ref, wq_ref, wk_ref, wv_ref, taps_ref, we_hbm, wr_hbm, wo_hbm,
    att_ref, q_ref, k_ref, v_ref, raw_ref, rinv_ref, emb_ref, nt_ref, att_own_ref, att_oth_ref,
    we_oth_hbm, wr_oth_hbm, wo_oth_hbm, terms_hbm,
    normed_ref, shift_ref, wcat_ref, qa_ref, ka_ref, va_ref, terms_ref, give_ref, got_ref,
    row_send, row_recv, att_send, att_recv, weight_send, weight_recv, terms_sem,
):
    slot = att_ref.shape[0]
    half = slot // 2
    blocks = slot // BLOCK
    step = pl.program_id(0)
    pairs = att_own_ref.shape[1] // LANES
    head = lax.axis_index("head")
    partner = 1 - head
    piece = half // PIECES

    def row_copy(k):
        rows = pl.ds(pl.multiple_of(head * half + k * piece, piece), piece)
        return remote(normed_ref.at[rows], normed_ref.at[rows], row_send.at[k], row_recv.at[k], head=partner)

    def att_copy(p):
        return remote(give_ref.at[p], got_ref.at[p], att_send.at[p], att_recv.at[p], head=partner)

    def weight_copy(k):
        src, dst = ((wo_hbm, wo_oth_hbm), (we_hbm, we_oth_hbm), (wr_hbm, wr_oth_hbm))[k]
        return remote(src, dst, weight_send.at[k], weight_recv.at[k], head=partner)

    def terms_copy(p, i):
        rows, cols = pl.ds(i * BLOCK, BLOCK), pl.ds(0, (i + 1) * BLOCK)
        return pltpu.make_async_copy(
            terms_ref.at[:, rows, cols], terms_hbm.at[pl.ds(2 * p, 2), rows, cols], terms_sem.at[i]
        )

    @pl.when(step == 0)
    def _():
        greet({"head": partner})
        base = head * half
        for k in range(PIECES):
            def embed_step(i, _):
                first = pl.multiple_of(k * piece + i * LANES, LANES)
                embed_rows(tok_ref, row_of(gain_ref), row_of(bias_ref), emb_ref, normed_ref, base, first)
                return 0

            lax.fori_loop(0, piece // LANES, embed_step, 0)
            row_copy(k).start()
        for k in range(3):
            weight_copy(k).start()
        for k in range(PIECES):
            row_copy(k).wait()

    for j, w_ref in enumerate((wq_ref, wk_ref, wv_ref)):
        wcat_ref[:, j * LANES : (j + 1) * LANES] = w_ref[...]
    shift_ref[:, 0:8, :] = jnp.zeros((3, 8, LANES), F32)
    lane = lane_ids(BLOCK)
    features = D // pairs
    some = pl.ds(pl.multiple_of(step * features, features), features)

    def project(r, _):
        first = pl.multiple_of(r * BLOCK, BLOCK)
        rows = pl.ds(first, BLOCK)
        raws = dot(normed_ref[rows, :], wcat_ref[...])
        raw_ref[rows, :] = raws.astype(BF16)
        nt_ref[some, rows] = normed_ref[rows, some].T
        mixed = []
        for j in range(3):
            raw = raws[:, j * LANES : (j + 1) * LANES]
            shift_ref[j, 8 : 8 + BLOCK, :] = raw
            one = shift_ref[j, 7 : 7 + BLOCK, :]
            two = shift_ref[j, 6 : 6 + BLOCK, :]
            value = taps_ref[j, 0:1, :] * raw + taps_ref[j, 1:2, :] * one + taps_ref[j, 2:3, :] * two
            mixed.append(value * SCALE if j == 0 else value)
            shift_ref[j, 0:8, :] = raw[BLOCK - 8 :, :]
        for ref, value in zip((q_ref, k_ref, v_ref), mixed):
            ref[rows, :] = value.astype(BF16)
        row = lax.broadcasted_iota(jnp.int32, (BLOCK, 1), 0) + first
        key_bias = jnp.where(row < len_ref[0], 0.0, NEGATIVE)
        for e in range(2):
            mine = (lane // HEAD_DIM) == e
            other = HEAD_DIM * (1 - e)
            qa_ref[e, rows, :] = jnp.where(mine, mixed[0], jnp.where(lane == other, 1.0, 0.0)).astype(BF16)
            ka_ref[e, rows, :] = jnp.where(mine, mixed[1], jnp.where(lane == other, key_bias, 0.0)).astype(BF16)
            va_ref[e, rows, :] = jnp.where(mine, mixed[2], jnp.where(lane == other, 1.0, 0.0)).astype(BF16)
        return 0

    lax.fori_loop(0, blocks, project, 0)

    @pl.when(step > 0)
    def _():
        for i in range(blocks):
            terms_copy(step - 1, i).wait()

    causal = lax.broadcasted_iota(jnp.int32, (BLOCK, BLOCK), 1) <= lax.broadcasted_iota(
        jnp.int32, (BLOCK, BLOCK), 0
    )
    tasks = [(i, e) for i in range(blocks) for e in range(2)]

    def scores_of(i, e):
        rows = slice(i * BLOCK, (i + 1) * BLOCK)
        query = qa_ref[e, rows, :]
        diagonal = jnp.where(causal, dot_nt(query, ka_ref[e, rows, :]), NEGATIVE)
        before = dot_nt(query, ka_ref[e, : i * BLOCK, :]) if i else None
        return diagonal, before

    coming = scores_of(*tasks[0])
    outs = []
    for t, (i, e) in enumerate(tasks):
        diagonal, before = coming
        if t + 1 < len(tasks):
            coming = scores_of(*tasks[t + 1])
        rows = slice(i * BLOCK, (i + 1) * BLOCK)
        other = HEAD_DIM * (1 - e)
        row_max = jnp.max(diagonal, axis=1, keepdims=True)
        if i:
            row_max = jnp.maximum(row_max, jnp.max(before, axis=1, keepdims=True))
        terms = jnp.exp(diagonal - row_max).astype(BF16)
        terms_ref[e, rows, rows] = terms
        out = dot(terms, va_ref[e, rows, :])
        if i:
            terms = jnp.exp(before - row_max).astype(BF16)
            terms_ref[e, rows, : i * BLOCK] = terms
            out += dot(terms, va_ref[e, : i * BLOCK, :])
        inverse = 1.0 / out[:, other : other + 1]
        outs.append((out, inverse))
        if e == 1:
            first_head = lane < HEAD_DIM
            inverse = jnp.where(first_head, outs[0][1], outs[1][1])
            att_ref[rows, :] = (jnp.where(first_head, outs[0][0], outs[1][0]) * inverse).astype(BF16)
            rinv_ref[rows, :] = inverse
            outs = []
            terms_copy(step, i).start()

    for p in range(pairs):
        @pl.when(step == p)
        def _():
            give_ref[p] = att_ref[rows_of(partner, half), :]
            att_copy(p).start()
            att_own_ref[:, p * LANES : (p + 1) * LANES] = att_ref[rows_of(head, half), :]

    @pl.when(step == pairs - 1)
    def _():
        for p in range(pairs):
            att_copy(p).wait()
            att_oth_ref[:, p * LANES : (p + 1) * LANES] = got_ref[p]
        for k in range(3):
            weight_copy(k).wait()
        for i in range(blocks):
            terms_copy(step, i).wait()


def plan_sums(entries, ready, points, tail, inner_bits, line_steps, orders, rate=0.05, hop=1.8):
    stages = inner_bits + line_steps + 1
    done, arrive, free, plan, begun = [0] * len(entries), {}, {}, {}, set()

    def step_of(n, now):
        chunk, size, kind = entries[n]
        stage = done[n]
        if stage < inner_bits:
            link, part = ("bit", orders[kind][stage]), size / 2 ** (stage + 1)
        else:
            t = stage - inner_bits
            link, part = ("in" if t <= line_steps // 2 else "out",), size / 2**inner_bits
        if stage < stages - 1:
            free[link] = max(free.get(link, 0.0), now) + part / rate
            arrive[n] = free[link] + hop
        done[n] += 1

    at, now, late = 0, 0.0, 0
    while at < len(points) or any(d < stages for d in done):
        if at < len(points):
            place, when = points[at]
            now, slack = max(now, when), 0.3 if place[0] != "tail" else 0.0
        else:
            place, slack = ("tail", tail + late), 0.0
            late += 1
            now = max(now, min(arrive[n] for n in range(len(entries)) if done[n] < stages))
        at += 1
        for n, (chunk, _, _) in enumerate(entries):
            if ready[chunk] == place:
                begun.add(n)
        while True:
            able = [n for n in begun if done[n] < stages and (done[n] == 0 or arrive[n] <= now - slack)]
            if not able:
                break
            n = min(able, key=lambda m: (-done[m], m))
            plan.setdefault(place, []).append((n, done[n]))
            step_of(n, now)
    return plan


def layer_kernel(
    inner_bits, outer,
    len_ref, gain_first_ref, gain_second_ref, bias_second_ref, taps_ref,
    att_own_hbm, att_oth_hbm, emb_hbm, cot_hbm, wo_own_hbm, wo_oth_hbm,
    we_own_hbm, we_oth_hbm, wr_own_hbm, wr_oth_hbm, wq_hbm, wk_hbm, wv_hbm,
    att_hbm, q_hbm, k_hbm, v_hbm, raw_hbm, rinv_hbm, nt_hbm, terms_hbm,
    sum_ref, small_ref, act_hbm, gin_hbm, sq_hbm,
    gh_ref, g_ref, rz_ref, rc_ref, do_ref, got_ref, got_go, got_first, acc_ref, got_small, late_ref, got_group, got_outer,
    load_sem, send_sem, recv_sem, small_send, small_recv, core_send, core_recv,
    group_send, group_recv, outer_send, outer_recv, *halves,
):
    half = gh_ref.shape[0]
    slot = 2 * half
    local = att_own_hbm.shape[1]
    units = we_own_hbm.shape[1]
    steps = units // D
    width = sum_ref.shape[2]
    split = D // width
    pairs = local // LANES
    fed = 2 * steps * split + 1
    blocks = slot // BLOCK
    head = lax.axis_index("head")
    partner = 1 - head
    mine = lax.axis_index("inner")
    line = lax.axis_index("outer")
    centre = outer // 2
    left = line < centre
    depth = jnp.where(left, centre - 1 - line, line - centre)
    inward = jnp.where(left, line + 1, line - 1)
    outward = jnp.where(left, line - 1, line + 1)
    bit = [(mine // (1 << b)) % 2 for b in range(inner_bits)]
    across = [mine + (1 << b) * (1 - 2 * bit[b]) for b in range(inner_bits)]

    def chunk_of(c, kind, k):
        return (2 * c + kind) * split + k

    entries = [(c, 0, width, c % 2) for c in range(fed + pairs - 1)]
    entries += [(fed + pairs - 1, j * LANES, LANES, j % 2) for j in range(3)]
    order_of = [tuple((b + first) % inner_bits for b in range(inner_bits)) for first in range(2)]
    line_steps = 2 * centre - 1
    stage_count = inner_bits + line_steps + 1

    def index_of(fixed):
        return tuple(fixed.get(b, slice(None)) for b in reversed(range(inner_bits)))

    def lanes(entry):
        return slice(entry[1], entry[1] + entry[2])

    def halving(n, s):
        c, _, _, kind = entries[n]
        order = order_of[kind]
        fixed = {b: bit[b] for b in order[:s]}
        b = order[s]
        give = g_ref.at[(c,) + index_of({**fixed, b: 1 - bit[b]}) + (slice(None), lanes(entries[n]))]
        land = halves[s].at[(c,) + (slice(None),) * (inner_bits - 1 - s) + (slice(None), lanes(entries[n]))]
        return remote(give, land, send_sem.at[n, s], recv_sem.at[n, s], inner=across[b])

    def add_half(n, s):
        c, _, _, kind = entries[n]
        order = order_of[kind]
        index = (c,) + index_of({b: bit[b] for b in order[: s + 1]}) + (slice(None), lanes(entries[n]))
        land = (c,) + (slice(None),) * (inner_bits - 1 - s) + (slice(None), lanes(entries[n]))
        g_ref[index] = g_ref[index] + halves[s][land]

    def own(n):
        return (entries[n][0],) + tuple(bit[b] for b in reversed(range(inner_bits))) + (slice(None), lanes(entries[n]))

    def flat(n):
        return (entries[n][0], slice(None), lanes(entries[n]))

    def line_sender(t):
        if t < centre - 1:
            return depth == centre - 1 - t
        if t == centre - 1:
            return depth == 0
        return depth == t - centre

    def line_copy(n, t):
        s = inner_bits + t
        sems = (send_sem.at[n, s], recv_sem.at[n, s])
        if t < centre - 1:
            return remote(g_ref.at[own(n)], rz_ref.at[flat(n)], *sems, outer=inward)
        if t == centre - 1:
            return remote(g_ref.at[own(n)], rc_ref.at[flat(n)], *sems, outer=inward)
        return remote(rc_ref.at[flat(n)], rc_ref.at[flat(n)], *sems, outer=outward)

    def line_finish(n, t):
        if t < centre - 1:
            @pl.when(depth == centre - 2 - t)
            def _():
                line_copy(n, t).wait_recv()
                g_ref[own(n)] = g_ref[own(n)] + rz_ref[flat(n)]
        elif t == centre - 1:
            @pl.when(depth == 0)
            def _():
                line_copy(n, t).wait_recv()
                rc_ref[flat(n)] = g_ref[own(n)] + rc_ref[flat(n)]
        else:
            pl.when(depth == t - centre + 1)(lambda: line_copy(n, t).wait_recv())

    def advance(n, stage):
        if 0 < stage <= inner_bits:
            halving(n, stage - 1).wait_recv()
            add_half(n, stage - 1)
        elif stage > inner_bits:
            line_finish(n, stage - inner_bits - 1)
        if stage < inner_bits:
            halving(n, stage).start()
        elif stage < stage_count - 1:
            t = stage - inner_bits
            pl.when(line_sender(t))(lambda: line_copy(n, t).start())
        else:
            sum_ref[flat(n)] = rc_ref[flat(n)]

    def drain(n):
        for s in range(inner_bits):
            halving(n, s).wait_send()
        for t in range(line_steps):
            pl.when(line_sender(t))(lambda t=t: line_copy(n, t).wait_send())

    points = []
    now = 6.0
    for c in range(steps):
        for k, spent in enumerate((2.8, 2.8, 0.3, 2.8, 2.8, 1.5)):
            now += spent
            points.append((("feed", c, k), now))
        now += 1.4
    for k in range(3):
        now += 1.5
        points.append((("norm", k), now))
    for p in range(pairs):
        now += 1.5
        for j in range(0, blocks, 2):
            points.append((("pair", p, j), now))
            now += 10.0 * (2 * (blocks - j) - 1) * 2 / (blocks * (blocks + 1))
        now += 3.5
        points.append((("taps", p), now))
    for k, spent in enumerate((0.0, 2.0, 2.0, 3.0, 3.0, 3.0)):
        now += spent
        points.append((("tail", k), now))
    ready = {}
    for c in range(steps):
        for k in range(split):
            ready[chunk_of(c, 0, k)] = ("feed", c, 2)
            ready[chunk_of(c, 1, k)] = ("feed", c, 5)
    ready[fed - 1] = ("norm", 2)
    for p in range(pairs):
        ready[fed + p] = ("taps", p) if p < pairs - 1 else ("tail", 0)
    plan = plan_sums(
        [(c, 2e-6 * D * wide, kind) for c, _, wide, kind in entries],
        ready, points, 6, inner_bits, line_steps, order_of,
    )

    def tick(place):
        for n, stage in plan.pop(place, ()):
            advance(n, stage)

    def small_copy(k):
        sems = (small_send.at[k], small_recv.at[k])
        if k == 0:
            return remote(acc_ref.at[0], got_small.at[0], *sems, head=partner)
        if k <= inner_bits:
            return remote(acc_ref.at[k], got_small.at[k], *sems, inner=across[k - 1])
        t = k - 1 - inner_bits
        if t <= centre - 1:
            return remote(acc_ref.at[inner_bits + 1], got_small.at[inner_bits + 1 + (t == centre - 1)], *sems, outer=inward)
        last = got_small.at[inner_bits + 2]
        return remote(last, last, *sems, outer=outward)

    def small_step(k):
        if 0 < k <= inner_bits + 1:
            small_copy(k - 1).wait_recv()
            acc_ref[k] = acc_ref[k - 1] + got_small[k - 1]
        elif k > inner_bits + 1:
            t = k - 2 - inner_bits
            if t < centre - 1:
                @pl.when(depth == centre - 2 - t)
                def _():
                    small_copy(k - 1).wait_recv()
                    acc_ref[inner_bits + 1] = acc_ref[inner_bits + 1] + got_small[inner_bits + 1]
            elif t == centre - 1:
                @pl.when(depth == 0)
                def _():
                    small_copy(k - 1).wait_recv()
                    got_small[inner_bits + 2] = acc_ref[inner_bits + 1] + got_small[inner_bits + 2]
            else:
                pl.when(depth == t - centre + 1)(lambda: small_copy(k - 1).wait_recv())
        if k <= inner_bits:
            small_copy(k).start()
        elif k <= inner_bits + line_steps:
            pl.when(line_sender(k - 1 - inner_bits))(lambda: small_copy(k).start())
        else:
            small_ref[...] = got_small[inner_bits + 2]

    small_steps = inner_bits + line_steps + 2

    inner = 1 << inner_bits
    group = 2 * inner
    seat = mine * 2 + head

    def group_place(k, way):
        other = lax.rem(seat + group + way * k, group)
        return other, {"inner": other // 2, "head": lax.rem(other, 2)}

    def outer_place(k, way):
        other = lax.rem(line + outer + way * k, outer)
        return other, {"outer": other}

    def late_copies(places, count, me, src, land, sends, recvs):
        give = [remote(src, land.at[me], sends.at[k], recvs.at[k], **places(k, 1)[1]) for k in range(1, count)]
        take = [
            remote(src, land.at[places(k, -1)[0]], sends.at[k], recvs.at[k], **places(k, 1)[1]) for k in range(1, count)
        ]
        return give, take

    group_give, group_take = late_copies(
        group_place, group, seat, late_ref.at[0], got_group, group_send, group_recv
    )
    outer_give, outer_take = late_copies(outer_place, outer, line, late_ref.at[1], got_outer, outer_send, outer_recv)

    load_count = iter(range(load_sem.shape[0]))

    def load(src, dst):
        return pltpu.make_async_copy(src, dst, load_sem.at[next(load_count)])

    row = lax.broadcasted_iota(jnp.int32, (half, 1), 0) + head * half
    valid = row < len_ref[0]

    def greet_all():
        barrier = pltpu.get_barrier_semaphore()
        places = [group_place(k, 1)[1] for k in range(1, group)] + [outer_place(k, 1)[1] for k in range(1, outer)]
        for place in places:
            pl.semaphore_signal(barrier, inc=1, device_id=place, device_id_type=pl.DeviceIdType.MESH)
        pl.semaphore_wait(barrier, len(places))

    two_rows = half // 2

    def halves_of(step):
        def run(r, _):
            step(r, pl.ds(pl.multiple_of(r * two_rows, two_rows), two_rows))
            return 0

        lax.fori_loop(0, 2, run, 0)

    def feed_forward(
        att_ref, wo_ref, we_ref, wr_ref, cot_ref, hid_ref, gn_ref,
        n2_ref, n2t_ref, gl_ref, glt_ref, give_ref, relu_ref, sq_ref,
    ):
        give_att = relu_ref.at[0, :, 0:local]
        give_go = relu_ref.at[1, :, 0:local]
        loads = {}
        for k, (att, wo) in enumerate(((att_own_hbm, wo_own_hbm), (att_oth_hbm, wo_oth_hbm))):
            loads["att", k] = load(att, att_ref.at[k])
            loads["wo", k] = load(wo, wo_ref.at[k])
        loads["emb"] = load(emb_hbm, hid_ref)
        loads["cot"] = load(cot_hbm, cot_ref)
        for c in range(steps):
            cols = pl.ds(c * D, D)
            for k, we in ((1, we_oth_hbm), (0, we_own_hbm)):
                loads["we", c, k] = load(we.at[:, cols], we_ref.at[c, k])
            for k, wr in ((1, wr_oth_hbm), (0, wr_own_hbm)):
                loads["wr", c, k] = load(wr.at[cols, :], wr_ref.at[c, k])
        for copy in loads.values():
            copy.start()
        greet_all()
        for key in (("att", 0), ("wo", 0), ("att", 1), ("wo", 1), "emb", "cot"):
            loads[key].wait()
        gain, bias = row_of(gain_second_ref), row_of(bias_second_ref)

        def open_rows(r, rows):
            hidden = hid_ref[rows, :] + dot(att_ref[0, rows, :], wo_ref[0]) + dot(att_ref[1, rows, :], wo_ref[1])
            hid_ref[rows, :] = hidden
            hat, _ = normalise(hidden)
            normed = (hat * gain + bias).astype(BF16)
            n2_ref[rows, :] = normed
            n2t_ref[:, rows] = normed.T
            position = lax.broadcasted_iota(jnp.int32, (two_rows, 1), 0) + head * half + r * two_rows
            grad = jnp.where(position < len_ref[0], cot_ref[rows, :], 0.0)
            cot_ref[rows, :] = grad
            gl_ref[rows, :] = grad.astype(BF16)
            glt_ref[:, rows] = grad.astype(BF16).T

        halves_of(open_rows)
        hid_store = load(hid_ref, act_hbm)
        hid_store.start()

        def grad_copy(c, kind):
            return remote(
                give_ref.at[kind], got_ref.at[c % 2, kind], core_send.at[c, kind], core_recv.at[c, kind], head=partner
            )

        def put_own(c, kind, r, value):
            for k in range(split):
                part = value[:, k * width : (k + 1) * width].astype(BF16)
                g_ref[chunk_of(c, kind, k), r] = part.reshape(g_ref.shape[2:])

        def add_other(c, kind):
            grad_copy(c, kind).wait_recv()
            for k in range(split):
                got = got_ref[c % 2, kind, :, k * width : (k + 1) * width]
                g_ref[chunk_of(c, kind, k)] += got.reshape(g_ref.shape[1:])

        def weight_grad(c, kind, k, left_ref, right_ref):
            def run(r, rows):
                grad = dot(left_ref[rows, :], right_ref[...])
                if k == 1:
                    give_ref[kind, rows, :] = grad.astype(BF16)
                else:
                    put_own(c, kind, r, grad)

            if k == 1 and c:
                grad_copy(c - 1, kind).wait_send()
            halves_of(run)
            if k == 1:
                grad_copy(c, kind).start()

        stores = []
        for c in range(steps):
            for k in (1, 0):
                loads["we", c, k].wait()

                def expand(r, rows):
                    relu = jnp.maximum(dot(n2_ref[rows, :], we_ref[c, k]), 0.0)
                    relu_ref[k, rows, :] = relu.astype(BF16)
                    sq_ref[c, k, rows, :] = (relu * relu).astype(BF16)

                halves_of(expand)
                stores.append(load(sq_ref.at[c, k], sq_hbm.at[c, k]))
                stores[-1].start()
                weight_grad(c, 0, k, glt_ref, sq_ref.at[c, k])
                tick(("feed", c, 1 - k))
            add_other(c, 0)
            tick(("feed", c, 2))
            for k in (1, 0):
                loads["wr", c, k].wait()

                def reduce_back(r, rows):
                    back = dot_nt(gl_ref[rows, :], wr_ref[c, k])
                    relu_ref[k, rows, :] = (back * (2.0 * relu_ref[k, rows, :].astype(F32))).astype(BF16)

                halves_of(reduce_back)
                weight_grad(c, 1, k, n2t_ref, relu_ref.at[k])
                tick(("feed", c, 4 - k))
            for k in (1, 0):
                def expand_back(r, rows):
                    gn = dot_nt(relu_ref[k, rows, :], we_ref[c, k])
                    if c == 0 and k == 1:
                        gn_ref[rows, :] = gn
                    else:
                        gn_ref[rows, :] += gn

                halves_of(expand_back)
                if k == 1:
                    add_other(c, 1)
                    tick(("feed", c, 5))
        acc_ref[0] = jnp.zeros(acc_ref.shape[1:], F32)

        def close_rows(r, rows):
            hat, scale = normalise(hid_ref[rows, :])
            grad_n = gn_ref[rows, :]
            acc_ref[0, 2:3, :] += jnp.sum(grad_n * hat, axis=0, keepdims=True)
            acc_ref[0, 3:4, :] += jnp.sum(grad_n, axis=0, keepdims=True)
            grad_h = cot_ref[rows, :] + norm_back(grad_n, hat, scale, gain)
            gh_ref[rows, :] = grad_h
            low = grad_h.astype(BF16)
            n2_ref[rows, :] = low
            n2t_ref[:, rows] = low.T
            give_att[rows, :] = dot_nt(low, wo_ref[1]).astype(BF16)

        halves_of(close_rows)
        own_rows = rows_of(head, half)
        att_copy = remote(give_att, do_ref.at[own_rows], core_send.at[steps, 0], core_recv.at[steps, 0], head=partner)
        att_copy.start()
        tick(("norm", 0))
        give_go[...] = dot(n2t_ref[...], att_ref[1]).astype(BF16)
        go_copy = remote(give_go, got_go, core_send.at[steps, 1], core_recv.at[steps, 1], head=partner)
        go_copy.start()
        do_ref[own_rows, :] = dot_nt(n2_ref[...], wo_ref[0]).astype(BF16)
        tick(("norm", 1))
        grad_o = dot(n2t_ref[...], att_ref[0]).astype(BF16)
        go_copy.wait()
        g_ref[fed - 1] = (grad_o + got_go[...]).reshape(g_ref.shape[1:])
        tick(("norm", 2))
        for kind in range(2):
            grad_copy(steps - 1, kind).wait_send()
        for copy in [hid_store] + stores:
            copy.wait()
        att_copy.wait()

    pl.run_scoped(
        feed_forward,
        pltpu.VMEM((2, half, local), BF16), pltpu.VMEM((2, local, D), BF16),
        pltpu.VMEM((steps, 2, D, D), BF16), pltpu.VMEM((steps, 2, D, D), BF16),
        pltpu.VMEM((half, D), F32), pltpu.VMEM((half, D), F32), pltpu.VMEM((half, D), F32),
        pltpu.VMEM((half, D), BF16), pltpu.VMEM((D, half), BF16),
        pltpu.VMEM((half, D), BF16), pltpu.VMEM((D, half), BF16),
        pltpu.VMEM((2, D, D), BF16), pltpu.VMEM((2, half, D), BF16), pltpu.VMEM((steps, 2, half, D), BF16),
    )

    def attention(
        all_ref, wcat_ref, nt_ref, mix_ref, late, dot_ref, qt_ref, doa_ref, kz_ref, va_ref, turned_ref,
        att_ref, q_ref, k_ref, v_ref, raw_ref, rinv_ref, terms_ref, pair_sem, terms_sem,
    ):
        def pair_loads(p, place):
            one = pl.ds(pl.multiple_of(p * LANES, LANES), LANES)
            three = pl.ds(pl.multiple_of(p * 3 * LANES, LANES), 3 * LANES)
            return [
                pltpu.make_async_copy(rinv_hbm.at[:, one], rinv_ref.at[place], pair_sem.at[place, 0]),
                pltpu.make_async_copy(att_hbm.at[:, one], att_ref.at[place], pair_sem.at[place, 1]),
                pltpu.make_async_copy(v_hbm.at[:, one], v_ref.at[place], pair_sem.at[place, 2]),
                pltpu.make_async_copy(q_hbm.at[:, one], q_ref.at[place], pair_sem.at[place, 3]),
                pltpu.make_async_copy(k_hbm.at[:, one], k_ref.at[place], pair_sem.at[place, 4]),
                pltpu.make_async_copy(raw_hbm.at[:, three], raw_ref.at[place], pair_sem.at[place, 5]),
            ]

        def terms_load(p, j):
            rows = pl.ds(j * BLOCK, slot - j * BLOCK)
            spot = lax.rem(blocks * p + j, 4)
            return pltpu.make_async_copy(
                terms_hbm.at[pl.ds(2 * p, 2), rows, pl.ds(j * BLOCK, BLOCK)],
                terms_ref.at[spot, :, rows, :],
                terms_sem.at[spot],
            )

        for copy in pair_loads(0, 0):
            copy.start()
        for j in range(2):
            terms_load(0, j).start()
        nt_load = load(nt_hbm, nt_ref)
        nt_load.start()
        for copy in late:
            copy.start()
        mix_ref[:, slot : slot + 8, :] = jnp.zeros((3, 8, LANES), F32)
        lane = lane_ids(slot)

        def at_pair(p, kind, *rest):
            for q in range(pairs):
                if plan.get((kind, q) + rest):
                    pl.when(p == q)(functools.partial(tick, (kind, q) + rest))

        def one_pair(p, _):
            place = lax.rem(p, 2)
            one = pl.ds(pl.multiple_of(p * LANES, LANES), LANES)

            @pl.when(p + 1 < pairs)
            def _():
                for copy in pair_loads(p + 1, 1 - place):
                    copy.start()

            for copy in pair_loads(p, place):
                copy.wait()
            scaled = (do_ref[:, one].astype(F32) * rinv_ref[place]).astype(BF16)
            dot_ref[...] = scaled.T
            qt_ref[...] = q_ref[place].T
            product = scaled.astype(F32) * att_ref[place].astype(F32)
            for e in range(2):
                in_head = (lane // HEAD_DIM) == e
                delta = -jnp.sum(jnp.where(in_head, product, 0.0), axis=1, keepdims=True)
                other = HEAD_DIM * (1 - e)
                ones = jnp.where((lane > other) & (lane < other + 4), 1.0, 0.0)
                doa_ref[e] = with_parts(jnp.where(in_head, scaled.astype(F32), 0.0), lane, other, delta).astype(BF16)
                va_ref[e] = jnp.where(in_head, v_ref[place].astype(F32), ones).astype(BF16)
                kz_ref[e] = jnp.where(in_head, k_ref[place].astype(F32), 0.0).astype(BF16)

            def grads_of(j, e):
                return dot_nt(doa_ref[e, j * BLOCK :, :], va_ref[e, j * BLOCK : (j + 1) * BLOCK, :])

            for j0 in range(0, blocks, 2):
                at_pair(p, "pair", j0)
                for j in (j0, j0 + 1):
                    terms_load(p, j).wait()
                    if j + 2 < blocks:
                        terms_load(p, j + 2).start()
                    else:
                        @pl.when(p + 1 < pairs)
                        def _():
                            terms_load(p + 1, j + 2 - blocks).start()
                tasks = [(j, e) for j in (j0, j0 + 1) for e in range(2)]
                coming = grads_of(*tasks[0])
                for t, (j, e) in enumerate(tasks):
                    back = coming
                    if t + 1 < len(tasks):
                        coming = grads_of(*tasks[t + 1])
                    first = j * BLOCK
                    keys = slice(first, first + BLOCK)
                    mine_rows = slice(e * HEAD_DIM, (e + 1) * HEAD_DIM)
                    terms = terms_ref[lax.rem(blocks * p + j, 4), e, first:, :]
                    grads = (terms.astype(F32) * back).astype(BF16)
                    part = dot(grads, kz_ref[e, keys, :])
                    if j == 0 and e == 0:
                        mix_ref[0, first:slot, :] = part
                    else:
                        mix_ref[0, first:slot, :] += part
                    turned_ref[0, mine_rows, keys] = dot(qt_ref[mine_rows, first:], grads)
                    turned_ref[1, mine_rows, keys] = dot(dot_ref[mine_rows, first:], terms)
            mix_ref[0, 0:slot, :] = mix_ref[0, 0:slot, :] * SCALE
            mix_ref[1, 0:slot, :] = turned_ref[0].T
            mix_ref[2, 0:slot, :] = turned_ref[1].T
            base = pl.multiple_of(p * 3 * LANES, LANES)
            for j in range(3):
                zero = mix_ref[j, 0:slot, :]
                one_on = mix_ref[j, 1 : 1 + slot, :]
                two_on = mix_ref[j, 2 : 2 + slot, :]
                raw = raw_ref[place, :, j * LANES : (j + 1) * LANES].astype(F32)
                cols = pl.ds(pl.multiple_of(head * local + p * LANES, LANES), LANES)
                value = 0.0
                for s, moved in enumerate((zero, one_on, two_on)):
                    total = jnp.sum(moved * raw, axis=0, keepdims=True)
                    acc_ref[0, 4 + 3 * j + s : 5 + 3 * j + s, cols] = total
                    value += taps_ref[j, s : s + 1, one] * moved
                all_ref[:, pl.ds(pl.multiple_of(base + j * LANES, LANES), LANES)] = value.astype(BF16)

            @pl.when(p == 0)
            def _():
                nt_load.wait()

            grads = dot(nt_ref[...], all_ref[:, pl.ds(base, 3 * LANES)]).astype(BF16)
            g_ref[fed + p] = grads.reshape(g_ref.shape[1:])
            at_pair(p, "taps")
            return 0

        lax.fori_loop(0, pairs, one_pair, 0)

    def tail(all_ref, wcat_ref, late, emb_ref, give_first, own_first, hid_ref, sq_ref, wr_ref):
        emb_load = load(emb_hbm, emb_ref)
        emb_load.start()
        tick(("tail", 0))
        hid_load = load(act_hbm, hid_ref)
        hid_load.start()
        ffn_loads = []
        for c in range(steps):
            for k, wr in ((1, wr_oth_hbm), (0, wr_own_hbm)):
                ffn_loads.append(load(sq_hbm.at[c, k], sq_ref.at[c, k]))
                ffn_loads.append(load(wr.at[pl.ds(c * D, D), :], wr_ref.at[c, k]))
        for copy in ffn_loads:
            copy.start()
        small_step(0)
        for copy in late:
            copy.wait()

        def other_rows(r, rows):
            there = pl.ds(pl.multiple_of(partner * half + r * two_rows, two_rows), two_rows)
            give_first[rows, :] = dot_nt(all_ref[there, :], wcat_ref[...]).astype(BF16)

        halves_of(other_rows)
        first_copy = remote(
            give_first, got_first, core_send.at[steps + 1, 0], core_recv.at[steps + 1, 0], head=partner
        )
        first_copy.start()
        tick(("tail", 1))
        small_step(1)

        def own_rows(r, rows):
            here = pl.ds(pl.multiple_of(head * half + r * two_rows, two_rows), two_rows)
            own_first[rows, :] = dot_nt(all_ref[here, :], wcat_ref[...])

        halves_of(own_rows)
        tick(("tail", 2))
        small_step(2)
        emb_load.wait()
        first_copy.wait()
        gain = row_of(gain_first_ref)
        late_ref[0] = jnp.zeros(late_ref.shape[1:], F32)

        def norm_rows(r, rows):
            grad_n = own_first[rows, :] + got_first[rows, :].astype(F32)
            hat, scale = normalise(emb_ref[rows, :])
            late_ref[0, 0:1, :] += jnp.sum(grad_n * hat, axis=0, keepdims=True)
            late_ref[0, 1:2, :] += jnp.sum(grad_n, axis=0, keepdims=True)
            gh_ref[rows, :] = gh_ref[rows, :] + norm_back(grad_n, hat, scale, gain)

        halves_of(norm_rows)
        for copy in group_give:
            copy.start()
        got_group[seat] = late_ref[0]
        gin_store = load(gh_ref, gin_hbm)
        gin_store.start()
        tick(("tail", 3))
        small_step(3)
        hid_load.wait()
        for copy in ffn_loads:
            copy.wait()

        def ffn_rows(first):
            rows = slice(first, first + two_rows)
            total = hid_ref[rows, :]
            for c in range(steps):
                for k in range(2):
                    total += dot(sq_ref[c, k, rows, :], wr_ref[c, k])
            hid_ref[rows, :] = total

        ffn_rows(0)
        tick(("tail", 4))
        for copy in group_take:
            copy.wait_recv()
        total = got_group[0]
        for k in range(1, group):
            total = total + got_group[k]
        late_ref[1] = total
        for copy in outer_give:
            copy.start()
        got_outer[line] = total
        small_step(4)
        ffn_rows(two_rows)
        act_store = load(hid_ref, act_hbm)
        act_store.start()
        tick(("tail", 5))
        small_step(5)
        for copy in outer_take:
            copy.wait_recv()
        total = got_outer[0]
        for k in range(1, outer):
            total = total + got_outer[k]
        now, k = 6, 6
        while plan or k < small_steps:
            tick(("tail", now))
            if k < small_steps:
                small_step(k)
            now, k = now + 1, k + 1
        small_ref[0:2, :] = total[0:2, :]
        gin_store.wait()
        act_store.wait()
        for copy in group_give + outer_give:
            copy.wait_send()

    def backward(all_ref, wcat_ref):
        late = []
        for p in range(pairs):
            for j, w_hbm in enumerate((wq_hbm, wk_hbm, wv_hbm)):
                base = (3 * p + j) * LANES
                late.append(load(w_hbm.at[:, pl.ds(p * LANES, LANES)], wcat_ref.at[:, pl.ds(base, LANES)]))
        pl.run_scoped(
            lambda nt, mix, *rest: attention(all_ref, wcat_ref, nt, mix, late, *rest),
            pltpu.VMEM((D, slot), BF16),
            pltpu.VMEM((3, slot + 8, LANES), F32),
            pltpu.VMEM((LANES, slot), BF16),
            pltpu.VMEM((LANES, slot), BF16),
            pltpu.VMEM((2, slot, LANES), BF16),
            pltpu.VMEM((2, slot, LANES), BF16),
            pltpu.VMEM((2, slot, LANES), BF16),
            pltpu.VMEM((2, LANES, slot), F32),
            pltpu.VMEM((2, slot, LANES), BF16),
            pltpu.VMEM((2, slot, LANES), BF16),
            pltpu.VMEM((2, slot, LANES), BF16),
            pltpu.VMEM((2, slot, LANES), BF16),
            pltpu.VMEM((2, slot, 3 * LANES), BF16),
            pltpu.VMEM((2, slot, LANES), F32),
            pltpu.VMEM((4, 2, slot, BLOCK), BF16),
            pltpu.SemaphoreType.DMA((2, 6)),
            pltpu.SemaphoreType.DMA((4,)),
        )
        pl.run_scoped(
            functools.partial(tail, all_ref, wcat_ref, late),
            pltpu.VMEM((half, D), F32),
            pltpu.VMEM((half, D), BF16),
            pltpu.VMEM((half, D), F32),
            pltpu.VMEM((half, D), F32),
            pltpu.VMEM((steps, 2, half, D), BF16),
            pltpu.VMEM((steps, 2, D, D), BF16),
        )

    pl.run_scoped(backward, pltpu.VMEM((slot, 3 * local), BF16), pltpu.VMEM((D, 3 * local), BF16))
    for n in range(len(entries)):
        drain(n)
    for k in range(inner_bits + 1):
        small_copy(k).wait_send()
    for k in range(inner_bits + 1, inner_bits + 1 + line_steps):
        pl.when(line_sender(k - 1 - inner_bits))(lambda k=k: small_copy(k).wait_send())


def finish_kernel(
    gr_in, ge_in, go_in, qkv_in, act_in, gin_in, small_in,
    act_ref, gin_ref, q_ref, k_ref, v_ref, go_ref, ge_ref, gr_ref, taps_ref, *vec_refs,
):
    act_ref[...] = act_in[...]
    gin_ref[...] = gin_in[...]
    for j, ref in enumerate((q_ref, k_ref, v_ref)):
        ref[...] = qkv_in[0, :, j * LANES : (j + 1) * LANES].astype(F32)
    ge_ref[...] = ge_in[0].astype(F32)
    gr_ref[...] = gr_in[0].astype(F32)

    @pl.when(pl.program_id(0) == 0)
    def _():
        go_ref[...] = go_in[0].astype(F32)
        for j in range(3):
            taps_ref[j] = small_in[4 + 3 * j : 7 + 3 * j, :]
        for k, ref in enumerate(vec_refs):
            ref[...] = small_in[k, :]


def params(vmem, **kw):
    return pltpu.CompilerParams(vmem_limit_bytes=vmem * MIB, **kw)


def body(
    token_ids, lengths, query_weight, key_weight, value_weight, output_weight,
    expand_weight, reduce_weight, dconv_taps, gain_first, bias_first,
    gain_second, bias_second, cotangent,
):
    half = token_ids.shape[1]
    slot = 2 * half
    local = query_weight.shape[1]
    units = expand_weight.shape[1]
    pairs = local // LANES
    outer = lax.axis_size("outer")
    inner = lax.axis_size("inner")
    inner_bits = inner.bit_length() - 1
    rows = D // inner
    width = 3 * LANES

    shape = jax.ShapeDtypeStruct
    smem = pl.BlockSpec(memory_space=pltpu.SMEM)
    anywhere = pl.BlockSpec(memory_space=pl.ANY)
    dma = pltpu.SemaphoreType.DMA
    hd = whole((half, D))
    hl = whole((half, local))
    ld = whole((local, D))
    vec = whole((D,))

    column = pl.BlockSpec((D, LANES), lambda p: (0, p))
    taps_spec = pl.BlockSpec((3, 3, LANES), lambda p: (0, 0, p))
    pair_rows = pl.BlockSpec((slot, LANES), lambda p: (0, p))
    raw_spec = pl.BlockSpec((slot, 3 * LANES), lambda p: (0, p))
    (
        attended, queries, key_rows, value_rows, raw, inverse, embedded, normed_t, att_own, att_oth,
        we_oth, wr_oth, wo_oth, terms,
    ) = pl.pallas_call(
        forward_kernel,
        grid=(pairs,),
        in_specs=[smem, whole((1, half)), vec, vec, column, column, column, taps_spec] + [anywhere] * 3,
        out_specs=[pair_rows] * 4 + [raw_spec, pair_rows, hd, whole((D, slot)), hl, hl] + [anywhere] * 4,
        out_shape=[shape((slot, local), BF16)] * 4
        + [shape((slot, 3 * local), BF16), shape((slot, local), F32), shape((half, D), F32), shape((D, slot), BF16)]
        + [shape((half, local), BF16)] * 2
        + [shape(w.shape, BF16) for w in (expand_weight, reduce_weight, output_weight)]
        + [shape((2 * pairs, slot, slot), BF16)],
        scratch_shapes=[
            pltpu.VMEM((slot, D), BF16),
            pltpu.VMEM((3, BLOCK + 8, LANES), F32),
            pltpu.VMEM((D, 3 * LANES), BF16),
            pltpu.VMEM((2, slot, LANES), BF16),
            pltpu.VMEM((2, slot, LANES), BF16),
            pltpu.VMEM((2, slot, LANES), BF16),
            pltpu.VMEM((2, slot, slot), BF16),
            pltpu.VMEM((pairs, half, LANES), BF16),
            pltpu.VMEM((pairs, half, LANES), BF16),
            dma((PIECES,)), dma((PIECES,)), dma((pairs,)), dma((pairs,)), dma((3,)), dma((3,)),
            dma((slot // BLOCK,)),
        ],
        compiler_params=params(58, collective_id=0, has_side_effects=True),
        name="attention_forward",
    )(
        lengths, token_ids, gain_first, bias_first,
        query_weight, key_weight, value_weight, dconv_taps, expand_weight, reduce_weight, output_weight,
    )

    steps = units // D
    split = D // width
    fed = 2 * steps * split + 1
    chunks = fed + pairs
    twos = (2,) * inner_bits
    line_stages = inner_bits + outer
    vmem = lambda dims, kind: pltpu.VMEM(dims, kind)
    sums, small, activations, grad_input, _ = pl.pallas_call(
        functools.partial(layer_kernel, inner_bits, outer),
        in_specs=[smem, vec, vec, vec, whole((3, 3, local))] + [anywhere] * 21,
        out_specs=[whole((chunks, rows, width)), whole((16, D)), anywhere, anywhere, anywhere],
        out_shape=[
            shape((chunks, rows, width), BF16), shape((16, D), F32), shape((half, D), F32), shape((half, D), F32),
            shape((steps, 2, half, D), BF16),
        ],
        scratch_shapes=[
            vmem((half, D), F32),
            vmem((chunks,) + twos + (rows, width), BF16),
            vmem((chunks, rows, width), BF16),
            vmem((chunks, rows, width), BF16),
            vmem((slot, local), BF16),
            vmem((2, 2, D, D), BF16),
            vmem((D, local), BF16),
            vmem((half, D), BF16),
            vmem((inner_bits + 2, 16, D), F32),
            vmem((inner_bits + 3, 16, D), F32),
            vmem((2, 8, D), F32),
            vmem((2 * inner, 8, D), F32),
            vmem((outer, 8, D), F32),
            dma((12 + 10 * steps + 3 * pairs,)),
            dma((chunks + 2, line_stages)), dma((chunks + 2, line_stages)),
            dma((line_stages + 1,)), dma((line_stages + 1,)),
            dma((steps + 2, 2)), dma((steps + 2, 2)),
            dma((2 * inner,)), dma((2 * inner,)), dma((outer,)), dma((outer,)),
        ]
        + [vmem((chunks,) + (2,) * (inner_bits - 1 - s) + (rows, width), BF16) for s in range(inner_bits)],
        compiler_params=params(63, collective_id=1, has_side_effects=True),
        name="layer",
    )(
        lengths, gain_first, gain_second, bias_second, dconv_taps,
        att_own, att_oth, embedded, cotangent[0], output_weight, wo_oth,
        expand_weight, we_oth, reduce_weight, wr_oth, query_weight, key_weight, value_weight,
        attended, queries, key_rows, value_rows, raw, inverse, normed_t, terms,
    )
    many = steps * split
    part = half // many
    some_rows = pl.BlockSpec((part, D), lambda i: (i, 0))
    pick = lambda index: pl.BlockSpec((1, rows, width), lambda i: (index(i), 0, 0))
    last = lambda i: jnp.minimum(i, pairs - 1)
    chunk_at = lambda i: (i // split) * 2 * split + i % split
    out_pair = pl.BlockSpec((rows, LANES), lambda i: (0, last(i)))
    activations, grad_input, gq, gk, gv, go_sum, ge_sum, gr_sum, tap_sum, *vec_sums = pl.pallas_call(
        finish_kernel,
        grid=(many,),
        in_specs=[
            pick(chunk_at), pick(lambda i: chunk_at(i) + split), pick(lambda i: fed - 1),
            pick(lambda i: fed + last(i)), some_rows, some_rows, whole((16, D)),
        ],
        out_specs=[
            some_rows, some_rows, out_pair, out_pair, out_pair, whole((rows, local)),
            pl.BlockSpec((rows, width), lambda i: (0, i)), pl.BlockSpec((rows, width), lambda i: (0, i)),
            whole((3, 3, D)), vec, vec, vec, vec,
        ],
        out_shape=[shape((half, D), F32)] * 2
        + [shape((rows, local), F32)] * 4
        + [shape((rows, units), F32)] * 2
        + [shape((3, 3, D), F32)]
        + [shape((D,), F32)] * 4,
        compiler_params=params(62),
        name="finish",
    )(sums, sums, sums, sums, activations, grad_input, small)
    return (
        activations[None],
        grad_input[None],
        gq,
        gk,
        gv,
        go_sum.T,
        ge_sum,
        gr_sum.T,
        tap_sum,
        *vec_sums,
    )


def solution(mesh):
    return jax.shard_map(
        body,
        mesh=mesh,
        in_specs=(
            P(("outer", "inner"), "head"),
            P(("outer", "inner")),
            P(None, "head"),
            P(None, "head"),
            P(None, "head"),
            P("head", None),
            P(None, "head"),
            P("head", None),
            P(None, None, "head"),
            P(),
            P(),
            P(),
            P(),
            P(("outer", "inner"), "head", None),
        ),
        out_specs=(
            P(("outer", "inner"), "head", None),
            P(("outer", "inner"), "head", None),
            P("inner", "head"),
            P("inner", "head"),
            P("inner", "head"),
            P("head", "inner"),
            P("inner", "head"),
            P("head", "inner"),
            P(),
            P(),
            P(),
            P(),
            P(),
        ),
        check_vma=False,
    )
```

```python
import functools
import math

import jax
import jax.numpy as jnp
from jax import lax
from jax.experimental import pallas as pl
from jax.experimental.pallas import tpu as pltpu
from jax.sharding import PartitionSpec as P

HEAD_DIM = 64
D = 768
BLOCK = 256
LANES = 128
EPS = 1e-05
MODULUS = 32749
NEGATIVE = -1e30
SCALE = HEAD_DIM ** (-0.5)
F32 = jnp.float32
BF16 = jnp.bfloat16
MIB = 1024 * 1024

SINE = (
    4.442882913726386,
    -7.308248583654593,
    3.606466623722958,
    -0.8474403474577161,
    0.11605422299047748,
    -0.010267162611370253,
    0.0005523348366953617,
)


def dot(a, b):
    return lax.dot_general(a, b, (((1,), (0,)), ((), ())), preferred_element_type=F32)


def dot_nt(a, b):
    return lax.dot_general(a, b, (((1,), (1,)), ((), ())), preferred_element_type=F32)


def whole(shape):
    return pl.BlockSpec(shape, lambda *_: (0,) * len(shape))


def normalise(values):
    centre = values - jnp.mean(values, axis=-1, keepdims=True)
    spread = jnp.mean(centre * centre, axis=-1, keepdims=True)
    scale = lax.rsqrt(spread + EPS)
    return centre * scale, scale


def norm_back(grad, hat, scale, gain):
    q = grad * gain
    mean_q = jnp.mean(q, axis=-1, keepdims=True)
    mean_qh = jnp.mean(q * hat, axis=-1, keepdims=True)
    return scale * (q - mean_q - hat * mean_qh)


def lane_ids(rows):
    return lax.broadcasted_iota(jnp.int32, (rows, LANES), 1)


def split_three(column):
    high = column.astype(BF16).astype(F32)
    rest = column - high
    middle = rest.astype(BF16).astype(F32)
    return high, middle, rest - middle


def with_parts(base, lane, offset, column):
    high, middle, small = split_three(column)
    base = jnp.where(lane == offset + 1, high, base)
    base = jnp.where(lane == offset + 2, middle, base)
    return jnp.where(lane == offset + 3, small, base)


def remote(src, dst, send, recv, **place):
    return pltpu.make_async_remote_copy(
        src_ref=src, dst_ref=dst, send_sem=send, recv_sem=recv,
        device_id=place, device_id_type=pl.DeviceIdType.MESH,
    )


def greet(*places):
    barrier = pltpu.get_barrier_semaphore()
    for place in places:
        pl.semaphore_signal(barrier, inc=1, device_id=place, device_id_type=pl.DeviceIdType.MESH)
    pl.semaphore_wait(barrier, len(places))


def rows_of(which, half):
    return pl.ds(pl.multiple_of(which * half, half), half)


def remainder(product):
    turns = jnp.floor(product.astype(F32) * (1.0 / MODULUS) + 0.5)
    return (product - turns.astype(jnp.int32) * MODULUS).astype(F32)


def embed_rows(tok_ref, gain, bias, emb_ref, normed_ref, base, first):
    tokens = jnp.broadcast_to(tok_ref[:, pl.ds(first, LANES)], (LANES, LANES)).T
    column = lax.broadcasted_iota(jnp.int32, (1, LANES), 1)
    start = remainder(tokens * (column + 1) + column * column)
    stride = remainder(tokens * LANES + column * (2 * LANES))
    parts = []
    for c in range(D // LANES):
        phase = start + (stride * float(c) + float(c * c * LANES * LANES))
        u = (phase - jnp.floor(phase * (1.0 / MODULUS) + 0.5) * float(MODULUS)) * (2.0 / MODULUS)
        z = u * u
        value = jnp.full_like(u, SINE[-1])
        for coefficient in SINE[-2::-1]:
            value = value * z + coefficient
        parts.append(value * u)
    embedded = jnp.concatenate(parts, axis=1)
    emb_ref[pl.ds(first, LANES), :] = embedded
    hat, _ = normalise(embedded)
    rows = pl.ds(pl.multiple_of(base + first, LANES), LANES)
    normed_ref[rows, :] = (hat * gain + bias).astype(BF16)


PIECES = 3


def row_of(ref):
    return ref[...].reshape(1, D)


def forward_kernel(
    len_ref, tok_ref, gain_ref, bias_ref, wq_ref, wk_ref, wv_ref, taps_ref, we_hbm, wr_hbm, wo_hbm,
    att_ref, q_ref, k_ref, v_ref, raw_ref, rinv_ref,
    emb_hbm, nt_hbm, att_oth_hbm, we_oth_hbm, wr_oth_hbm, wo_oth_hbm, terms_hbm,
    emb_ref, nt_ref, normed_ref, shift_ref, wcat_ref, qa_ref, ka_ref, va_ref, terms_ref, give_ref,
    row_send, row_recv, att_send, att_recv, weight_send, weight_recv, terms_sem, store_sem,
):
    slot = att_ref.shape[0]
    half = slot // 2
    blocks = slot // BLOCK
    step = pl.program_id(0)
    pairs = att_oth_hbm.shape[1] // LANES
    head = lax.axis_index("head")
    partner = 1 - head
    piece = half // PIECES

    def row_copy(k):
        rows = pl.ds(pl.multiple_of(head * half + k * piece, piece), piece)
        return remote(normed_ref.at[rows], normed_ref.at[rows], row_send.at[k], row_recv.at[k], head=partner)

    def att_copy(p):
        land = att_oth_hbm.at[:, pl.ds(p * LANES, LANES)]
        return remote(give_ref.at[p], land, att_send.at[p], att_recv.at[p], head=partner)

    def weight_copy(k):
        src, dst = ((wo_hbm, wo_oth_hbm), (we_hbm, we_oth_hbm), (wr_hbm, wr_oth_hbm))[k]
        return remote(src, dst, weight_send.at[k], weight_recv.at[k], head=partner)

    def emb_store():
        return pltpu.make_async_copy(emb_ref, emb_hbm, store_sem.at[0])

    def nt_store(p):
        part = pl.ds(p * (D // pairs), D // pairs)
        return pltpu.make_async_copy(nt_ref.at[part], nt_hbm.at[part], store_sem.at[1 + p])

    def terms_copy(p, i):
        rows, cols = pl.ds(i * BLOCK, BLOCK), pl.ds(0, (i + 1) * BLOCK)
        return pltpu.make_async_copy(
            terms_ref.at[:, rows, cols], terms_hbm.at[pl.ds(2 * p, 2), rows, cols], terms_sem.at[i]
        )

    @pl.when(step == 0)
    def _():
        greet({"head": partner})
        base = head * half
        for k in range(PIECES):
            def embed_step(i, _):
                first = pl.multiple_of(k * piece + i * LANES, LANES)
                embed_rows(tok_ref, row_of(gain_ref), row_of(bias_ref), emb_ref, normed_ref, base, first)
                return 0

            lax.fori_loop(0, piece // LANES, embed_step, 0)
            row_copy(k).start()
        for k in range(3):
            weight_copy(k).start()
        emb_store().start()
        for k in range(PIECES):
            row_copy(k).wait()

    for j, w_ref in enumerate((wq_ref, wk_ref, wv_ref)):
        wcat_ref[:, j * LANES : (j + 1) * LANES] = w_ref[...]
    shift_ref[:, 0:8, :] = jnp.zeros((3, 8, LANES), F32)
    lane = lane_ids(BLOCK)
    features = D // pairs
    some = pl.ds(pl.multiple_of(step * features, features), features)

    def project(r, _):
        first = pl.multiple_of(r * BLOCK, BLOCK)
        rows = pl.ds(first, BLOCK)
        raws = dot(normed_ref[rows, :], wcat_ref[...])
        raw_ref[rows, :] = raws.astype(BF16)
        nt_ref[some, rows] = normed_ref[rows, some].T
        mixed = []
        for j in range(3):
            raw = raws[:, j * LANES : (j + 1) * LANES]
            shift_ref[j, 8 : 8 + BLOCK, :] = raw
            one = shift_ref[j, 7 : 7 + BLOCK, :]
            two = shift_ref[j, 6 : 6 + BLOCK, :]
            value = taps_ref[j, 0:1, :] * raw + taps_ref[j, 1:2, :] * one + taps_ref[j, 2:3, :] * two
            mixed.append(value * SCALE if j == 0 else value)
            shift_ref[j, 0:8, :] = raw[BLOCK - 8 :, :]
        for ref, value in zip((q_ref, k_ref, v_ref), mixed):
            ref[rows, :] = value.astype(BF16)
        row = lax.broadcasted_iota(jnp.int32, (BLOCK, 1), 0) + first
        key_bias = jnp.where(row < len_ref[0], 0.0, NEGATIVE)
        for e in range(2):
            mine = (lane // HEAD_DIM) == e
            other = HEAD_DIM * (1 - e)
            qa_ref[e, rows, :] = jnp.where(mine, mixed[0], jnp.where(lane == other, 1.0, 0.0)).astype(BF16)
            ka_ref[e, rows, :] = jnp.where(mine, mixed[1], jnp.where(lane == other, key_bias, 0.0)).astype(BF16)
            va_ref[e, rows, :] = jnp.where(mine, mixed[2], jnp.where(lane == other, 1.0, 0.0)).astype(BF16)
        return 0

    lax.fori_loop(0, blocks, project, 0)

    @pl.when(step > 0)
    def _():
        for i in range(blocks):
            terms_copy(step - 1, i).wait()

    causal = lax.broadcasted_iota(jnp.int32, (BLOCK, BLOCK), 1) <= lax.broadcasted_iota(
        jnp.int32, (BLOCK, BLOCK), 0
    )
    tasks = [(i, e) for i in range(blocks) for e in range(2)]

    def scores_of(i, e):
        rows = slice(i * BLOCK, (i + 1) * BLOCK)
        query = qa_ref[e, rows, :]
        diagonal = jnp.where(causal, dot_nt(query, ka_ref[e, rows, :]), NEGATIVE)
        before = dot_nt(query, ka_ref[e, : i * BLOCK, :]) if i else None
        return diagonal, before

    coming = scores_of(*tasks[0])
    outs = []
    for t, (i, e) in enumerate(tasks):
        diagonal, before = coming
        if t + 1 < len(tasks):
            coming = scores_of(*tasks[t + 1])
        rows = slice(i * BLOCK, (i + 1) * BLOCK)
        other = HEAD_DIM * (1 - e)
        row_max = jnp.max(diagonal, axis=1, keepdims=True)
        if i:
            row_max = jnp.maximum(row_max, jnp.max(before, axis=1, keepdims=True))
        terms = jnp.exp(diagonal - row_max).astype(BF16)
        terms_ref[e, rows, rows] = terms
        out = dot(terms, va_ref[e, rows, :])
        if i:
            terms = jnp.exp(before - row_max).astype(BF16)
            terms_ref[e, rows, : i * BLOCK] = terms
            out += dot(terms, va_ref[e, : i * BLOCK, :])
        inverse = 1.0 / out[:, other : other + 1]
        outs.append((out, inverse))
        if e == 1:
            first_head = lane < HEAD_DIM
            inverse = jnp.where(first_head, outs[0][1], outs[1][1])
            att_ref[rows, :] = (jnp.where(first_head, outs[0][0], outs[1][0]) * inverse).astype(BF16)
            rinv_ref[rows, :] = inverse
            outs = []
            terms_copy(step, i).start()

    for p in range(pairs):
        @pl.when(step == p)
        def _():
            give_ref[p] = att_ref[rows_of(partner, half), :]
            att_copy(p).start()
            nt_store(p).start()

    @pl.when(step == pairs - 1)
    def _():
        for p in range(pairs):
            att_copy(p).wait()
            nt_store(p).wait()
        emb_store().wait()
        for k in range(3):
            weight_copy(k).wait()
        for i in range(blocks):
            terms_copy(step, i).wait()


def plan_sums(entries, ready, points, tail, inner_bits, line_steps, orders, rate=0.05, hop=1.8):
    stages = inner_bits + line_steps + 1
    done, arrive, free, plan, begun = [0] * len(entries), {}, {}, {}, set()

    def step_of(n, now):
        chunk, size, kind = entries[n]
        stage = done[n]
        if stage < inner_bits:
            link, part = ("bit", orders[kind][stage]), size / 2 ** (stage + 1)
        else:
            t = stage - inner_bits
            link, part = ("in" if t <= line_steps // 2 else "out",), size / 2**inner_bits
        if stage < stages - 1:
            free[link] = max(free.get(link, 0.0), now) + part / rate
            arrive[n] = free[link] + hop
        done[n] += 1

    at, now, late = 0, 0.0, 0
    while at < len(points) or any(d < stages for d in done):
        if at < len(points):
            place, when = points[at]
            now, slack = max(now, when), 0.3 if place[0] != "tail" else 0.0
        else:
            place, slack = ("tail", tail + late), 0.0
            late += 1
            now = max(now, min(arrive[n] for n in range(len(entries)) if done[n] < stages))
        at += 1
        for n, (chunk, _, _) in enumerate(entries):
            if ready[chunk] == place:
                begun.add(n)
        while True:
            able = [n for n in begun if done[n] < stages and (done[n] == 0 or arrive[n] <= now - slack)]
            if not able:
                break
            n = min(able, key=lambda m: (-done[m], m))
            plan.setdefault(place, []).append((n, done[n]))
            step_of(n, now)
    return plan


def layer_kernel(
    inner_bits, outer,
    len_ref, gain_first_ref, gain_second_ref, bias_second_ref, taps_ref,
    att_oth_hbm, emb_hbm, cot_hbm, wo_own_hbm, wo_oth_hbm,
    we_own_hbm, we_oth_hbm, wr_own_hbm, wr_oth_hbm, wq_hbm, wk_hbm, wv_hbm,
    att_hbm, q_hbm, k_hbm, v_hbm, raw_hbm, rinv_hbm, nt_hbm, terms_hbm,
    sum_ref, small_ref, act_hbm, gin_hbm, sq_hbm,
    gh_ref, g_ref, rz_ref, rc_ref, do_ref, got_ref, got_go, got_first, acc_ref, got_small, late_ref, got_group, got_outer,
    load_sem, send_sem, recv_sem, small_send, small_recv, core_send, core_recv,
    group_send, group_recv, outer_send, outer_recv, *halves,
):
    half = gh_ref.shape[0]
    slot = 2 * half
    local = att_oth_hbm.shape[1]
    units = we_own_hbm.shape[1]
    steps = units // D
    width = sum_ref.shape[2]
    split = D // width
    pairs = local // LANES
    fed = 2 * steps * split + 1
    blocks = slot // BLOCK
    head = lax.axis_index("head")
    partner = 1 - head
    mine = lax.axis_index("inner")
    line = lax.axis_index("outer")
    centre = outer // 2
    left = line < centre
    depth = jnp.where(left, centre - 1 - line, line - centre)
    inward = jnp.where(left, line + 1, line - 1)
    outward = jnp.where(left, line - 1, line + 1)
    bit = [(mine // (1 << b)) % 2 for b in range(inner_bits)]
    across = [mine + (1 << b) * (1 - 2 * bit[b]) for b in range(inner_bits)]

    def chunk_of(c, kind, k):
        return (2 * c + kind) * split + k

    entries = []
    for c in range(fed + pairs - 1):
        entries += [(c, 0, 2 * LANES, c % 2), (c, 2 * LANES, LANES, 1 - c % 2)]
    entries += [(fed + pairs - 1, j * LANES, LANES, j % 2) for j in range(3)]
    order_of = [tuple((b + first) % inner_bits for b in range(inner_bits)) for first in range(2)]
    line_steps = 2 * centre - 1
    stage_count = inner_bits + line_steps + 1

    def index_of(fixed):
        return tuple(fixed.get(b, slice(None)) for b in reversed(range(inner_bits)))

    def lanes(entry):
        return slice(entry[1], entry[1] + entry[2])

    def halving(n, s):
        c, _, _, kind = entries[n]
        order = order_of[kind]
        fixed = {b: bit[b] for b in order[:s]}
        b = order[s]
        give = g_ref.at[(c,) + index_of({**fixed, b: 1 - bit[b]}) + (slice(None), lanes(entries[n]))]
        land = halves[s].at[(c,) + (slice(None),) * (inner_bits - 1 - s) + (slice(None), lanes(entries[n]))]
        return remote(give, land, send_sem.at[n, s], recv_sem.at[n, s], inner=across[b])

    def add_half(n, s):
        c, _, _, kind = entries[n]
        order = order_of[kind]
        index = (c,) + index_of({b: bit[b] for b in order[: s + 1]}) + (slice(None), lanes(entries[n]))
        land = (c,) + (slice(None),) * (inner_bits - 1 - s) + (slice(None), lanes(entries[n]))
        g_ref[index] = g_ref[index] + halves[s][land]

    def own(n):
        return (entries[n][0],) + tuple(bit[b] for b in reversed(range(inner_bits))) + (slice(None), lanes(entries[n]))

    def flat(n):
        return (entries[n][0], slice(None), lanes(entries[n]))

    def line_sender(t):
        if t < centre - 1:
            return depth == centre - 1 - t
        if t == centre - 1:
            return depth == 0
        return depth == t - centre

    def line_copy(n, t):
        s = inner_bits + t
        sems = (send_sem.at[n, s], recv_sem.at[n, s])
        if t < centre - 1:
            return remote(g_ref.at[own(n)], rz_ref.at[flat(n)], *sems, outer=inward)
        if t == centre - 1:
            return remote(g_ref.at[own(n)], rc_ref.at[flat(n)], *sems, outer=inward)
        return remote(rc_ref.at[flat(n)], rc_ref.at[flat(n)], *sems, outer=outward)

    def line_finish(n, t):
        if t < centre - 1:
            @pl.when(depth == centre - 2 - t)
            def _():
                line_copy(n, t).wait_recv()
                g_ref[own(n)] = g_ref[own(n)] + rz_ref[flat(n)]
        elif t == centre - 1:
            @pl.when(depth == 0)
            def _():
                line_copy(n, t).wait_recv()
                rc_ref[flat(n)] = g_ref[own(n)] + rc_ref[flat(n)]
        else:
            pl.when(depth == t - centre + 1)(lambda: line_copy(n, t).wait_recv())

    def advance(n, stage):
        if 0 < stage <= inner_bits:
            halving(n, stage - 1).wait_recv()
            add_half(n, stage - 1)
        elif stage > inner_bits:
            line_finish(n, stage - inner_bits - 1)
        if stage < inner_bits:
            halving(n, stage).start()
        elif stage < stage_count - 1:
            t = stage - inner_bits
            pl.when(line_sender(t))(lambda: line_copy(n, t).start())
        else:
            sum_ref[flat(n)] = rc_ref[flat(n)]

    def drain(n):
        for s in range(inner_bits):
            halving(n, s).wait_send()
        for t in range(line_steps):
            pl.when(line_sender(t))(lambda t=t: line_copy(n, t).wait_send())

    points = []
    now = 6.0
    for c in range(steps):
        for k, spent in enumerate((2.8, 2.8, 0.3, 2.8, 2.8, 1.5)):
            now += spent
            points.append((("feed", c, k), now))
        now += 1.4
    for k in range(3):
        now += 1.5
        points.append((("norm", k), now))
    for p in range(pairs):
        now += 1.5
        for j in range(0, blocks, 2):
            points.append((("pair", p, j), now))
            now += 10.0 * (2 * (blocks - j) - 1) * 2 / (blocks * (blocks + 1))
        now += 3.5
        points.append((("taps", p), now))
    for k, spent in enumerate((0.0, 2.0, 2.0, 3.0, 3.0, 3.0)):
        now += spent
        points.append((("tail", k), now))
    ready = {}
    for c in range(steps):
        for k in range(split):
            ready[chunk_of(c, 0, k)] = ("feed", c, 2)
            ready[chunk_of(c, 1, k)] = ("feed", c, 5)
    ready[fed - 1] = ("norm", 2)
    for p in range(pairs):
        ready[fed + p] = ("taps", p) if p < pairs - 1 else ("tail", 0)
    plan = plan_sums(
        [(c, 2e-6 * D * wide, kind) for c, _, wide, kind in entries],
        ready, points, 6, inner_bits, line_steps, order_of,
    )

    def tick(place):
        for n, stage in plan.pop(place, ()):
            advance(n, stage)

    def small_copy(k):
        sems = (small_send.at[k], small_recv.at[k])
        if k == 0:
            return remote(acc_ref.at[0], got_small.at[0], *sems, head=partner)
        if k <= inner_bits:
            return remote(acc_ref.at[k], got_small.at[k], *sems, inner=across[k - 1])
        t = k - 1 - inner_bits
        if t <= centre - 1:
            return remote(acc_ref.at[inner_bits + 1], got_small.at[inner_bits + 1 + (t == centre - 1)], *sems, outer=inward)
        last = got_small.at[inner_bits + 2]
        return remote(last, last, *sems, outer=outward)

    def small_step(k):
        if 0 < k <= inner_bits + 1:
            small_copy(k - 1).wait_recv()
            acc_ref[k] = acc_ref[k - 1] + got_small[k - 1]
        elif k > inner_bits + 1:
            t = k - 2 - inner_bits
            if t < centre - 1:
                @pl.when(depth == centre - 2 - t)
                def _():
                    small_copy(k - 1).wait_recv()
                    acc_ref[inner_bits + 1] = acc_ref[inner_bits + 1] + got_small[inner_bits + 1]
            elif t == centre - 1:
                @pl.when(depth == 0)
                def _():
                    small_copy(k - 1).wait_recv()
                    got_small[inner_bits + 2] = acc_ref[inner_bits + 1] + got_small[inner_bits + 2]
            else:
                pl.when(depth == t - centre + 1)(lambda: small_copy(k - 1).wait_recv())
        if k <= inner_bits:
            small_copy(k).start()
        elif k <= inner_bits + line_steps:
            pl.when(line_sender(k - 1 - inner_bits))(lambda: small_copy(k).start())
        else:
            small_ref[...] = got_small[inner_bits + 2]

    small_steps = inner_bits + line_steps + 2

    inner = 1 << inner_bits
    group = 2 * inner
    seat = mine * 2 + head

    def group_place(k, way):
        other = lax.rem(seat + group + way * k, group)
        return other, {"inner": other // 2, "head": lax.rem(other, 2)}

    def outer_place(k, way):
        other = lax.rem(line + outer + way * k, outer)
        return other, {"outer": other}

    def late_copies(places, count, me, src, land, sends, recvs):
        give = [remote(src, land.at[me], sends.at[k], recvs.at[k], **places(k, 1)[1]) for k in range(1, count)]
        take = [
            remote(src, land.at[places(k, -1)[0]], sends.at[k], recvs.at[k], **places(k, 1)[1]) for k in range(1, count)
        ]
        return give, take

    group_give, group_take = late_copies(
        group_place, group, seat, late_ref.at[0], got_group, group_send, group_recv
    )
    outer_give, outer_take = late_copies(outer_place, outer, line, late_ref.at[1], got_outer, outer_send, outer_recv)

    load_count = iter(range(load_sem.shape[0]))

    def load(src, dst):
        return pltpu.make_async_copy(src, dst, load_sem.at[next(load_count)])

    row = lax.broadcasted_iota(jnp.int32, (half, 1), 0) + head * half
    valid = row < len_ref[0]

    def greet_all():
        barrier = pltpu.get_barrier_semaphore()
        places = [group_place(k, 1)[1] for k in range(1, group)] + [outer_place(k, 1)[1] for k in range(1, outer)]
        for place in places:
            pl.semaphore_signal(barrier, inc=1, device_id=place, device_id_type=pl.DeviceIdType.MESH)
        pl.semaphore_wait(barrier, len(places))

    two_rows = half // 2

    def halves_of(step):
        def run(r, _):
            step(r, pl.ds(pl.multiple_of(r * two_rows, two_rows), two_rows))
            return 0

        lax.fori_loop(0, 2, run, 0)

    def feed_forward(
        att_ref, wo_ref, we_ref, wr_ref, cot_ref, hid_ref, gn_ref,
        n2_ref, n2t_ref, gl_ref, glt_ref, give_ref, relu_ref, sq_ref,
    ):
        give_att = relu_ref.at[0, :, 0:local]
        give_go = relu_ref.at[1, :, 0:local]
        loads = {}
        for k, (att, wo) in enumerate(((att_hbm.at[rows_of(head, half), :], wo_own_hbm), (att_oth_hbm, wo_oth_hbm))):
            loads["att", k] = load(att, att_ref.at[k])
            loads["wo", k] = load(wo, wo_ref.at[k])
        loads["emb"] = load(emb_hbm, hid_ref)
        loads["cot"] = load(cot_hbm, cot_ref)
        for c in range(steps):
            cols = pl.ds(c * D, D)
            for k, we in ((1, we_oth_hbm), (0, we_own_hbm)):
                loads["we", c, k] = load(we.at[:, cols], we_ref.at[c, k])
            for k, wr in ((1, wr_oth_hbm), (0, wr_own_hbm)):
                loads["wr", c, k] = load(wr.at[cols, :], wr_ref.at[c, k])
        for copy in loads.values():
            copy.start()
        greet_all()
        for key in (("att", 0), ("wo", 0), ("att", 1), ("wo", 1), "emb", "cot"):
            loads[key].wait()
        gain, bias = row_of(gain_second_ref), row_of(bias_second_ref)

        def open_rows(r, rows):
            hidden = hid_ref[rows, :] + dot(att_ref[0, rows, :], wo_ref[0]) + dot(att_ref[1, rows, :], wo_ref[1])
            hid_ref[rows, :] = hidden
            hat, _ = normalise(hidden)
            normed = (hat * gain + bias).astype(BF16)
            n2_ref[rows, :] = normed
            n2t_ref[:, rows] = normed.T
            position = lax.broadcasted_iota(jnp.int32, (two_rows, 1), 0) + head * half + r * two_rows
            grad = jnp.where(position < len_ref[0], cot_ref[rows, :], 0.0)
            cot_ref[rows, :] = grad
            gl_ref[rows, :] = grad.astype(BF16)
            glt_ref[:, rows] = grad.astype(BF16).T

        halves_of(open_rows)
        hid_store = load(hid_ref, act_hbm)
        hid_store.start()

        def grad_copy(c, kind):
            return remote(
                give_ref.at[kind], got_ref.at[c % 2, kind], core_send.at[c, kind], core_recv.at[c, kind], head=partner
            )

        def put_own(c, kind, r, value):
            for k in range(split):
                part = value[:, k * width : (k + 1) * width].astype(BF16)
                g_ref[chunk_of(c, kind, k), r] = part.reshape(g_ref.shape[2:])

        def add_other(c, kind):
            grad_copy(c, kind).wait_recv()
            for k in range(split):
                got = got_ref[c % 2, kind, :, k * width : (k + 1) * width]
                g_ref[chunk_of(c, kind, k)] += got.reshape(g_ref.shape[1:])

        def weight_grad(c, kind, k, left_ref, right_ref):
            def run(r, rows):
                grad = dot(left_ref[rows, :], right_ref[...])
                if k == 1:
                    give_ref[kind, rows, :] = grad.astype(BF16)
                else:
                    put_own(c, kind, r, grad)

            if k == 1 and c:
                grad_copy(c - 1, kind).wait_send()
            halves_of(run)
            if k == 1:
                grad_copy(c, kind).start()

        stores = []
        for c in range(steps):
            for k in (1, 0):
                loads["we", c, k].wait()

                def expand(r, rows):
                    relu = jnp.maximum(dot(n2_ref[rows, :], we_ref[c, k]), 0.0)
                    relu_ref[k, rows, :] = relu.astype(BF16)
                    sq_ref[c, k, rows, :] = (relu * relu).astype(BF16)

                halves_of(expand)
                stores.append(load(sq_ref.at[c, k], sq_hbm.at[c, k]))
                stores[-1].start()
                weight_grad(c, 0, k, glt_ref, sq_ref.at[c, k])
                tick(("feed", c, 1 - k))
            add_other(c, 0)
            tick(("feed", c, 2))
            for k in (1, 0):
                loads["wr", c, k].wait()

                def reduce_back(r, rows):
                    back = dot_nt(gl_ref[rows, :], wr_ref[c, k])
                    relu_ref[k, rows, :] = (back * (2.0 * relu_ref[k, rows, :].astype(F32))).astype(BF16)

                halves_of(reduce_back)
                weight_grad(c, 1, k, n2t_ref, relu_ref.at[k])
                tick(("feed", c, 4 - k))
            for k in (1, 0):
                def expand_back(r, rows):
                    gn = dot_nt(relu_ref[k, rows, :], we_ref[c, k])
                    if c == 0 and k == 1:
                        gn_ref[rows, :] = gn
                    else:
                        gn_ref[rows, :] += gn

                halves_of(expand_back)
                if k == 1:
                    add_other(c, 1)
                    tick(("feed", c, 5))
        acc_ref[0] = jnp.zeros(acc_ref.shape[1:], F32)

        def close_rows(r, rows):
            hat, scale = normalise(hid_ref[rows, :])
            grad_n = gn_ref[rows, :]
            acc_ref[0, 2:3, :] += jnp.sum(grad_n * hat, axis=0, keepdims=True)
            acc_ref[0, 3:4, :] += jnp.sum(grad_n, axis=0, keepdims=True)
            grad_h = cot_ref[rows, :] + norm_back(grad_n, hat, scale, gain)
            gh_ref[rows, :] = grad_h
            low = grad_h.astype(BF16)
            n2_ref[rows, :] = low
            n2t_ref[:, rows] = low.T
            give_att[rows, :] = dot_nt(low, wo_ref[1]).astype(BF16)

        halves_of(close_rows)
        own_rows = rows_of(head, half)
        att_copy = remote(give_att, do_ref.at[own_rows], core_send.at[steps, 0], core_recv.at[steps, 0], head=partner)
        att_copy.start()
        tick(("norm", 0))
        give_go[...] = dot(n2t_ref[...], att_ref[1]).astype(BF16)
        go_copy = remote(give_go, got_go, core_send.at[steps, 1], core_recv.at[steps, 1], head=partner)
        go_copy.start()
        do_ref[own_rows, :] = dot_nt(n2_ref[...], wo_ref[0]).astype(BF16)
        tick(("norm", 1))
        grad_o = dot(n2t_ref[...], att_ref[0]).astype(BF16)
        go_copy.wait()
        g_ref[fed - 1] = (grad_o + got_go[...]).reshape(g_ref.shape[1:])
        tick(("norm", 2))
        for kind in range(2):
            grad_copy(steps - 1, kind).wait_send()
        for copy in [hid_store] + stores:
            copy.wait()
        att_copy.wait()

    pl.run_scoped(
        feed_forward,
        pltpu.VMEM((2, half, local), BF16), pltpu.VMEM((2, local, D), BF16),
        pltpu.VMEM((steps, 2, D, D), BF16), pltpu.VMEM((steps, 2, D, D), BF16),
        pltpu.VMEM((half, D), F32), pltpu.VMEM((half, D), F32), pltpu.VMEM((half, D), F32),
        pltpu.VMEM((half, D), BF16), pltpu.VMEM((D, half), BF16),
        pltpu.VMEM((half, D), BF16), pltpu.VMEM((D, half), BF16),
        pltpu.VMEM((2, D, D), BF16), pltpu.VMEM((2, half, D), BF16), pltpu.VMEM((steps, 2, half, D), BF16),
    )

    def attention(
        all_ref, wcat_ref, nt_ref, mix_ref, late, dot_ref, qt_ref, doa_ref, kz_ref, va_ref, turned_ref,
        att_ref, q_ref, k_ref, v_ref, raw_ref, rinv_ref, terms_ref, pair_sem, terms_sem,
    ):
        def pair_loads(p, place):
            one = pl.ds(pl.multiple_of(p * LANES, LANES), LANES)
            three = pl.ds(pl.multiple_of(p * 3 * LANES, LANES), 3 * LANES)
            return [
                pltpu.make_async_copy(rinv_hbm.at[:, one], rinv_ref.at[place], pair_sem.at[place, 0]),
                pltpu.make_async_copy(att_hbm.at[:, one], att_ref.at[place], pair_sem.at[place, 1]),
                pltpu.make_async_copy(v_hbm.at[:, one], v_ref.at[place], pair_sem.at[place, 2]),
                pltpu.make_async_copy(q_hbm.at[:, one], q_ref.at[place], pair_sem.at[place, 3]),
                pltpu.make_async_copy(k_hbm.at[:, one], k_ref.at[place], pair_sem.at[place, 4]),
                pltpu.make_async_copy(raw_hbm.at[:, three], raw_ref.at[place], pair_sem.at[place, 5]),
            ]

        def terms_load(p, j):
            rows = pl.ds(j * BLOCK, slot - j * BLOCK)
            spot = lax.rem(blocks * p + j, 4)
            return pltpu.make_async_copy(
                terms_hbm.at[pl.ds(2 * p, 2), rows, pl.ds(j * BLOCK, BLOCK)],
                terms_ref.at[spot, :, rows, :],
                terms_sem.at[spot],
            )

        for copy in pair_loads(0, 0):
            copy.start()
        for j in range(2):
            terms_load(0, j).start()
        nt_load = load(nt_hbm, nt_ref)
        nt_load.start()
        for copy in late:
            copy.start()
        mix_ref[:, slot : slot + 8, :] = jnp.zeros((3, 8, LANES), F32)
        lane = lane_ids(slot)

        def at_pair(p, kind, *rest):
            for q in range(pairs):
                if plan.get((kind, q) + rest):
                    pl.when(p == q)(functools.partial(tick, (kind, q) + rest))

        def one_pair(p, _):
            place = lax.rem(p, 2)
            one = pl.ds(pl.multiple_of(p * LANES, LANES), LANES)

            @pl.when(p + 1 < pairs)
            def _():
                for copy in pair_loads(p + 1, 1 - place):
                    copy.start()

            for copy in pair_loads(p, place):
                copy.wait()
            scaled = (do_ref[:, one].astype(F32) * rinv_ref[place]).astype(BF16)
            dot_ref[...] = scaled.T
            qt_ref[...] = q_ref[place].T
            product = scaled.astype(F32) * att_ref[place].astype(F32)
            for e in range(2):
                in_head = (lane // HEAD_DIM) == e
                delta = -jnp.sum(jnp.where(in_head, product, 0.0), axis=1, keepdims=True)
                other = HEAD_DIM * (1 - e)
                ones = jnp.where((lane > other) & (lane < other + 4), 1.0, 0.0)
                doa_ref[e] = with_parts(jnp.where(in_head, scaled.astype(F32), 0.0), lane, other, delta).astype(BF16)
                va_ref[e] = jnp.where(in_head, v_ref[place].astype(F32), ones).astype(BF16)
                kz_ref[e] = jnp.where(in_head, k_ref[place].astype(F32), 0.0).astype(BF16)

            def grads_of(j, e):
                return dot_nt(doa_ref[e, j * BLOCK :, :], va_ref[e, j * BLOCK : (j + 1) * BLOCK, :])

            for j0 in range(0, blocks, 2):
                at_pair(p, "pair", j0)
                for j in (j0, j0 + 1):
                    terms_load(p, j).wait()
                    if j + 2 < blocks:
                        terms_load(p, j + 2).start()
                    else:
                        @pl.when(p + 1 < pairs)
                        def _():
                            terms_load(p + 1, j + 2 - blocks).start()
                tasks = [(j, e) for j in (j0, j0 + 1) for e in range(2)]
                coming = grads_of(*tasks[0])
                for t, (j, e) in enumerate(tasks):
                    back = coming
                    if t + 1 < len(tasks):
                        coming = grads_of(*tasks[t + 1])
                    first = j * BLOCK
                    keys = slice(first, first + BLOCK)
                    mine_rows = slice(e * HEAD_DIM, (e + 1) * HEAD_DIM)
                    terms = terms_ref[lax.rem(blocks * p + j, 4), e, first:, :]
                    grads = (terms.astype(F32) * back).astype(BF16)
                    part = dot(grads, kz_ref[e, keys, :])
                    if j == 0 and e == 0:
                        mix_ref[0, first:slot, :] = part
                    else:
                        mix_ref[0, first:slot, :] += part
                    turned_ref[0, mine_rows, keys] = dot(qt_ref[mine_rows, first:], grads)
                    turned_ref[1, mine_rows, keys] = dot(dot_ref[mine_rows, first:], terms)
            mix_ref[0, 0:slot, :] = mix_ref[0, 0:slot, :] * SCALE
            mix_ref[1, 0:slot, :] = turned_ref[0].T
            mix_ref[2, 0:slot, :] = turned_ref[1].T
            base = pl.multiple_of(p * 3 * LANES, LANES)
            for j in range(3):
                zero = mix_ref[j, 0:slot, :]
                one_on = mix_ref[j, 1 : 1 + slot, :]
                two_on = mix_ref[j, 2 : 2 + slot, :]
                raw = raw_ref[place, :, j * LANES : (j + 1) * LANES].astype(F32)
                cols = pl.ds(pl.multiple_of(head * local + p * LANES, LANES), LANES)
                value = 0.0
                for s, moved in enumerate((zero, one_on, two_on)):
                    total = jnp.sum(moved * raw, axis=0, keepdims=True)
                    acc_ref[0, 4 + 3 * j + s : 5 + 3 * j + s, cols] = total
                    value += taps_ref[j, s : s + 1, one] * moved
                all_ref[:, pl.ds(pl.multiple_of(base + j * LANES, LANES), LANES)] = value.astype(BF16)

            @pl.when(p == 0)
            def _():
                nt_load.wait()

            grads = dot(nt_ref[...], all_ref[:, pl.ds(base, 3 * LANES)]).astype(BF16)
            g_ref[fed + p] = grads.reshape(g_ref.shape[1:])
            at_pair(p, "taps")
            return 0

        lax.fori_loop(0, pairs, one_pair, 0)

    def tail(all_ref, wcat_ref, late, emb_ref, give_first, own_first, hid_ref, sq_ref, wr_ref):
        emb_load = load(emb_hbm, emb_ref)
        emb_load.start()
        tick(("tail", 0))
        hid_load = load(act_hbm, hid_ref)
        hid_load.start()
        ffn_loads = []
        for c in range(steps):
            for k, wr in ((1, wr_oth_hbm), (0, wr_own_hbm)):
                ffn_loads.append(load(sq_hbm.at[c, k], sq_ref.at[c, k]))
                ffn_loads.append(load(wr.at[pl.ds(c * D, D), :], wr_ref.at[c, k]))
        for copy in ffn_loads:
            copy.start()
        small_step(0)
        for copy in late:
            copy.wait()

        def other_rows(r, rows):
            there = pl.ds(pl.multiple_of(partner * half + r * two_rows, two_rows), two_rows)
            give_first[rows, :] = dot_nt(all_ref[there, :], wcat_ref[...]).astype(BF16)

        halves_of(other_rows)
        first_copy = remote(
            give_first, got_first, core_send.at[steps + 1, 0], core_recv.at[steps + 1, 0], head=partner
        )
        first_copy.start()
        tick(("tail", 1))
        small_step(1)

        def own_rows(r, rows):
            here = pl.ds(pl.multiple_of(head * half + r * two_rows, two_rows), two_rows)
            own_first[rows, :] = dot_nt(all_ref[here, :], wcat_ref[...])

        halves_of(own_rows)
        tick(("tail", 2))
        small_step(2)
        emb_load.wait()
        first_copy.wait()
        gain = row_of(gain_first_ref)
        late_ref[0] = jnp.zeros(late_ref.shape[1:], F32)

        def norm_rows(r, rows):
            grad_n = own_first[rows, :] + got_first[rows, :].astype(F32)
            hat, scale = normalise(emb_ref[rows, :])
            late_ref[0, 0:1, :] += jnp.sum(grad_n * hat, axis=0, keepdims=True)
            late_ref[0, 1:2, :] += jnp.sum(grad_n, axis=0, keepdims=True)
            gh_ref[rows, :] = gh_ref[rows, :] + norm_back(grad_n, hat, scale, gain)

        halves_of(norm_rows)
        for copy in group_give:
            copy.start()
        got_group[seat] = late_ref[0]
        gin_store = load(gh_ref, gin_hbm)
        gin_store.start()
        tick(("tail", 3))
        small_step(3)
        hid_load.wait()
        for copy in ffn_loads:
            copy.wait()

        def ffn_rows(first):
            rows = slice(first, first + two_rows)
            total = hid_ref[rows, :]
            for c in range(steps):
                for k in range(2):
                    total += dot(sq_ref[c, k, rows, :], wr_ref[c, k])
            hid_ref[rows, :] = total

        ffn_rows(0)
        tick(("tail", 4))
        for copy in group_take:
            copy.wait_recv()
        total = got_group[0]
        for k in range(1, group):
            total = total + got_group[k]
        late_ref[1] = total
        for copy in outer_give:
            copy.start()
        got_outer[line] = total
        small_step(4)
        ffn_rows(two_rows)
        act_store = load(hid_ref, act_hbm)
        act_store.start()
        tick(("tail", 5))
        small_step(5)
        for copy in outer_take:
            copy.wait_recv()
        total = got_outer[0]
        for k in range(1, outer):
            total = total + got_outer[k]
        now, k = 6, 6
        while plan or k < small_steps:
            tick(("tail", now))
            if k < small_steps:
                small_step(k)
            now, k = now + 1, k + 1
        small_ref[0:2, :] = total[0:2, :]
        gin_store.wait()
        act_store.wait()
        for copy in group_give + outer_give:
            copy.wait_send()

    def backward(all_ref, wcat_ref):
        late = []
        for p in range(pairs):
            for j, w_hbm in enumerate((wq_hbm, wk_hbm, wv_hbm)):
                base = (3 * p + j) * LANES
                late.append(load(w_hbm.at[:, pl.ds(p * LANES, LANES)], wcat_ref.at[:, pl.ds(base, LANES)]))
        pl.run_scoped(
            lambda nt, mix, *rest: attention(all_ref, wcat_ref, nt, mix, late, *rest),
            pltpu.VMEM((D, slot), BF16),
            pltpu.VMEM((3, slot + 8, LANES), F32),
            pltpu.VMEM((LANES, slot), BF16),
            pltpu.VMEM((LANES, slot), BF16),
            pltpu.VMEM((2, slot, LANES), BF16),
            pltpu.VMEM((2, slot, LANES), BF16),
            pltpu.VMEM((2, slot, LANES), BF16),
            pltpu.VMEM((2, LANES, slot), F32),
            pltpu.VMEM((2, slot, LANES), BF16),
            pltpu.VMEM((2, slot, LANES), BF16),
            pltpu.VMEM((2, slot, LANES), BF16),
            pltpu.VMEM((2, slot, LANES), BF16),
            pltpu.VMEM((2, slot, 3 * LANES), BF16),
            pltpu.VMEM((2, slot, LANES), F32),
            pltpu.VMEM((4, 2, slot, BLOCK), BF16),
            pltpu.SemaphoreType.DMA((2, 6)),
            pltpu.SemaphoreType.DMA((4,)),
        )
        pl.run_scoped(
            functools.partial(tail, all_ref, wcat_ref, late),
            pltpu.VMEM((half, D), F32),
            pltpu.VMEM((half, D), BF16),
            pltpu.VMEM((half, D), F32),
            pltpu.VMEM((half, D), F32),
            pltpu.VMEM((steps, 2, half, D), BF16),
            pltpu.VMEM((steps, 2, D, D), BF16),
        )

    pl.run_scoped(backward, pltpu.VMEM((slot, 3 * local), BF16), pltpu.VMEM((D, 3 * local), BF16))
    for n in range(len(entries)):
        drain(n)
    for k in range(inner_bits + 1):
        small_copy(k).wait_send()
    for k in range(inner_bits + 1, inner_bits + 1 + line_steps):
        pl.when(line_sender(k - 1 - inner_bits))(lambda k=k: small_copy(k).wait_send())


def finish_kernel(
    gr_in, ge_in, go_in, qkv_in, act_in, gin_in, small_in,
    act_ref, gin_ref, q_ref, k_ref, v_ref, go_ref, ge_ref, gr_ref, taps_ref, *vec_refs,
):
    act_ref[...] = act_in[...]
    gin_ref[...] = gin_in[...]
    for j, ref in enumerate((q_ref, k_ref, v_ref)):
        ref[...] = qkv_in[0, :, j * LANES : (j + 1) * LANES].astype(F32)
    ge_ref[...] = ge_in[0].astype(F32)
    gr_ref[...] = gr_in[0].astype(F32)

    @pl.when(pl.program_id(0) == 0)
    def _():
        go_ref[...] = go_in[0].astype(F32)
        for j in range(3):
            taps_ref[j] = small_in[4 + 3 * j : 7 + 3 * j, :]
        for k, ref in enumerate(vec_refs):
            ref[...] = small_in[k, :]


def params(vmem, **kw):
    return pltpu.CompilerParams(vmem_limit_bytes=vmem * MIB, **kw)


def body(
    token_ids, lengths, query_weight, key_weight, value_weight, output_weight,
    expand_weight, reduce_weight, dconv_taps, gain_first, bias_first,
    gain_second, bias_second, cotangent,
):
    half = token_ids.shape[1]
    slot = 2 * half
    local = query_weight.shape[1]
    units = expand_weight.shape[1]
    pairs = local // LANES
    outer = lax.axis_size("outer")
    inner = lax.axis_size("inner")
    inner_bits = inner.bit_length() - 1
    rows = D // inner
    width = 3 * LANES

    shape = jax.ShapeDtypeStruct
    smem = pl.BlockSpec(memory_space=pltpu.SMEM)
    anywhere = pl.BlockSpec(memory_space=pl.ANY)
    dma = pltpu.SemaphoreType.DMA
    vec = whole((D,))

    column = pl.BlockSpec((D, LANES), lambda p: (0, p))
    taps_spec = pl.BlockSpec((3, 3, LANES), lambda p: (0, 0, p))
    pair_rows = pl.BlockSpec((slot, LANES), lambda p: (0, p))
    raw_spec = pl.BlockSpec((slot, 3 * LANES), lambda p: (0, p))
    (
        attended, queries, key_rows, value_rows, raw, inverse, embedded, normed_t, att_oth,
        we_oth, wr_oth, wo_oth, terms,
    ) = pl.pallas_call(
        forward_kernel,
        grid=(pairs,),
        in_specs=[smem, whole((1, half)), vec, vec, column, column, column, taps_spec] + [anywhere] * 3,
        out_specs=[pair_rows] * 4 + [raw_spec, pair_rows] + [anywhere] * 7,
        out_shape=[shape((slot, local), BF16)] * 4
        + [shape((slot, 3 * local), BF16), shape((slot, local), F32), shape((half, D), F32), shape((D, slot), BF16)]
        + [shape((half, local), BF16)]
        + [shape(w.shape, BF16) for w in (expand_weight, reduce_weight, output_weight)]
        + [shape((2 * pairs, slot, slot), BF16)],
        scratch_shapes=[
            pltpu.VMEM((half, D), F32),
            pltpu.VMEM((D, slot), BF16),
            pltpu.VMEM((slot, D), BF16),
            pltpu.VMEM((3, BLOCK + 8, LANES), F32),
            pltpu.VMEM((D, 3 * LANES), BF16),
            pltpu.VMEM((2, slot, LANES), BF16),
            pltpu.VMEM((2, slot, LANES), BF16),
            pltpu.VMEM((2, slot, LANES), BF16),
            pltpu.VMEM((2, slot, slot), BF16),
            pltpu.VMEM((pairs, half, LANES), BF16),
            dma((PIECES,)), dma((PIECES,)), dma((pairs,)), dma((pairs,)), dma((3,)), dma((3,)),
            dma((slot // BLOCK,)), dma((1 + pairs,)),
        ],
        compiler_params=params(58, collective_id=0, has_side_effects=True),
        name="attention_forward",
    )(
        lengths, token_ids, gain_first, bias_first,
        query_weight, key_weight, value_weight, dconv_taps, expand_weight, reduce_weight, output_weight,
    )

    steps = units // D
    split = D // width
    fed = 2 * steps * split + 1
    chunks = fed + pairs
    twos = (2,) * inner_bits
    line_stages = inner_bits + outer
    vmem = lambda dims, kind: pltpu.VMEM(dims, kind)
    sums, small, activations, grad_input, _ = pl.pallas_call(
        functools.partial(layer_kernel, inner_bits, outer),
        in_specs=[smem, vec, vec, vec, whole((3, 3, local))] + [anywhere] * 20,
        out_specs=[whole((chunks, rows, width)), whole((16, D)), anywhere, anywhere, anywhere],
        out_shape=[
            shape((chunks, rows, width), BF16), shape((16, D), F32), shape((half, D), F32), shape((half, D), F32),
            shape((steps, 2, half, D), BF16),
        ],
        scratch_shapes=[
            vmem((half, D), F32),
            vmem((chunks,) + twos + (rows, width), BF16),
            vmem((chunks, rows, width), BF16),
            vmem((chunks, rows, width), BF16),
            vmem((slot, local), BF16),
            vmem((2, 2, D, D), BF16),
            vmem((D, local), BF16),
            vmem((half, D), BF16),
            vmem((inner_bits + 2, 16, D), F32),
            vmem((inner_bits + 3, 16, D), F32),
            vmem((2, 8, D), F32),
            vmem((2 * inner, 8, D), F32),
            vmem((outer, 8, D), F32),
            dma((12 + 10 * steps + 3 * pairs,)),
            dma((2 * chunks + 1, line_stages)), dma((2 * chunks + 1, line_stages)),
            dma((line_stages + 1,)), dma((line_stages + 1,)),
            dma((steps + 2, 2)), dma((steps + 2, 2)),
            dma((2 * inner,)), dma((2 * inner,)), dma((outer,)), dma((outer,)),
        ]
        + [vmem((chunks,) + (2,) * (inner_bits - 1 - s) + (rows, width), BF16) for s in range(inner_bits)],
        compiler_params=params(63, collective_id=1, has_side_effects=True),
        name="layer",
    )(
        lengths, gain_first, gain_second, bias_second, dconv_taps,
        att_oth, embedded, cotangent[0], output_weight, wo_oth,
        expand_weight, we_oth, reduce_weight, wr_oth, query_weight, key_weight, value_weight,
        attended, queries, key_rows, value_rows, raw, inverse, normed_t, terms,
    )
    many = steps * split
    part = half // many
    some_rows = pl.BlockSpec((part, D), lambda i: (i, 0))
    pick = lambda index: pl.BlockSpec((1, rows, width), lambda i: (index(i), 0, 0))
    last = lambda i: jnp.minimum(i, pairs - 1)
    chunk_at = lambda i: (i // split) * 2 * split + i % split
    out_pair = pl.BlockSpec((rows, LANES), lambda i: (0, last(i)))
    activations, grad_input, gq, gk, gv, go_sum, ge_sum, gr_sum, tap_sum, *vec_sums = pl.pallas_call(
        finish_kernel,
        grid=(many,),
        in_specs=[
            pick(chunk_at), pick(lambda i: chunk_at(i) + split), pick(lambda i: fed - 1),
            pick(lambda i: fed + last(i)), some_rows, some_rows, whole((16, D)),
        ],
        out_specs=[
            some_rows, some_rows, out_pair, out_pair, out_pair, whole((rows, local)),
            pl.BlockSpec((rows, width), lambda i: (0, i)), pl.BlockSpec((rows, width), lambda i: (0, i)),
            whole((3, 3, D)), vec, vec, vec, vec,
        ],
        out_shape=[shape((half, D), F32)] * 2
        + [shape((rows, local), F32)] * 4
        + [shape((rows, units), F32)] * 2
        + [shape((3, 3, D), F32)]
        + [shape((D,), F32)] * 4,
        compiler_params=params(62),
        name="finish",
    )(sums, sums, sums, sums, activations, grad_input, small)
    return (
        activations[None],
        grad_input[None],
        gq,
        gk,
        gv,
        go_sum.T,
        ge_sum,
        gr_sum.T,
        tap_sum,
        *vec_sums,
    )


def solution(mesh):
    return jax.shard_map(
        body,
        mesh=mesh,
        in_specs=(
            P(("outer", "inner"), "head"),
            P(("outer", "inner")),
            P(None, "head"),
            P(None, "head"),
            P(None, "head"),
            P("head", None),
            P(None, "head"),
            P("head", None),
            P(None, None, "head"),
            P(),
            P(),
            P(),
            P(),
            P(("outer", "inner"), "head", None),
        ),
        out_specs=(
            P(("outer", "inner"), "head", None),
            P(("outer", "inner"), "head", None),
            P("inner", "head"),
            P("inner", "head"),
            P("inner", "head"),
            P("head", "inner"),
            P("inner", "head"),
            P("head", "inner"),
            P(),
            P(),
            P(),
            P(),
            P(),
        ),
        check_vma=False,
    )
```

```python
import functools
import math

import jax
import jax.numpy as jnp
from jax import lax
from jax.experimental import pallas as pl
from jax.experimental.pallas import tpu as pltpu
from jax.sharding import PartitionSpec as P

HEAD_DIM = 64
D = 768
BLOCK = 256
LANES = 128
EPS = 1e-05
MODULUS = 32749
NEGATIVE = -1e30
SCALE = HEAD_DIM ** (-0.5)
F32 = jnp.float32
BF16 = jnp.bfloat16
MIB = 1024 * 1024

SINE = (
    4.442882913726386,
    -7.308248583654593,
    3.606466623722958,
    -0.8474403474577161,
    0.11605422299047748,
    -0.010267162611370253,
    0.0005523348366953617,
)


def dot(a, b):
    return lax.dot_general(a, b, (((1,), (0,)), ((), ())), preferred_element_type=F32)


def dot_nt(a, b):
    return lax.dot_general(a, b, (((1,), (1,)), ((), ())), preferred_element_type=F32)


def whole(shape):
    return pl.BlockSpec(shape, lambda *_: (0,) * len(shape))


def normalise(values):
    centre = values - jnp.mean(values, axis=-1, keepdims=True)
    spread = jnp.mean(centre * centre, axis=-1, keepdims=True)
    scale = lax.rsqrt(spread + EPS)
    return centre * scale, scale


def norm_back(grad, hat, scale, gain):
    q = grad * gain
    mean_q = jnp.mean(q, axis=-1, keepdims=True)
    mean_qh = jnp.mean(q * hat, axis=-1, keepdims=True)
    return scale * (q - mean_q - hat * mean_qh)


def lane_ids(rows):
    return lax.broadcasted_iota(jnp.int32, (rows, LANES), 1)


def split_three(column):
    high = column.astype(BF16).astype(F32)
    rest = column - high
    middle = rest.astype(BF16).astype(F32)
    return high, middle, rest - middle


def with_parts(base, lane, offset, column):
    high, middle, small = split_three(column)
    base = jnp.where(lane == offset + 1, high, base)
    base = jnp.where(lane == offset + 2, middle, base)
    return jnp.where(lane == offset + 3, small, base)


def remote(src, dst, send, recv, **place):
    return pltpu.make_async_remote_copy(
        src_ref=src, dst_ref=dst, send_sem=send, recv_sem=recv,
        device_id=place, device_id_type=pl.DeviceIdType.MESH,
    )


def greet(*places):
    barrier = pltpu.get_barrier_semaphore()
    for place in places:
        pl.semaphore_signal(barrier, inc=1, device_id=place, device_id_type=pl.DeviceIdType.MESH)
    pl.semaphore_wait(barrier, len(places))


def rows_of(which, half):
    return pl.ds(pl.multiple_of(which * half, half), half)


def remainder(product):
    turns = jnp.floor(product.astype(F32) * (1.0 / MODULUS) + 0.5)
    return (product - turns.astype(jnp.int32) * MODULUS).astype(F32)


def embed_rows(tok_ref, gain, bias, emb_ref, normed_ref, base, first):
    tokens = jnp.broadcast_to(tok_ref[:, pl.ds(first, LANES)], (LANES, LANES)).T
    column = lax.broadcasted_iota(jnp.int32, (1, LANES), 1)
    start = remainder(tokens * (column + 1) + column * column)
    stride = remainder(tokens * LANES + column * (2 * LANES))
    parts = []
    for c in range(D // LANES):
        phase = start + (stride * float(c) + float(c * c * LANES * LANES))
        u = (phase - jnp.floor(phase * (1.0 / MODULUS) + 0.5) * float(MODULUS)) * (2.0 / MODULUS)
        z = u * u
        value = jnp.full_like(u, SINE[-1])
        for coefficient in SINE[-2::-1]:
            value = value * z + coefficient
        parts.append(value * u)
    embedded = jnp.concatenate(parts, axis=1)
    emb_ref[pl.ds(first, LANES), :] = embedded
    hat, _ = normalise(embedded)
    rows = pl.ds(pl.multiple_of(base + first, LANES), LANES)
    normed_ref[rows, :] = (hat * gain + bias).astype(BF16)


PIECES = 3


def row_of(ref):
    return ref[...].reshape(1, D)


def forward_kernel(
    len_ref, tok_ref, gain_ref, bias_ref, wq_ref, wk_ref, wv_ref, taps_ref, we_hbm, wr_hbm, wo_hbm,
    att_ref, q_ref, k_ref, v_ref, raw_ref, rinv_ref,
    emb_hbm, nt_hbm, att_oth_hbm, we_oth_hbm, wr_oth_hbm, wo_oth_hbm, terms_hbm,
    emb_ref, nt_ref, normed_ref, shift_ref, wcat_ref, qa_ref, ka_ref, va_ref, terms_ref, give_ref,
    row_send, row_recv, att_send, att_recv, weight_send, weight_recv, terms_sem, store_sem,
):
    slot = att_ref.shape[0]
    half = slot // 2
    blocks = slot // BLOCK
    step = pl.program_id(0)
    pairs = att_oth_hbm.shape[1] // LANES
    head = lax.axis_index("head")
    partner = 1 - head
    piece = half // PIECES

    def row_copy(k):
        rows = pl.ds(pl.multiple_of(head * half + k * piece, piece), piece)
        return remote(normed_ref.at[rows], normed_ref.at[rows], row_send.at[k], row_recv.at[k], head=partner)

    def att_copy(p):
        land = att_oth_hbm.at[:, pl.ds(p * LANES, LANES)]
        return remote(give_ref.at[p], land, att_send.at[p], att_recv.at[p], head=partner)

    def weight_copy(k):
        src, dst = ((wo_hbm, wo_oth_hbm), (we_hbm, we_oth_hbm), (wr_hbm, wr_oth_hbm))[k]
        return remote(src, dst, weight_send.at[k], weight_recv.at[k], head=partner)

    def emb_store():
        return pltpu.make_async_copy(emb_ref, emb_hbm, store_sem.at[0])

    def nt_store(p):
        part = pl.ds(p * (D // pairs), D // pairs)
        return pltpu.make_async_copy(nt_ref.at[part], nt_hbm.at[part], store_sem.at[1 + p])

    def terms_copy(p, i):
        rows, cols = pl.ds(i * BLOCK, BLOCK), pl.ds(0, (i + 1) * BLOCK)
        return pltpu.make_async_copy(
            terms_ref.at[:, rows, cols], terms_hbm.at[pl.ds(2 * p, 2), rows, cols], terms_sem.at[i]
        )

    @pl.when(step == 0)
    def _():
        greet({"head": partner})
        base = head * half
        for k in range(PIECES):
            def embed_step(i, _):
                first = pl.multiple_of(k * piece + i * LANES, LANES)
                embed_rows(tok_ref, row_of(gain_ref), row_of(bias_ref), emb_ref, normed_ref, base, first)
                return 0

            lax.fori_loop(0, piece // LANES, embed_step, 0)
            row_copy(k).start()
        for k in range(3):
            weight_copy(k).start()
        emb_store().start()
        for k in range(PIECES):
            row_copy(k).wait()

    for j, w_ref in enumerate((wq_ref, wk_ref, wv_ref)):
        wcat_ref[:, j * LANES : (j + 1) * LANES] = w_ref[...]
    shift_ref[0, :, 0:8, :] = jnp.zeros((3, 8, LANES), F32)
    lane = lane_ids(BLOCK)
    features = D // pairs
    some = pl.ds(pl.multiple_of(step * features, features), features)

    def raws_of(r):
        return dot(normed_ref[r * BLOCK : (r + 1) * BLOCK, :], wcat_ref[...])

    coming = raws_of(0)
    for r in range(blocks):
        rows = slice(r * BLOCK, (r + 1) * BLOCK)
        raws = coming
        if r + 1 < blocks:
            coming = raws_of(r + 1)
        raw_ref[rows, :] = raws.astype(BF16)
        nt_ref[some, rows] = normed_ref[rows, some].T
        mixed = []
        this, after = r % 2, (r + 1) % 2
        for j in range(3):
            raw = raws[:, j * LANES : (j + 1) * LANES]
            shift_ref[this, j, 8 : 8 + BLOCK, :] = raw
            one = shift_ref[this, j, 7 : 7 + BLOCK, :]
            two = shift_ref[this, j, 6 : 6 + BLOCK, :]
            value = taps_ref[j, 0:1, :] * raw + taps_ref[j, 1:2, :] * one + taps_ref[j, 2:3, :] * two
            mixed.append(value * SCALE if j == 0 else value)
            shift_ref[after, j, 0:8, :] = raw[BLOCK - 8 :, :]
        for ref, value in zip((q_ref, k_ref, v_ref), mixed):
            ref[rows, :] = value.astype(BF16)
        row = lax.broadcasted_iota(jnp.int32, (BLOCK, 1), 0) + r * BLOCK
        key_bias = jnp.where(row < len_ref[0], 0.0, NEGATIVE)
        for e in range(2):
            mine = (lane // HEAD_DIM) == e
            other = HEAD_DIM * (1 - e)
            qa_ref[e, rows, :] = jnp.where(mine, mixed[0], jnp.where(lane == other, 1.0, 0.0)).astype(BF16)
            ka_ref[e, rows, :] = jnp.where(mine, mixed[1], jnp.where(lane == other, key_bias, 0.0)).astype(BF16)
            va_ref[e, rows, :] = jnp.where(mine, mixed[2], jnp.where(lane == other, 1.0, 0.0)).astype(BF16)

    @pl.when(step > 0)
    def _():
        for i in range(blocks):
            terms_copy(step - 1, i).wait()

    causal = lax.broadcasted_iota(jnp.int32, (BLOCK, BLOCK), 1) <= lax.broadcasted_iota(
        jnp.int32, (BLOCK, BLOCK), 0
    )
    tasks = [(i, e) for i in range(blocks) for e in range(2)]

    def scores_of(i, e):
        rows = slice(i * BLOCK, (i + 1) * BLOCK)
        query = qa_ref[e, rows, :]
        diagonal = jnp.where(causal, dot_nt(query, ka_ref[e, rows, :]), NEGATIVE)
        before = dot_nt(query, ka_ref[e, : i * BLOCK, :]) if i else None
        return diagonal, before

    coming = scores_of(*tasks[0])
    outs = []
    for t, (i, e) in enumerate(tasks):
        diagonal, before = coming
        if t + 1 < len(tasks):
            coming = scores_of(*tasks[t + 1])
        rows = slice(i * BLOCK, (i + 1) * BLOCK)
        other = HEAD_DIM * (1 - e)
        row_max = jnp.max(diagonal, axis=1, keepdims=True)
        if i:
            row_max = jnp.maximum(row_max, jnp.max(before, axis=1, keepdims=True))
        terms = jnp.exp(diagonal - row_max).astype(BF16)
        terms_ref[e, rows, rows] = terms
        out = dot(terms, va_ref[e, rows, :])
        if i:
            terms = jnp.exp(before - row_max).astype(BF16)
            terms_ref[e, rows, : i * BLOCK] = terms
            out += dot(terms, va_ref[e, : i * BLOCK, :])
        inverse = 1.0 / out[:, other : other + 1]
        outs.append((out, inverse))
        if e == 1:
            first_head = lane < HEAD_DIM
            inverse = jnp.where(first_head, outs[0][1], outs[1][1])
            att_ref[rows, :] = (jnp.where(first_head, outs[0][0], outs[1][0]) * inverse).astype(BF16)
            rinv_ref[rows, :] = inverse
            outs = []
            terms_copy(step, i).start()

    for p in range(pairs):
        @pl.when(step == p)
        def _():
            give_ref[p] = att_ref[rows_of(partner, half), :]
            att_copy(p).start()
            nt_store(p).start()

    @pl.when(step == pairs - 1)
    def _():
        for p in range(pairs):
            att_copy(p).wait()
            nt_store(p).wait()
        emb_store().wait()
        for k in range(3):
            weight_copy(k).wait()
        for i in range(blocks):
            terms_copy(step, i).wait()


def plan_sums(entries, ready, points, tail, inner_bits, line_steps, orders, rate=0.05, hop=1.8):
    stages = inner_bits + line_steps + 1
    done, arrive, free, plan, begun = [0] * len(entries), {}, {}, {}, set()

    def step_of(n, now):
        chunk, size, kind = entries[n]
        stage = done[n]
        if stage < inner_bits:
            link, part = ("bit", orders[kind][stage]), size / 2 ** (stage + 1)
        else:
            t = stage - inner_bits
            link, part = ("in" if t <= line_steps // 2 else "out",), size / 2**inner_bits
        if stage < stages - 1:
            free[link] = max(free.get(link, 0.0), now) + part / rate
            arrive[n] = free[link] + hop
        done[n] += 1

    at, now, late = 0, 0.0, 0
    while at < len(points) or any(d < stages for d in done):
        if at < len(points):
            place, when = points[at]
            now, slack = max(now, when), 0.3 if place[0] != "tail" else 0.0
        else:
            place, slack = ("tail", tail + late), 0.0
            late += 1
            now = max(now, min(arrive[n] for n in range(len(entries)) if done[n] < stages))
        at += 1
        for n, (chunk, _, _) in enumerate(entries):
            if ready[chunk] == place:
                begun.add(n)
        while True:
            able = [n for n in begun if done[n] < stages and (done[n] == 0 or arrive[n] <= now - slack)]
            if not able:
                break
            n = min(able, key=lambda m: (-done[m], m))
            plan.setdefault(place, []).append((n, done[n]))
            step_of(n, now)
    return plan


def layer_kernel(
    inner_bits, outer,
    len_ref, gain_first_ref, gain_second_ref, bias_second_ref, taps_ref,
    att_oth_hbm, emb_hbm, cot_hbm, wo_own_hbm, wo_oth_hbm,
    we_own_hbm, we_oth_hbm, wr_own_hbm, wr_oth_hbm, wq_hbm, wk_hbm, wv_hbm,
    att_hbm, q_hbm, k_hbm, v_hbm, raw_hbm, rinv_hbm, nt_hbm, terms_hbm,
    sum_ref, small_ref, act_hbm, gin_hbm, sq_hbm,
    gh_ref, g_ref, rz_ref, rc_ref, do_ref, got_ref, got_go, got_first, acc_ref, got_small, late_ref, got_group, got_outer,
    load_sem, send_sem, recv_sem, small_send, small_recv, core_send, core_recv,
    group_send, group_recv, outer_send, outer_recv, *halves,
):
    half = gh_ref.shape[0]
    slot = 2 * half
    local = att_oth_hbm.shape[1]
    units = we_own_hbm.shape[1]
    steps = units // D
    width = sum_ref.shape[2]
    split = D // width
    pairs = local // LANES
    fed = 2 * steps * split + 1
    blocks = slot // BLOCK
    head = lax.axis_index("head")
    partner = 1 - head
    mine = lax.axis_index("inner")
    line = lax.axis_index("outer")
    centre = outer // 2
    left = line < centre
    depth = jnp.where(left, centre - 1 - line, line - centre)
    inward = jnp.where(left, line + 1, line - 1)
    outward = jnp.where(left, line - 1, line + 1)
    bit = [(mine // (1 << b)) % 2 for b in range(inner_bits)]
    across = [mine + (1 << b) * (1 - 2 * bit[b]) for b in range(inner_bits)]

    def chunk_of(c, kind, k):
        return (2 * c + kind) * split + k

    entries = []
    for c in range(fed + pairs - 1):
        entries += [(c, 0, 2 * LANES, c % 2), (c, 2 * LANES, LANES, 1 - c % 2)]
    entries += [(fed + pairs - 1, j * LANES, LANES, j % 2) for j in range(3)]
    order_of = [tuple((b + first) % inner_bits for b in range(inner_bits)) for first in range(2)]
    line_steps = 2 * centre - 1
    stage_count = inner_bits + line_steps + 1

    def index_of(fixed):
        return tuple(fixed.get(b, slice(None)) for b in reversed(range(inner_bits)))

    def lanes(entry):
        return slice(entry[1], entry[1] + entry[2])

    def halving(n, s):
        c, _, _, kind = entries[n]
        order = order_of[kind]
        fixed = {b: bit[b] for b in order[:s]}
        b = order[s]
        give = g_ref.at[(c,) + index_of({**fixed, b: 1 - bit[b]}) + (slice(None), lanes(entries[n]))]
        land = halves[s].at[(c,) + (slice(None),) * (inner_bits - 1 - s) + (slice(None), lanes(entries[n]))]
        return remote(give, land, send_sem.at[n, s], recv_sem.at[n, s], inner=across[b])

    def add_half(n, s):
        c, _, _, kind = entries[n]
        order = order_of[kind]
        index = (c,) + index_of({b: bit[b] for b in order[: s + 1]}) + (slice(None), lanes(entries[n]))
        land = (c,) + (slice(None),) * (inner_bits - 1 - s) + (slice(None), lanes(entries[n]))
        g_ref[index] = g_ref[index] + halves[s][land]

    def own(n):
        return (entries[n][0],) + tuple(bit[b] for b in reversed(range(inner_bits))) + (slice(None), lanes(entries[n]))

    def flat(n):
        return (entries[n][0], slice(None), lanes(entries[n]))

    def line_sender(t):
        if t < centre - 1:
            return depth == centre - 1 - t
        if t == centre - 1:
            return depth == 0
        return depth == t - centre

    def line_copy(n, t):
        s = inner_bits + t
        sems = (send_sem.at[n, s], recv_sem.at[n, s])
        if t < centre - 1:
            return remote(g_ref.at[own(n)], rz_ref.at[flat(n)], *sems, outer=inward)
        if t == centre - 1:
            return remote(g_ref.at[own(n)], rc_ref.at[flat(n)], *sems, outer=inward)
        return remote(rc_ref.at[flat(n)], rc_ref.at[flat(n)], *sems, outer=outward)

    def line_finish(n, t):
        if t < centre - 1:
            @pl.when(depth == centre - 2 - t)
            def _():
                line_copy(n, t).wait_recv()
                g_ref[own(n)] = g_ref[own(n)] + rz_ref[flat(n)]
        elif t == centre - 1:
            @pl.when(depth == 0)
            def _():
                line_copy(n, t).wait_recv()
                rc_ref[flat(n)] = g_ref[own(n)] + rc_ref[flat(n)]
        else:
            pl.when(depth == t - centre + 1)(lambda: line_copy(n, t).wait_recv())

    def advance(n, stage):
        if 0 < stage <= inner_bits:
            halving(n, stage - 1).wait_recv()
            add_half(n, stage - 1)
        elif stage > inner_bits:
            line_finish(n, stage - inner_bits - 1)
        if stage < inner_bits:
            halving(n, stage).start()
        elif stage < stage_count - 1:
            t = stage - inner_bits
            pl.when(line_sender(t))(lambda: line_copy(n, t).start())
        else:
            sum_ref[flat(n)] = rc_ref[flat(n)]

    def drain(n):
        for s in range(inner_bits):
            halving(n, s).wait_send()
        for t in range(line_steps):
            pl.when(line_sender(t))(lambda t=t: line_copy(n, t).wait_send())

    points = []
    now = 6.0
    for c in range(steps):
        for k, spent in enumerate((2.8, 2.8, 0.3, 2.8, 2.8, 1.5)):
            now += spent
            points.append((("feed", c, k), now))
        now += 1.4
    for k in range(3):
        now += 1.5
        points.append((("norm", k), now))
    for p in range(pairs):
        now += 1.5
        for j in range(0, blocks, 2):
            points.append((("pair", p, j), now))
            now += 10.0 * (2 * (blocks - j) - 1) * 2 / (blocks * (blocks + 1))
        now += 3.5
        points.append((("taps", p), now))
    for k, spent in enumerate((0.0, 2.0, 2.0, 3.0, 3.0, 3.0)):
        now += spent
        points.append((("tail", k), now))
    ready = {}
    for c in range(steps):
        for k in range(split):
            ready[chunk_of(c, 0, k)] = ("feed", c, 2)
            ready[chunk_of(c, 1, k)] = ("feed", c, 5)
    ready[fed - 1] = ("norm", 2)
    for p in range(pairs):
        ready[fed + p] = ("taps", p) if p < pairs - 1 else ("tail", 0)
    plan = plan_sums(
        [(c, 2e-6 * D * wide, kind) for c, _, wide, kind in entries],
        ready, points, 6, inner_bits, line_steps, order_of,
    )

    def tick(place):
        for n, stage in plan.pop(place, ()):
            advance(n, stage)

    def small_copy(k):
        sems = (small_send.at[k], small_recv.at[k])
        if k == 0:
            return remote(acc_ref.at[0], got_small.at[0], *sems, head=partner)
        if k <= inner_bits:
            return remote(acc_ref.at[k], got_small.at[k], *sems, inner=across[k - 1])
        t = k - 1 - inner_bits
        if t <= centre - 1:
            return remote(acc_ref.at[inner_bits + 1], got_small.at[inner_bits + 1 + (t == centre - 1)], *sems, outer=inward)
        last = got_small.at[inner_bits + 2]
        return remote(last, last, *sems, outer=outward)

    def small_step(k):
        if 0 < k <= inner_bits + 1:
            small_copy(k - 1).wait_recv()
            acc_ref[k] = acc_ref[k - 1] + got_small[k - 1]
        elif k > inner_bits + 1:
            t = k - 2 - inner_bits
            if t < centre - 1:
                @pl.when(depth == centre - 2 - t)
                def _():
                    small_copy(k - 1).wait_recv()
                    acc_ref[inner_bits + 1] = acc_ref[inner_bits + 1] + got_small[inner_bits + 1]
            elif t == centre - 1:
                @pl.when(depth == 0)
                def _():
                    small_copy(k - 1).wait_recv()
                    got_small[inner_bits + 2] = acc_ref[inner_bits + 1] + got_small[inner_bits + 2]
            else:
                pl.when(depth == t - centre + 1)(lambda: small_copy(k - 1).wait_recv())
        if k <= inner_bits:
            small_copy(k).start()
        elif k <= inner_bits + line_steps:
            pl.when(line_sender(k - 1 - inner_bits))(lambda: small_copy(k).start())
        else:
            small_ref[...] = got_small[inner_bits + 2]

    small_steps = inner_bits + line_steps + 2

    inner = 1 << inner_bits
    group = 2 * inner
    seat = mine * 2 + head

    def group_place(k, way):
        other = lax.rem(seat + group + way * k, group)
        return other, {"inner": other // 2, "head": lax.rem(other, 2)}

    def outer_place(k, way):
        other = lax.rem(line + outer + way * k, outer)
        return other, {"outer": other}

    def late_copies(places, count, me, src, land, sends, recvs):
        give = [remote(src, land.at[me], sends.at[k], recvs.at[k], **places(k, 1)[1]) for k in range(1, count)]
        take = [
            remote(src, land.at[places(k, -1)[0]], sends.at[k], recvs.at[k], **places(k, 1)[1]) for k in range(1, count)
        ]
        return give, take

    group_give, group_take = late_copies(
        group_place, group, seat, late_ref.at[0], got_group, group_send, group_recv
    )
    outer_give, outer_take = late_copies(outer_place, outer, line, late_ref.at[1], got_outer, outer_send, outer_recv)

    load_count = iter(range(load_sem.shape[0]))

    def load(src, dst):
        return pltpu.make_async_copy(src, dst, load_sem.at[next(load_count)])

    row = lax.broadcasted_iota(jnp.int32, (half, 1), 0) + head * half
    valid = row < len_ref[0]

    def greet_all():
        barrier = pltpu.get_barrier_semaphore()
        places = [group_place(k, 1)[1] for k in range(1, group)] + [outer_place(k, 1)[1] for k in range(1, outer)]
        for place in places:
            pl.semaphore_signal(barrier, inc=1, device_id=place, device_id_type=pl.DeviceIdType.MESH)
        pl.semaphore_wait(barrier, len(places))

    two_rows = half // 2

    def halves_of(step):
        for r in range(2):
            step(r, pl.ds(r * two_rows, two_rows))

    def feed_forward(
        att_ref, wo_ref, we_ref, wr_ref, cot_ref, hid_ref, gn_ref,
        n2_ref, n2t_ref, gl_ref, glt_ref, give_ref, relu_ref, sq_ref,
    ):
        give_att = relu_ref.at[0, :, 0:local]
        give_go = relu_ref.at[1, :, 0:local]
        loads = {}
        for k, (att, wo) in enumerate(((att_hbm.at[rows_of(head, half), :], wo_own_hbm), (att_oth_hbm, wo_oth_hbm))):
            loads["att", k] = load(att, att_ref.at[k])
            loads["wo", k] = load(wo, wo_ref.at[k])
        loads["emb"] = load(emb_hbm, hid_ref)
        loads["cot"] = load(cot_hbm, cot_ref)
        for c in range(steps):
            cols = pl.ds(c * D, D)
            for k, we in ((1, we_oth_hbm), (0, we_own_hbm)):
                loads["we", c, k] = load(we.at[:, cols], we_ref.at[c, k])
            for k, wr in ((1, wr_oth_hbm), (0, wr_own_hbm)):
                loads["wr", c, k] = load(wr.at[cols, :], wr_ref.at[c, k])
        for copy in loads.values():
            copy.start()
        greet_all()
        for key in (("att", 0), ("wo", 0), ("att", 1), ("wo", 1), "emb", "cot"):
            loads[key].wait()
        gain, bias = row_of(gain_second_ref), row_of(bias_second_ref)

        def open_rows(r, rows):
            hidden = hid_ref[rows, :] + dot(att_ref[0, rows, :], wo_ref[0]) + dot(att_ref[1, rows, :], wo_ref[1])
            hid_ref[rows, :] = hidden
            hat, _ = normalise(hidden)
            normed = (hat * gain + bias).astype(BF16)
            n2_ref[rows, :] = normed
            n2t_ref[:, rows] = normed.T
            position = lax.broadcasted_iota(jnp.int32, (two_rows, 1), 0) + head * half + r * two_rows
            grad = jnp.where(position < len_ref[0], cot_ref[rows, :], 0.0)
            cot_ref[rows, :] = grad
            gl_ref[rows, :] = grad.astype(BF16)
            glt_ref[:, rows] = grad.astype(BF16).T

        halves_of(open_rows)
        hid_store = load(hid_ref, act_hbm)
        hid_store.start()

        def grad_copy(c, kind):
            return remote(
                give_ref.at[kind], got_ref.at[c % 2, kind], core_send.at[c, kind], core_recv.at[c, kind], head=partner
            )

        def put_own(c, kind, value):
            for k in range(split):
                part = value[:, k * width : (k + 1) * width].astype(BF16)
                g_ref[chunk_of(c, kind, k)] = part.reshape(g_ref.shape[1:])

        def add_other(c, kind):
            grad_copy(c, kind).wait_recv()
            for k in range(split):
                got = got_ref[c % 2, kind, :, k * width : (k + 1) * width]
                g_ref[chunk_of(c, kind, k)] += got.reshape(g_ref.shape[1:])

        def weight_grad(c, kind, k, left_ref, right):
            grad = dot(left_ref[...], right)
            if k == 1:
                if c:
                    grad_copy(c - 1, kind).wait_send()
                give_ref[kind] = grad.astype(BF16)
                grad_copy(c, kind).start()
            else:
                put_own(c, kind, grad)

        stores = []
        for c in range(steps):
            for k in (1, 0):
                loads["we", c, k].wait()
                relu = jnp.maximum(dot(n2_ref[...], we_ref[c, k]), 0.0)
                relu_ref[k] = relu.astype(BF16)
                sq_ref[c, k] = (relu * relu).astype(BF16)
                stores.append(load(sq_ref.at[c, k], sq_hbm.at[c, k]))
                stores[-1].start()
                weight_grad(c, 0, k, glt_ref, sq_ref[c, k])
                tick(("feed", c, 1 - k))
            add_other(c, 0)
            tick(("feed", c, 2))
            for k in (1, 0):
                loads["wr", c, k].wait()
                back = dot_nt(gl_ref[...], wr_ref[c, k])
                relu_ref[k] = (back * (2.0 * relu_ref[k].astype(F32))).astype(BF16)
                weight_grad(c, 1, k, n2t_ref, relu_ref[k])
                tick(("feed", c, 4 - k))
            for k in (1, 0):
                gn = dot_nt(relu_ref[k], we_ref[c, k])
                if c == 0 and k == 1:
                    gn_ref[...] = gn
                else:
                    gn_ref[...] += gn
                if k == 1:
                    add_other(c, 1)
                    tick(("feed", c, 5))
        acc_ref[0] = jnp.zeros(acc_ref.shape[1:], F32)

        def close_rows(r, rows):
            hat, scale = normalise(hid_ref[rows, :])
            grad_n = gn_ref[rows, :]
            acc_ref[0, 2:3, :] += jnp.sum(grad_n * hat, axis=0, keepdims=True)
            acc_ref[0, 3:4, :] += jnp.sum(grad_n, axis=0, keepdims=True)
            grad_h = cot_ref[rows, :] + norm_back(grad_n, hat, scale, gain)
            gh_ref[rows, :] = grad_h
            low = grad_h.astype(BF16)
            n2_ref[rows, :] = low
            n2t_ref[:, rows] = low.T
            give_att[rows, :] = dot_nt(low, wo_ref[1]).astype(BF16)

        halves_of(close_rows)
        own_rows = rows_of(head, half)
        att_copy = remote(give_att, do_ref.at[own_rows], core_send.at[steps, 0], core_recv.at[steps, 0], head=partner)
        att_copy.start()
        tick(("norm", 0))
        give_go[...] = dot(n2t_ref[...], att_ref[1]).astype(BF16)
        go_copy = remote(give_go, got_go, core_send.at[steps, 1], core_recv.at[steps, 1], head=partner)
        go_copy.start()
        do_ref[own_rows, :] = dot_nt(n2_ref[...], wo_ref[0]).astype(BF16)
        tick(("norm", 1))
        grad_o = dot(n2t_ref[...], att_ref[0]).astype(BF16)
        go_copy.wait()
        g_ref[fed - 1] = (grad_o + got_go[...]).reshape(g_ref.shape[1:])
        tick(("norm", 2))
        for kind in range(2):
            grad_copy(steps - 1, kind).wait_send()
        for copy in [hid_store] + stores:
            copy.wait()
        att_copy.wait()

    pl.run_scoped(
        feed_forward,
        pltpu.VMEM((2, half, local), BF16), pltpu.VMEM((2, local, D), BF16),
        pltpu.VMEM((steps, 2, D, D), BF16), pltpu.VMEM((steps, 2, D, D), BF16),
        pltpu.VMEM((half, D), F32), pltpu.VMEM((half, D), F32), pltpu.VMEM((half, D), F32),
        pltpu.VMEM((half, D), BF16), pltpu.VMEM((D, half), BF16),
        pltpu.VMEM((half, D), BF16), pltpu.VMEM((D, half), BF16),
        pltpu.VMEM((2, D, D), BF16), pltpu.VMEM((2, half, D), BF16), pltpu.VMEM((steps, 2, half, D), BF16),
    )

    def attention(
        all_ref, wcat_ref, nt_ref, mix_ref, late, dot_ref, qt_ref, doa_ref, kz_ref, va_ref, turned_ref,
        att_ref, q_ref, k_ref, v_ref, raw_ref, rinv_ref, terms_ref, pair_sem, terms_sem,
    ):
        def pair_loads(p, place):
            one = pl.ds(pl.multiple_of(p * LANES, LANES), LANES)
            three = pl.ds(pl.multiple_of(p * 3 * LANES, LANES), 3 * LANES)
            return [
                pltpu.make_async_copy(rinv_hbm.at[:, one], rinv_ref.at[place], pair_sem.at[place, 0]),
                pltpu.make_async_copy(att_hbm.at[:, one], att_ref.at[place], pair_sem.at[place, 1]),
                pltpu.make_async_copy(v_hbm.at[:, one], v_ref.at[place], pair_sem.at[place, 2]),
                pltpu.make_async_copy(q_hbm.at[:, one], q_ref.at[place], pair_sem.at[place, 3]),
                pltpu.make_async_copy(k_hbm.at[:, one], k_ref.at[place], pair_sem.at[place, 4]),
                pltpu.make_async_copy(raw_hbm.at[:, three], raw_ref.at[place], pair_sem.at[place, 5]),
            ]

        def terms_load(p, j):
            rows = pl.ds(j * BLOCK, slot - j * BLOCK)
            spot = lax.rem(blocks * p + j, 4)
            return pltpu.make_async_copy(
                terms_hbm.at[pl.ds(2 * p, 2), rows, pl.ds(j * BLOCK, BLOCK)],
                terms_ref.at[spot, :, rows, :],
                terms_sem.at[spot],
            )

        for copy in pair_loads(0, 0):
            copy.start()
        for j in range(2):
            terms_load(0, j).start()
        nt_load = load(nt_hbm, nt_ref)
        nt_load.start()
        for copy in late:
            copy.start()
        mix_ref[:, slot : slot + 8, :] = jnp.zeros((3, 8, LANES), F32)
        lane = lane_ids(slot)

        def at_pair(p, kind, *rest):
            for q in range(pairs):
                if plan.get((kind, q) + rest):
                    pl.when(p == q)(functools.partial(tick, (kind, q) + rest))

        def one_pair(p, _):
            place = lax.rem(p, 2)
            one = pl.ds(pl.multiple_of(p * LANES, LANES), LANES)

            @pl.when(p + 1 < pairs)
            def _():
                for copy in pair_loads(p + 1, 1 - place):
                    copy.start()

            for copy in pair_loads(p, place):
                copy.wait()
            scaled = (do_ref[:, one].astype(F32) * rinv_ref[place]).astype(BF16)
            dot_ref[...] = scaled.T
            qt_ref[...] = q_ref[place].T
            product = scaled.astype(F32) * att_ref[place].astype(F32)
            for e in range(2):
                in_head = (lane // HEAD_DIM) == e
                delta = -jnp.sum(jnp.where(in_head, product, 0.0), axis=1, keepdims=True)
                other = HEAD_DIM * (1 - e)
                ones = jnp.where((lane > other) & (lane < other + 4), 1.0, 0.0)
                doa_ref[e] = with_parts(jnp.where(in_head, scaled.astype(F32), 0.0), lane, other, delta).astype(BF16)
                va_ref[e] = jnp.where(in_head, v_ref[place].astype(F32), ones).astype(BF16)
                kz_ref[e] = jnp.where(in_head, k_ref[place].astype(F32), 0.0).astype(BF16)

            def grads_of(j, e):
                return dot_nt(doa_ref[e, j * BLOCK :, :], va_ref[e, j * BLOCK : (j + 1) * BLOCK, :])

            for j0 in range(0, blocks, 2):
                at_pair(p, "pair", j0)
                for j in (j0, j0 + 1):
                    terms_load(p, j).wait()
                    if j + 2 < blocks:
                        terms_load(p, j + 2).start()
                    else:
                        @pl.when(p + 1 < pairs)
                        def _():
                            terms_load(p + 1, j + 2 - blocks).start()
                tasks = [(j, e) for j in (j0, j0 + 1) for e in range(2)]
                coming = grads_of(*tasks[0])
                for t, (j, e) in enumerate(tasks):
                    back = coming
                    if t + 1 < len(tasks):
                        coming = grads_of(*tasks[t + 1])
                    first = j * BLOCK
                    keys = slice(first, first + BLOCK)
                    mine_rows = slice(e * HEAD_DIM, (e + 1) * HEAD_DIM)
                    terms = terms_ref[lax.rem(blocks * p + j, 4), e, first:, :]
                    grads = (terms.astype(F32) * back).astype(BF16)
                    part = dot(grads, kz_ref[e, keys, :])
                    if j == 0 and e == 0:
                        mix_ref[0, first:slot, :] = part
                    else:
                        mix_ref[0, first:slot, :] += part
                    turned_ref[0, mine_rows, keys] = dot(qt_ref[mine_rows, first:], grads)
                    turned_ref[1, mine_rows, keys] = dot(dot_ref[mine_rows, first:], terms)
            mix_ref[0, 0:slot, :] = mix_ref[0, 0:slot, :] * SCALE
            mix_ref[1, 0:slot, :] = turned_ref[0].T
            mix_ref[2, 0:slot, :] = turned_ref[1].T
            base = pl.multiple_of(p * 3 * LANES, LANES)
            for j in range(3):
                zero = mix_ref[j, 0:slot, :]
                one_on = mix_ref[j, 1 : 1 + slot, :]
                two_on = mix_ref[j, 2 : 2 + slot, :]
                raw = raw_ref[place, :, j * LANES : (j + 1) * LANES].astype(F32)
                cols = pl.ds(pl.multiple_of(head * local + p * LANES, LANES), LANES)
                value = 0.0
                for s, moved in enumerate((zero, one_on, two_on)):
                    total = jnp.sum(moved * raw, axis=0, keepdims=True)
                    acc_ref[0, 4 + 3 * j + s : 5 + 3 * j + s, cols] = total
                    value += taps_ref[j, s : s + 1, one] * moved
                all_ref[:, pl.ds(pl.multiple_of(base + j * LANES, LANES), LANES)] = value.astype(BF16)

            @pl.when(p == 0)
            def _():
                nt_load.wait()

            grads = dot(nt_ref[...], all_ref[:, pl.ds(base, 3 * LANES)]).astype(BF16)
            g_ref[fed + p] = grads.reshape(g_ref.shape[1:])
            at_pair(p, "taps")
            return 0

        lax.fori_loop(0, pairs, one_pair, 0)

    def tail(all_ref, wcat_ref, late, emb_ref, give_first, own_first, hid_ref, sq_ref, wr_ref):
        emb_load = load(emb_hbm, emb_ref)
        emb_load.start()
        tick(("tail", 0))
        hid_load = load(act_hbm, hid_ref)
        hid_load.start()
        ffn_loads = []
        for c in range(steps):
            for k, wr in ((1, wr_oth_hbm), (0, wr_own_hbm)):
                ffn_loads.append(load(sq_hbm.at[c, k], sq_ref.at[c, k]))
                ffn_loads.append(load(wr.at[pl.ds(c * D, D), :], wr_ref.at[c, k]))
        for copy in ffn_loads:
            copy.start()
        small_step(0)
        for copy in late:
            copy.wait()

        def other_rows(r, rows):
            there = pl.ds(pl.multiple_of(partner * half + r * two_rows, two_rows), two_rows)
            give_first[rows, :] = dot_nt(all_ref[there, :], wcat_ref[...]).astype(BF16)

        halves_of(other_rows)
        first_copy = remote(
            give_first, got_first, core_send.at[steps + 1, 0], core_recv.at[steps + 1, 0], head=partner
        )
        first_copy.start()
        tick(("tail", 1))
        small_step(1)

        def own_rows(r, rows):
            here = pl.ds(pl.multiple_of(head * half + r * two_rows, two_rows), two_rows)
            own_first[rows, :] = dot_nt(all_ref[here, :], wcat_ref[...])

        halves_of(own_rows)
        tick(("tail", 2))
        small_step(2)
        emb_load.wait()
        first_copy.wait()
        gain = row_of(gain_first_ref)
        late_ref[0] = jnp.zeros(late_ref.shape[1:], F32)

        def norm_rows(r, rows):
            grad_n = own_first[rows, :] + got_first[rows, :].astype(F32)
            hat, scale = normalise(emb_ref[rows, :])
            late_ref[0, 0:1, :] += jnp.sum(grad_n * hat, axis=0, keepdims=True)
            late_ref[0, 1:2, :] += jnp.sum(grad_n, axis=0, keepdims=True)
            gh_ref[rows, :] = gh_ref[rows, :] + norm_back(grad_n, hat, scale, gain)

        halves_of(norm_rows)
        for copy in group_give:
            copy.start()
        got_group[seat] = late_ref[0]
        gin_store = load(gh_ref, gin_hbm)
        gin_store.start()
        tick(("tail", 3))
        small_step(3)
        hid_load.wait()
        for copy in ffn_loads:
            copy.wait()

        def ffn_rows(first):
            rows = slice(first, first + two_rows)
            total = hid_ref[rows, :]
            for c in range(steps):
                for k in range(2):
                    total += dot(sq_ref[c, k, rows, :], wr_ref[c, k])
            hid_ref[rows, :] = total

        ffn_rows(0)
        tick(("tail", 4))
        for copy in group_take:
            copy.wait_recv()
        total = got_group[0]
        for k in range(1, group):
            total = total + got_group[k]
        late_ref[1] = total
        for copy in outer_give:
            copy.start()
        got_outer[line] = total
        small_step(4)
        ffn_rows(two_rows)
        act_store = load(hid_ref, act_hbm)
        act_store.start()
        tick(("tail", 5))
        small_step(5)
        for copy in outer_take:
            copy.wait_recv()
        total = got_outer[0]
        for k in range(1, outer):
            total = total + got_outer[k]
        now, k = 6, 6
        while plan or k < small_steps:
            tick(("tail", now))
            if k < small_steps:
                small_step(k)
            now, k = now + 1, k + 1
        small_ref[0:2, :] = total[0:2, :]
        gin_store.wait()
        act_store.wait()
        for copy in group_give + outer_give:
            copy.wait_send()

    def backward(all_ref, wcat_ref):
        late = []
        for p in range(pairs):
            for j, w_hbm in enumerate((wq_hbm, wk_hbm, wv_hbm)):
                base = (3 * p + j) * LANES
                late.append(load(w_hbm.at[:, pl.ds(p * LANES, LANES)], wcat_ref.at[:, pl.ds(base, LANES)]))
        pl.run_scoped(
            lambda nt, mix, *rest: attention(all_ref, wcat_ref, nt, mix, late, *rest),
            pltpu.VMEM((D, slot), BF16),
            pltpu.VMEM((3, slot + 8, LANES), F32),
            pltpu.VMEM((LANES, slot), BF16),
            pltpu.VMEM((LANES, slot), BF16),
            pltpu.VMEM((2, slot, LANES), BF16),
            pltpu.VMEM((2, slot, LANES), BF16),
            pltpu.VMEM((2, slot, LANES), BF16),
            pltpu.VMEM((2, LANES, slot), F32),
            pltpu.VMEM((2, slot, LANES), BF16),
            pltpu.VMEM((2, slot, LANES), BF16),
            pltpu.VMEM((2, slot, LANES), BF16),
            pltpu.VMEM((2, slot, LANES), BF16),
            pltpu.VMEM((2, slot, 3 * LANES), BF16),
            pltpu.VMEM((2, slot, LANES), F32),
            pltpu.VMEM((4, 2, slot, BLOCK), BF16),
            pltpu.SemaphoreType.DMA((2, 6)),
            pltpu.SemaphoreType.DMA((4,)),
        )
        pl.run_scoped(
            functools.partial(tail, all_ref, wcat_ref, late),
            pltpu.VMEM((half, D), F32),
            pltpu.VMEM((half, D), BF16),
            pltpu.VMEM((half, D), F32),
            pltpu.VMEM((half, D), F32),
            pltpu.VMEM((steps, 2, half, D), BF16),
            pltpu.VMEM((steps, 2, D, D), BF16),
        )

    pl.run_scoped(backward, pltpu.VMEM((slot, 3 * local), BF16), pltpu.VMEM((D, 3 * local), BF16))
    for n in range(len(entries)):
        drain(n)
    for k in range(inner_bits + 1):
        small_copy(k).wait_send()
    for k in range(inner_bits + 1, inner_bits + 1 + line_steps):
        pl.when(line_sender(k - 1 - inner_bits))(lambda k=k: small_copy(k).wait_send())


def finish_kernel(
    gr_in, ge_in, go_in, qkv_in, act_in, gin_in, small_in,
    act_ref, gin_ref, q_ref, k_ref, v_ref, go_ref, ge_ref, gr_ref, taps_ref, *vec_refs,
):
    act_ref[...] = act_in[...]
    gin_ref[...] = gin_in[...]
    for j, ref in enumerate((q_ref, k_ref, v_ref)):
        ref[...] = qkv_in[0, :, j * LANES : (j + 1) * LANES].astype(F32)
    ge_ref[...] = ge_in[0].astype(F32)
    gr_ref[...] = gr_in[0].astype(F32)

    @pl.when(pl.program_id(0) == 0)
    def _():
        go_ref[...] = go_in[0].astype(F32)
        for j in range(3):
            taps_ref[j] = small_in[4 + 3 * j : 7 + 3 * j, :]
        for k, ref in enumerate(vec_refs):
            ref[...] = small_in[k, :]


def params(vmem, **kw):
    return pltpu.CompilerParams(vmem_limit_bytes=vmem * MIB, **kw)


def body(
    token_ids, lengths, query_weight, key_weight, value_weight, output_weight,
    expand_weight, reduce_weight, dconv_taps, gain_first, bias_first,
    gain_second, bias_second, cotangent,
):
    half = token_ids.shape[1]
    slot = 2 * half
    local = query_weight.shape[1]
    units = expand_weight.shape[1]
    pairs = local // LANES
    outer = lax.axis_size("outer")
    inner = lax.axis_size("inner")
    inner_bits = inner.bit_length() - 1
    rows = D // inner
    width = 3 * LANES

    shape = jax.ShapeDtypeStruct
    smem = pl.BlockSpec(memory_space=pltpu.SMEM)
    anywhere = pl.BlockSpec(memory_space=pl.ANY)
    dma = pltpu.SemaphoreType.DMA
    vec = whole((D,))

    column = pl.BlockSpec((D, LANES), lambda p: (0, p))
    taps_spec = pl.BlockSpec((3, 3, LANES), lambda p: (0, 0, p))
    pair_rows = pl.BlockSpec((slot, LANES), lambda p: (0, p))
    raw_spec = pl.BlockSpec((slot, 3 * LANES), lambda p: (0, p))
    (
        attended, queries, key_rows, value_rows, raw, inverse, embedded, normed_t, att_oth,
        we_oth, wr_oth, wo_oth, terms,
    ) = pl.pallas_call(
        forward_kernel,
        grid=(pairs,),
        in_specs=[smem, whole((1, half)), vec, vec, column, column, column, taps_spec] + [anywhere] * 3,
        out_specs=[pair_rows] * 4 + [raw_spec, pair_rows] + [anywhere] * 7,
        out_shape=[shape((slot, local), BF16)] * 4
        + [shape((slot, 3 * local), BF16), shape((slot, local), F32), shape((half, D), F32), shape((D, slot), BF16)]
        + [shape((half, local), BF16)]
        + [shape(w.shape, BF16) for w in (expand_weight, reduce_weight, output_weight)]
        + [shape((2 * pairs, slot, slot), BF16)],
        scratch_shapes=[
            pltpu.VMEM((half, D), F32),
            pltpu.VMEM((D, slot), BF16),
            pltpu.VMEM((slot, D), BF16),
            pltpu.VMEM((2, 3, BLOCK + 8, LANES), F32),
            pltpu.VMEM((D, 3 * LANES), BF16),
            pltpu.VMEM((2, slot, LANES), BF16),
            pltpu.VMEM((2, slot, LANES), BF16),
            pltpu.VMEM((2, slot, LANES), BF16),
            pltpu.VMEM((2, slot, slot), BF16),
            pltpu.VMEM((pairs, half, LANES), BF16),
            dma((PIECES,)), dma((PIECES,)), dma((pairs,)), dma((pairs,)), dma((3,)), dma((3,)),
            dma((slot // BLOCK,)), dma((1 + pairs,)),
        ],
        compiler_params=params(58, collective_id=0, has_side_effects=True),
        name="attention_forward",
    )(
        lengths, token_ids, gain_first, bias_first,
        query_weight, key_weight, value_weight, dconv_taps, expand_weight, reduce_weight, output_weight,
    )

    steps = units // D
    split = D // width
    fed = 2 * steps * split + 1
    chunks = fed + pairs
    twos = (2,) * inner_bits
    line_stages = inner_bits + outer
    vmem = lambda dims, kind: pltpu.VMEM(dims, kind)
    sums, small, activations, grad_input, _ = pl.pallas_call(
        functools.partial(layer_kernel, inner_bits, outer),
        in_specs=[smem, vec, vec, vec, whole((3, 3, local))] + [anywhere] * 20,
        out_specs=[whole((chunks, rows, width)), whole((16, D)), anywhere, anywhere, anywhere],
        out_shape=[
            shape((chunks, rows, width), BF16), shape((16, D), F32), shape((half, D), F32), shape((half, D), F32),
            shape((steps, 2, half, D), BF16),
        ],
        scratch_shapes=[
            vmem((half, D), F32),
            vmem((chunks,) + twos + (rows, width), BF16),
            vmem((chunks, rows, width), BF16),
            vmem((chunks, rows, width), BF16),
            vmem((slot, local), BF16),
            vmem((2, 2, D, D), BF16),
            vmem((D, local), BF16),
            vmem((half, D), BF16),
            vmem((inner_bits + 2, 16, D), F32),
            vmem((inner_bits + 3, 16, D), F32),
            vmem((2, 8, D), F32),
            vmem((2 * inner, 8, D), F32),
            vmem((outer, 8, D), F32),
            dma((12 + 10 * steps + 3 * pairs,)),
            dma((2 * chunks + 1, line_stages)), dma((2 * chunks + 1, line_stages)),
            dma((line_stages + 1,)), dma((line_stages + 1,)),
            dma((steps + 2, 2)), dma((steps + 2, 2)),
            dma((2 * inner,)), dma((2 * inner,)), dma((outer,)), dma((outer,)),
        ]
        + [vmem((chunks,) + (2,) * (inner_bits - 1 - s) + (rows, width), BF16) for s in range(inner_bits)],
        compiler_params=params(63, collective_id=1, has_side_effects=True),
        name="layer",
    )(
        lengths, gain_first, gain_second, bias_second, dconv_taps,
        att_oth, embedded, cotangent[0], output_weight, wo_oth,
        expand_weight, we_oth, reduce_weight, wr_oth, query_weight, key_weight, value_weight,
        attended, queries, key_rows, value_rows, raw, inverse, normed_t, terms,
    )
    many = steps * split
    part = half // many
    some_rows = pl.BlockSpec((part, D), lambda i: (i, 0))
    pick = lambda index: pl.BlockSpec((1, rows, width), lambda i: (index(i), 0, 0))
    last = lambda i: jnp.minimum(i, pairs - 1)
    chunk_at = lambda i: (i // split) * 2 * split + i % split
    out_pair = pl.BlockSpec((rows, LANES), lambda i: (0, last(i)))
    activations, grad_input, gq, gk, gv, go_sum, ge_sum, gr_sum, tap_sum, *vec_sums = pl.pallas_call(
        finish_kernel,
        grid=(many,),
        in_specs=[
            pick(chunk_at), pick(lambda i: chunk_at(i) + split), pick(lambda i: fed - 1),
            pick(lambda i: fed + last(i)), some_rows, some_rows, whole((16, D)),
        ],
        out_specs=[
            some_rows, some_rows, out_pair, out_pair, out_pair, whole((rows, local)),
            pl.BlockSpec((rows, width), lambda i: (0, i)), pl.BlockSpec((rows, width), lambda i: (0, i)),
            whole((3, 3, D)), vec, vec, vec, vec,
        ],
        out_shape=[shape((half, D), F32)] * 2
        + [shape((rows, local), F32)] * 4
        + [shape((rows, units), F32)] * 2
        + [shape((3, 3, D), F32)]
        + [shape((D,), F32)] * 4,
        compiler_params=params(62),
        name="finish",
    )(sums, sums, sums, sums, activations, grad_input, small)
    return (
        activations[None],
        grad_input[None],
        gq,
        gk,
        gv,
        go_sum.T,
        ge_sum,
        gr_sum.T,
        tap_sum,
        *vec_sums,
    )


def solution(mesh):
    return jax.shard_map(
        body,
        mesh=mesh,
        in_specs=(
            P(("outer", "inner"), "head"),
            P(("outer", "inner")),
            P(None, "head"),
            P(None, "head"),
            P(None, "head"),
            P("head", None),
            P(None, "head"),
            P("head", None),
            P(None, None, "head"),
            P(),
            P(),
            P(),
            P(),
            P(("outer", "inner"), "head", None),
        ),
        out_specs=(
            P(("outer", "inner"), "head", None),
            P(("outer", "inner"), "head", None),
            P("inner", "head"),
            P("inner", "head"),
            P("inner", "head"),
            P("head", "inner"),
            P("inner", "head"),
            P("head", "inner"),
            P(),
            P(),
            P(),
            P(),
            P(),
        ),
        check_vma=False,
    )
```

```python
import functools
import math

import jax
import jax.numpy as jnp
from jax import lax
from jax.experimental import pallas as pl
from jax.experimental.pallas import tpu as pltpu
from jax.sharding import PartitionSpec as P

HEAD_DIM = 64
D = 768
BLOCK = 256
LANES = 128
EPS = 1e-05
MODULUS = 32749
NEGATIVE = -1e30
SCALE = HEAD_DIM ** (-0.5)
F32 = jnp.float32
BF16 = jnp.bfloat16
MIB = 1024 * 1024

SINE = (
    4.442882913726386,
    -7.308248583654593,
    3.606466623722958,
    -0.8474403474577161,
    0.11605422299047748,
    -0.010267162611370253,
    0.0005523348366953617,
)


def dot(a, b):
    return lax.dot_general(a, b, (((1,), (0,)), ((), ())), preferred_element_type=F32)


def dot_nt(a, b):
    return lax.dot_general(a, b, (((1,), (1,)), ((), ())), preferred_element_type=F32)


def whole(shape):
    return pl.BlockSpec(shape, lambda *_: (0,) * len(shape))


def normalise(values):
    centre = values - jnp.mean(values, axis=-1, keepdims=True)
    spread = jnp.mean(centre * centre, axis=-1, keepdims=True)
    scale = lax.rsqrt(spread + EPS)
    return centre * scale, scale


def norm_back(grad, hat, scale, gain):
    q = grad * gain
    mean_q = jnp.mean(q, axis=-1, keepdims=True)
    mean_qh = jnp.mean(q * hat, axis=-1, keepdims=True)
    return scale * (q - mean_q - hat * mean_qh)


def lane_ids(rows):
    return lax.broadcasted_iota(jnp.int32, (rows, LANES), 1)


def split_three(column):
    high = column.astype(BF16).astype(F32)
    rest = column - high
    middle = rest.astype(BF16).astype(F32)
    return high, middle, rest - middle


def with_parts(base, lane, offset, column):
    high, middle, small = split_three(column)
    base = jnp.where(lane == offset + 1, high, base)
    base = jnp.where(lane == offset + 2, middle, base)
    return jnp.where(lane == offset + 3, small, base)


def remote(src, dst, send, recv, **place):
    return pltpu.make_async_remote_copy(
        src_ref=src, dst_ref=dst, send_sem=send, recv_sem=recv,
        device_id=place, device_id_type=pl.DeviceIdType.MESH,
    )


def greet(*places):
    barrier = pltpu.get_barrier_semaphore()
    for place in places:
        pl.semaphore_signal(barrier, inc=1, device_id=place, device_id_type=pl.DeviceIdType.MESH)
    pl.semaphore_wait(barrier, len(places))


def rows_of(which, half):
    return pl.ds(pl.multiple_of(which * half, half), half)


def remainder(product):
    turns = jnp.floor(product.astype(F32) * (1.0 / MODULUS) + 0.5)
    return (product - turns.astype(jnp.int32) * MODULUS).astype(F32)


def embed_rows(tok_ref, gain, bias, emb_ref, normed_ref, base, first):
    tokens = jnp.broadcast_to(tok_ref[:, pl.ds(first, LANES)], (LANES, LANES)).T
    column = lax.broadcasted_iota(jnp.int32, (1, LANES), 1)
    start = remainder(tokens * (column + 1) + column * column)
    stride = remainder(tokens * LANES + column * (2 * LANES))
    parts = []
    for c in range(D // LANES):
        phase = start + (stride * float(c) + float(c * c * LANES * LANES))
        u = (phase - jnp.floor(phase * (1.0 / MODULUS) + 0.5) * float(MODULUS)) * (2.0 / MODULUS)
        z = u * u
        value = jnp.full_like(u, SINE[-1])
        for coefficient in SINE[-2::-1]:
            value = value * z + coefficient
        parts.append(value * u)
    embedded = jnp.concatenate(parts, axis=1)
    emb_ref[pl.ds(first, LANES), :] = embedded
    hat, _ = normalise(embedded)
    rows = pl.ds(pl.multiple_of(base + first, LANES), LANES)
    normed_ref[rows, :] = (hat * gain + bias).astype(BF16)


PIECES = 3


def row_of(ref):
    return ref[...].reshape(1, D)


def forward_kernel(
    len_ref, tok_ref, gain_ref, bias_ref, wq_ref, wk_ref, wv_ref, taps_ref, we_hbm, wr_hbm, wo_hbm,
    att_ref, q_ref, k_ref, v_ref, raw_ref, rinv_ref,
    emb_hbm, nt_hbm, att_oth_hbm, we_oth_hbm, wr_oth_hbm, wo_oth_hbm, terms_hbm,
    emb_ref, nt_ref, normed_ref, shift_ref, wcat_ref, qa_ref, ka_ref, va_ref, terms_ref, give_ref,
    row_send, row_recv, att_send, att_recv, weight_send, weight_recv, terms_sem, store_sem,
):
    slot = att_ref.shape[0]
    half = slot // 2
    blocks = slot // BLOCK
    step = pl.program_id(0)
    pairs = att_oth_hbm.shape[1] // LANES
    head = lax.axis_index("head")
    partner = 1 - head
    piece = half // PIECES

    def row_copy(k):
        rows = pl.ds(pl.multiple_of(head * half + k * piece, piece), piece)
        return remote(normed_ref.at[rows], normed_ref.at[rows], row_send.at[k], row_recv.at[k], head=partner)

    def att_copy(p, i):
        rows = pl.ds(i * BLOCK, BLOCK)
        land = att_oth_hbm.at[rows, pl.ds(pl.multiple_of(p * LANES, LANES), LANES)]
        return remote(give_ref.at[p, rows], land, att_send.at[p, i], att_recv.at[p, i], head=partner)

    def weight_copy(k):
        src, dst = ((wo_hbm, wo_oth_hbm), (we_hbm, we_oth_hbm), (wr_hbm, wr_oth_hbm))[k]
        return remote(src, dst, weight_send.at[k], weight_recv.at[k], head=partner)

    def emb_store():
        return pltpu.make_async_copy(emb_ref, emb_hbm, store_sem.at[0])

    def nt_store(p):
        part = pl.ds(p * (D // pairs), D // pairs)
        return pltpu.make_async_copy(nt_ref.at[part], nt_hbm.at[part], store_sem.at[1 + p])

    def terms_copy(p, i):
        rows, cols = pl.ds(i * BLOCK, BLOCK), pl.ds(0, (i + 1) * BLOCK)
        return pltpu.make_async_copy(
            terms_ref.at[:, rows, cols], terms_hbm.at[pl.ds(2 * p, 2), rows, cols], terms_sem.at[i]
        )

    @pl.when(step == 0)
    def _():
        greet({"head": partner})
        base = head * half
        for k in range(PIECES):
            def embed_step(i, _):
                first = pl.multiple_of(k * piece + i * LANES, LANES)
                embed_rows(tok_ref, row_of(gain_ref), row_of(bias_ref), emb_ref, normed_ref, base, first)
                return 0

            lax.fori_loop(0, piece // LANES, embed_step, 0)
            row_copy(k).start()
        for k in range(3):
            weight_copy(k).start()
        emb_store().start()
        for k in range(PIECES):
            row_copy(k).wait()

    for j, w_ref in enumerate((wq_ref, wk_ref, wv_ref)):
        wcat_ref[:, j * LANES : (j + 1) * LANES] = w_ref[...]
    shift_ref[0, :, 0:8, :] = jnp.zeros((3, 8, LANES), F32)
    lane = lane_ids(BLOCK)
    features = D // pairs
    some = pl.ds(pl.multiple_of(step * features, features), features)

    def raws_of(r):
        return dot(normed_ref[r * BLOCK : (r + 1) * BLOCK, :], wcat_ref[...])

    coming = raws_of(0)
    for r in range(blocks):
        rows = slice(r * BLOCK, (r + 1) * BLOCK)
        raws = coming
        if r + 1 < blocks:
            coming = raws_of(r + 1)
        raw_ref[rows, :] = raws.astype(BF16)
        nt_ref[some, rows] = normed_ref[rows, some].T
        mixed = []
        this, after = r % 2, (r + 1) % 2
        for j in range(3):
            raw = raws[:, j * LANES : (j + 1) * LANES]
            shift_ref[this, j, 8 : 8 + BLOCK, :] = raw
            one = shift_ref[this, j, 7 : 7 + BLOCK, :]
            two = shift_ref[this, j, 6 : 6 + BLOCK, :]
            value = taps_ref[j, 0:1, :] * raw + taps_ref[j, 1:2, :] * one + taps_ref[j, 2:3, :] * two
            mixed.append(value * SCALE if j == 0 else value)
            shift_ref[after, j, 0:8, :] = raw[BLOCK - 8 :, :]
        for ref, value in zip((q_ref, k_ref, v_ref), mixed):
            ref[rows, :] = value.astype(BF16)
        row = lax.broadcasted_iota(jnp.int32, (BLOCK, 1), 0) + r * BLOCK
        key_bias = jnp.where(row < len_ref[0], 0.0, NEGATIVE)
        for e in range(2):
            mine = (lane // HEAD_DIM) == e
            other = HEAD_DIM * (1 - e)
            qa_ref[e, rows, :] = jnp.where(mine, mixed[0], jnp.where(lane == other, 1.0, 0.0)).astype(BF16)
            ka_ref[e, rows, :] = jnp.where(mine, mixed[1], jnp.where(lane == other, key_bias, 0.0)).astype(BF16)
            va_ref[e, rows, :] = jnp.where(mine, mixed[2], jnp.where(lane == other, 1.0, 0.0)).astype(BF16)

    @pl.when(step > 0)
    def _():
        for i in range(blocks):
            terms_copy(step - 1, i).wait()

    causal = lax.broadcasted_iota(jnp.int32, (BLOCK, BLOCK), 1) <= lax.broadcasted_iota(
        jnp.int32, (BLOCK, BLOCK), 0
    )
    tasks = [(i, e) for i in range(blocks) for e in range(2)]

    def scores_of(i, e):
        rows = slice(i * BLOCK, (i + 1) * BLOCK)
        query = qa_ref[e, rows, :]
        diagonal = jnp.where(causal, dot_nt(query, ka_ref[e, rows, :]), NEGATIVE)
        before = dot_nt(query, ka_ref[e, : i * BLOCK, :]) if i else None
        return diagonal, before

    coming = scores_of(*tasks[0])
    outs = []
    for t, (i, e) in enumerate(tasks):
        diagonal, before = coming
        if t + 1 < len(tasks):
            coming = scores_of(*tasks[t + 1])
        rows = slice(i * BLOCK, (i + 1) * BLOCK)
        other = HEAD_DIM * (1 - e)
        row_max = jnp.max(diagonal, axis=1, keepdims=True)
        if i:
            row_max = jnp.maximum(row_max, jnp.max(before, axis=1, keepdims=True))
        terms = jnp.exp(diagonal - row_max).astype(BF16)
        terms_ref[e, rows, rows] = terms
        out = dot(terms, va_ref[e, rows, :])
        if i:
            terms = jnp.exp(before - row_max).astype(BF16)
            terms_ref[e, rows, : i * BLOCK] = terms
            out += dot(terms, va_ref[e, : i * BLOCK, :])
        inverse = 1.0 / out[:, other : other + 1]
        outs.append((out, inverse))
        if e == 1:
            first_head = lane < HEAD_DIM
            inverse = jnp.where(first_head, outs[0][1], outs[1][1])
            attended = (jnp.where(first_head, outs[0][0], outs[1][0]) * inverse).astype(BF16)
            att_ref[rows, :] = attended
            give_ref[step, rows, :] = attended
            att_copy(step, i).start()
            rinv_ref[rows, :] = inverse
            outs = []
            terms_copy(step, i).start()

    for p in range(pairs):
        @pl.when(step == p)
        def _():
            nt_store(p).start()

    @pl.when(step == pairs - 1)
    def _():
        for p in range(pairs):
            for i in range(blocks):
                att_copy(p, i).wait()
            nt_store(p).wait()
        emb_store().wait()
        for k in range(3):
            weight_copy(k).wait()
        for i in range(blocks):
            terms_copy(step, i).wait()


def plan_sums(entries, ready, points, tail, inner_bits, line_steps, orders, rate=0.05, hop=1.8):
    stages = inner_bits + line_steps + 1
    done, arrive, free, plan, begun = [0] * len(entries), {}, {}, {}, set()

    def step_of(n, now):
        chunk, size, kind = entries[n]
        stage = done[n]
        if stage < inner_bits:
            link, part = ("bit", orders[kind][stage]), size / 2 ** (stage + 1)
        else:
            t = stage - inner_bits
            link, part = ("line", t), size / 2**inner_bits
        if stage < stages - 1:
            free[link] = max(free.get(link, 0.0), now) + part / rate
            arrive[n] = free[link] + hop
        done[n] += 1

    at, now, late = 0, 0.0, 0
    while at < len(points) or any(d < stages for d in done):
        if at < len(points):
            place, when = points[at]
            now, slack = max(now, when), 0.3 if place[0] != "tail" else 0.0
        else:
            place, slack = ("tail", tail + late), 0.0
            late += 1
            now = max(now, min(arrive[n] for n in range(len(entries)) if done[n] < stages))
        at += 1
        for n, (chunk, _, _) in enumerate(entries):
            if ready[chunk] == place:
                begun.add(n)
        while True:
            able = [n for n in begun if done[n] < stages and (done[n] == 0 or arrive[n] <= now - slack)]
            if not able:
                break
            n = min(able, key=lambda m: (-done[m], m))
            plan.setdefault(place, []).append((n, done[n]))
            step_of(n, now)
    return plan


def layer_kernel(
    inner_bits, outer,
    len_ref, gain_first_ref, gain_second_ref, bias_second_ref, taps_ref,
    att_oth_hbm, emb_hbm, cot_hbm, wo_own_hbm, wo_oth_hbm,
    we_own_hbm, we_oth_hbm, wr_own_hbm, wr_oth_hbm, wq_hbm, wk_hbm, wv_hbm,
    att_hbm, q_hbm, k_hbm, v_hbm, raw_hbm, rinv_hbm, nt_hbm, terms_hbm,
    sum_ref, small_ref, act_hbm, gin_hbm, sq_hbm,
    gh_ref, g_ref, rz_ref, rc_ref, do_ref, got_ref, got_go, got_first, acc_ref, got_small, late_ref, got_group, got_outer,
    load_sem, send_sem, recv_sem, small_send, small_recv, core_send, core_recv,
    group_send, group_recv, outer_send, outer_recv, *halves,
):
    half = gh_ref.shape[0]
    slot = 2 * half
    local = att_oth_hbm.shape[1]
    units = we_own_hbm.shape[1]
    steps = units // D
    width = sum_ref.shape[2]
    split = D // width
    pairs = local // LANES
    fed = 2 * steps * split + 1
    blocks = slot // BLOCK
    head = lax.axis_index("head")
    partner = 1 - head
    mine = lax.axis_index("inner")
    line = lax.axis_index("outer")
    centre = outer // 2
    left = line < centre
    depth = jnp.where(left, centre - 1 - line, line - centre)
    inward = jnp.where(left, line + 1, line - 1)
    outward = jnp.where(left, line - 1, line + 1)
    bit = [(mine // (1 << b)) % 2 for b in range(inner_bits)]
    across = [mine + (1 << b) * (1 - 2 * bit[b]) for b in range(inner_bits)]

    def chunk_of(c, kind, k):
        return (2 * c + kind) * split + k

    entries = []
    for c in range(fed + pairs - 1):
        entries += [(c, 0, 2 * LANES, c % 2), (c, 2 * LANES, LANES, 1 - c % 2)]
    entries += [(fed + pairs - 1, j * LANES, LANES, j % 2) for j in range(3)]
    order_of = [tuple((b + first) % inner_bits for b in range(inner_bits)) for first in range(2)]
    line_steps = 2 * centre - 1
    stage_count = inner_bits + line_steps + 1

    def index_of(fixed):
        return tuple(fixed.get(b, slice(None)) for b in reversed(range(inner_bits)))

    def lanes(entry):
        return slice(entry[1], entry[1] + entry[2])

    def halving(n, s):
        c, _, _, kind = entries[n]
        order = order_of[kind]
        fixed = {b: bit[b] for b in order[:s]}
        b = order[s]
        give = g_ref.at[(c,) + index_of({**fixed, b: 1 - bit[b]}) + (slice(None), lanes(entries[n]))]
        land = halves[s].at[(c,) + (slice(None),) * (inner_bits - 1 - s) + (slice(None), lanes(entries[n]))]
        return remote(give, land, send_sem.at[n, s], recv_sem.at[n, s], inner=across[b])

    def add_half(n, s):
        c, _, _, kind = entries[n]
        order = order_of[kind]
        index = (c,) + index_of({b: bit[b] for b in order[: s + 1]}) + (slice(None), lanes(entries[n]))
        land = (c,) + (slice(None),) * (inner_bits - 1 - s) + (slice(None), lanes(entries[n]))
        g_ref[index] = g_ref[index] + halves[s][land]

    def own(n):
        return (entries[n][0],) + tuple(bit[b] for b in reversed(range(inner_bits))) + (slice(None), lanes(entries[n]))

    def flat(n):
        return (entries[n][0], slice(None), lanes(entries[n]))

    def line_sender(t):
        if t < centre - 1:
            return depth == centre - 1 - t
        if t == centre - 1:
            return depth == 0
        return depth == t - centre

    def line_copy(n, t):
        s = inner_bits + t
        sems = (send_sem.at[n, s], recv_sem.at[n, s])
        if t < centre - 1:
            return remote(g_ref.at[own(n)], rz_ref.at[flat(n)], *sems, outer=inward)
        if t == centre - 1:
            return remote(g_ref.at[own(n)], rc_ref.at[flat(n)], *sems, outer=inward)
        return remote(rc_ref.at[flat(n)], rc_ref.at[flat(n)], *sems, outer=outward)

    def line_finish(n, t):
        if t < centre - 1:
            @pl.when(depth == centre - 2 - t)
            def _():
                line_copy(n, t).wait_recv()
                g_ref[own(n)] = g_ref[own(n)] + rz_ref[flat(n)]
        elif t == centre - 1:
            @pl.when(depth == 0)
            def _():
                line_copy(n, t).wait_recv()
                rc_ref[flat(n)] = g_ref[own(n)] + rc_ref[flat(n)]
        else:
            pl.when(depth == t - centre + 1)(lambda: line_copy(n, t).wait_recv())

    def advance(n, stage):
        if 0 < stage <= inner_bits:
            halving(n, stage - 1).wait_recv()
            add_half(n, stage - 1)
        elif stage > inner_bits:
            line_finish(n, stage - inner_bits - 1)
        if stage < inner_bits:
            halving(n, stage).start()
        elif stage < stage_count - 1:
            t = stage - inner_bits
            pl.when(line_sender(t))(lambda: line_copy(n, t).start())
        else:
            sum_ref[flat(n)] = rc_ref[flat(n)]

    def drain(n):
        for s in range(inner_bits):
            halving(n, s).wait_send()
        for t in range(line_steps):
            pl.when(line_sender(t))(lambda t=t: line_copy(n, t).wait_send())

    points = []
    now = 6.0
    for c in range(steps):
        for k, spent in enumerate((2.3, 2.3, 0.3, 2.3, 2.3, 1.2)):
            now += spent
            points.append((("feed", c, k), now))
        now += 1.1
    for k in range(3):
        now += 1.2
        points.append((("norm", k), now))
    for p in range(pairs):
        now += 1.2
        for j in range(0, blocks, 2):
            points.append((("pair", p, j), now))
            now += 8.0 * (2 * (blocks - j) - 1) * 2 / (blocks * (blocks + 1))
        now += 2.8
        points.append((("taps", p), now))
    for k, spent in enumerate((0.0, 2.0, 2.0, 3.0, 3.0, 3.0)):
        now += spent
        points.append((("tail", k), now))
    ready = {}
    for c in range(steps):
        for k in range(split):
            ready[chunk_of(c, 0, k)] = ("feed", c, 2)
            ready[chunk_of(c, 1, k)] = ("feed", c, 5)
    ready[fed - 1] = ("norm", 2)
    for p in range(pairs):
        ready[fed + p] = ("taps", p) if p < pairs - 1 else ("tail", 0)
    plan = plan_sums(
        [(c, 2e-6 * D * wide, kind) for c, _, wide, kind in entries],
        ready, points, 6, inner_bits, line_steps, order_of,
    )

    def tick(place):
        for n, stage in plan.pop(place, ()):
            advance(n, stage)

    def small_copy(k):
        sems = (small_send.at[k], small_recv.at[k])
        if k == 0:
            return remote(acc_ref.at[0], got_small.at[0], *sems, head=partner)
        if k <= inner_bits:
            return remote(acc_ref.at[k], got_small.at[k], *sems, inner=across[k - 1])
        t = k - 1 - inner_bits
        if t <= centre - 1:
            return remote(acc_ref.at[inner_bits + 1], got_small.at[inner_bits + 1 + (t == centre - 1)], *sems, outer=inward)
        last = got_small.at[inner_bits + 2]
        return remote(last, last, *sems, outer=outward)

    def small_step(k):
        if 0 < k <= inner_bits + 1:
            small_copy(k - 1).wait_recv()
            acc_ref[k] = acc_ref[k - 1] + got_small[k - 1]
        elif k > inner_bits + 1:
            t = k - 2 - inner_bits
            if t < centre - 1:
                @pl.when(depth == centre - 2 - t)
                def _():
                    small_copy(k - 1).wait_recv()
                    acc_ref[inner_bits + 1] = acc_ref[inner_bits + 1] + got_small[inner_bits + 1]
            elif t == centre - 1:
                @pl.when(depth == 0)
                def _():
                    small_copy(k - 1).wait_recv()
                    got_small[inner_bits + 2] = acc_ref[inner_bits + 1] + got_small[inner_bits + 2]
            else:
                pl.when(depth == t - centre + 1)(lambda: small_copy(k - 1).wait_recv())
        if k <= inner_bits:
            small_copy(k).start()
        elif k <= inner_bits + line_steps:
            pl.when(line_sender(k - 1 - inner_bits))(lambda: small_copy(k).start())
        else:
            small_ref[...] = got_small[inner_bits + 2]

    small_steps = inner_bits + line_steps + 2

    inner = 1 << inner_bits
    group = 2 * inner
    seat = mine * 2 + head

    def group_place(k, way):
        other = lax.rem(seat + group + way * k, group)
        return other, {"inner": other // 2, "head": lax.rem(other, 2)}

    def outer_place(k, way):
        other = lax.rem(line + outer + way * k, outer)
        return other, {"outer": other}

    def late_copies(places, count, me, src, land, sends, recvs):
        give = [remote(src, land.at[me], sends.at[k], recvs.at[k], **places(k, 1)[1]) for k in range(1, count)]
        take = [
            remote(src, land.at[places(k, -1)[0]], sends.at[k], recvs.at[k], **places(k, 1)[1]) for k in range(1, count)
        ]
        return give, take

    group_give, group_take = late_copies(
        group_place, group, seat, late_ref.at[0], got_group, group_send, group_recv
    )
    outer_give, outer_take = late_copies(outer_place, outer, line, late_ref.at[1], got_outer, outer_send, outer_recv)

    load_count = iter(range(load_sem.shape[0]))

    def load(src, dst):
        return pltpu.make_async_copy(src, dst, load_sem.at[next(load_count)])

    row = lax.broadcasted_iota(jnp.int32, (half, 1), 0) + head * half
    valid = row < len_ref[0]

    def greet_all():
        barrier = pltpu.get_barrier_semaphore()
        places = [group_place(k, 1)[1] for k in range(1, group)] + [outer_place(k, 1)[1] for k in range(1, outer)]
        for place in places:
            pl.semaphore_signal(barrier, inc=1, device_id=place, device_id_type=pl.DeviceIdType.MESH)
        pl.semaphore_wait(barrier, len(places))

    two_rows = half // 2

    def halves_of(step):
        for r in range(2):
            step(r, pl.ds(r * two_rows, two_rows))

    def feed_forward(
        att_ref, wo_ref, we_ref, wr_ref, cot_ref, hid_ref, gn_ref,
        n2_ref, n2t_ref, gl_ref, glt_ref, give_ref, relu_ref, sq_ref,
    ):
        give_att = relu_ref.at[0, :, 0:local]
        give_go = relu_ref.at[1, :, 0:local]
        loads = {}
        for k, (att, wo) in enumerate(((att_hbm.at[rows_of(head, half), :], wo_own_hbm), (att_oth_hbm.at[rows_of(head, half), :], wo_oth_hbm))):
            loads["att", k] = load(att, att_ref.at[k])
            loads["wo", k] = load(wo, wo_ref.at[k])
        loads["emb"] = load(emb_hbm, hid_ref)
        loads["cot"] = load(cot_hbm, cot_ref)
        for c in range(steps):
            cols = pl.ds(c * D, D)
            for k, we in ((1, we_oth_hbm), (0, we_own_hbm)):
                loads["we", c, k] = load(we.at[:, cols], we_ref.at[c, k])
            for k, wr in ((1, wr_oth_hbm), (0, wr_own_hbm)):
                loads["wr", c, k] = load(wr.at[cols, :], wr_ref.at[c, k])
        weights = {c: [copy for key, copy in loads.items() if key[0] in ("we", "wr") and key[1] == c] for c in range(steps)}
        for key, copy in loads.items():
            if key[0] not in ("we", "wr"):
                copy.start()
        greet_all()
        for key in (("att", 0), ("wo", 0), ("att", 1), ("wo", 1), "emb", "cot"):
            loads[key].wait()
        for copy in weights[0]:
            copy.start()
        gain, bias = row_of(gain_second_ref), row_of(bias_second_ref)

        def open_rows(r, rows):
            hidden = hid_ref[rows, :] + dot(att_ref[0, rows, :], wo_ref[0]) + dot(att_ref[1, rows, :], wo_ref[1])
            hid_ref[rows, :] = hidden
            hat, _ = normalise(hidden)
            normed = (hat * gain + bias).astype(BF16)
            n2_ref[rows, :] = normed
            n2t_ref[:, rows] = normed.T
            position = lax.broadcasted_iota(jnp.int32, (two_rows, 1), 0) + head * half + r * two_rows
            grad = jnp.where(position < len_ref[0], cot_ref[rows, :], 0.0)
            cot_ref[rows, :] = grad
            gl_ref[rows, :] = grad.astype(BF16)
            glt_ref[:, rows] = grad.astype(BF16).T

        halves_of(open_rows)
        hid_store = load(hid_ref, act_hbm)
        hid_store.start()

        def grad_copy(c, kind):
            return remote(
                give_ref.at[kind], got_ref.at[c % 2, kind], core_send.at[c, kind], core_recv.at[c, kind], head=partner
            )

        def put_own(c, kind, value):
            for k in range(split):
                part = value[:, k * width : (k + 1) * width].astype(BF16)
                g_ref[chunk_of(c, kind, k)] = part.reshape(g_ref.shape[1:])

        def add_other(c, kind):
            grad_copy(c, kind).wait_recv()
            for k in range(split):
                got = got_ref[c % 2, kind, :, k * width : (k + 1) * width]
                g_ref[chunk_of(c, kind, k)] += got.reshape(g_ref.shape[1:])

        def weight_grad(c, kind, k, left_ref, right):
            grad = dot(left_ref[...], right)
            if k == 1:
                if c:
                    grad_copy(c - 1, kind).wait_send()
                give_ref[kind] = grad.astype(BF16)
                grad_copy(c, kind).start()
            else:
                put_own(c, kind, grad)

        stores = []
        for c in range(steps):
            for k in (1, 0):
                loads["we", c, k].wait()
                relu = jnp.maximum(dot(n2_ref[...], we_ref[c, k]), 0.0)
                relu_ref[k] = relu.astype(BF16)
                sq_ref[c, k] = (relu * relu).astype(BF16)
                stores.append(load(sq_ref.at[c, k], sq_hbm.at[c, k]))
                stores[-1].start()
                weight_grad(c, 0, k, glt_ref, sq_ref[c, k])
                tick(("feed", c, 1 - k))
            if c + 1 < steps:
                for copy in weights[c + 1]:
                    copy.start()
            add_other(c, 0)
            tick(("feed", c, 2))
            for k in (1, 0):
                loads["wr", c, k].wait()
                back = dot_nt(gl_ref[...], wr_ref[c, k])
                relu_ref[k] = (back * (2.0 * relu_ref[k].astype(F32))).astype(BF16)
                weight_grad(c, 1, k, n2t_ref, relu_ref[k])
                tick(("feed", c, 4 - k))
            for k in (1, 0):
                gn = dot_nt(relu_ref[k], we_ref[c, k])
                if c == 0 and k == 1:
                    gn_ref[...] = gn
                else:
                    gn_ref[...] += gn
                if k == 1:
                    add_other(c, 1)
                    tick(("feed", c, 5))
        acc_ref[0] = jnp.zeros(acc_ref.shape[1:], F32)

        def close_rows(r, rows):
            hat, scale = normalise(hid_ref[rows, :])
            grad_n = gn_ref[rows, :]
            acc_ref[0, 2:3, :] += jnp.sum(grad_n * hat, axis=0, keepdims=True)
            acc_ref[0, 3:4, :] += jnp.sum(grad_n, axis=0, keepdims=True)
            grad_h = cot_ref[rows, :] + norm_back(grad_n, hat, scale, gain)
            gh_ref[rows, :] = grad_h
            low = grad_h.astype(BF16)
            n2_ref[rows, :] = low
            n2t_ref[:, rows] = low.T
            give_att[rows, :] = dot_nt(low, wo_ref[1]).astype(BF16)

        halves_of(close_rows)
        own_rows = rows_of(head, half)
        att_copy = remote(give_att, do_ref.at[own_rows], core_send.at[steps, 0], core_recv.at[steps, 0], head=partner)
        att_copy.start()
        tick(("norm", 0))
        give_go[...] = dot(n2t_ref[...], att_ref[1]).astype(BF16)
        go_copy = remote(give_go, got_go, core_send.at[steps, 1], core_recv.at[steps, 1], head=partner)
        go_copy.start()
        do_ref[own_rows, :] = dot_nt(n2_ref[...], wo_ref[0]).astype(BF16)
        tick(("norm", 1))
        grad_o = dot(n2t_ref[...], att_ref[0]).astype(BF16)
        go_copy.wait()
        g_ref[fed - 1] = (grad_o + got_go[...]).reshape(g_ref.shape[1:])
        tick(("norm", 2))
        for kind in range(2):
            grad_copy(steps - 1, kind).wait_send()
        for copy in [hid_store] + stores:
            copy.wait()
        att_copy.wait()

    pl.run_scoped(
        feed_forward,
        pltpu.VMEM((2, half, local), BF16), pltpu.VMEM((2, local, D), BF16),
        pltpu.VMEM((steps, 2, D, D), BF16), pltpu.VMEM((steps, 2, D, D), BF16),
        pltpu.VMEM((half, D), F32), pltpu.VMEM((half, D), F32), pltpu.VMEM((half, D), F32),
        pltpu.VMEM((half, D), BF16), pltpu.VMEM((D, half), BF16),
        pltpu.VMEM((half, D), BF16), pltpu.VMEM((D, half), BF16),
        pltpu.VMEM((2, D, D), BF16), pltpu.VMEM((2, half, D), BF16), pltpu.VMEM((steps, 2, half, D), BF16),
    )

    def attention(
        all_ref, wcat_ref, nt_ref, mix_ref, late, dot_ref, qt_ref, doa_ref, kz_ref, va_ref, turned_ref,
        att_ref, q_ref, k_ref, v_ref, raw_ref, rinv_ref, terms_ref, pair_sem, terms_sem,
    ):
        def pair_loads(p, place):
            one = pl.ds(pl.multiple_of(p * LANES, LANES), LANES)
            three = pl.ds(pl.multiple_of(p * 3 * LANES, LANES), 3 * LANES)
            return [
                pltpu.make_async_copy(rinv_hbm.at[:, one], rinv_ref.at[place], pair_sem.at[place, 0]),
                pltpu.make_async_copy(att_hbm.at[:, one], att_ref.at[place], pair_sem.at[place, 1]),
                pltpu.make_async_copy(v_hbm.at[:, one], v_ref.at[place], pair_sem.at[place, 2]),
                pltpu.make_async_copy(q_hbm.at[:, one], q_ref.at[place], pair_sem.at[place, 3]),
                pltpu.make_async_copy(k_hbm.at[:, one], k_ref.at[place], pair_sem.at[place, 4]),
                pltpu.make_async_copy(raw_hbm.at[:, three], raw_ref.at[place], pair_sem.at[place, 5]),
            ]

        def terms_load(p, j):
            rows = pl.ds(j * BLOCK, slot - j * BLOCK)
            spot = lax.rem(blocks * p + j, 4)
            return pltpu.make_async_copy(
                terms_hbm.at[pl.ds(2 * p, 2), rows, pl.ds(j * BLOCK, BLOCK)],
                terms_ref.at[spot, :, rows, :],
                terms_sem.at[spot],
            )

        for copy in pair_loads(0, 0):
            copy.start()
        for j in range(2):
            terms_load(0, j).start()
        nt_load = load(nt_hbm, nt_ref)
        nt_load.start()
        for copy in late:
            copy.start()
        mix_ref[:, slot : slot + 8, :] = jnp.zeros((3, 8, LANES), F32)
        lane = lane_ids(slot)

        def at_pair(p, kind, *rest):
            for q in range(pairs):
                if plan.get((kind, q) + rest):
                    pl.when(p == q)(functools.partial(tick, (kind, q) + rest))

        def one_pair(p, _):
            place = lax.rem(p, 2)
            one = pl.ds(pl.multiple_of(p * LANES, LANES), LANES)

            @pl.when(p + 1 < pairs)
            def _():
                for copy in pair_loads(p + 1, 1 - place):
                    copy.start()

            for copy in pair_loads(p, place):
                copy.wait()
            scaled = (do_ref[:, one].astype(F32) * rinv_ref[place]).astype(BF16)
            dot_ref[...] = scaled.T
            qt_ref[...] = q_ref[place].T
            product = scaled.astype(F32) * att_ref[place].astype(F32)
            for e in range(2):
                in_head = (lane // HEAD_DIM) == e
                delta = -jnp.sum(jnp.where(in_head, product, 0.0), axis=1, keepdims=True)
                other = HEAD_DIM * (1 - e)
                ones = jnp.where((lane > other) & (lane < other + 4), 1.0, 0.0)
                doa_ref[e] = with_parts(jnp.where(in_head, scaled.astype(F32), 0.0), lane, other, delta).astype(BF16)
                va_ref[e] = jnp.where(in_head, v_ref[place].astype(F32), ones).astype(BF16)
                kz_ref[e] = jnp.where(in_head, k_ref[place].astype(F32), 0.0).astype(BF16)

            def grads_of(j, e):
                return dot_nt(doa_ref[e, j * BLOCK :, :], va_ref[e, j * BLOCK : (j + 1) * BLOCK, :])

            for j0 in range(0, blocks, 2):
                at_pair(p, "pair", j0)
                for j in (j0, j0 + 1):
                    terms_load(p, j).wait()
                    if j + 2 < blocks:
                        terms_load(p, j + 2).start()
                    else:
                        @pl.when(p + 1 < pairs)
                        def _():
                            terms_load(p + 1, j + 2 - blocks).start()
                tasks = [(j, e) for j in (j0, j0 + 1) for e in range(2)]
                coming = grads_of(*tasks[0])
                for t, (j, e) in enumerate(tasks):
                    back = coming
                    if t + 1 < len(tasks):
                        coming = grads_of(*tasks[t + 1])
                    first = j * BLOCK
                    keys = slice(first, first + BLOCK)
                    mine_rows = slice(e * HEAD_DIM, (e + 1) * HEAD_DIM)
                    terms = terms_ref[lax.rem(blocks * p + j, 4), e, first:, :]
                    grads = (terms.astype(F32) * back).astype(BF16)
                    part = dot(grads, kz_ref[e, keys, :])
                    if j == 0 and e == 0:
                        mix_ref[0, first:slot, :] = part
                    else:
                        mix_ref[0, first:slot, :] += part
                    turned_ref[0, mine_rows, keys] = dot(qt_ref[mine_rows, first:], grads)
                    turned_ref[1, mine_rows, keys] = dot(dot_ref[mine_rows, first:], terms)
            mix_ref[0, 0:slot, :] = mix_ref[0, 0:slot, :] * SCALE
            mix_ref[1, 0:slot, :] = turned_ref[0].T
            mix_ref[2, 0:slot, :] = turned_ref[1].T
            base = pl.multiple_of(p * 3 * LANES, LANES)
            for j in range(3):
                zero = mix_ref[j, 0:slot, :]
                one_on = mix_ref[j, 1 : 1 + slot, :]
                two_on = mix_ref[j, 2 : 2 + slot, :]
                raw = raw_ref[place, :, j * LANES : (j + 1) * LANES].astype(F32)
                cols = pl.ds(pl.multiple_of(head * local + p * LANES, LANES), LANES)
                value = 0.0
                for s, moved in enumerate((zero, one_on, two_on)):
                    total = jnp.sum(moved * raw, axis=0, keepdims=True)
                    acc_ref[0, 4 + 3 * j + s : 5 + 3 * j + s, cols] = total
                    value += taps_ref[j, s : s + 1, one] * moved
                all_ref[:, pl.ds(pl.multiple_of(base + j * LANES, LANES), LANES)] = value.astype(BF16)

            @pl.when(p == 0)
            def _():
                nt_load.wait()

            grads = dot(nt_ref[...], all_ref[:, pl.ds(base, 3 * LANES)]).astype(BF16)
            g_ref[fed + p] = grads.reshape(g_ref.shape[1:])
            at_pair(p, "taps")
            return 0

        lax.fori_loop(0, pairs, one_pair, 0)

    def tail(all_ref, wcat_ref, late, emb_ref, give_first, own_first, hid_ref, sq_ref, wr_ref):
        emb_load = load(emb_hbm, emb_ref)
        emb_load.start()
        tick(("tail", 0))
        hid_load = load(act_hbm, hid_ref)
        hid_load.start()
        ffn_loads = []
        for c in range(steps):
            for k, wr in ((1, wr_oth_hbm), (0, wr_own_hbm)):
                ffn_loads.append(load(sq_hbm.at[c, k], sq_ref.at[c, k]))
                ffn_loads.append(load(wr.at[pl.ds(c * D, D), :], wr_ref.at[c, k]))
        for copy in ffn_loads:
            copy.start()
        small_step(0)
        for copy in late:
            copy.wait()

        def other_rows(r, rows):
            there = pl.ds(pl.multiple_of(partner * half + r * two_rows, two_rows), two_rows)
            give_first[rows, :] = dot_nt(all_ref[there, :], wcat_ref[...]).astype(BF16)

        halves_of(other_rows)
        first_copy = remote(
            give_first, got_first, core_send.at[steps + 1, 0], core_recv.at[steps + 1, 0], head=partner
        )
        first_copy.start()
        tick(("tail", 1))
        small_step(1)

        def own_rows(r, rows):
            here = pl.ds(pl.multiple_of(head * half + r * two_rows, two_rows), two_rows)
            own_first[rows, :] = dot_nt(all_ref[here, :], wcat_ref[...])

        halves_of(own_rows)
        tick(("tail", 2))
        small_step(2)
        emb_load.wait()
        first_copy.wait()
        gain = row_of(gain_first_ref)
        late_ref[0] = jnp.zeros(late_ref.shape[1:], F32)

        def norm_rows(r, rows):
            grad_n = own_first[rows, :] + got_first[rows, :].astype(F32)
            hat, scale = normalise(emb_ref[rows, :])
            late_ref[0, 0:1, :] += jnp.sum(grad_n * hat, axis=0, keepdims=True)
            late_ref[0, 1:2, :] += jnp.sum(grad_n, axis=0, keepdims=True)
            gh_ref[rows, :] = gh_ref[rows, :] + norm_back(grad_n, hat, scale, gain)

        halves_of(norm_rows)
        for copy in group_give:
            copy.start()
        got_group[seat] = late_ref[0]
        gin_store = load(gh_ref, gin_hbm)
        gin_store.start()
        tick(("tail", 3))
        small_step(3)
        hid_load.wait()
        for copy in ffn_loads:
            copy.wait()

        def ffn_rows(first):
            rows = slice(first, first + two_rows)
            total = hid_ref[rows, :]
            for c in range(steps):
                for k in range(2):
                    total += dot(sq_ref[c, k, rows, :], wr_ref[c, k])
            hid_ref[rows, :] = total

        ffn_rows(0)
        tick(("tail", 4))
        for copy in group_take:
            copy.wait_recv()
        total = got_group[0]
        for k in range(1, group):
            total = total + got_group[k]
        late_ref[1] = total
        for copy in outer_give:
            copy.start()
        got_outer[line] = total
        small_step(4)
        ffn_rows(two_rows)
        act_store = load(hid_ref, act_hbm)
        act_store.start()
        tick(("tail", 5))
        small_step(5)
        for copy in outer_take:
            copy.wait_recv()
        total = got_outer[0]
        for k in range(1, outer):
            total = total + got_outer[k]
        now, k = 6, 6
        while plan or k < small_steps:
            tick(("tail", now))
            if k < small_steps:
                small_step(k)
            now, k = now + 1, k + 1
        small_ref[0:2, :] = total[0:2, :]
        gin_store.wait()
        act_store.wait()
        for copy in group_give + outer_give:
            copy.wait_send()

    def backward(all_ref, wcat_ref):
        late = []
        for p in range(pairs):
            for j, w_hbm in enumerate((wq_hbm, wk_hbm, wv_hbm)):
                base = (3 * p + j) * LANES
                late.append(load(w_hbm.at[:, pl.ds(p * LANES, LANES)], wcat_ref.at[:, pl.ds(base, LANES)]))
        pl.run_scoped(
            lambda nt, mix, *rest: attention(all_ref, wcat_ref, nt, mix, late, *rest),
            pltpu.VMEM((D, slot), BF16),
            pltpu.VMEM((3, slot + 8, LANES), F32),
            pltpu.VMEM((LANES, slot), BF16),
            pltpu.VMEM((LANES, slot), BF16),
            pltpu.VMEM((2, slot, LANES), BF16),
            pltpu.VMEM((2, slot, LANES), BF16),
            pltpu.VMEM((2, slot, LANES), BF16),
            pltpu.VMEM((2, LANES, slot), F32),
            pltpu.VMEM((2, slot, LANES), BF16),
            pltpu.VMEM((2, slot, LANES), BF16),
            pltpu.VMEM((2, slot, LANES), BF16),
            pltpu.VMEM((2, slot, LANES), BF16),
            pltpu.VMEM((2, slot, 3 * LANES), BF16),
            pltpu.VMEM((2, slot, LANES), F32),
            pltpu.VMEM((4, 2, slot, BLOCK), BF16),
            pltpu.SemaphoreType.DMA((2, 6)),
            pltpu.SemaphoreType.DMA((4,)),
        )
        pl.run_scoped(
            functools.partial(tail, all_ref, wcat_ref, late),
            pltpu.VMEM((half, D), F32),
            pltpu.VMEM((half, D), BF16),
            pltpu.VMEM((half, D), F32),
            pltpu.VMEM((half, D), F32),
            pltpu.VMEM((steps, 2, half, D), BF16),
            pltpu.VMEM((steps, 2, D, D), BF16),
        )

    pl.run_scoped(backward, pltpu.VMEM((slot, 3 * local), BF16), pltpu.VMEM((D, 3 * local), BF16))
    for n in range(len(entries)):
        drain(n)
    for k in range(inner_bits + 1):
        small_copy(k).wait_send()
    for k in range(inner_bits + 1, inner_bits + 1 + line_steps):
        pl.when(line_sender(k - 1 - inner_bits))(lambda k=k: small_copy(k).wait_send())


def finish_kernel(
    gr_in, ge_in, go_in, qkv_in, act_in, gin_in, small_in,
    act_ref, gin_ref, q_ref, k_ref, v_ref, go_ref, ge_ref, gr_ref, taps_ref, *vec_refs,
):
    act_ref[...] = act_in[...]
    gin_ref[...] = gin_in[...]
    for j, ref in enumerate((q_ref, k_ref, v_ref)):
        ref[...] = qkv_in[0, :, j * LANES : (j + 1) * LANES].astype(F32)
    ge_ref[...] = ge_in[0].astype(F32)
    gr_ref[...] = gr_in[0].astype(F32)

    @pl.when(pl.program_id(0) == 0)
    def _():
        go_ref[...] = go_in[0].astype(F32)
        for j in range(3):
            taps_ref[j] = small_in[4 + 3 * j : 7 + 3 * j, :]
        for k, ref in enumerate(vec_refs):
            ref[...] = small_in[k, :]


def params(vmem, **kw):
    return pltpu.CompilerParams(vmem_limit_bytes=vmem * MIB, **kw)


def body(
    token_ids, lengths, query_weight, key_weight, value_weight, output_weight,
    expand_weight, reduce_weight, dconv_taps, gain_first, bias_first,
    gain_second, bias_second, cotangent,
):
    half = token_ids.shape[1]
    slot = 2 * half
    local = query_weight.shape[1]
    units = expand_weight.shape[1]
    pairs = local // LANES
    outer = lax.axis_size("outer")
    inner = lax.axis_size("inner")
    inner_bits = inner.bit_length() - 1
    rows = D // inner
    width = 3 * LANES

    shape = jax.ShapeDtypeStruct
    smem = pl.BlockSpec(memory_space=pltpu.SMEM)
    anywhere = pl.BlockSpec(memory_space=pl.ANY)
    dma = pltpu.SemaphoreType.DMA
    vec = whole((D,))

    column = pl.BlockSpec((D, LANES), lambda p: (0, p))
    taps_spec = pl.BlockSpec((3, 3, LANES), lambda p: (0, 0, p))
    pair_rows = pl.BlockSpec((slot, LANES), lambda p: (0, p))
    raw_spec = pl.BlockSpec((slot, 3 * LANES), lambda p: (0, p))
    (
        attended, queries, key_rows, value_rows, raw, inverse, embedded, normed_t, att_oth,
        we_oth, wr_oth, wo_oth, terms,
    ) = pl.pallas_call(
        forward_kernel,
        grid=(pairs,),
        in_specs=[smem, whole((1, half)), vec, vec, column, column, column, taps_spec] + [anywhere] * 3,
        out_specs=[pair_rows] * 4 + [raw_spec, pair_rows] + [anywhere] * 7,
        out_shape=[shape((slot, local), BF16)] * 4
        + [shape((slot, 3 * local), BF16), shape((slot, local), F32), shape((half, D), F32), shape((D, slot), BF16)]
        + [shape((slot, local), BF16)]
        + [shape(w.shape, BF16) for w in (expand_weight, reduce_weight, output_weight)]
        + [shape((2 * pairs, slot, slot), BF16)],
        scratch_shapes=[
            pltpu.VMEM((half, D), F32),
            pltpu.VMEM((D, slot), BF16),
            pltpu.VMEM((slot, D), BF16),
            pltpu.VMEM((2, 3, BLOCK + 8, LANES), F32),
            pltpu.VMEM((D, 3 * LANES), BF16),
            pltpu.VMEM((2, slot, LANES), BF16),
            pltpu.VMEM((2, slot, LANES), BF16),
            pltpu.VMEM((2, slot, LANES), BF16),
            pltpu.VMEM((2, slot, slot), BF16),
            pltpu.VMEM((pairs, slot, LANES), BF16),
            dma((PIECES,)), dma((PIECES,)), dma((pairs, slot // BLOCK)), dma((pairs, slot // BLOCK)), dma((3,)), dma((3,)),
            dma((slot // BLOCK,)), dma((1 + pairs,)),
        ],
        compiler_params=params(58, collective_id=0, has_side_effects=True),
        name="attention_forward",
    )(
        lengths, token_ids, gain_first, bias_first,
        query_weight, key_weight, value_weight, dconv_taps, expand_weight, reduce_weight, output_weight,
    )

    steps = units // D
    split = D // width
    fed = 2 * steps * split + 1
    chunks = fed + pairs
    twos = (2,) * inner_bits
    line_stages = inner_bits + outer
    vmem = lambda dims, kind: pltpu.VMEM(dims, kind)
    sums, small, activations, grad_input, _ = pl.pallas_call(
        functools.partial(layer_kernel, inner_bits, outer),
        in_specs=[smem, vec, vec, vec, whole((3, 3, local))] + [anywhere] * 20,
        out_specs=[whole((chunks, rows, width)), whole((16, D)), anywhere, anywhere, anywhere],
        out_shape=[
            shape((chunks, rows, width), BF16), shape((16, D), F32), shape((half, D), F32), shape((half, D), F32),
            shape((steps, 2, half, D), BF16),
        ],
        scratch_shapes=[
            vmem((half, D), F32),
            vmem((chunks,) + twos + (rows, width), BF16),
            vmem((chunks, rows, width), BF16),
            vmem((chunks, rows, width), BF16),
            vmem((slot, local), BF16),
            vmem((2, 2, D, D), BF16),
            vmem((D, local), BF16),
            vmem((half, D), BF16),
            vmem((inner_bits + 2, 16, D), F32),
            vmem((inner_bits + 3, 16, D), F32),
            vmem((2, 8, D), F32),
            vmem((2 * inner, 8, D), F32),
            vmem((outer, 8, D), F32),
            dma((12 + 10 * steps + 3 * pairs,)),
            dma((2 * chunks + 1, line_stages)), dma((2 * chunks + 1, line_stages)),
            dma((line_stages + 1,)), dma((line_stages + 1,)),
            dma((steps + 2, 2)), dma((steps + 2, 2)),
            dma((2 * inner,)), dma((2 * inner,)), dma((outer,)), dma((outer,)),
        ]
        + [vmem((chunks,) + (2,) * (inner_bits - 1 - s) + (rows, width), BF16) for s in range(inner_bits)],
        compiler_params=params(63, collective_id=1, has_side_effects=True),
        name="layer",
    )(
        lengths, gain_first, gain_second, bias_second, dconv_taps,
        att_oth, embedded, cotangent[0], output_weight, wo_oth,
        expand_weight, we_oth, reduce_weight, wr_oth, query_weight, key_weight, value_weight,
        attended, queries, key_rows, value_rows, raw, inverse, normed_t, terms,
    )
    many = steps * split
    part = half // many
    some_rows = pl.BlockSpec((part, D), lambda i: (i, 0))
    pick = lambda index: pl.BlockSpec((1, rows, width), lambda i: (index(i), 0, 0))
    last = lambda i: jnp.minimum(i, pairs - 1)
    chunk_at = lambda i: (i // split) * 2 * split + i % split
    out_pair = pl.BlockSpec((rows, LANES), lambda i: (0, last(i)))
    activations, grad_input, gq, gk, gv, go_sum, ge_sum, gr_sum, tap_sum, *vec_sums = pl.pallas_call(
        finish_kernel,
        grid=(many,),
        in_specs=[
            pick(chunk_at), pick(lambda i: chunk_at(i) + split), pick(lambda i: fed - 1),
            pick(lambda i: fed + last(i)), some_rows, some_rows, whole((16, D)),
        ],
        out_specs=[
            some_rows, some_rows, out_pair, out_pair, out_pair, whole((rows, local)),
            pl.BlockSpec((rows, width), lambda i: (0, i)), pl.BlockSpec((rows, width), lambda i: (0, i)),
            whole((3, 3, D)), vec, vec, vec, vec,
        ],
        out_shape=[shape((half, D), F32)] * 2
        + [shape((rows, local), F32)] * 4
        + [shape((rows, units), F32)] * 2
        + [shape((3, 3, D), F32)]
        + [shape((D,), F32)] * 4,
        compiler_params=params(62),
        name="finish",
    )(sums, sums, sums, sums, activations, grad_input, small)
    return (
        activations[None],
        grad_input[None],
        gq,
        gk,
        gv,
        go_sum.T,
        ge_sum,
        gr_sum.T,
        tap_sum,
        *vec_sums,
    )


def solution(mesh):
    return jax.shard_map(
        body,
        mesh=mesh,
        in_specs=(
            P(("outer", "inner"), "head"),
            P(("outer", "inner")),
            P(None, "head"),
            P(None, "head"),
            P(None, "head"),
            P("head", None),
            P(None, "head"),
            P("head", None),
            P(None, None, "head"),
            P(),
            P(),
            P(),
            P(),
            P(("outer", "inner"), "head", None),
        ),
        out_specs=(
            P(("outer", "inner"), "head", None),
            P(("outer", "inner"), "head", None),
            P("inner", "head"),
            P("inner", "head"),
            P("inner", "head"),
            P("head", "inner"),
            P("inner", "head"),
            P("head", "inner"),
            P(),
            P(),
            P(),
            P(),
            P(),
        ),
        check_vma=False,
    )
```

```python
import functools
import math

import jax
import jax.numpy as jnp
from jax import lax
from jax.experimental import pallas as pl
from jax.experimental.pallas import tpu as pltpu
from jax.sharding import PartitionSpec as P

HEAD_DIM = 64
D = 768
BLOCK = 256
LANES = 128
EPS = 1e-05
MODULUS = 32749
NEGATIVE = -1e30
SCALE = HEAD_DIM ** (-0.5)
F32 = jnp.float32
BF16 = jnp.bfloat16
MIB = 1024 * 1024

SINE = (
    4.442882913726386,
    -7.308248583654593,
    3.606466623722958,
    -0.8474403474577161,
    0.11605422299047748,
    -0.010267162611370253,
    0.0005523348366953617,
)


def dot(a, b):
    return lax.dot_general(a, b, (((1,), (0,)), ((), ())), preferred_element_type=F32)


def dot_nt(a, b):
    return lax.dot_general(a, b, (((1,), (1,)), ((), ())), preferred_element_type=F32)


def whole(shape):
    return pl.BlockSpec(shape, lambda *_: (0,) * len(shape))


def normalise(values):
    centre = values - jnp.mean(values, axis=-1, keepdims=True)
    spread = jnp.mean(centre * centre, axis=-1, keepdims=True)
    scale = lax.rsqrt(spread + EPS)
    return centre * scale, scale


def norm_back(grad, hat, scale, gain):
    q = grad * gain
    mean_q = jnp.mean(q, axis=-1, keepdims=True)
    mean_qh = jnp.mean(q * hat, axis=-1, keepdims=True)
    return scale * (q - mean_q - hat * mean_qh)


def lane_ids(rows):
    return lax.broadcasted_iota(jnp.int32, (rows, LANES), 1)


def split_three(column):
    high = column.astype(BF16).astype(F32)
    rest = column - high
    middle = rest.astype(BF16).astype(F32)
    return high, middle, rest - middle


def with_parts(base, lane, offset, column):
    high, middle, small = split_three(column)
    base = jnp.where(lane == offset + 1, high, base)
    base = jnp.where(lane == offset + 2, middle, base)
    return jnp.where(lane == offset + 3, small, base)


def remote(src, dst, send, recv, **place):
    return pltpu.make_async_remote_copy(
        src_ref=src, dst_ref=dst, send_sem=send, recv_sem=recv,
        device_id=place, device_id_type=pl.DeviceIdType.MESH,
    )


def greet(*places):
    barrier = pltpu.get_barrier_semaphore()
    for place in places:
        pl.semaphore_signal(barrier, inc=1, device_id=place, device_id_type=pl.DeviceIdType.MESH)
    pl.semaphore_wait(barrier, len(places))


def rows_of(which, half):
    return pl.ds(pl.multiple_of(which * half, half), half)


def remainder(product):
    turns = jnp.floor(product.astype(F32) * (1.0 / MODULUS) + 0.5)
    return (product - turns.astype(jnp.int32) * MODULUS).astype(F32)


def embed_rows(tok_ref, gain, bias, emb_ref, normed_ref, base, first):
    tokens = jnp.broadcast_to(tok_ref[:, pl.ds(first, LANES)], (LANES, LANES)).T
    column = lax.broadcasted_iota(jnp.int32, (1, LANES), 1)
    start = remainder(tokens * (column + 1) + column * column)
    stride = remainder(tokens * LANES + column * (2 * LANES))
    parts = []
    for c in range(D // LANES):
        phase = start + (stride * float(c) + float(c * c * LANES * LANES))
        u = (phase - jnp.floor(phase * (1.0 / MODULUS) + 0.5) * float(MODULUS)) * (2.0 / MODULUS)
        z = u * u
        value = jnp.full_like(u, SINE[-1])
        for coefficient in SINE[-2::-1]:
            value = value * z + coefficient
        parts.append(value * u)
    embedded = jnp.concatenate(parts, axis=1)
    emb_ref[pl.ds(first, LANES), :] = embedded
    hat, _ = normalise(embedded)
    rows = pl.ds(pl.multiple_of(base + first, LANES), LANES)
    normed_ref[rows, :] = (hat * gain + bias).astype(BF16)


PIECES = 3


def row_of(ref):
    return ref[...].reshape(1, D)


def forward_kernel(
    len_ref, tok_ref, gain_ref, bias_ref, wq_ref, wk_ref, wv_ref, taps_ref, we_hbm, wr_hbm, wo_hbm,
    att_ref, q_ref, k_ref, v_ref, raw_ref, rinv_ref,
    emb_hbm, nt_hbm, att_oth_hbm, we_oth_hbm, wr_oth_hbm, wo_oth_hbm, terms_hbm,
    emb_ref, nt_ref, normed_ref, shift_ref, wcat_ref, qa_ref, ka_ref, va_ref, terms_ref, give_ref,
    row_send, row_recv, att_send, att_recv, weight_send, weight_recv, terms_sem, store_sem,
):
    slot = att_ref.shape[0]
    half = slot // 2
    blocks = slot // BLOCK
    step = pl.program_id(0)
    pairs = att_oth_hbm.shape[1] // LANES
    head = lax.axis_index("head")
    partner = 1 - head
    piece = half // PIECES

    def row_copy(k):
        rows = pl.ds(pl.multiple_of(head * half + k * piece, piece), piece)
        return remote(normed_ref.at[rows], normed_ref.at[rows], row_send.at[k], row_recv.at[k], head=partner)

    def att_copy(p, i):
        rows = pl.ds(i * BLOCK, BLOCK)
        land = att_oth_hbm.at[rows, pl.ds(pl.multiple_of(p * LANES, LANES), LANES)]
        return remote(give_ref.at[p, rows], land, att_send.at[p, i], att_recv.at[p, i], head=partner)

    def weight_copy(k):
        src, dst = ((wo_hbm, wo_oth_hbm), (we_hbm, we_oth_hbm), (wr_hbm, wr_oth_hbm))[k]
        return remote(src, dst, weight_send.at[k], weight_recv.at[k], head=partner)

    def emb_store():
        return pltpu.make_async_copy(emb_ref, emb_hbm, store_sem.at[0])

    def nt_store(p):
        part = pl.ds(p * (D // pairs), D // pairs)
        return pltpu.make_async_copy(nt_ref.at[part], nt_hbm.at[part], store_sem.at[1 + p])

    def terms_copy(p, i):
        rows, cols = pl.ds(i * BLOCK, BLOCK), pl.ds(0, (i + 1) * BLOCK)
        return pltpu.make_async_copy(
            terms_ref.at[:, rows, cols], terms_hbm.at[pl.ds(2 * p, 2), rows, cols], terms_sem.at[i]
        )

    @pl.when(step == 0)
    def _():
        greet({"head": partner})
        base = head * half
        for k in range(PIECES):
            def embed_step(i, _):
                first = pl.multiple_of(k * piece + i * LANES, LANES)
                embed_rows(tok_ref, row_of(gain_ref), row_of(bias_ref), emb_ref, normed_ref, base, first)
                return 0

            lax.fori_loop(0, piece // LANES, embed_step, 0)
            row_copy(k).start()
        for k in range(3):
            weight_copy(k).start()
        emb_store().start()
        for k in range(PIECES):
            row_copy(k).wait()

    for j, w_ref in enumerate((wq_ref, wk_ref, wv_ref)):
        wcat_ref[:, j * LANES : (j + 1) * LANES] = w_ref[...]
    shift_ref[0, :, 0:8, :] = jnp.zeros((3, 8, LANES), F32)
    lane = lane_ids(BLOCK)
    features = D // pairs
    some = pl.ds(pl.multiple_of(step * features, features), features)

    def raws_of(r):
        return dot(normed_ref[r * BLOCK : (r + 1) * BLOCK, :], wcat_ref[...])

    coming = raws_of(0)
    for r in range(blocks):
        rows = slice(r * BLOCK, (r + 1) * BLOCK)
        raws = coming
        if r + 1 < blocks:
            coming = raws_of(r + 1)
        raw_ref[rows, :] = raws.astype(BF16)
        nt_ref[some, rows] = normed_ref[rows, some].T
        mixed = []
        this, after = r % 2, (r + 1) % 2
        for j in range(3):
            raw = raws[:, j * LANES : (j + 1) * LANES]
            shift_ref[this, j, 8 : 8 + BLOCK, :] = raw
            one = shift_ref[this, j, 7 : 7 + BLOCK, :]
            two = shift_ref[this, j, 6 : 6 + BLOCK, :]
            value = taps_ref[j, 0:1, :] * raw + taps_ref[j, 1:2, :] * one + taps_ref[j, 2:3, :] * two
            mixed.append(value * SCALE if j == 0 else value)
            shift_ref[after, j, 0:8, :] = raw[BLOCK - 8 :, :]
        for ref, value in zip((q_ref, k_ref, v_ref), mixed):
            ref[rows, :] = value.astype(BF16)
        row = lax.broadcasted_iota(jnp.int32, (BLOCK, 1), 0) + r * BLOCK
        key_bias = jnp.where(row < len_ref[0], 0.0, NEGATIVE)
        for e in range(2):
            mine = (lane // HEAD_DIM) == e
            other = HEAD_DIM * (1 - e)
            qa_ref[e, rows, :] = jnp.where(mine, mixed[0], jnp.where(lane == other, 1.0, 0.0)).astype(BF16)
            key = jnp.where(mine, mixed[1], jnp.where(lane == other, key_bias, 0.0)).astype(BF16)
            ka_ref[e, :, rows] = key.T
            va_ref[e, rows, :] = jnp.where(mine, mixed[2], jnp.where(lane == other, 1.0, 0.0)).astype(BF16)

    @pl.when(step > 0)
    def _():
        for i in range(blocks):
            terms_copy(step - 1, i).wait()

    causal = lax.broadcasted_iota(jnp.int32, (BLOCK, BLOCK), 1) <= lax.broadcasted_iota(
        jnp.int32, (BLOCK, BLOCK), 0
    )
    tasks = [(i, e) for i in range(blocks) for e in range(2)]

    def scores_of(i, e):
        rows = slice(i * BLOCK, (i + 1) * BLOCK)
        query = qa_ref[e, rows, :]
        diagonal = jnp.where(causal, dot(query, ka_ref[e, :, rows]), NEGATIVE)
        before = dot(query, ka_ref[e, :, : i * BLOCK]) if i else None
        return diagonal, before

    coming = scores_of(*tasks[0])
    outs = []
    for t, (i, e) in enumerate(tasks):
        diagonal, before = coming
        if t + 1 < len(tasks):
            coming = scores_of(*tasks[t + 1])
        rows = slice(i * BLOCK, (i + 1) * BLOCK)
        other = HEAD_DIM * (1 - e)
        row_max = jnp.max(diagonal, axis=1, keepdims=True)
        if i:
            row_max = jnp.maximum(row_max, jnp.max(before, axis=1, keepdims=True))
        terms = jnp.exp(diagonal - row_max).astype(BF16)
        terms_ref[e, rows, rows] = terms
        out = dot(terms, va_ref[e, rows, :])
        if i:
            terms = jnp.exp(before - row_max).astype(BF16)
            terms_ref[e, rows, : i * BLOCK] = terms
            out += dot(terms, va_ref[e, : i * BLOCK, :])
        inverse = 1.0 / out[:, other : other + 1]
        outs.append((out, inverse))
        if e == 1:
            first_head = lane < HEAD_DIM
            inverse = jnp.where(first_head, outs[0][1], outs[1][1])
            attended = (jnp.where(first_head, outs[0][0], outs[1][0]) * inverse).astype(BF16)
            att_ref[rows, :] = attended
            give_ref[step, rows, :] = attended
            att_copy(step, i).start()
            rinv_ref[rows, :] = inverse
            outs = []
            terms_copy(step, i).start()

    for p in range(pairs):
        @pl.when(step == p)
        def _():
            nt_store(p).start()

    @pl.when(step == pairs - 1)
    def _():
        for p in range(pairs):
            for i in range(blocks):
                att_copy(p, i).wait()
            nt_store(p).wait()
        emb_store().wait()
        for k in range(3):
            weight_copy(k).wait()
        for i in range(blocks):
            terms_copy(step, i).wait()


def plan_sums(entries, ready, points, tail, inner_bits, line_steps, orders, rate=0.05, hop=1.8):
    stages = inner_bits + line_steps + 1
    done, arrive, free, plan, begun = [0] * len(entries), {}, {}, {}, set()

    def step_of(n, now):
        chunk, size, kind = entries[n]
        stage = done[n]
        if stage < inner_bits:
            link, part = ("bit", orders[kind][stage]), size / 2 ** (stage + 1)
        else:
            t = stage - inner_bits
            link, part = ("line", t), size / 2**inner_bits
        if stage < stages - 1:
            free[link] = max(free.get(link, 0.0), now) + part / rate
            arrive[n] = free[link] + hop
        done[n] += 1

    at, now, late = 0, 0.0, 0
    while at < len(points) or any(d < stages for d in done):
        if at < len(points):
            place, when = points[at]
            now, slack = max(now, when), 0.3 if place[0] != "tail" else 0.0
        else:
            place, slack = ("tail", tail + late), 0.0
            late += 1
            now = max(now, min(arrive[n] for n in range(len(entries)) if done[n] < stages))
        at += 1
        for n, (chunk, _, _) in enumerate(entries):
            if ready[n] == place:
                begun.add(n)
        while True:
            able = [n for n in begun if done[n] < stages and (done[n] == 0 or arrive[n] <= now - slack)]
            if not able:
                break
            n = min(able, key=lambda m: (-done[m], m))
            plan.setdefault(place, []).append((n, done[n]))
            step_of(n, now)
    return plan


def layer_kernel(
    inner_bits, outer,
    len_ref, gain_first_ref, gain_second_ref, bias_second_ref, taps_ref,
    att_oth_hbm, emb_hbm, cot_hbm, wo_own_hbm, wo_oth_hbm,
    we_own_hbm, we_oth_hbm, wr_own_hbm, wr_oth_hbm, wq_hbm, wk_hbm, wv_hbm,
    att_hbm, q_hbm, k_hbm, v_hbm, raw_hbm, rinv_hbm, nt_hbm, terms_hbm,
    sum_ref, small_ref, act_hbm, gin_hbm, sq_hbm,
    gh_ref, g_ref, rz_ref, rc_ref, do_ref, got_ref, got_go, got_first, acc_ref, got_small, late_ref, got_group, got_outer,
    load_sem, send_sem, recv_sem, small_send, small_recv, core_send, core_recv,
    group_send, group_recv, outer_send, outer_recv, *halves,
):
    half = gh_ref.shape[0]
    slot = 2 * half
    local = att_oth_hbm.shape[1]
    units = we_own_hbm.shape[1]
    steps = units // D
    width = sum_ref.shape[2]
    split = D // width
    pairs = local // LANES
    fed = 2 * steps * split + 1
    blocks = slot // BLOCK
    head = lax.axis_index("head")
    partner = 1 - head
    mine = lax.axis_index("inner")
    line = lax.axis_index("outer")
    centre = outer // 2
    left = line < centre
    depth = jnp.where(left, centre - 1 - line, line - centre)
    inward = jnp.where(left, line + 1, line - 1)
    outward = jnp.where(left, line - 1, line + 1)
    bit = [(mine // (1 << b)) % 2 for b in range(inner_bits)]
    across = [mine + (1 << b) * (1 - 2 * bit[b]) for b in range(inner_bits)]

    def chunk_of(c, kind, k):
        return (2 * c + kind) * split + k

    entries = []
    for c in range(fed):
        entries.append((c, 0, width, c % 2))
    for c in range(fed, fed + pairs - 1):
        entries += [(c, 0, 2 * LANES, c % 2), (c, 2 * LANES, LANES, 1 - c % 2)]
    entries += [(fed + pairs - 1, j * LANES, LANES, j % 2) for j in range(3)]
    order_of = [tuple((b + first) % inner_bits for b in range(inner_bits)) for first in range(2)]
    line_steps = 2 * centre - 1
    stage_count = inner_bits + line_steps + 1

    def index_of(fixed):
        return tuple(fixed.get(b, slice(None)) for b in reversed(range(inner_bits)))

    def lanes(entry):
        return slice(entry[1], entry[1] + entry[2])

    def halving(n, s):
        c, _, _, kind = entries[n]
        order = order_of[kind]
        fixed = {b: bit[b] for b in order[:s]}
        b = order[s]
        give = g_ref.at[(c,) + index_of({**fixed, b: 1 - bit[b]}) + (slice(None), lanes(entries[n]))]
        land = halves[s].at[(c,) + (slice(None),) * (inner_bits - 1 - s) + (slice(None), lanes(entries[n]))]
        return remote(give, land, send_sem.at[n, s], recv_sem.at[n, s], inner=across[b])

    def add_half(n, s):
        c, _, _, kind = entries[n]
        order = order_of[kind]
        index = (c,) + index_of({b: bit[b] for b in order[: s + 1]}) + (slice(None), lanes(entries[n]))
        land = (c,) + (slice(None),) * (inner_bits - 1 - s) + (slice(None), lanes(entries[n]))
        g_ref[index] = g_ref[index] + halves[s][land]

    def own(n):
        return (entries[n][0],) + tuple(bit[b] for b in reversed(range(inner_bits))) + (slice(None), lanes(entries[n]))

    def flat(n):
        return (entries[n][0], slice(None), lanes(entries[n]))

    def line_sender(t):
        if t < centre - 1:
            return depth == centre - 1 - t
        if t == centre - 1:
            return depth == 0
        return depth == t - centre

    def line_copy(n, t):
        s = inner_bits + t
        sems = (send_sem.at[n, s], recv_sem.at[n, s])
        if t < centre - 1:
            return remote(g_ref.at[own(n)], rz_ref.at[flat(n)], *sems, outer=inward)
        if t == centre - 1:
            return remote(g_ref.at[own(n)], rc_ref.at[flat(n)], *sems, outer=inward)
        return remote(rc_ref.at[flat(n)], rc_ref.at[flat(n)], *sems, outer=outward)

    def line_finish(n, t):
        if t < centre - 1:
            @pl.when(depth == centre - 2 - t)
            def _():
                line_copy(n, t).wait_recv()
                g_ref[own(n)] = g_ref[own(n)] + rz_ref[flat(n)]
        elif t == centre - 1:
            @pl.when(depth == 0)
            def _():
                line_copy(n, t).wait_recv()
                rc_ref[flat(n)] = g_ref[own(n)] + rc_ref[flat(n)]
        else:
            pl.when(depth == t - centre + 1)(lambda: line_copy(n, t).wait_recv())

    def advance(n, stage):
        if 0 < stage <= inner_bits:
            halving(n, stage - 1).wait_recv()
            add_half(n, stage - 1)
        elif stage > inner_bits:
            line_finish(n, stage - inner_bits - 1)
        if stage < inner_bits:
            halving(n, stage).start()
        elif stage < stage_count - 1:
            t = stage - inner_bits
            pl.when(line_sender(t))(lambda: line_copy(n, t).start())
        else:
            sum_ref[flat(n)] = rc_ref[flat(n)]

    def drain(n):
        for s in range(inner_bits):
            halving(n, s).wait_send()
        for t in range(line_steps):
            pl.when(line_sender(t))(lambda t=t: line_copy(n, t).wait_send())

    points = []
    now = 6.0
    for c in range(steps):
        for k, spent in enumerate((2.3, 2.3, 0.3, 2.3, 2.3, 1.2)):
            now += spent
            points.append((("feed", c, k), now))
        now += 1.1
    for k in range(3):
        now += 1.2
        points.append((("norm", k), now))
    for p in range(pairs):
        now += 1.2
        for j in range(0, blocks, 2):
            points.append((("pair", p, j), now))
            now += 8.0 * (2 * (blocks - j) - 1) * 2 / (blocks * (blocks + 1))
        if p < pairs - 1:
            now += 2.8
            points.append((("taps", p), now))
    for j in (2, 1, 0):
        now += 1.3
        points.append((("last", j), now))
    for k, spent in enumerate((0.8, 0.8, 0.8, 0.8, 1.5, 1.5, 1.4, 1.4, 1.4, 1.4)):
        now += spent
        points.append((("tail", k), now))
    ready = {}
    for c in range(steps):
        for k in range(split):
            ready[chunk_of(c, 0, k)] = ("feed", c, 2)
            ready[chunk_of(c, 1, k)] = ("feed", c, 5)
    ready[fed - 1] = ("norm", 2)
    for p in range(pairs - 1):
        ready[fed + p] = ("taps", p)
    ready_at = [ready[c] if c in ready else ("last", first // LANES) for c, first, _, _ in entries]
    plan = plan_sums(
        [(c, 2e-6 * D * wide, kind) for c, _, wide, kind in entries],
        ready_at, points, 10, inner_bits, line_steps, order_of,
    )

    def tick(place):
        for n, stage in plan.pop(place, ()):
            advance(n, stage)

    def small_copy(k):
        sems = (small_send.at[k], small_recv.at[k])
        if k == 0:
            return remote(acc_ref.at[0], got_small.at[0], *sems, head=partner)
        if k <= inner_bits:
            return remote(acc_ref.at[k], got_small.at[k], *sems, inner=across[k - 1])
        t = k - 1 - inner_bits
        if t <= centre - 1:
            return remote(acc_ref.at[inner_bits + 1], got_small.at[inner_bits + 1 + (t == centre - 1)], *sems, outer=inward)
        last = got_small.at[inner_bits + 2]
        return remote(last, last, *sems, outer=outward)

    def small_step(k):
        if 0 < k <= inner_bits + 1:
            small_copy(k - 1).wait_recv()
            acc_ref[k] = acc_ref[k - 1] + got_small[k - 1]
        elif k > inner_bits + 1:
            t = k - 2 - inner_bits
            if t < centre - 1:
                @pl.when(depth == centre - 2 - t)
                def _():
                    small_copy(k - 1).wait_recv()
                    acc_ref[inner_bits + 1] = acc_ref[inner_bits + 1] + got_small[inner_bits + 1]
            elif t == centre - 1:
                @pl.when(depth == 0)
                def _():
                    small_copy(k - 1).wait_recv()
                    got_small[inner_bits + 2] = acc_ref[inner_bits + 1] + got_small[inner_bits + 2]
            else:
                pl.when(depth == t - centre + 1)(lambda: small_copy(k - 1).wait_recv())
        if k <= inner_bits:
            small_copy(k).start()
        elif k <= inner_bits + line_steps:
            pl.when(line_sender(k - 1 - inner_bits))(lambda: small_copy(k).start())
        else:
            small_ref[...] = got_small[inner_bits + 2]

    small_steps = inner_bits + line_steps + 2

    inner = 1 << inner_bits
    group = 2 * inner
    seat = mine * 2 + head

    def group_place(k, way):
        other = lax.rem(seat + group + way * k, group)
        return other, {"inner": other // 2, "head": lax.rem(other, 2)}

    def outer_place(k, way):
        other = lax.rem(line + outer + way * k, outer)
        return other, {"outer": other}

    def late_copies(places, count, me, src, land, sends, recvs):
        give = [remote(src, land.at[me], sends.at[k], recvs.at[k], **places(k, 1)[1]) for k in range(1, count)]
        take = [
            remote(src, land.at[places(k, -1)[0]], sends.at[k], recvs.at[k], **places(k, 1)[1]) for k in range(1, count)
        ]
        return give, take

    group_give, group_take = late_copies(
        group_place, group, seat, late_ref.at[0], got_group, group_send, group_recv
    )
    outer_give, outer_take = late_copies(outer_place, outer, line, late_ref.at[1], got_outer, outer_send, outer_recv)

    load_count = iter(range(load_sem.shape[0]))

    def load(src, dst):
        return pltpu.make_async_copy(src, dst, load_sem.at[next(load_count)])

    row = lax.broadcasted_iota(jnp.int32, (half, 1), 0) + head * half
    valid = row < len_ref[0]

    def greet_all():
        barrier = pltpu.get_barrier_semaphore()
        places = [group_place(k, 1)[1] for k in range(1, group)] + [outer_place(k, 1)[1] for k in range(1, outer)]
        for place in places:
            pl.semaphore_signal(barrier, inc=1, device_id=place, device_id_type=pl.DeviceIdType.MESH)
        pl.semaphore_wait(barrier, len(places))

    two_rows = half // 2

    def halves_of(step):
        for r in range(2):
            step(r, pl.ds(r * two_rows, two_rows))

    def feed_forward(
        att_ref, wo_ref, we_ref, wr_ref, cot_ref, hid_ref, gn_ref,
        n2_ref, n2t_ref, gl_ref, glt_ref, give_ref, relu_ref, sq_ref,
    ):
        give_att = relu_ref.at[0, :, 0:local]
        give_go = relu_ref.at[1, :, 0:local]
        loads = {}
        for k, (att, wo) in enumerate(((att_hbm.at[rows_of(head, half), :], wo_own_hbm), (att_oth_hbm.at[rows_of(head, half), :], wo_oth_hbm))):
            loads["att", k] = load(att, att_ref.at[k])
            loads["wo", k] = load(wo, wo_ref.at[k])
        loads["emb"] = load(emb_hbm, hid_ref)
        loads["cot"] = load(cot_hbm, cot_ref)
        for c in range(steps):
            cols = pl.ds(c * D, D)
            for k, we in ((1, we_oth_hbm), (0, we_own_hbm)):
                loads["we", c, k] = load(we.at[:, cols], we_ref.at[c, k])
            for k, wr in ((1, wr_oth_hbm), (0, wr_own_hbm)):
                loads["wr", c, k] = load(wr.at[cols, :], wr_ref.at[c, k])
        weights = {c: [copy for key, copy in loads.items() if key[0] in ("we", "wr") and key[1] == c] for c in range(steps)}
        for key, copy in loads.items():
            if key[0] not in ("we", "wr"):
                copy.start()
        greet_all()
        for key in (("att", 0), ("wo", 0), ("att", 1), ("wo", 1), "emb", "cot"):
            loads[key].wait()
        for copy in weights[0]:
            copy.start()
        gain, bias = row_of(gain_second_ref), row_of(bias_second_ref)

        def open_rows(r, rows):
            hidden = hid_ref[rows, :] + dot(att_ref[0, rows, :], wo_ref[0]) + dot(att_ref[1, rows, :], wo_ref[1])
            hid_ref[rows, :] = hidden
            hat, _ = normalise(hidden)
            normed = (hat * gain + bias).astype(BF16)
            n2_ref[rows, :] = normed
            n2t_ref[:, rows] = normed.T
            position = lax.broadcasted_iota(jnp.int32, (two_rows, 1), 0) + head * half + r * two_rows
            grad = jnp.where(position < len_ref[0], cot_ref[rows, :], 0.0)
            cot_ref[rows, :] = grad
            gl_ref[rows, :] = grad.astype(BF16)
            glt_ref[:, rows] = grad.astype(BF16).T

        halves_of(open_rows)
        hid_store = load(hid_ref, act_hbm)
        hid_store.start()

        def grad_copy(c, kind):
            return remote(
                give_ref.at[kind], got_ref.at[c % 2, kind], core_send.at[c, kind], core_recv.at[c, kind], head=partner
            )

        def put_own(c, kind, value):
            for k in range(split):
                part = value[:, k * width : (k + 1) * width].astype(BF16)
                g_ref[chunk_of(c, kind, k)] = part.reshape(g_ref.shape[1:])

        def add_other(c, kind):
            grad_copy(c, kind).wait_recv()
            for k in range(split):
                got = got_ref[c % 2, kind, :, k * width : (k + 1) * width]
                g_ref[chunk_of(c, kind, k)] += got.reshape(g_ref.shape[1:])

        def weight_grad(c, kind, k, left_ref, right):
            grad = dot(left_ref[...], right)
            if k == 1:
                if c:
                    grad_copy(c - 1, kind).wait_send()
                give_ref[kind] = grad.astype(BF16)
                grad_copy(c, kind).start()
            else:
                put_own(c, kind, grad)

        stores = []
        for c in range(steps):
            for k in (1, 0):
                loads["we", c, k].wait()
                relu = jnp.maximum(dot(n2_ref[...], we_ref[c, k]), 0.0)
                relu_ref[k] = relu.astype(BF16)
                sq_ref[c, k] = (relu * relu).astype(BF16)
                stores.append(load(sq_ref.at[c, k], sq_hbm.at[c, k]))
                stores[-1].start()
                weight_grad(c, 0, k, glt_ref, sq_ref[c, k])
                tick(("feed", c, 1 - k))
            if c + 1 < steps:
                for copy in weights[c + 1]:
                    copy.start()
            add_other(c, 0)
            tick(("feed", c, 2))
            for k in (1, 0):
                loads["wr", c, k].wait()
                back = dot_nt(gl_ref[...], wr_ref[c, k])
                relu_ref[k] = (back * (2.0 * relu_ref[k].astype(F32))).astype(BF16)
                weight_grad(c, 1, k, n2t_ref, relu_ref[k])
                tick(("feed", c, 4 - k))
            for k in (1, 0):
                gn = dot_nt(relu_ref[k], we_ref[c, k])
                if c == 0 and k == 1:
                    gn_ref[...] = gn
                else:
                    gn_ref[...] += gn
                if k == 1:
                    add_other(c, 1)
                    tick(("feed", c, 5))
        acc_ref[0] = jnp.zeros(acc_ref.shape[1:], F32)

        def close_rows(r, rows):
            hat, scale = normalise(hid_ref[rows, :])
            grad_n = gn_ref[rows, :]
            acc_ref[0, 2:3, :] += jnp.sum(grad_n * hat, axis=0, keepdims=True)
            acc_ref[0, 3:4, :] += jnp.sum(grad_n, axis=0, keepdims=True)
            grad_h = cot_ref[rows, :] + norm_back(grad_n, hat, scale, gain)
            gh_ref[rows, :] = grad_h
            low = grad_h.astype(BF16)
            n2_ref[rows, :] = low
            n2t_ref[:, rows] = low.T
            give_att[rows, :] = dot_nt(low, wo_ref[1]).astype(BF16)

        halves_of(close_rows)
        own_rows = rows_of(head, half)
        att_copy = remote(give_att, do_ref.at[own_rows], core_send.at[steps, 0], core_recv.at[steps, 0], head=partner)
        att_copy.start()
        tick(("norm", 0))
        give_go[...] = dot(n2t_ref[...], att_ref[1]).astype(BF16)
        go_copy = remote(give_go, got_go, core_send.at[steps, 1], core_recv.at[steps, 1], head=partner)
        go_copy.start()
        do_ref[own_rows, :] = dot_nt(n2_ref[...], wo_ref[0]).astype(BF16)
        tick(("norm", 1))
        grad_o = dot(n2t_ref[...], att_ref[0]).astype(BF16)
        go_copy.wait()
        g_ref[fed - 1] = (grad_o + got_go[...]).reshape(g_ref.shape[1:])
        tick(("norm", 2))
        for kind in range(2):
            grad_copy(steps - 1, kind).wait_send()
        for copy in [hid_store] + stores:
            copy.wait()
        att_copy.wait()

    pl.run_scoped(
        feed_forward,
        pltpu.VMEM((2, half, local), BF16), pltpu.VMEM((2, local, D), BF16),
        pltpu.VMEM((steps, 2, D, D), BF16), pltpu.VMEM((steps, 2, D, D), BF16),
        pltpu.VMEM((half, D), F32), pltpu.VMEM((half, D), F32), pltpu.VMEM((half, D), F32),
        pltpu.VMEM((half, D), BF16), pltpu.VMEM((D, half), BF16),
        pltpu.VMEM((half, D), BF16), pltpu.VMEM((D, half), BF16),
        pltpu.VMEM((2, D, D), BF16), pltpu.VMEM((2, half, D), BF16), pltpu.VMEM((steps, 2, half, D), BF16),
    )

    def attention(
        all_ref, wcat_ref, nt_ref, mix_ref, late, dot_ref, qt_ref, doa_ref, kz_ref, va_ref, turned_ref,
        att_ref, q_ref, k_ref, v_ref, raw_ref, rinv_ref, terms_ref, pair_sem, terms_sem,
    ):
        def pair_loads(p, place):
            one = pl.ds(pl.multiple_of(p * LANES, LANES), LANES)
            three = pl.ds(pl.multiple_of(p * 3 * LANES, LANES), 3 * LANES)
            return [
                pltpu.make_async_copy(rinv_hbm.at[:, one], rinv_ref.at[place], pair_sem.at[place, 0]),
                pltpu.make_async_copy(att_hbm.at[:, one], att_ref.at[place], pair_sem.at[place, 1]),
                pltpu.make_async_copy(v_hbm.at[:, one], v_ref.at[place], pair_sem.at[place, 2]),
                pltpu.make_async_copy(q_hbm.at[:, one], q_ref.at[place], pair_sem.at[place, 3]),
                pltpu.make_async_copy(k_hbm.at[:, one], k_ref.at[place], pair_sem.at[place, 4]),
                pltpu.make_async_copy(raw_hbm.at[:, three], raw_ref.at[place], pair_sem.at[place, 5]),
            ]

        def terms_load(p, j):
            rows = pl.ds(j * BLOCK, slot - j * BLOCK)
            spot = lax.rem(blocks * p + j, 4)
            return pltpu.make_async_copy(
                terms_hbm.at[pl.ds(2 * p, 2), rows, pl.ds(j * BLOCK, BLOCK)],
                terms_ref.at[spot, :, rows, :],
                terms_sem.at[spot],
            )

        for copy in pair_loads(0, 0):
            copy.start()
        for j in range(2):
            terms_load(0, j).start()
        nt_load = load(nt_hbm, nt_ref)
        nt_load.start()
        for copy in late:
            copy.start()
        mix_ref[:, slot : slot + 8, :] = jnp.zeros((3, 8, LANES), F32)
        lane = lane_ids(slot)

        def at_pair(p, kind, *rest):
            for q in range(pairs):
                if plan.get((kind, q) + rest):
                    pl.when(p == q)(functools.partial(tick, (kind, q) + rest))

        def one_pair(p, _):
            place = lax.rem(p, 2)
            one = pl.ds(pl.multiple_of(p * LANES, LANES), LANES)

            @pl.when(p + 1 < pairs)
            def _():
                for copy in pair_loads(p + 1, 1 - place):
                    copy.start()

            for copy in pair_loads(p, place):
                copy.wait()
            scaled = (do_ref[:, one].astype(F32) * rinv_ref[place]).astype(BF16)
            dot_ref[...] = scaled.T
            qt_ref[...] = q_ref[place].T
            product = scaled.astype(F32) * att_ref[place].astype(F32)
            for e in range(2):
                in_head = (lane // HEAD_DIM) == e
                delta = -jnp.sum(jnp.where(in_head, product, 0.0), axis=1, keepdims=True)
                other = HEAD_DIM * (1 - e)
                ones = jnp.where((lane > other) & (lane < other + 4), 1.0, 0.0)
                doa_ref[e] = with_parts(jnp.where(in_head, scaled.astype(F32), 0.0), lane, other, delta).astype(BF16)
                va_ref[e] = jnp.where(in_head, v_ref[place].astype(F32), ones).astype(BF16)
                kz_ref[e] = jnp.where(in_head, k_ref[place].astype(F32), 0.0).astype(BF16)

            def grads_of(j, e):
                return dot_nt(doa_ref[e, j * BLOCK :, :], va_ref[e, j * BLOCK : (j + 1) * BLOCK, :])

            for j0 in range(0, blocks, 2):
                at_pair(p, "pair", j0)
                for j in (j0, j0 + 1):
                    terms_load(p, j).wait()
                    if j + 2 < blocks:
                        terms_load(p, j + 2).start()
                    else:
                        @pl.when(p + 1 < pairs)
                        def _():
                            terms_load(p + 1, j + 2 - blocks).start()
                tasks = [(j, e) for j in (j0, j0 + 1) for e in range(2)]
                coming = grads_of(*tasks[0])
                for t, (j, e) in enumerate(tasks):
                    back = coming
                    if t + 1 < len(tasks):
                        coming = grads_of(*tasks[t + 1])
                    first = j * BLOCK
                    keys = slice(first, first + BLOCK)
                    mine_rows = slice(e * HEAD_DIM, (e + 1) * HEAD_DIM)
                    terms = terms_ref[lax.rem(blocks * p + j, 4), e, first:, :]
                    grads = (terms.astype(F32) * back).astype(BF16)
                    part = dot(grads, kz_ref[e, keys, :])
                    if j == 0 and e == 0:
                        mix_ref[0, first:slot, :] = part
                    else:
                        mix_ref[0, first:slot, :] += part
                    turned_ref[0, mine_rows, keys] = dot(qt_ref[mine_rows, first:], grads)
                    turned_ref[1, mine_rows, keys] = dot(dot_ref[mine_rows, first:], terms)
            mix_ref[0, 0:slot, :] = mix_ref[0, 0:slot, :] * SCALE
            mix_ref[1, 0:slot, :] = turned_ref[0].T
            mix_ref[2, 0:slot, :] = turned_ref[1].T
            base = pl.multiple_of(p * 3 * LANES, LANES)

            @pl.when(p == 0)
            def _():
                nt_load.wait()

            for j in (2, 1, 0):
                zero = mix_ref[j, 0:slot, :]
                one_on = mix_ref[j, 1 : 1 + slot, :]
                two_on = mix_ref[j, 2 : 2 + slot, :]
                raw = raw_ref[place, :, j * LANES : (j + 1) * LANES].astype(F32)
                cols = pl.ds(pl.multiple_of(head * local + p * LANES, LANES), LANES)
                value = 0.0
                for s, moved in enumerate((zero, one_on, two_on)):
                    total = jnp.sum(moved * raw, axis=0, keepdims=True)
                    acc_ref[0, 4 + 3 * j + s : 5 + 3 * j + s, cols] = total
                    value += taps_ref[j, s : s + 1, one] * moved
                mine_cols = pl.ds(pl.multiple_of(base + j * LANES, LANES), LANES)
                all_ref[:, mine_cols] = value.astype(BF16)

                @pl.when(p == pairs - 1)
                def _():
                    grads = dot(nt_ref[...], all_ref[:, mine_cols]).astype(BF16)
                    spot = (fed + pairs - 1,) + (slice(None),) * (inner_bits + 1) + (slice(j * LANES, (j + 1) * LANES),)
                    g_ref[spot] = grads.reshape(g_ref.shape[1:-1] + (LANES,))
                    tick(("last", j))

            @pl.when(p < pairs - 1)
            def _():
                grads = dot(nt_ref[...], all_ref[:, pl.ds(base, 3 * LANES)]).astype(BF16)
                g_ref[fed + p] = grads.reshape(g_ref.shape[1:])

            at_pair(p, "taps")
            return 0

        lax.fori_loop(0, pairs, one_pair, 0)

    def tail(all_ref, wcat_ref, late, emb_ref, give_first, own_first, hid_ref, sq_ref, wr_ref):
        emb_load = load(emb_hbm, emb_ref)
        emb_load.start()
        hid_load = load(act_hbm, hid_ref)
        hid_load.start()
        ffn_loads = []
        for c in range(steps):
            for k, wr in ((1, wr_oth_hbm), (0, wr_own_hbm)):
                ffn_loads.append(load(sq_hbm.at[c, k], sq_ref.at[c, k]))
                ffn_loads.append(load(wr.at[pl.ds(c * D, D), :], wr_ref.at[c, k]))
        for copy in ffn_loads:
            copy.start()
        small_step(0)
        for copy in late:
            copy.wait()

        def other_rows(r, rows):
            there = pl.ds(pl.multiple_of(partner * half + r * two_rows, two_rows), two_rows)
            give_first[rows, :] = dot_nt(all_ref[there, :], wcat_ref[...]).astype(BF16)
            tick(("tail", r))

        halves_of(other_rows)
        first_copy = remote(
            give_first, got_first, core_send.at[steps + 1, 0], core_recv.at[steps + 1, 0], head=partner
        )
        first_copy.start()
        small_step(1)

        def own_rows(r, rows):
            here = pl.ds(pl.multiple_of(head * half + r * two_rows, two_rows), two_rows)
            own_first[rows, :] = dot_nt(all_ref[here, :], wcat_ref[...])
            tick(("tail", 2 + r))

        halves_of(own_rows)
        small_step(2)
        emb_load.wait()
        first_copy.wait()
        gain = row_of(gain_first_ref)
        late_ref[0] = jnp.zeros(late_ref.shape[1:], F32)

        def norm_rows(r, rows):
            grad_n = own_first[rows, :] + got_first[rows, :].astype(F32)
            hat, scale = normalise(emb_ref[rows, :])
            late_ref[0, 0:1, :] += jnp.sum(grad_n * hat, axis=0, keepdims=True)
            late_ref[0, 1:2, :] += jnp.sum(grad_n, axis=0, keepdims=True)
            gh_ref[rows, :] = gh_ref[rows, :] + norm_back(grad_n, hat, scale, gain)
            tick(("tail", 4 + r))

        halves_of(norm_rows)
        for copy in group_give:
            copy.start()
        got_group[seat] = late_ref[0]
        gin_store = load(gh_ref, gin_hbm)
        gin_store.start()
        small_step(3)
        hid_load.wait()
        for copy in ffn_loads:
            copy.wait()

        def ffn_rows(first, c):
            rows = slice(first, first + two_rows)
            hid_ref[rows, :] += dot(sq_ref[c, 1, rows, :], wr_ref[c, 1]) + dot(sq_ref[c, 0, rows, :], wr_ref[c, 0])

        for c in range(steps):
            ffn_rows(0, c)
            if c < 2:
                tick(("tail", 6 + c))
        for copy in group_take:
            copy.wait_recv()
        total = got_group[0]
        for k in range(1, group):
            total = total + got_group[k]
        late_ref[1] = total
        for copy in outer_give:
            copy.start()
        got_outer[line] = total
        small_step(4)
        for c in range(steps):
            ffn_rows(two_rows, c)
            if c < 2:
                tick(("tail", 8 + c))
        act_store = load(hid_ref, act_hbm)
        act_store.start()
        small_step(5)
        for copy in outer_take:
            copy.wait_recv()
        total = got_outer[0]
        for k in range(1, outer):
            total = total + got_outer[k]
        now, k = 6, 6
        while plan or k < small_steps:
            tick(("tail", now))
            if k < small_steps:
                small_step(k)
            now, k = now + 1, k + 1
        small_ref[0:2, :] = total[0:2, :]
        gin_store.wait()
        act_store.wait()
        for copy in group_give + outer_give:
            copy.wait_send()

    def backward(all_ref, wcat_ref):
        late = []
        for p in range(pairs):
            for j, w_hbm in enumerate((wq_hbm, wk_hbm, wv_hbm)):
                base = (3 * p + j) * LANES
                late.append(load(w_hbm.at[:, pl.ds(p * LANES, LANES)], wcat_ref.at[:, pl.ds(base, LANES)]))
        pl.run_scoped(
            lambda nt, mix, *rest: attention(all_ref, wcat_ref, nt, mix, late, *rest),
            pltpu.VMEM((D, slot), BF16),
            pltpu.VMEM((3, slot + 8, LANES), F32),
            pltpu.VMEM((LANES, slot), BF16),
            pltpu.VMEM((LANES, slot), BF16),
            pltpu.VMEM((2, slot, LANES), BF16),
            pltpu.VMEM((2, slot, LANES), BF16),
            pltpu.VMEM((2, slot, LANES), BF16),
            pltpu.VMEM((2, LANES, slot), F32),
            pltpu.VMEM((2, slot, LANES), BF16),
            pltpu.VMEM((2, slot, LANES), BF16),
            pltpu.VMEM((2, slot, LANES), BF16),
            pltpu.VMEM((2, slot, LANES), BF16),
            pltpu.VMEM((2, slot, 3 * LANES), BF16),
            pltpu.VMEM((2, slot, LANES), F32),
            pltpu.VMEM((4, 2, slot, BLOCK), BF16),
            pltpu.SemaphoreType.DMA((2, 6)),
            pltpu.SemaphoreType.DMA((4,)),
        )
        pl.run_scoped(
            functools.partial(tail, all_ref, wcat_ref, late),
            pltpu.VMEM((half, D), F32),
            pltpu.VMEM((half, D), BF16),
            pltpu.VMEM((half, D), F32),
            pltpu.VMEM((half, D), F32),
            pltpu.VMEM((steps, 2, half, D), BF16),
            pltpu.VMEM((steps, 2, D, D), BF16),
        )

    pl.run_scoped(backward, pltpu.VMEM((slot, 3 * local), BF16), pltpu.VMEM((D, 3 * local), BF16))
    for n in range(len(entries)):
        drain(n)
    for k in range(inner_bits + 1):
        small_copy(k).wait_send()
    for k in range(inner_bits + 1, inner_bits + 1 + line_steps):
        pl.when(line_sender(k - 1 - inner_bits))(lambda k=k: small_copy(k).wait_send())


def finish_kernel(
    gr_in, ge_in, go_in, qkv_in, act_in, gin_in, small_in,
    act_ref, gin_ref, q_ref, k_ref, v_ref, go_ref, ge_ref, gr_ref, taps_ref, *vec_refs,
):
    act_ref[...] = act_in[...]
    gin_ref[...] = gin_in[...]
    for j, ref in enumerate((q_ref, k_ref, v_ref)):
        ref[...] = qkv_in[0, :, j * LANES : (j + 1) * LANES].astype(F32)
    ge_ref[...] = ge_in[0].astype(F32)
    gr_ref[...] = gr_in[0].astype(F32)

    @pl.when(pl.program_id(0) == 0)
    def _():
        go_ref[...] = go_in[0].astype(F32)
        for j in range(3):
            taps_ref[j] = small_in[4 + 3 * j : 7 + 3 * j, :]
        for k, ref in enumerate(vec_refs):
            ref[...] = small_in[k, :]


def params(vmem, **kw):
    return pltpu.CompilerParams(vmem_limit_bytes=vmem * MIB, **kw)


def body(
    token_ids, lengths, query_weight, key_weight, value_weight, output_weight,
    expand_weight, reduce_weight, dconv_taps, gain_first, bias_first,
    gain_second, bias_second, cotangent,
):
    half = token_ids.shape[1]
    slot = 2 * half
    local = query_weight.shape[1]
    units = expand_weight.shape[1]
    pairs = local // LANES
    outer = lax.axis_size("outer")
    inner = lax.axis_size("inner")
    inner_bits = inner.bit_length() - 1
    rows = D // inner
    width = 3 * LANES

    shape = jax.ShapeDtypeStruct
    smem = pl.BlockSpec(memory_space=pltpu.SMEM)
    anywhere = pl.BlockSpec(memory_space=pl.ANY)
    dma = pltpu.SemaphoreType.DMA
    vec = whole((D,))

    column = pl.BlockSpec((D, LANES), lambda p: (0, p))
    taps_spec = pl.BlockSpec((3, 3, LANES), lambda p: (0, 0, p))
    pair_rows = pl.BlockSpec((slot, LANES), lambda p: (0, p))
    raw_spec = pl.BlockSpec((slot, 3 * LANES), lambda p: (0, p))
    (
        attended, queries, key_rows, value_rows, raw, inverse, embedded, normed_t, att_oth,
        we_oth, wr_oth, wo_oth, terms,
    ) = pl.pallas_call(
        forward_kernel,
        grid=(pairs,),
        in_specs=[smem, whole((1, half)), vec, vec, column, column, column, taps_spec] + [anywhere] * 3,
        out_specs=[pair_rows] * 4 + [raw_spec, pair_rows] + [anywhere] * 7,
        out_shape=[shape((slot, local), BF16)] * 4
        + [shape((slot, 3 * local), BF16), shape((slot, local), F32), shape((half, D), F32), shape((D, slot), BF16)]
        + [shape((slot, local), BF16)]
        + [shape(w.shape, BF16) for w in (expand_weight, reduce_weight, output_weight)]
        + [shape((2 * pairs, slot, slot), BF16)],
        scratch_shapes=[
            pltpu.VMEM((half, D), F32),
            pltpu.VMEM((D, slot), BF16),
            pltpu.VMEM((slot, D), BF16),
            pltpu.VMEM((2, 3, BLOCK + 8, LANES), F32),
            pltpu.VMEM((D, 3 * LANES), BF16),
            pltpu.VMEM((2, slot, LANES), BF16),
            pltpu.VMEM((2, LANES, slot), BF16),
            pltpu.VMEM((2, slot, LANES), BF16),
            pltpu.VMEM((2, slot, slot), BF16),
            pltpu.VMEM((pairs, slot, LANES), BF16),
            dma((PIECES,)), dma((PIECES,)), dma((pairs, slot // BLOCK)), dma((pairs, slot // BLOCK)), dma((3,)), dma((3,)),
            dma((slot // BLOCK,)), dma((1 + pairs,)),
        ],
        compiler_params=params(58, collective_id=0, has_side_effects=True),
        name="attention_forward",
    )(
        lengths, token_ids, gain_first, bias_first,
        query_weight, key_weight, value_weight, dconv_taps, expand_weight, reduce_weight, output_weight,
    )

    steps = units // D
    split = D // width
    fed = 2 * steps * split + 1
    chunks = fed + pairs
    twos = (2,) * inner_bits
    line_stages = inner_bits + outer
    vmem = lambda dims, kind: pltpu.VMEM(dims, kind)
    sums, small, activations, grad_input, _ = pl.pallas_call(
        functools.partial(layer_kernel, inner_bits, outer),
        in_specs=[smem, vec, vec, vec, whole((3, 3, local))] + [anywhere] * 20,
        out_specs=[whole((chunks, rows, width)), whole((16, D)), anywhere, anywhere, anywhere],
        out_shape=[
            shape((chunks, rows, width), BF16), shape((16, D), F32), shape((half, D), F32), shape((half, D), F32),
            shape((steps, 2, half, D), BF16),
        ],
        scratch_shapes=[
            vmem((half, D), F32),
            vmem((chunks,) + twos + (rows, width), BF16),
            vmem((chunks, rows, width), BF16),
            vmem((chunks, rows, width), BF16),
            vmem((slot, local), BF16),
            vmem((2, 2, D, D), BF16),
            vmem((D, local), BF16),
            vmem((half, D), BF16),
            vmem((inner_bits + 2, 16, D), F32),
            vmem((inner_bits + 3, 16, D), F32),
            vmem((2, 8, D), F32),
            vmem((2 * inner, 8, D), F32),
            vmem((outer, 8, D), F32),
            dma((12 + 10 * steps + 3 * pairs,)),
            dma((2 * chunks + 1, line_stages)), dma((2 * chunks + 1, line_stages)),
            dma((line_stages + 1,)), dma((line_stages + 1,)),
            dma((steps + 2, 2)), dma((steps + 2, 2)),
            dma((2 * inner,)), dma((2 * inner,)), dma((outer,)), dma((outer,)),
        ]
        + [vmem((chunks,) + (2,) * (inner_bits - 1 - s) + (rows, width), BF16) for s in range(inner_bits)],
        compiler_params=params(63, collective_id=1, has_side_effects=True),
        name="layer",
    )(
        lengths, gain_first, gain_second, bias_second, dconv_taps,
        att_oth, embedded, cotangent[0], output_weight, wo_oth,
        expand_weight, we_oth, reduce_weight, wr_oth, query_weight, key_weight, value_weight,
        attended, queries, key_rows, value_rows, raw, inverse, normed_t, terms,
    )
    many = steps * split
    part = half // many
    some_rows = pl.BlockSpec((part, D), lambda i: (i, 0))
    pick = lambda index: pl.BlockSpec((1, rows, width), lambda i: (index(i), 0, 0))
    last = lambda i: jnp.minimum(i, pairs - 1)
    chunk_at = lambda i: (i // split) * 2 * split + i % split
    out_pair = pl.BlockSpec((rows, LANES), lambda i: (0, last(i)))
    activations, grad_input, gq, gk, gv, go_sum, ge_sum, gr_sum, tap_sum, *vec_sums = pl.pallas_call(
        finish_kernel,
        grid=(many,),
        in_specs=[
            pick(chunk_at), pick(lambda i: chunk_at(i) + split), pick(lambda i: fed - 1),
            pick(lambda i: fed + last(i)), some_rows, some_rows, whole((16, D)),
        ],
        out_specs=[
            some_rows, some_rows, out_pair, out_pair, out_pair, whole((rows, local)),
            pl.BlockSpec((rows, width), lambda i: (0, i)), pl.BlockSpec((rows, width), lambda i: (0, i)),
            whole((3, 3, D)), vec, vec, vec, vec,
        ],
        out_shape=[shape((half, D), F32)] * 2
        + [shape((rows, local), F32)] * 4
        + [shape((rows, units), F32)] * 2
        + [shape((3, 3, D), F32)]
        + [shape((D,), F32)] * 4,
        compiler_params=params(62),
        name="finish",
    )(sums, sums, sums, sums, activations, grad_input, small)
    return (
        activations[None],
        grad_input[None],
        gq,
        gk,
        gv,
        go_sum.T,
        ge_sum,
        gr_sum.T,
        tap_sum,
        *vec_sums,
    )


def solution(mesh):
    return jax.shard_map(
        body,
        mesh=mesh,
        in_specs=(
            P(("outer", "inner"), "head"),
            P(("outer", "inner")),
            P(None, "head"),
            P(None, "head"),
            P(None, "head"),
            P("head", None),
            P(None, "head"),
            P("head", None),
            P(None, None, "head"),
            P(),
            P(),
            P(),
            P(),
            P(("outer", "inner"), "head", None),
        ),
        out_specs=(
            P(("outer", "inner"), "head", None),
            P(("outer", "inner"), "head", None),
            P("inner", "head"),
            P("inner", "head"),
            P("inner", "head"),
            P("head", "inner"),
            P("inner", "head"),
            P("head", "inner"),
            P(),
            P(),
            P(),
            P(),
            P(),
        ),
        check_vma=False,
    )
```

```python
import functools
import math

import jax
import jax.numpy as jnp
from jax import lax
from jax.experimental import pallas as pl
from jax.experimental.pallas import tpu as pltpu
from jax.sharding import PartitionSpec as P

HEAD_DIM = 64
D = 768
BLOCK = 256
LANES = 128
EPS = 1e-05
MODULUS = 32749
NEGATIVE = -1e30
SCALE = HEAD_DIM ** (-0.5)
F32 = jnp.float32
BF16 = jnp.bfloat16
MIB = 1024 * 1024

SINE = (
    4.442882913726386,
    -7.308248583654593,
    3.606466623722958,
    -0.8474403474577161,
    0.11605422299047748,
    -0.010267162611370253,
    0.0005523348366953617,
)


def dot(a, b):
    return lax.dot_general(a, b, (((1,), (0,)), ((), ())), preferred_element_type=F32)


def dot_nt(a, b):
    return lax.dot_general(a, b, (((1,), (1,)), ((), ())), preferred_element_type=F32)


def whole(shape):
    return pl.BlockSpec(shape, lambda *_: (0,) * len(shape))


def normalise(values):
    centre = values - jnp.mean(values, axis=-1, keepdims=True)
    spread = jnp.mean(centre * centre, axis=-1, keepdims=True)
    scale = lax.rsqrt(spread + EPS)
    return centre * scale, scale


def norm_back(grad, hat, scale, gain):
    q = grad * gain
    mean_q = jnp.mean(q, axis=-1, keepdims=True)
    mean_qh = jnp.mean(q * hat, axis=-1, keepdims=True)
    return scale * (q - mean_q - hat * mean_qh)


def lane_ids(rows):
    return lax.broadcasted_iota(jnp.int32, (rows, LANES), 1)


def split_three(column):
    high = column.astype(BF16).astype(F32)
    rest = column - high
    middle = rest.astype(BF16).astype(F32)
    return high, middle, rest - middle


def with_parts(base, lane, offset, column):
    high, middle, small = split_three(column)
    base = jnp.where(lane == offset + 1, high, base)
    base = jnp.where(lane == offset + 2, middle, base)
    return jnp.where(lane == offset + 3, small, base)


def remote(src, dst, send, recv, **place):
    return pltpu.make_async_remote_copy(
        src_ref=src, dst_ref=dst, send_sem=send, recv_sem=recv,
        device_id=place, device_id_type=pl.DeviceIdType.MESH,
    )


def greet(*places):
    barrier = pltpu.get_barrier_semaphore()
    for place in places:
        pl.semaphore_signal(barrier, inc=1, device_id=place, device_id_type=pl.DeviceIdType.MESH)
    pl.semaphore_wait(barrier, len(places))


def rows_of(which, half):
    return pl.ds(pl.multiple_of(which * half, half), half)


def remainder(product):
    turns = jnp.floor(product.astype(F32) * (1.0 / MODULUS) + 0.5)
    return (product - turns.astype(jnp.int32) * MODULUS).astype(F32)


def embed_rows(tok_ref, gain, bias, emb_ref, normed_ref, base, first):
    tokens = jnp.broadcast_to(tok_ref[:, pl.ds(first, LANES)], (LANES, LANES)).T
    column = lax.broadcasted_iota(jnp.int32, (1, LANES), 1)
    start = remainder(tokens * (column + 1) + column * column)
    stride = remainder(tokens * LANES + column * (2 * LANES))
    parts = []
    for c in range(D // LANES):
        phase = start + (stride * float(c) + float(c * c * LANES * LANES))
        u = (phase - jnp.floor(phase * (1.0 / MODULUS) + 0.5) * float(MODULUS)) * (2.0 / MODULUS)
        z = u * u
        value = jnp.full_like(u, SINE[-1])
        for coefficient in SINE[-2::-1]:
            value = value * z + coefficient
        parts.append(value * u)
    embedded = jnp.concatenate(parts, axis=1)
    emb_ref[pl.ds(first, LANES), :] = embedded
    hat, _ = normalise(embedded)
    rows = pl.ds(pl.multiple_of(base + first, LANES), LANES)
    normed_ref[rows, :] = (hat * gain + bias).astype(BF16)


PIECES = 3


def row_of(ref):
    return ref[...].reshape(1, D)


def forward_kernel(
    len_ref, tok_ref, gain_ref, bias_ref, wq_ref, wk_ref, wv_ref, taps_ref, we_hbm, wr_hbm, wo_hbm,
    att_ref, q_ref, k_ref, v_ref, raw_ref, rinv_ref,
    emb_hbm, nt_hbm, att_oth_hbm, we_oth_hbm, wr_oth_hbm, wo_oth_hbm, terms_hbm,
    emb_ref, nt_ref, normed_ref, shift_ref, wcat_ref, qa_ref, ka_ref, va_ref, terms_ref, give_ref,
    row_send, row_recv, att_send, att_recv, weight_send, weight_recv, terms_sem, store_sem,
):
    slot = att_ref.shape[0]
    half = slot // 2
    blocks = slot // BLOCK
    step = pl.program_id(0)
    pairs = att_oth_hbm.shape[1] // LANES
    head = lax.axis_index("head")
    partner = 1 - head
    piece = half // PIECES

    def row_copy(k):
        rows = pl.ds(pl.multiple_of(head * half + k * piece, piece), piece)
        return remote(normed_ref.at[rows], normed_ref.at[rows], row_send.at[k], row_recv.at[k], head=partner)

    def att_copy(p, i):
        rows = pl.ds(i * BLOCK, BLOCK)
        land = att_oth_hbm.at[rows, pl.ds(pl.multiple_of(p * LANES, LANES), LANES)]
        return remote(give_ref.at[p, rows], land, att_send.at[p, i], att_recv.at[p, i], head=partner)

    def weight_copy(k):
        src, dst = ((wo_hbm, wo_oth_hbm), (we_hbm, we_oth_hbm), (wr_hbm, wr_oth_hbm))[k]
        return remote(src, dst, weight_send.at[k], weight_recv.at[k], head=partner)

    def emb_store():
        return pltpu.make_async_copy(emb_ref, emb_hbm, store_sem.at[0])

    def nt_store(p):
        part = pl.ds(p * (D // pairs), D // pairs)
        return pltpu.make_async_copy(nt_ref.at[part], nt_hbm.at[part], store_sem.at[1 + p])

    def terms_copy(p, i):
        rows, cols = pl.ds(i * BLOCK, BLOCK), pl.ds(0, (i + 1) * BLOCK)
        return pltpu.make_async_copy(
            terms_ref.at[:, rows, cols], terms_hbm.at[pl.ds(2 * p, 2), rows, cols], terms_sem.at[i]
        )

    @pl.when(step == 0)
    def _():
        greet({"head": partner})
        base = head * half
        for k in range(PIECES):
            def embed_step(i, _):
                first = pl.multiple_of(k * piece + i * LANES, LANES)
                embed_rows(tok_ref, row_of(gain_ref), row_of(bias_ref), emb_ref, normed_ref, base, first)
                return 0

            lax.fori_loop(0, piece // LANES, embed_step, 0)
            row_copy(k).start()
        for k in range(3):
            weight_copy(k).start()
        emb_store().start()
        for k in range(PIECES):
            row_copy(k).wait()

    for j, w_ref in enumerate((wq_ref, wk_ref, wv_ref)):
        wcat_ref[:, j * LANES : (j + 1) * LANES] = w_ref[...]
    shift_ref[0, :, 0:8, :] = jnp.zeros((3, 8, LANES), F32)
    lane = lane_ids(BLOCK)
    features = D // pairs
    some = pl.ds(pl.multiple_of(step * features, features), features)

    def raws_of(r):
        return dot(normed_ref[r * BLOCK : (r + 1) * BLOCK, :], wcat_ref[...])

    coming = raws_of(0)
    for r in range(blocks):
        rows = slice(r * BLOCK, (r + 1) * BLOCK)
        raws = coming
        if r + 1 < blocks:
            coming = raws_of(r + 1)
        raw_ref[rows, :] = raws.astype(BF16)
        nt_ref[some, rows] = normed_ref[rows, some].T
        mixed = []
        this, after = r % 2, (r + 1) % 2
        for j in range(3):
            raw = raws[:, j * LANES : (j + 1) * LANES]
            shift_ref[this, j, 8 : 8 + BLOCK, :] = raw
            one = shift_ref[this, j, 7 : 7 + BLOCK, :]
            two = shift_ref[this, j, 6 : 6 + BLOCK, :]
            value = taps_ref[j, 0:1, :] * raw + taps_ref[j, 1:2, :] * one + taps_ref[j, 2:3, :] * two
            mixed.append(value * SCALE if j == 0 else value)
            shift_ref[after, j, 0:8, :] = raw[BLOCK - 8 :, :]
        for ref, value in zip((q_ref, k_ref, v_ref), mixed):
            ref[rows, :] = value.astype(BF16)
        row = lax.broadcasted_iota(jnp.int32, (BLOCK, 1), 0) + r * BLOCK
        key_bias = jnp.where(row < len_ref[0], 0.0, NEGATIVE)
        for e in range(2):
            mine = (lane // HEAD_DIM) == e
            other = HEAD_DIM * (1 - e)
            qa_ref[e, rows, :] = jnp.where(mine, mixed[0], jnp.where(lane == other, 1.0, 0.0)).astype(BF16)
            key = jnp.where(mine, mixed[1], jnp.where(lane == other, key_bias, 0.0)).astype(BF16)
            ka_ref[e, :, rows] = key.T
            va_ref[e, rows, :] = jnp.where(mine, mixed[2], jnp.where(lane == other, 1.0, 0.0)).astype(BF16)

    @pl.when(step > 0)
    def _():
        for i in range(blocks):
            terms_copy(step - 1, i).wait()

    causal = lax.broadcasted_iota(jnp.int32, (BLOCK, BLOCK), 1) <= lax.broadcasted_iota(
        jnp.int32, (BLOCK, BLOCK), 0
    )
    tasks = [(i, e) for i in range(blocks) for e in range(2)]

    def scores_of(i, e):
        rows = slice(i * BLOCK, (i + 1) * BLOCK)
        query = qa_ref[e, rows, :]
        diagonal = jnp.where(causal, dot(query, ka_ref[e, :, rows]), NEGATIVE)
        before = dot(query, ka_ref[e, :, : i * BLOCK]) if i else None
        return diagonal, before

    coming = scores_of(*tasks[0])
    outs = []
    for t, (i, e) in enumerate(tasks):
        diagonal, before = coming
        if t + 1 < len(tasks):
            coming = scores_of(*tasks[t + 1])
        rows = slice(i * BLOCK, (i + 1) * BLOCK)
        other = HEAD_DIM * (1 - e)
        row_max = jnp.max(diagonal, axis=1, keepdims=True)
        if i:
            row_max = jnp.maximum(row_max, jnp.max(before, axis=1, keepdims=True))
        terms = jnp.exp(diagonal - row_max).astype(BF16)
        terms_ref[e, rows, rows] = terms
        out = dot(terms, va_ref[e, rows, :])
        if i:
            terms = jnp.exp(before - row_max).astype(BF16)
            terms_ref[e, rows, : i * BLOCK] = terms
            out += dot(terms, va_ref[e, : i * BLOCK, :])
        inverse = 1.0 / out[:, other : other + 1]
        outs.append((out, inverse))
        if e == 1:
            first_head = lane < HEAD_DIM
            inverse = jnp.where(first_head, outs[0][1], outs[1][1])
            attended = (jnp.where(first_head, outs[0][0], outs[1][0]) * inverse).astype(BF16)
            att_ref[rows, :] = attended
            give_ref[step, rows, :] = attended
            att_copy(step, i).start()
            rinv_ref[rows, :] = inverse
            outs = []
            terms_copy(step, i).start()

    for p in range(pairs):
        @pl.when(step == p)
        def _():
            nt_store(p).start()

    @pl.when(step == pairs - 1)
    def _():
        for p in range(pairs):
            for i in range(blocks):
                att_copy(p, i).wait()
            nt_store(p).wait()
        emb_store().wait()
        for k in range(3):
            weight_copy(k).wait()
        for i in range(blocks):
            terms_copy(step, i).wait()


def plan_sums(entries, ready, points, tail, inner_bits, line_steps, orders, rate=0.05, hop=1.8):
    stages = inner_bits + line_steps + 1
    done, arrive, free, plan, begun = [0] * len(entries), {}, {}, {}, set()

    def step_of(n, now):
        chunk, size, kind = entries[n]
        stage = done[n]
        if stage < inner_bits:
            link, part = ("bit", orders[kind][stage]), size / 2 ** (stage + 1)
        else:
            t = stage - inner_bits
            link, part = ("line", t), size / 2**inner_bits
        if stage < stages - 1:
            free[link] = max(free.get(link, 0.0), now) + part / rate
            arrive[n] = free[link] + hop
        done[n] += 1

    at, now, late = 0, 0.0, 0
    while at < len(points) or any(d < stages for d in done):
        if at < len(points):
            place, when = points[at]
            now, slack = max(now, when), 0.3 if place[0] != "tail" else 0.0
        else:
            place, slack = ("tail", tail + late), 0.0
            late += 1
            now = max(now, min(arrive[n] for n in range(len(entries)) if done[n] < stages))
        at += 1
        for n, (chunk, _, _) in enumerate(entries):
            if ready[n] == place:
                begun.add(n)
        while True:
            able = [n for n in begun if done[n] < stages and (done[n] == 0 or arrive[n] <= now - slack)]
            if not able:
                break
            n = min(able, key=lambda m: (-done[m], m))
            plan.setdefault(place, []).append((n, done[n]))
            step_of(n, now)
    return plan


def layer_kernel(
    inner_bits, outer,
    len_ref, gain_first_ref, gain_second_ref, bias_second_ref, taps_ref,
    att_oth_hbm, emb_hbm, cot_hbm, wo_own_hbm, wo_oth_hbm,
    we_own_hbm, we_oth_hbm, wr_own_hbm, wr_oth_hbm, wq_hbm, wk_hbm, wv_hbm,
    att_hbm, q_hbm, k_hbm, v_hbm, raw_hbm, rinv_hbm, nt_hbm, terms_hbm,
    sum_ref, small_ref, act_hbm, gin_hbm, sq_hbm,
    gh_ref, g_ref, rz_ref, rc_ref, do_ref, got_ref, got_go, got_first, acc_ref, got_small, late_ref, got_group, got_outer,
    load_sem, send_sem, recv_sem, small_send, small_recv, core_send, core_recv,
    group_send, group_recv, outer_send, outer_recv, *halves,
):
    half = gh_ref.shape[0]
    slot = 2 * half
    local = att_oth_hbm.shape[1]
    units = we_own_hbm.shape[1]
    steps = units // D
    width = sum_ref.shape[2]
    split = D // width
    pairs = local // LANES
    fed = 2 * steps * split + 1
    blocks = slot // BLOCK
    head = lax.axis_index("head")
    partner = 1 - head
    mine = lax.axis_index("inner")
    line = lax.axis_index("outer")
    centre = outer // 2
    left = line < centre
    depth = jnp.where(left, centre - 1 - line, line - centre)
    inward = jnp.where(left, line + 1, line - 1)
    outward = jnp.where(left, line - 1, line + 1)
    bit = [(mine // (1 << b)) % 2 for b in range(inner_bits)]
    across = [mine + (1 << b) * (1 - 2 * bit[b]) for b in range(inner_bits)]

    def chunk_of(c, kind, k):
        return (2 * c + kind) * split + k

    entries = []
    for c in range(fed):
        entries.append((c, 0, width, c % 2))
    for c in range(fed, fed + pairs - 1):
        entries += [(c, 0, 2 * LANES, c % 2), (c, 2 * LANES, LANES, 1 - c % 2)]
    entries += [(fed + pairs - 1, j * LANES, LANES, j % 2) for j in range(3)]
    order_of = [tuple((b + first) % inner_bits for b in range(inner_bits)) for first in range(2)]
    line_steps = 2 * centre - 1
    stage_count = inner_bits + line_steps + 1

    def index_of(fixed):
        return tuple(fixed.get(b, slice(None)) for b in reversed(range(inner_bits)))

    def lanes(entry):
        return slice(entry[1], entry[1] + entry[2])

    def halving(n, s):
        c, _, _, kind = entries[n]
        order = order_of[kind]
        fixed = {b: bit[b] for b in order[:s]}
        b = order[s]
        give = g_ref.at[(c,) + index_of({**fixed, b: 1 - bit[b]}) + (slice(None), lanes(entries[n]))]
        land = halves[s].at[(c,) + (slice(None),) * (inner_bits - 1 - s) + (slice(None), lanes(entries[n]))]
        return remote(give, land, send_sem.at[n, s], recv_sem.at[n, s], inner=across[b])

    def add_half(n, s):
        c, _, _, kind = entries[n]
        order = order_of[kind]
        index = (c,) + index_of({b: bit[b] for b in order[: s + 1]}) + (slice(None), lanes(entries[n]))
        land = (c,) + (slice(None),) * (inner_bits - 1 - s) + (slice(None), lanes(entries[n]))
        g_ref[index] = g_ref[index] + halves[s][land]

    def own(n):
        return (entries[n][0],) + tuple(bit[b] for b in reversed(range(inner_bits))) + (slice(None), lanes(entries[n]))

    def flat(n):
        return (entries[n][0], slice(None), lanes(entries[n]))

    def line_sender(t):
        if t < centre - 1:
            return depth == centre - 1 - t
        if t == centre - 1:
            return depth == 0
        return depth == t - centre

    def line_copy(n, t):
        s = inner_bits + t
        sems = (send_sem.at[n, s], recv_sem.at[n, s])
        if t < centre - 1:
            return remote(g_ref.at[own(n)], rz_ref.at[flat(n)], *sems, outer=inward)
        if t == centre - 1:
            return remote(g_ref.at[own(n)], rc_ref.at[flat(n)], *sems, outer=inward)
        return remote(rc_ref.at[flat(n)], rc_ref.at[flat(n)], *sems, outer=outward)

    def line_finish(n, t):
        if t < centre - 1:
            @pl.when(depth == centre - 2 - t)
            def _():
                line_copy(n, t).wait_recv()
                g_ref[own(n)] = g_ref[own(n)] + rz_ref[flat(n)]
        elif t == centre - 1:
            @pl.when(depth == 0)
            def _():
                line_copy(n, t).wait_recv()
                rc_ref[flat(n)] = g_ref[own(n)] + rc_ref[flat(n)]
        else:
            pl.when(depth == t - centre + 1)(lambda: line_copy(n, t).wait_recv())

    def advance(n, stage):
        if 0 < stage <= inner_bits:
            halving(n, stage - 1).wait_recv()
            add_half(n, stage - 1)
        elif stage > inner_bits:
            line_finish(n, stage - inner_bits - 1)
        if stage < inner_bits:
            halving(n, stage).start()
        elif stage < stage_count - 1:
            t = stage - inner_bits
            pl.when(line_sender(t))(lambda: line_copy(n, t).start())
        else:
            sum_ref[flat(n)] = rc_ref[flat(n)]

    def drain(n):
        for s in range(inner_bits):
            halving(n, s).wait_send()
        for t in range(line_steps):
            pl.when(line_sender(t))(lambda t=t: line_copy(n, t).wait_send())

    points = []
    now = 6.0
    for c in range(steps):
        for k, spent in enumerate((2.3, 2.3, 0.3, 2.3, 2.3, 1.2)):
            now += spent
            points.append((("feed", c, k), now))
        now += 1.1
    for k in range(3):
        now += 1.2
        points.append((("norm", k), now))
    for p in range(pairs):
        now += 1.2
        for j in range(0, blocks, 2):
            points.append((("pair", p, j), now))
            now += 8.0 * (2 * (blocks - j) - 1) * 2 / (blocks * (blocks + 1))
        if p < pairs - 1:
            now += 2.8
            points.append((("taps", p), now))
    for j in (2, 1, 0):
        now += 1.3
        points.append((("last", j), now))
    for k, spent in enumerate((0.8, 0.8, 0.8, 0.8, 1.5, 1.5, 1.4, 1.4, 1.4, 1.4)):
        now += spent
        points.append((("tail", k), now))
    ready = {}
    for c in range(steps):
        for k in range(split):
            ready[chunk_of(c, 0, k)] = ("feed", c, 2)
            ready[chunk_of(c, 1, k)] = ("feed", c, 5)
    ready[fed - 1] = ("norm", 2)
    for p in range(pairs - 1):
        ready[fed + p] = ("taps", p)
    ready_at = [ready[c] if c in ready else ("last", first // LANES) for c, first, _, _ in entries]
    plan = plan_sums(
        [(c, 2e-6 * D * wide, kind) for c, _, wide, kind in entries],
        ready_at, points, 10, inner_bits, line_steps, order_of,
    )

    def tick(place):
        for n, stage in plan.pop(place, ()):
            advance(n, stage)

    def small_copy(k):
        sems = (small_send.at[k], small_recv.at[k])
        if k == 0:
            return remote(acc_ref.at[0], got_small.at[0], *sems, head=partner)
        if k <= inner_bits:
            return remote(acc_ref.at[k], got_small.at[k], *sems, inner=across[k - 1])
        t = k - 1 - inner_bits
        if t <= centre - 1:
            return remote(acc_ref.at[inner_bits + 1], got_small.at[inner_bits + 1 + (t == centre - 1)], *sems, outer=inward)
        last = got_small.at[inner_bits + 2]
        return remote(last, last, *sems, outer=outward)

    def small_step(k):
        if 0 < k <= inner_bits + 1:
            small_copy(k - 1).wait_recv()
            acc_ref[k] = acc_ref[k - 1] + got_small[k - 1]
        elif k > inner_bits + 1:
            t = k - 2 - inner_bits
            if t < centre - 1:
                @pl.when(depth == centre - 2 - t)
                def _():
                    small_copy(k - 1).wait_recv()
                    acc_ref[inner_bits + 1] = acc_ref[inner_bits + 1] + got_small[inner_bits + 1]
            elif t == centre - 1:
                @pl.when(depth == 0)
                def _():
                    small_copy(k - 1).wait_recv()
                    got_small[inner_bits + 2] = acc_ref[inner_bits + 1] + got_small[inner_bits + 2]
            else:
                pl.when(depth == t - centre + 1)(lambda: small_copy(k - 1).wait_recv())
        if k <= inner_bits:
            small_copy(k).start()
        elif k <= inner_bits + line_steps:
            pl.when(line_sender(k - 1 - inner_bits))(lambda: small_copy(k).start())
        else:
            small_ref[...] = got_small[inner_bits + 2]

    small_steps = inner_bits + line_steps + 2

    inner = 1 << inner_bits
    group = 2 * inner
    seat = mine * 2 + head

    def group_place(k, way):
        other = lax.rem(seat + group + way * k, group)
        return other, {"inner": other // 2, "head": lax.rem(other, 2)}

    def outer_place(k, way):
        other = lax.rem(line + outer + way * k, outer)
        return other, {"outer": other}

    def late_copies(places, count, me, src, land, sends, recvs):
        give = [remote(src, land.at[me], sends.at[k], recvs.at[k], **places(k, 1)[1]) for k in range(1, count)]
        take = [
            remote(src, land.at[places(k, -1)[0]], sends.at[k], recvs.at[k], **places(k, 1)[1]) for k in range(1, count)
        ]
        return give, take

    group_give, group_take = late_copies(
        group_place, group, seat, late_ref.at[0], got_group, group_send, group_recv
    )
    outer_give, outer_take = late_copies(outer_place, outer, line, late_ref.at[1], got_outer, outer_send, outer_recv)

    load_count = iter(range(load_sem.shape[0]))

    def load(src, dst):
        return pltpu.make_async_copy(src, dst, load_sem.at[next(load_count)])

    row = lax.broadcasted_iota(jnp.int32, (half, 1), 0) + head * half
    valid = row < len_ref[0]

    def greet_all():
        barrier = pltpu.get_barrier_semaphore()
        places = [group_place(k, 1)[1] for k in range(1, group)] + [outer_place(k, 1)[1] for k in range(1, outer)]
        for place in places:
            pl.semaphore_signal(barrier, inc=1, device_id=place, device_id_type=pl.DeviceIdType.MESH)
        return lambda: pl.semaphore_wait(barrier, len(places))

    two_rows = half // 2

    def halves_of(step):
        for r in range(2):
            step(r, pl.ds(r * two_rows, two_rows))

    def feed_forward(
        att_ref, wo_ref, we_ref, wr_ref, cot_ref, hid_ref, gn_ref,
        n2_ref, n2t_ref, gl_ref, glt_ref, give_ref, relu_ref, sq_ref,
    ):
        give_att = relu_ref.at[0, :, 0:local]
        give_go = relu_ref.at[1, :, 0:local]
        loads = {}
        for k, (att, wo) in enumerate(((att_hbm.at[rows_of(head, half), :], wo_own_hbm), (att_oth_hbm.at[rows_of(head, half), :], wo_oth_hbm))):
            loads["att", k] = load(att, att_ref.at[k])
            loads["wo", k] = load(wo, wo_ref.at[k])
        loads["emb"] = load(emb_hbm, hid_ref)
        loads["cot"] = load(cot_hbm, cot_ref)
        for c in range(steps):
            cols = pl.ds(c * D, D)
            for k, we in ((1, we_oth_hbm), (0, we_own_hbm)):
                loads["we", c, k] = load(we.at[:, cols], we_ref.at[c, k])
            for k, wr in ((1, wr_oth_hbm), (0, wr_own_hbm)):
                loads["wr", c, k] = load(wr.at[cols, :], wr_ref.at[c, k])
        weights = {c: [copy for key, copy in loads.items() if key[0] in ("we", "wr") and key[1] == c] for c in range(steps)}
        for key, copy in loads.items():
            if key[0] not in ("we", "wr"):
                copy.start()
        all_here = greet_all()
        for key in (("att", 0), ("wo", 0), ("att", 1), ("wo", 1), "emb", "cot"):
            loads[key].wait()
        for copy in weights[0]:
            copy.start()
        gain, bias = row_of(gain_second_ref), row_of(bias_second_ref)

        def open_rows(r, rows):
            hidden = hid_ref[rows, :] + dot(att_ref[0, rows, :], wo_ref[0]) + dot(att_ref[1, rows, :], wo_ref[1])
            hid_ref[rows, :] = hidden
            hat, _ = normalise(hidden)
            normed = (hat * gain + bias).astype(BF16)
            n2_ref[rows, :] = normed
            n2t_ref[:, rows] = normed.T
            position = lax.broadcasted_iota(jnp.int32, (two_rows, 1), 0) + head * half + r * two_rows
            grad = jnp.where(position < len_ref[0], cot_ref[rows, :], 0.0)
            cot_ref[rows, :] = grad
            gl_ref[rows, :] = grad.astype(BF16)
            glt_ref[:, rows] = grad.astype(BF16).T

        halves_of(open_rows)
        hid_store = load(hid_ref, act_hbm)
        hid_store.start()

        def grad_copy(c, kind):
            return remote(
                give_ref.at[kind], got_ref.at[c % 2, kind], core_send.at[c, kind], core_recv.at[c, kind], head=partner
            )

        def put_own(c, kind, value):
            for k in range(split):
                part = value[:, k * width : (k + 1) * width].astype(BF16)
                g_ref[chunk_of(c, kind, k)] = part.reshape(g_ref.shape[1:])

        def add_other(c, kind):
            grad_copy(c, kind).wait_recv()
            for k in range(split):
                got = got_ref[c % 2, kind, :, k * width : (k + 1) * width]
                g_ref[chunk_of(c, kind, k)] += got.reshape(g_ref.shape[1:])

        def weight_grad(c, kind, k, left_ref, right):
            grad = dot(left_ref[...], right)
            if k == 1:
                if c:
                    grad_copy(c - 1, kind).wait_send()
                elif kind == 0:
                    all_here()
                give_ref[kind] = grad.astype(BF16)
                grad_copy(c, kind).start()
            else:
                put_own(c, kind, grad)

        stores = []
        for c in range(steps):
            for k in (1, 0):
                loads["we", c, k].wait()
                relu = jnp.maximum(dot(n2_ref[...], we_ref[c, k]), 0.0)
                relu_ref[k] = relu.astype(BF16)
                sq_ref[c, k] = (relu * relu).astype(BF16)
                stores.append(load(sq_ref.at[c, k], sq_hbm.at[c, k]))
                stores[-1].start()
                weight_grad(c, 0, k, glt_ref, sq_ref[c, k])
                tick(("feed", c, 1 - k))
            if c + 1 < steps:
                for copy in weights[c + 1]:
                    copy.start()
            add_other(c, 0)
            tick(("feed", c, 2))
            for k in (1, 0):
                loads["wr", c, k].wait()
                back = dot_nt(gl_ref[...], wr_ref[c, k])
                relu_ref[k] = (back * (2.0 * relu_ref[k].astype(F32))).astype(BF16)
                weight_grad(c, 1, k, n2t_ref, relu_ref[k])
                tick(("feed", c, 4 - k))
            for k in (1, 0):
                gn = dot_nt(relu_ref[k], we_ref[c, k])
                if c == 0 and k == 1:
                    gn_ref[...] = gn
                else:
                    gn_ref[...] += gn
                if k == 1:
                    add_other(c, 1)
                    tick(("feed", c, 5))
        acc_ref[0] = jnp.zeros(acc_ref.shape[1:], F32)

        def close_rows(r, rows):
            hat, scale = normalise(hid_ref[rows, :])
            grad_n = gn_ref[rows, :]
            acc_ref[0, 2:3, :] += jnp.sum(grad_n * hat, axis=0, keepdims=True)
            acc_ref[0, 3:4, :] += jnp.sum(grad_n, axis=0, keepdims=True)
            grad_h = cot_ref[rows, :] + norm_back(grad_n, hat, scale, gain)
            gh_ref[rows, :] = grad_h
            low = grad_h.astype(BF16)
            n2_ref[rows, :] = low
            n2t_ref[:, rows] = low.T
            give_att[rows, :] = dot_nt(low, wo_ref[1]).astype(BF16)

        halves_of(close_rows)
        own_rows = rows_of(head, half)
        att_copy = remote(give_att, do_ref.at[own_rows], core_send.at[steps, 0], core_recv.at[steps, 0], head=partner)
        att_copy.start()
        tick(("norm", 0))
        give_go[...] = dot(n2t_ref[...], att_ref[1]).astype(BF16)
        go_copy = remote(give_go, got_go, core_send.at[steps, 1], core_recv.at[steps, 1], head=partner)
        go_copy.start()
        do_ref[own_rows, :] = dot_nt(n2_ref[...], wo_ref[0]).astype(BF16)
        tick(("norm", 1))
        grad_o = dot(n2t_ref[...], att_ref[0]).astype(BF16)
        go_copy.wait()
        g_ref[fed - 1] = (grad_o + got_go[...]).reshape(g_ref.shape[1:])
        tick(("norm", 2))
        for kind in range(2):
            grad_copy(steps - 1, kind).wait_send()
        for copy in [hid_store] + stores:
            copy.wait()
        att_copy.wait()

    pl.run_scoped(
        feed_forward,
        pltpu.VMEM((2, half, local), BF16), pltpu.VMEM((2, local, D), BF16),
        pltpu.VMEM((steps, 2, D, D), BF16), pltpu.VMEM((steps, 2, D, D), BF16),
        pltpu.VMEM((half, D), F32), pltpu.VMEM((half, D), F32), pltpu.VMEM((half, D), F32),
        pltpu.VMEM((half, D), BF16), pltpu.VMEM((D, half), BF16),
        pltpu.VMEM((half, D), BF16), pltpu.VMEM((D, half), BF16),
        pltpu.VMEM((2, D, D), BF16), pltpu.VMEM((2, half, D), BF16), pltpu.VMEM((steps, 2, half, D), BF16),
    )

    def attention(
        all_ref, wcat_ref, nt_ref, mix_ref, late, dot_ref, qt_ref, doa_ref, kz_ref, va_ref, turned_ref,
        att_ref, q_ref, k_ref, v_ref, raw_ref, rinv_ref, terms_ref, pair_sem, terms_sem,
    ):
        def pair_loads(p, place):
            one = pl.ds(p * LANES, LANES)
            three = pl.ds(p * 3 * LANES, 3 * LANES)
            return [
                pltpu.make_async_copy(rinv_hbm.at[:, one], rinv_ref.at[place], pair_sem.at[place, 0]),
                pltpu.make_async_copy(att_hbm.at[:, one], att_ref.at[place], pair_sem.at[place, 1]),
                pltpu.make_async_copy(v_hbm.at[:, one], v_ref.at[place], pair_sem.at[place, 2]),
                pltpu.make_async_copy(q_hbm.at[:, one], q_ref.at[place], pair_sem.at[place, 3]),
                pltpu.make_async_copy(k_hbm.at[:, one], k_ref.at[place], pair_sem.at[place, 4]),
                pltpu.make_async_copy(raw_hbm.at[:, three], raw_ref.at[place], pair_sem.at[place, 5]),
            ]

        def terms_load(p, j):
            rows = pl.ds(j * BLOCK, slot - j * BLOCK)
            spot = (blocks * p + j) % 4
            return pltpu.make_async_copy(
                terms_hbm.at[pl.ds(2 * p, 2), rows, pl.ds(j * BLOCK, BLOCK)],
                terms_ref.at[spot, :, rows, :],
                terms_sem.at[spot],
            )

        for copy in pair_loads(0, 0):
            copy.start()
        for j in range(2):
            terms_load(0, j).start()
        nt_load = load(nt_hbm, nt_ref)
        nt_load.start()
        for copy in late:
            copy.start()
        mix_ref[:, slot : slot + 8, :] = jnp.zeros((3, 8, LANES), F32)
        lane = lane_ids(slot)

        def at_pair(p, kind, *rest):
            tick((kind, p) + rest)

        def one_pair(p):
            place = p % 2
            one = pl.ds(p * LANES, LANES)
            if p + 1 < pairs:
                for copy in pair_loads(p + 1, 1 - place):
                    copy.start()

            for copy in pair_loads(p, place):
                copy.wait()
            scaled = (do_ref[:, one].astype(F32) * rinv_ref[place]).astype(BF16)
            dot_ref[...] = scaled.T
            qt_ref[...] = q_ref[place].T
            product = scaled.astype(F32) * att_ref[place].astype(F32)
            for e in range(2):
                in_head = (lane // HEAD_DIM) == e
                delta = -jnp.sum(jnp.where(in_head, product, 0.0), axis=1, keepdims=True)
                other = HEAD_DIM * (1 - e)
                ones = jnp.where((lane > other) & (lane < other + 4), 1.0, 0.0)
                doa_ref[e] = with_parts(jnp.where(in_head, scaled.astype(F32), 0.0), lane, other, delta).astype(BF16)
                va_ref[e] = jnp.where(in_head, v_ref[place].astype(F32), ones).astype(BF16)
                kz_ref[e] = jnp.where(in_head, k_ref[place].astype(F32), 0.0).astype(BF16)

            def grads_of(j, e):
                return dot_nt(doa_ref[e, j * BLOCK :, :], va_ref[e, j * BLOCK : (j + 1) * BLOCK, :])

            for j0 in range(0, blocks, 2):
                at_pair(p, "pair", j0)
                for j in (j0, j0 + 1):
                    terms_load(p, j).wait()
                    if j + 2 < blocks:
                        terms_load(p, j + 2).start()
                    elif p + 1 < pairs:
                        terms_load(p + 1, j + 2 - blocks).start()
                tasks = [(j, e) for j in (j0, j0 + 1) for e in range(2)]
                coming = grads_of(*tasks[0])
                for t, (j, e) in enumerate(tasks):
                    back = coming
                    if t + 1 < len(tasks):
                        coming = grads_of(*tasks[t + 1])
                    first = j * BLOCK
                    keys = slice(first, first + BLOCK)
                    mine_rows = slice(e * HEAD_DIM, (e + 1) * HEAD_DIM)
                    terms = terms_ref[(blocks * p + j) % 4, e, first:, :]
                    grads = (terms.astype(F32) * back).astype(BF16)
                    part = dot(grads, kz_ref[e, keys, :])
                    if j == 0 and e == 0:
                        mix_ref[0, first:slot, :] = part
                    else:
                        mix_ref[0, first:slot, :] += part
                    turned_ref[0, mine_rows, keys] = dot(qt_ref[mine_rows, first:], grads)
                    turned_ref[1, mine_rows, keys] = dot(dot_ref[mine_rows, first:], terms)
            mix_ref[0, 0:slot, :] = mix_ref[0, 0:slot, :] * SCALE
            mix_ref[1, 0:slot, :] = turned_ref[0].T
            mix_ref[2, 0:slot, :] = turned_ref[1].T
            base = p * 3 * LANES
            if p == 0:
                nt_load.wait()

            for j in (2, 1, 0):
                zero = mix_ref[j, 0:slot, :]
                one_on = mix_ref[j, 1 : 1 + slot, :]
                two_on = mix_ref[j, 2 : 2 + slot, :]
                raw = raw_ref[place, :, j * LANES : (j + 1) * LANES].astype(F32)
                cols = pl.ds(pl.multiple_of(head * local + p * LANES, LANES), LANES)
                value = 0.0
                for s, moved in enumerate((zero, one_on, two_on)):
                    total = jnp.sum(moved * raw, axis=0, keepdims=True)
                    acc_ref[0, 4 + 3 * j + s : 5 + 3 * j + s, cols] = total
                    value += taps_ref[j, s : s + 1, one] * moved
                mine_cols = pl.ds(base + j * LANES, LANES)
                all_ref[:, mine_cols] = value.astype(BF16)
                if p == pairs - 1:
                    grads = dot(nt_ref[...], all_ref[:, mine_cols]).astype(BF16)
                    spot = (fed + pairs - 1,) + (slice(None),) * (inner_bits + 1) + (slice(j * LANES, (j + 1) * LANES),)
                    g_ref[spot] = grads.reshape(g_ref.shape[1:-1] + (LANES,))
                    tick(("last", j))

            if p < pairs - 1:
                grads = dot(nt_ref[...], all_ref[:, pl.ds(base, 3 * LANES)]).astype(BF16)
                g_ref[fed + p] = grads.reshape(g_ref.shape[1:])
                at_pair(p, "taps")

        for p in range(pairs):
            one_pair(p)

    def tail(all_ref, wcat_ref, late, emb_ref, give_first, own_first, hid_ref, sq_ref, wr_ref):
        emb_load = load(emb_hbm, emb_ref)
        emb_load.start()
        hid_load = load(act_hbm, hid_ref)
        hid_load.start()
        ffn_loads = []
        for c in range(steps):
            for k, wr in ((1, wr_oth_hbm), (0, wr_own_hbm)):
                ffn_loads.append(load(sq_hbm.at[c, k], sq_ref.at[c, k]))
                ffn_loads.append(load(wr.at[pl.ds(c * D, D), :], wr_ref.at[c, k]))
        for copy in ffn_loads:
            copy.start()
        small_step(0)
        for copy in late:
            copy.wait()

        def other_rows(r, rows):
            there = pl.ds(pl.multiple_of(partner * half + r * two_rows, two_rows), two_rows)
            give_first[rows, :] = dot_nt(all_ref[there, :], wcat_ref[...]).astype(BF16)
            tick(("tail", r))

        halves_of(other_rows)
        first_copy = remote(
            give_first, got_first, core_send.at[steps + 1, 0], core_recv.at[steps + 1, 0], head=partner
        )
        first_copy.start()
        small_step(1)

        def own_rows(r, rows):
            here = pl.ds(pl.multiple_of(head * half + r * two_rows, two_rows), two_rows)
            own_first[rows, :] = dot_nt(all_ref[here, :], wcat_ref[...])
            tick(("tail", 2 + r))

        halves_of(own_rows)
        small_step(2)
        emb_load.wait()
        first_copy.wait()
        gain = row_of(gain_first_ref)
        late_ref[0] = jnp.zeros(late_ref.shape[1:], F32)

        def norm_rows(r, rows):
            grad_n = own_first[rows, :] + got_first[rows, :].astype(F32)
            hat, scale = normalise(emb_ref[rows, :])
            late_ref[0, 0:1, :] += jnp.sum(grad_n * hat, axis=0, keepdims=True)
            late_ref[0, 1:2, :] += jnp.sum(grad_n, axis=0, keepdims=True)
            gh_ref[rows, :] = gh_ref[rows, :] + norm_back(grad_n, hat, scale, gain)
            tick(("tail", 4 + r))

        halves_of(norm_rows)
        for copy in group_give:
            copy.start()
        got_group[seat] = late_ref[0]
        gin_store = load(gh_ref, gin_hbm)
        gin_store.start()
        small_step(3)
        hid_load.wait()
        for copy in ffn_loads:
            copy.wait()

        def ffn_rows(first, c):
            rows = slice(first, first + two_rows)
            hid_ref[rows, :] += dot(sq_ref[c, 1, rows, :], wr_ref[c, 1]) + dot(sq_ref[c, 0, rows, :], wr_ref[c, 0])

        for c in range(steps):
            ffn_rows(0, c)
            if c < 2:
                tick(("tail", 6 + c))
        for copy in group_take:
            copy.wait_recv()
        total = got_group[0]
        for k in range(1, group):
            total = total + got_group[k]
        late_ref[1] = total
        for copy in outer_give:
            copy.start()
        got_outer[line] = total
        small_step(4)
        for c in range(steps):
            ffn_rows(two_rows, c)
            if c < 2:
                tick(("tail", 8 + c))
        act_store = load(hid_ref, act_hbm)
        act_store.start()
        small_step(5)
        for copy in outer_take:
            copy.wait_recv()
        total = got_outer[0]
        for k in range(1, outer):
            total = total + got_outer[k]
        now, k = 6, 6
        while plan or k < small_steps:
            tick(("tail", now))
            if k < small_steps:
                small_step(k)
            now, k = now + 1, k + 1
        small_ref[0:2, :] = total[0:2, :]
        gin_store.wait()
        act_store.wait()
        for copy in group_give + outer_give:
            copy.wait_send()

    def backward(all_ref, wcat_ref):
        late = []
        for p in range(pairs):
            for j, w_hbm in enumerate((wq_hbm, wk_hbm, wv_hbm)):
                base = (3 * p + j) * LANES
                late.append(load(w_hbm.at[:, pl.ds(p * LANES, LANES)], wcat_ref.at[:, pl.ds(base, LANES)]))
        pl.run_scoped(
            lambda nt, mix, *rest: attention(all_ref, wcat_ref, nt, mix, late, *rest),
            pltpu.VMEM((D, slot), BF16),
            pltpu.VMEM((3, slot + 8, LANES), F32),
            pltpu.VMEM((LANES, slot), BF16),
            pltpu.VMEM((LANES, slot), BF16),
            pltpu.VMEM((2, slot, LANES), BF16),
            pltpu.VMEM((2, slot, LANES), BF16),
            pltpu.VMEM((2, slot, LANES), BF16),
            pltpu.VMEM((2, LANES, slot), F32),
            pltpu.VMEM((2, slot, LANES), BF16),
            pltpu.VMEM((2, slot, LANES), BF16),
            pltpu.VMEM((2, slot, LANES), BF16),
            pltpu.VMEM((2, slot, LANES), BF16),
            pltpu.VMEM((2, slot, 3 * LANES), BF16),
            pltpu.VMEM((2, slot, LANES), F32),
            pltpu.VMEM((4, 2, slot, BLOCK), BF16),
            pltpu.SemaphoreType.DMA((2, 6)),
            pltpu.SemaphoreType.DMA((4,)),
        )
        pl.run_scoped(
            functools.partial(tail, all_ref, wcat_ref, late),
            pltpu.VMEM((half, D), F32),
            pltpu.VMEM((half, D), BF16),
            pltpu.VMEM((half, D), F32),
            pltpu.VMEM((half, D), F32),
            pltpu.VMEM((steps, 2, half, D), BF16),
            pltpu.VMEM((steps, 2, D, D), BF16),
        )

    pl.run_scoped(backward, pltpu.VMEM((slot, 3 * local), BF16), pltpu.VMEM((D, 3 * local), BF16))
    for n in range(len(entries)):
        drain(n)
    for k in range(inner_bits + 1):
        small_copy(k).wait_send()
    for k in range(inner_bits + 1, inner_bits + 1 + line_steps):
        pl.when(line_sender(k - 1 - inner_bits))(lambda k=k: small_copy(k).wait_send())


def finish_kernel(
    split, sum_hbm, act_hbm, gin_hbm, small_ref,
    act_out, gin_out, q_out, k_out, v_out, go_out, ge_out, gr_out, taps_ref, *rest,
):
    vec_refs, (sum_ref, wide_ref, load_sem, store_sem, copy_sem) = rest[:-5], rest[-5:]
    chunks, _, width = sum_hbm.shape
    pairs = q_out.shape[1] // LANES
    fed = chunks - pairs
    copies = []
    half = act_hbm.shape[0] // 2
    for k, (src, dst) in enumerate(((act_hbm, act_out), (gin_hbm, gin_out))):
        for r in range(2):
            rows = pl.ds(r * half, half)
            copies.append(pltpu.make_async_copy(src.at[rows], dst.at[rows], copy_sem.at[2 * k + r]))
    loads = [pltpu.make_async_copy(sum_hbm.at[c], sum_ref.at[c], load_sem.at[c]) for c in range(chunks)]
    for copy in loads + copies:
        copy.start()
    for j in range(3):
        taps_ref[j] = small_ref[4 + 3 * j : 7 + 3 * j, :]
    for k, ref in enumerate(vec_refs):
        ref[...] = small_ref[k, :]
    stores = []

    def store(src, dst):
        stores.append(pltpu.make_async_copy(src, dst, store_sem.at[len(stores)]))
        stores[-1].start()

    for c in range(chunks):
        loads[c].wait()
        wide_ref[c] = sum_ref[c].astype(F32)
        if c < fed - 1:
            step, kind, k = c // (2 * split), (c // split) % 2, c % split
            store(wide_ref.at[c], (gr_out, ge_out)[kind].at[:, pl.ds((step * split + k) * width, width)])
        elif c == fed - 1:
            store(wide_ref.at[c], go_out)
        else:
            for j, out in enumerate((q_out, k_out, v_out)):
                part = wide_ref.at[c, :, pl.ds(j * LANES, LANES)]
                store(part, out.at[:, pl.ds((c - fed) * LANES, LANES)])
    for copy in stores + copies:
        copy.wait()


def params(vmem, **kw):
    return pltpu.CompilerParams(vmem_limit_bytes=vmem * MIB, **kw)


def body(
    token_ids, lengths, query_weight, key_weight, value_weight, output_weight,
    expand_weight, reduce_weight, dconv_taps, gain_first, bias_first,
    gain_second, bias_second, cotangent,
):
    half = token_ids.shape[1]
    slot = 2 * half
    local = query_weight.shape[1]
    units = expand_weight.shape[1]
    pairs = local // LANES
    outer = lax.axis_size("outer")
    inner = lax.axis_size("inner")
    inner_bits = inner.bit_length() - 1
    rows = D // inner
    width = 3 * LANES

    shape = jax.ShapeDtypeStruct
    smem = pl.BlockSpec(memory_space=pltpu.SMEM)
    anywhere = pl.BlockSpec(memory_space=pl.ANY)
    dma = pltpu.SemaphoreType.DMA
    vec = whole((D,))

    column = pl.BlockSpec((D, LANES), lambda p: (0, p))
    taps_spec = pl.BlockSpec((3, 3, LANES), lambda p: (0, 0, p))
    pair_rows = pl.BlockSpec((slot, LANES), lambda p: (0, p))
    raw_spec = pl.BlockSpec((slot, 3 * LANES), lambda p: (0, p))
    (
        attended, queries, key_rows, value_rows, raw, inverse, embedded, normed_t, att_oth,
        we_oth, wr_oth, wo_oth, terms,
    ) = pl.pallas_call(
        forward_kernel,
        grid=(pairs,),
        in_specs=[smem, whole((1, half)), vec, vec, column, column, column, taps_spec] + [anywhere] * 3,
        out_specs=[pair_rows] * 4 + [raw_spec, pair_rows] + [anywhere] * 7,
        out_shape=[shape((slot, local), BF16)] * 4
        + [shape((slot, 3 * local), BF16), shape((slot, local), F32), shape((half, D), F32), shape((D, slot), BF16)]
        + [shape((slot, local), BF16)]
        + [shape(w.shape, BF16) for w in (expand_weight, reduce_weight, output_weight)]
        + [shape((2 * pairs, slot, slot), BF16)],
        scratch_shapes=[
            pltpu.VMEM((half, D), F32),
            pltpu.VMEM((D, slot), BF16),
            pltpu.VMEM((slot, D), BF16),
            pltpu.VMEM((2, 3, BLOCK + 8, LANES), F32),
            pltpu.VMEM((D, 3 * LANES), BF16),
            pltpu.VMEM((2, slot, LANES), BF16),
            pltpu.VMEM((2, LANES, slot), BF16),
            pltpu.VMEM((2, slot, LANES), BF16),
            pltpu.VMEM((2, slot, slot), BF16),
            pltpu.VMEM((pairs, slot, LANES), BF16),
            dma((PIECES,)), dma((PIECES,)), dma((pairs, slot // BLOCK)), dma((pairs, slot // BLOCK)), dma((3,)), dma((3,)),
            dma((slot // BLOCK,)), dma((1 + pairs,)),
        ],
        compiler_params=params(58, collective_id=0, has_side_effects=True),
        name="attention_forward",
    )(
        lengths, token_ids, gain_first, bias_first,
        query_weight, key_weight, value_weight, dconv_taps, expand_weight, reduce_weight, output_weight,
    )

    steps = units // D
    split = D // width
    fed = 2 * steps * split + 1
    chunks = fed + pairs
    twos = (2,) * inner_bits
    line_stages = inner_bits + outer
    vmem = lambda dims, kind: pltpu.VMEM(dims, kind)
    sums, small, activations, grad_input, _ = pl.pallas_call(
        functools.partial(layer_kernel, inner_bits, outer),
        in_specs=[smem, vec, vec, vec, whole((3, 3, local))] + [anywhere] * 20,
        out_specs=[whole((chunks, rows, width)), whole((16, D)), anywhere, anywhere, anywhere],
        out_shape=[
            shape((chunks, rows, width), BF16), shape((16, D), F32), shape((half, D), F32), shape((half, D), F32),
            shape((steps, 2, half, D), BF16),
        ],
        scratch_shapes=[
            vmem((half, D), F32),
            vmem((chunks,) + twos + (rows, width), BF16),
            vmem((chunks, rows, width), BF16),
            vmem((chunks, rows, width), BF16),
            vmem((slot, local), BF16),
            vmem((2, 2, D, D), BF16),
            vmem((D, local), BF16),
            vmem((half, D), BF16),
            vmem((inner_bits + 2, 16, D), F32),
            vmem((inner_bits + 3, 16, D), F32),
            vmem((2, 8, D), F32),
            vmem((2 * inner, 8, D), F32),
            vmem((outer, 8, D), F32),
            dma((12 + 10 * steps + 3 * pairs,)),
            dma((2 * chunks + 1, line_stages)), dma((2 * chunks + 1, line_stages)),
            dma((line_stages + 1,)), dma((line_stages + 1,)),
            dma((steps + 2, 2)), dma((steps + 2, 2)),
            dma((2 * inner,)), dma((2 * inner,)), dma((outer,)), dma((outer,)),
        ]
        + [vmem((chunks,) + (2,) * (inner_bits - 1 - s) + (rows, width), BF16) for s in range(inner_bits)],
        compiler_params=params(63, collective_id=1, has_side_effects=True),
        name="layer",
    )(
        lengths, gain_first, gain_second, bias_second, dconv_taps,
        att_oth, embedded, cotangent[0], output_weight, wo_oth,
        expand_weight, we_oth, reduce_weight, wr_oth, query_weight, key_weight, value_weight,
        attended, queries, key_rows, value_rows, raw, inverse, normed_t, terms,
    )
    vmem_all = pl.BlockSpec(memory_space=pltpu.VMEM)
    activations, grad_input, gq, gk, gv, go_sum, ge_sum, gr_sum, tap_sum, *vec_sums = pl.pallas_call(
        functools.partial(finish_kernel, split),
        in_specs=[anywhere] * 3 + [vmem_all],
        out_specs=[anywhere] * 8 + [vmem_all] * 5,
        out_shape=[shape((half, D), F32)] * 2
        + [shape((rows, local), F32)] * 4
        + [shape((rows, units), F32)] * 2
        + [shape((3, 3, D), F32)]
        + [shape((D,), F32)] * 4,
        scratch_shapes=[
            vmem((chunks, rows, width), BF16), vmem((chunks, rows, width), F32),
            dma((chunks,)), dma((fed + 3 * pairs,)), dma((4,)),
        ],
        compiler_params=params(62),
        name="finish",
    )(sums, activations, grad_input, small)
    return (
        activations[None],
        grad_input[None],
        gq,
        gk,
        gv,
        go_sum.T,
        ge_sum,
        gr_sum.T,
        tap_sum,
        *vec_sums,
    )


def solution(mesh):
    return jax.shard_map(
        body,
        mesh=mesh,
        in_specs=(
            P(("outer", "inner"), "head"),
            P(("outer", "inner")),
            P(None, "head"),
            P(None, "head"),
            P(None, "head"),
            P("head", None),
            P(None, "head"),
            P("head", None),
            P(None, None, "head"),
            P(),
            P(),
            P(),
            P(),
            P(("outer", "inner"), "head", None),
        ),
        out_specs=(
            P(("outer", "inner"), "head", None),
            P(("outer", "inner"), "head", None),
            P("inner", "head"),
            P("inner", "head"),
            P("inner", "head"),
            P("head", "inner"),
            P("inner", "head"),
            P("head", "inner"),
            P(),
            P(),
            P(),
            P(),
            P(),
        ),
        check_vma=False,
    )
```

```python
import functools
import math

import jax
import jax.numpy as jnp
from jax import lax
from jax.experimental import pallas as pl
from jax.experimental.pallas import tpu as pltpu
from jax.sharding import PartitionSpec as P

HEAD_DIM = 64
D = 768
BLOCK = 256
LANES = 128
EPS = 1e-05
MODULUS = 32749
NEGATIVE = -1e30
SCALE = HEAD_DIM ** (-0.5)
F32 = jnp.float32
BF16 = jnp.bfloat16
MIB = 1024 * 1024

SINE = (
    4.442882913726386,
    -7.308248583654593,
    3.606466623722958,
    -0.8474403474577161,
    0.11605422299047748,
    -0.010267162611370253,
    0.0005523348366953617,
)


def dot(a, b):
    return lax.dot_general(a, b, (((1,), (0,)), ((), ())), preferred_element_type=F32)


def dot_nt(a, b):
    return lax.dot_general(a, b, (((1,), (1,)), ((), ())), preferred_element_type=F32)


def whole(shape):
    return pl.BlockSpec(shape, lambda *_: (0,) * len(shape))


def normalise(values):
    centre = values - jnp.mean(values, axis=-1, keepdims=True)
    spread = jnp.mean(centre * centre, axis=-1, keepdims=True)
    scale = lax.rsqrt(spread + EPS)
    return centre * scale, scale


def norm_back(grad, hat, scale, gain):
    q = grad * gain
    mean_q = jnp.mean(q, axis=-1, keepdims=True)
    mean_qh = jnp.mean(q * hat, axis=-1, keepdims=True)
    return scale * (q - mean_q - hat * mean_qh)


def lane_ids(rows):
    return lax.broadcasted_iota(jnp.int32, (rows, LANES), 1)


def split_three(column):
    high = column.astype(BF16).astype(F32)
    rest = column - high
    middle = rest.astype(BF16).astype(F32)
    return high, middle, rest - middle


def with_parts(base, lane, offset, column):
    high, middle, small = split_three(column)
    base = jnp.where(lane == offset + 1, high, base)
    base = jnp.where(lane == offset + 2, middle, base)
    return jnp.where(lane == offset + 3, small, base)


def remote(src, dst, send, recv, **place):
    return pltpu.make_async_remote_copy(
        src_ref=src, dst_ref=dst, send_sem=send, recv_sem=recv,
        device_id=place, device_id_type=pl.DeviceIdType.MESH,
    )


def greet(*places):
    barrier = pltpu.get_barrier_semaphore()
    for place in places:
        pl.semaphore_signal(barrier, inc=1, device_id=place, device_id_type=pl.DeviceIdType.MESH)
    pl.semaphore_wait(barrier, len(places))


def rows_of(which, half):
    return pl.ds(pl.multiple_of(which * half, half), half)


def remainder(product):
    turns = jnp.floor(product.astype(F32) * (1.0 / MODULUS) + 0.5)
    return (product - turns.astype(jnp.int32) * MODULUS).astype(F32)


def embed_rows(tok_ref, gain, bias, emb_ref, normed_ref, base, first):
    tokens = jnp.broadcast_to(tok_ref[:, pl.ds(first, LANES)], (LANES, LANES)).T
    column = lax.broadcasted_iota(jnp.int32, (1, LANES), 1)
    start = remainder(tokens * (column + 1) + column * column)
    stride = remainder(tokens * LANES + column * (2 * LANES))
    parts = []
    for c in range(D // LANES):
        phase = start + (stride * float(c) + float(c * c * LANES * LANES))
        u = (phase - jnp.floor(phase * (1.0 / MODULUS) + 0.5) * float(MODULUS)) * (2.0 / MODULUS)
        z = u * u
        value = jnp.full_like(u, SINE[-1])
        for coefficient in SINE[-2::-1]:
            value = value * z + coefficient
        parts.append(value * u)
    embedded = jnp.concatenate(parts, axis=1)
    emb_ref[pl.ds(first, LANES), :] = embedded
    hat, _ = normalise(embedded)
    rows = pl.ds(pl.multiple_of(base + first, LANES), LANES)
    normed_ref[rows, :] = (hat * gain + bias).astype(BF16)


PIECES = 3


def row_of(ref):
    return ref[...].reshape(1, D)


def forward_kernel(
    len_ref, tok_ref, gain_ref, bias_ref, wq_ref, wk_ref, wv_ref, taps_ref, we_hbm, wr_hbm, wo_hbm,
    att_ref, q_ref, k_ref, v_ref, raw_ref, rinv_ref,
    emb_hbm, nt_hbm, att_oth_hbm, we_oth_hbm, wr_oth_hbm, wo_oth_hbm, terms_hbm,
    wo_ref, we_ref, wr_ref, emb_ref, nt_ref, normed_ref, shift_ref, wcat_ref, qa_ref, ka_ref, va_ref, terms_ref, give_ref,
    row_send, row_recv, att_send, att_recv, weight_send, weight_recv, terms_sem, store_sem,
):
    slot = att_ref.shape[0]
    half = slot // 2
    blocks = slot // BLOCK
    step = pl.program_id(0)
    pairs = att_oth_hbm.shape[1] // LANES
    head = lax.axis_index("head")
    partner = 1 - head
    piece = half // PIECES

    def row_copy(k):
        rows = pl.ds(pl.multiple_of(head * half + k * piece, piece), piece)
        return remote(normed_ref.at[rows], normed_ref.at[rows], row_send.at[k], row_recv.at[k], head=partner)

    def att_copy(p, i):
        rows = pl.ds(i * BLOCK, BLOCK)
        land = att_oth_hbm.at[rows, pl.ds(pl.multiple_of(p * LANES, LANES), LANES)]
        return remote(give_ref.at[p, rows], land, att_send.at[p, i], att_recv.at[p, i], head=partner)

    def weight_copy(k):
        src, dst = ((wo_ref, wo_oth_hbm), (we_ref, we_oth_hbm), (wr_ref, wr_oth_hbm))[k]
        return remote(src, dst, weight_send.at[k], weight_recv.at[k], head=partner)

    def weight_load(k):
        src, dst = ((wo_hbm, wo_ref), (we_hbm, we_ref), (wr_hbm, wr_ref))[k]
        return pltpu.make_async_copy(src, dst, store_sem.at[1 + pairs + k])

    def emb_store():
        return pltpu.make_async_copy(emb_ref, emb_hbm, store_sem.at[0])

    def nt_store(p):
        part = pl.ds(pl.multiple_of(p * (D // pairs), D // pairs), D // pairs)
        return pltpu.make_async_copy(nt_ref.at[part], nt_hbm.at[part], store_sem.at[1 + p])

    def terms_copy(p, i):
        rows, cols = pl.ds(i * BLOCK, BLOCK), pl.ds(0, (i + 1) * BLOCK)
        return pltpu.make_async_copy(
            terms_ref.at[:, rows, cols], terms_hbm.at[pl.ds(2 * p, 2), rows, cols], terms_sem.at[i]
        )

    @pl.when(step == 0)
    def _():
        for k in range(3):
            weight_load(k).start()
        greet({"head": partner})
        base = head * half
        for k in range(PIECES):
            def embed_step(i, _):
                first = pl.multiple_of(k * piece + i * LANES, LANES)
                embed_rows(tok_ref, row_of(gain_ref), row_of(bias_ref), emb_ref, normed_ref, base, first)
                return 0

            lax.fori_loop(0, piece // LANES, embed_step, 0)
            row_copy(k).start()
        for k in range(3):
            weight_load(k).wait()
            weight_copy(k).start()
        emb_store().start()
        for k in range(PIECES):
            row_copy(k).wait()

    for j, w_ref in enumerate((wq_ref, wk_ref, wv_ref)):
        wcat_ref[:, j * LANES : (j + 1) * LANES] = w_ref[...]
    shift_ref[0, :, 0:8, :] = jnp.zeros((3, 8, LANES), F32)
    lane = lane_ids(BLOCK)
    features = D // pairs
    some = pl.ds(pl.multiple_of(step * features, features), features)

    def raws_of(r):
        return dot(normed_ref[r * BLOCK : (r + 1) * BLOCK, :], wcat_ref[...])

    coming = raws_of(0)
    for r in range(blocks):
        rows = slice(r * BLOCK, (r + 1) * BLOCK)
        raws = coming
        if r + 1 < blocks:
            coming = raws_of(r + 1)
        raw_ref[rows, :] = raws.astype(BF16)
        nt_ref[some, rows] = normed_ref[rows, some].T
        mixed = []
        this, after = r % 2, (r + 1) % 2
        for j in range(3):
            raw = raws[:, j * LANES : (j + 1) * LANES]
            shift_ref[this, j, 8 : 8 + BLOCK, :] = raw
            one = shift_ref[this, j, 7 : 7 + BLOCK, :]
            two = shift_ref[this, j, 6 : 6 + BLOCK, :]
            value = taps_ref[j, 0:1, :] * raw + taps_ref[j, 1:2, :] * one + taps_ref[j, 2:3, :] * two
            mixed.append(value * SCALE if j == 0 else value)
            shift_ref[after, j, 0:8, :] = raw[BLOCK - 8 :, :]
        for ref, value in zip((q_ref, k_ref, v_ref), mixed):
            ref[rows, :] = value.astype(BF16)
        row = lax.broadcasted_iota(jnp.int32, (BLOCK, 1), 0) + r * BLOCK
        key_bias = jnp.where(row < len_ref[0], 0.0, NEGATIVE)
        for e in range(2):
            mine = (lane // HEAD_DIM) == e
            other = HEAD_DIM * (1 - e)
            qa_ref[e, rows, :] = jnp.where(mine, mixed[0], jnp.where(lane == other, 1.0, 0.0)).astype(BF16)
            key = jnp.where(mine, mixed[1], jnp.where(lane == other, key_bias, 0.0)).astype(BF16)
            ka_ref[e, :, rows] = key.T
            va_ref[e, rows, :] = jnp.where(mine, mixed[2], jnp.where(lane == other, 1.0, 0.0)).astype(BF16)

    nt_store(step).start()

    @pl.when(step > 0)
    def _():
        for i in range(blocks):
            terms_copy(step - 1, i).wait()

    causal = lax.broadcasted_iota(jnp.int32, (BLOCK, BLOCK), 1) <= lax.broadcasted_iota(
        jnp.int32, (BLOCK, BLOCK), 0
    )
    tasks = [(i, e) for i in range(blocks) for e in range(2)]

    def scores_of(i, e):
        rows = slice(i * BLOCK, (i + 1) * BLOCK)
        query = qa_ref[e, rows, :]
        diagonal = jnp.where(causal, dot(query, ka_ref[e, :, rows]), NEGATIVE)
        before = dot(query, ka_ref[e, :, : i * BLOCK]) if i else None
        return diagonal, before

    coming = scores_of(*tasks[0])
    outs = []
    for t, (i, e) in enumerate(tasks):
        diagonal, before = coming
        if t + 1 < len(tasks):
            coming = scores_of(*tasks[t + 1])
        rows = slice(i * BLOCK, (i + 1) * BLOCK)
        other = HEAD_DIM * (1 - e)
        row_max = jnp.max(diagonal, axis=1, keepdims=True)
        if i:
            row_max = jnp.maximum(row_max, jnp.max(before, axis=1, keepdims=True))
        terms = jnp.exp(diagonal - row_max).astype(BF16)
        terms_ref[e, rows, rows] = terms
        out = dot(terms, va_ref[e, rows, :])
        if i:
            terms = jnp.exp(before - row_max).astype(BF16)
            terms_ref[e, rows, : i * BLOCK] = terms
            out += dot(terms, va_ref[e, : i * BLOCK, :])
        inverse = 1.0 / out[:, other : other + 1]
        outs.append((out, inverse))
        if e == 1:
            first_head = lane < HEAD_DIM
            inverse = jnp.where(first_head, outs[0][1], outs[1][1])
            attended = (jnp.where(first_head, outs[0][0], outs[1][0]) * inverse).astype(BF16)
            att_ref[rows, :] = attended
            give_ref[step, rows, :] = attended
            att_copy(step, i).start()
            rinv_ref[rows, :] = inverse
            outs = []
            terms_copy(step, i).start()

    @pl.when(step == pairs - 1)
    def _():
        for p in range(pairs):
            for i in range(blocks):
                att_copy(p, i).wait()
            nt_store(p).wait()
        emb_store().wait()
        for k in range(3):
            weight_copy(k).wait()
        for i in range(blocks):
            terms_copy(step, i).wait()


def plan_sums(entries, ready, points, tail, inner_bits, line_steps, orders, rate=0.05, hop=1.8):
    stages = inner_bits + line_steps + 1
    done, arrive, free, plan, begun = [0] * len(entries), {}, {}, {}, set()

    def step_of(n, now):
        chunk, size, kind = entries[n]
        stage = done[n]
        if stage < inner_bits:
            link, part = ("bit", orders[kind][stage]), size / 2 ** (stage + 1)
        else:
            t = stage - inner_bits
            link, part = ("line", t), size / 2**inner_bits
        if stage < stages - 1:
            free[link] = max(free.get(link, 0.0), now) + part / rate
            arrive[n] = free[link] + hop
        done[n] += 1

    at, now, late = 0, 0.0, 0
    while at < len(points) or any(d < stages for d in done):
        if at < len(points):
            place, when = points[at]
            now, slack = max(now, when), 0.3 if place[0] != "tail" else 0.0
        else:
            place, slack = ("tail", tail + late), 0.0
            late += 1
            now = max(now, min(arrive[n] for n in range(len(entries)) if done[n] < stages))
        at += 1
        for n, (chunk, _, _) in enumerate(entries):
            if ready[n] == place:
                begun.add(n)
        while True:
            able = [n for n in begun if done[n] < stages and (done[n] == 0 or arrive[n] <= now - slack)]
            if not able:
                break
            n = min(able, key=lambda m: (-done[m], m))
            plan.setdefault(place, []).append((n, done[n]))
            step_of(n, now)
    return plan


def layer_kernel(
    inner_bits, outer,
    len_ref, gain_first_ref, gain_second_ref, bias_second_ref, taps_ref,
    att_oth_hbm, emb_hbm, cot_hbm, wo_own_hbm, wo_oth_hbm,
    we_own_hbm, we_oth_hbm, wr_own_hbm, wr_oth_hbm, wq_hbm, wk_hbm, wv_hbm,
    att_hbm, q_hbm, k_hbm, v_hbm, raw_hbm, rinv_hbm, nt_hbm, terms_hbm,
    sum_ref, small_ref, act_hbm, gin_hbm, sq_hbm,
    gh_ref, g_ref, rz_ref, rc_ref, do_ref, got_ref, got_go, got_first, acc_ref, got_small, late_ref, got_group, got_outer,
    load_sem, send_sem, recv_sem, small_send, small_recv, core_send, core_recv,
    group_send, group_recv, outer_send, outer_recv, *halves,
):
    half = gh_ref.shape[0]
    slot = 2 * half
    local = att_oth_hbm.shape[1]
    units = we_own_hbm.shape[1]
    steps = units // D
    width = sum_ref.shape[2]
    split = D // width
    pairs = local // LANES
    fed = 2 * steps * split + 1
    blocks = slot // BLOCK
    head = lax.axis_index("head")
    partner = 1 - head
    mine = lax.axis_index("inner")
    line = lax.axis_index("outer")
    centre = outer // 2
    left = line < centre
    depth = jnp.where(left, centre - 1 - line, line - centre)
    inward = jnp.where(left, line + 1, line - 1)
    outward = jnp.where(left, line - 1, line + 1)
    bit = [(mine // (1 << b)) % 2 for b in range(inner_bits)]
    across = [mine + (1 << b) * (1 - 2 * bit[b]) for b in range(inner_bits)]

    def chunk_of(c, kind, k):
        return (2 * c + kind) * split + k

    entries = []
    for c in range(fed):
        entries.append((c, 0, width, c % 2))
    for c in range(fed, fed + pairs - 1):
        entries += [(c, 0, 2 * LANES, c % 2), (c, 2 * LANES, LANES, 1 - c % 2)]
    entries += [(fed + pairs - 1, j * LANES, LANES, j % 2) for j in range(3)]
    order_of = [tuple((b + first) % inner_bits for b in range(inner_bits)) for first in range(2)]
    line_steps = 2 * centre - 1
    stage_count = inner_bits + line_steps + 1

    def index_of(fixed):
        return tuple(fixed.get(b, slice(None)) for b in reversed(range(inner_bits)))

    def lanes(entry):
        return slice(entry[1], entry[1] + entry[2])

    def halving(n, s):
        c, _, _, kind = entries[n]
        order = order_of[kind]
        fixed = {b: bit[b] for b in order[:s]}
        b = order[s]
        give = g_ref.at[(c,) + index_of({**fixed, b: 1 - bit[b]}) + (slice(None), lanes(entries[n]))]
        land = halves[s].at[(c,) + (slice(None),) * (inner_bits - 1 - s) + (slice(None), lanes(entries[n]))]
        return remote(give, land, send_sem.at[n, s], recv_sem.at[n, s], inner=across[b])

    def add_half(n, s):
        c, _, _, kind = entries[n]
        order = order_of[kind]
        index = (c,) + index_of({b: bit[b] for b in order[: s + 1]}) + (slice(None), lanes(entries[n]))
        land = (c,) + (slice(None),) * (inner_bits - 1 - s) + (slice(None), lanes(entries[n]))
        g_ref[index] = g_ref[index] + halves[s][land]

    def own(n):
        return (entries[n][0],) + tuple(bit[b] for b in reversed(range(inner_bits))) + (slice(None), lanes(entries[n]))

    def flat(n):
        return (entries[n][0], slice(None), lanes(entries[n]))

    def line_sender(t):
        if t < centre - 1:
            return depth == centre - 1 - t
        if t == centre - 1:
            return depth == 0
        return depth == t - centre

    def line_copy(n, t):
        s = inner_bits + t
        sems = (send_sem.at[n, s], recv_sem.at[n, s])
        if t < centre - 1:
            return remote(g_ref.at[own(n)], rz_ref.at[flat(n)], *sems, outer=inward)
        if t == centre - 1:
            return remote(g_ref.at[own(n)], rc_ref.at[flat(n)], *sems, outer=inward)
        return remote(rc_ref.at[flat(n)], rc_ref.at[flat(n)], *sems, outer=outward)

    def line_finish(n, t):
        if t < centre - 1:
            @pl.when(depth == centre - 2 - t)
            def _():
                line_copy(n, t).wait_recv()
                g_ref[own(n)] = g_ref[own(n)] + rz_ref[flat(n)]
        elif t == centre - 1:
            @pl.when(depth == 0)
            def _():
                line_copy(n, t).wait_recv()
                rc_ref[flat(n)] = g_ref[own(n)] + rc_ref[flat(n)]
        else:
            pl.when(depth == t - centre + 1)(lambda: line_copy(n, t).wait_recv())

    def advance(n, stage):
        if 0 < stage <= inner_bits:
            halving(n, stage - 1).wait_recv()
            add_half(n, stage - 1)
        elif stage > inner_bits:
            line_finish(n, stage - inner_bits - 1)
        if stage < inner_bits:
            halving(n, stage).start()
        elif stage < stage_count - 1:
            t = stage - inner_bits
            pl.when(line_sender(t))(lambda: line_copy(n, t).start())
        else:
            sum_ref[flat(n)] = rc_ref[flat(n)]

    def drain(n):
        for s in range(inner_bits):
            halving(n, s).wait_send()
        for t in range(line_steps):
            pl.when(line_sender(t))(lambda t=t: line_copy(n, t).wait_send())

    points = []
    now = 6.0
    for c in range(steps):
        for k, spent in enumerate((2.3, 2.3, 0.3, 2.3, 2.3, 1.2)):
            now += spent
            points.append((("feed", c, k), now))
        now += 1.1
    for k in range(3):
        now += 1.2
        points.append((("norm", k), now))
    for p in range(pairs):
        now += 1.2
        for j in range(0, blocks, 2):
            points.append((("pair", p, j), now))
            now += 8.0 * (2 * (blocks - j) - 1) * 2 / (blocks * (blocks + 1))
        if p < pairs - 1:
            now += 2.8
            points.append((("taps", p), now))
    for j in (2, 1, 0):
        now += 1.3
        points.append((("last", j), now))
    for k, spent in enumerate((0.8, 0.8, 0.8, 0.8, 1.5, 1.5, 1.4, 1.4, 1.4, 1.4)):
        now += spent
        points.append((("tail", k), now))
    ready = {}
    for c in range(steps):
        for k in range(split):
            ready[chunk_of(c, 0, k)] = ("feed", c, 2)
            ready[chunk_of(c, 1, k)] = ("feed", c, 5)
    ready[fed - 1] = ("norm", 2)
    for p in range(pairs - 1):
        ready[fed + p] = ("taps", p)
    ready_at = [ready[c] if c in ready else ("last", first // LANES) for c, first, _, _ in entries]
    plan = plan_sums(
        [(c, 2e-6 * D * wide, kind) for c, _, wide, kind in entries],
        ready_at, points, 10, inner_bits, line_steps, order_of,
    )

    def tick(place):
        for n, stage in plan.pop(place, ()):
            advance(n, stage)

    def small_copy(k):
        sems = (small_send.at[k], small_recv.at[k])
        if k == 0:
            return remote(acc_ref.at[0], got_small.at[0], *sems, head=partner)
        if k <= inner_bits:
            return remote(acc_ref.at[k], got_small.at[k], *sems, inner=across[k - 1])
        t = k - 1 - inner_bits
        if t <= centre - 1:
            return remote(acc_ref.at[inner_bits + 1], got_small.at[inner_bits + 1 + (t == centre - 1)], *sems, outer=inward)
        last = got_small.at[inner_bits + 2]
        return remote(last, last, *sems, outer=outward)

    def small_step(k):
        if 0 < k <= inner_bits + 1:
            small_copy(k - 1).wait_recv()
            acc_ref[k] = acc_ref[k - 1] + got_small[k - 1]
        elif k > inner_bits + 1:
            t = k - 2 - inner_bits
            if t < centre - 1:
                @pl.when(depth == centre - 2 - t)
                def _():
                    small_copy(k - 1).wait_recv()
                    acc_ref[inner_bits + 1] = acc_ref[inner_bits + 1] + got_small[inner_bits + 1]
            elif t == centre - 1:
                @pl.when(depth == 0)
                def _():
                    small_copy(k - 1).wait_recv()
                    got_small[inner_bits + 2] = acc_ref[inner_bits + 1] + got_small[inner_bits + 2]
            else:
                pl.when(depth == t - centre + 1)(lambda: small_copy(k - 1).wait_recv())
        if k <= inner_bits:
            small_copy(k).start()
        elif k <= inner_bits + line_steps:
            pl.when(line_sender(k - 1 - inner_bits))(lambda: small_copy(k).start())
        else:
            small_ref[...] = got_small[inner_bits + 2]

    small_steps = inner_bits + line_steps + 2

    inner = 1 << inner_bits
    group = 2 * inner
    seat = mine * 2 + head

    def group_place(k, way):
        other = lax.rem(seat + group + way * k, group)
        return other, {"inner": other // 2, "head": lax.rem(other, 2)}

    def outer_place(k, way):
        other = lax.rem(line + outer + way * k, outer)
        return other, {"outer": other}

    def late_copies(places, count, me, src, land, sends, recvs):
        give = [remote(src, land.at[me], sends.at[k], recvs.at[k], **places(k, 1)[1]) for k in range(1, count)]
        take = [
            remote(src, land.at[places(k, -1)[0]], sends.at[k], recvs.at[k], **places(k, 1)[1]) for k in range(1, count)
        ]
        return give, take

    group_give, group_take = late_copies(
        group_place, group, seat, late_ref.at[0], got_group, group_send, group_recv
    )
    outer_give, outer_take = late_copies(outer_place, outer, line, late_ref.at[1], got_outer, outer_send, outer_recv)

    load_count = iter(range(load_sem.shape[0]))

    def load(src, dst):
        return pltpu.make_async_copy(src, dst, load_sem.at[next(load_count)])

    row = lax.broadcasted_iota(jnp.int32, (half, 1), 0) + head * half
    valid = row < len_ref[0]

    def greet_all():
        barrier = pltpu.get_barrier_semaphore()
        places = [group_place(k, 1)[1] for k in range(1, group)] + [outer_place(k, 1)[1] for k in range(1, outer)]
        for place in places:
            pl.semaphore_signal(barrier, inc=1, device_id=place, device_id_type=pl.DeviceIdType.MESH)
        return lambda: pl.semaphore_wait(barrier, len(places))

    two_rows = half // 2

    def halves_of(step):
        for r in range(2):
            step(r, pl.ds(r * two_rows, two_rows))

    def feed_forward(
        att_ref, wo_ref, we_ref, wr_ref, cot_ref, hid_ref, gn_ref,
        n2_ref, n2t_ref, gl_ref, glt_ref, give_ref, relu_ref, sq_ref,
    ):
        give_att = relu_ref.at[0, :, 0:local]
        give_go = relu_ref.at[1, :, 0:local]
        loads = {}
        for k, (att, wo) in enumerate(((att_hbm.at[rows_of(head, half), :], wo_own_hbm), (att_oth_hbm.at[rows_of(head, half), :], wo_oth_hbm))):
            loads["att", k] = load(att, att_ref.at[k])
            loads["wo", k] = load(wo, wo_ref.at[k])
        loads["emb"] = load(emb_hbm, hid_ref)
        loads["cot"] = load(cot_hbm, cot_ref)
        for c in range(steps):
            cols = pl.ds(c * D, D)
            for k, we in ((1, we_oth_hbm), (0, we_own_hbm)):
                loads["we", c, k] = load(we.at[:, cols], we_ref.at[c, k])
            for k, wr in ((1, wr_oth_hbm), (0, wr_own_hbm)):
                loads["wr", c, k] = load(wr.at[cols, :], wr_ref.at[c, k])
        weights = {c: [copy for key, copy in loads.items() if key[0] in ("we", "wr") and key[1] == c] for c in range(steps)}
        for key, copy in loads.items():
            if key[0] not in ("we", "wr"):
                copy.start()
        all_here = greet_all()
        for key in (("att", 0), ("wo", 0), ("att", 1), ("wo", 1), "emb", "cot"):
            loads[key].wait()
        for copy in weights[0]:
            copy.start()
        gain, bias = row_of(gain_second_ref), row_of(bias_second_ref)

        def open_rows(r, rows):
            hidden = hid_ref[rows, :] + dot(att_ref[0, rows, :], wo_ref[0]) + dot(att_ref[1, rows, :], wo_ref[1])
            hid_ref[rows, :] = hidden
            hat, _ = normalise(hidden)
            normed = (hat * gain + bias).astype(BF16)
            n2_ref[rows, :] = normed
            n2t_ref[:, rows] = normed.T
            position = lax.broadcasted_iota(jnp.int32, (two_rows, 1), 0) + head * half + r * two_rows
            grad = jnp.where(position < len_ref[0], cot_ref[rows, :], 0.0)
            cot_ref[rows, :] = grad
            gl_ref[rows, :] = grad.astype(BF16)
            glt_ref[:, rows] = grad.astype(BF16).T

        halves_of(open_rows)
        hid_store = load(hid_ref, act_hbm)
        hid_store.start()

        def grad_copy(c, kind):
            return remote(
                give_ref.at[kind], got_ref.at[c % 2, kind], core_send.at[c, kind], core_recv.at[c, kind], head=partner
            )

        def put_own(c, kind, value):
            for k in range(split):
                part = value[:, k * width : (k + 1) * width].astype(BF16)
                g_ref[chunk_of(c, kind, k)] = part.reshape(g_ref.shape[1:])

        def add_other(c, kind):
            grad_copy(c, kind).wait_recv()
            for k in range(split):
                got = got_ref[c % 2, kind, :, k * width : (k + 1) * width]
                g_ref[chunk_of(c, kind, k)] += got.reshape(g_ref.shape[1:])

        def weight_grad(c, kind, k, left_ref, right):
            grad = dot(left_ref[...], right)
            if k == 1:
                if c:
                    grad_copy(c - 1, kind).wait_send()
                elif kind == 0:
                    all_here()
                give_ref[kind] = grad.astype(BF16)
                grad_copy(c, kind).start()
            else:
                put_own(c, kind, grad)

        stores = []
        for c in range(steps):
            for k in (1, 0):
                loads["we", c, k].wait()
                relu = jnp.maximum(dot(n2_ref[...], we_ref[c, k]), 0.0)
                relu_ref[k] = relu.astype(BF16)
                sq_ref[c, k] = (relu * relu).astype(BF16)
                stores.append(load(sq_ref.at[c, k], sq_hbm.at[c, k]))
                stores[-1].start()
                weight_grad(c, 0, k, glt_ref, sq_ref[c, k])
                tick(("feed", c, 1 - k))
            if c + 1 < steps:
                for copy in weights[c + 1]:
                    copy.start()
            add_other(c, 0)
            tick(("feed", c, 2))
            for k in (1, 0):
                loads["wr", c, k].wait()
                back = dot_nt(gl_ref[...], wr_ref[c, k])
                relu_ref[k] = (back * (2.0 * relu_ref[k].astype(F32))).astype(BF16)
                weight_grad(c, 1, k, n2t_ref, relu_ref[k])
                tick(("feed", c, 4 - k))
            for k in (1, 0):
                gn = dot_nt(relu_ref[k], we_ref[c, k])
                if c == 0 and k == 1:
                    gn_ref[...] = gn
                else:
                    gn_ref[...] += gn
                if k == 1:
                    add_other(c, 1)
                    tick(("feed", c, 5))
        acc_ref[0] = jnp.zeros(acc_ref.shape[1:], F32)

        def close_rows(r, rows):
            hat, scale = normalise(hid_ref[rows, :])
            grad_n = gn_ref[rows, :]
            acc_ref[0, 2:3, :] += jnp.sum(grad_n * hat, axis=0, keepdims=True)
            acc_ref[0, 3:4, :] += jnp.sum(grad_n, axis=0, keepdims=True)
            grad_h = cot_ref[rows, :] + norm_back(grad_n, hat, scale, gain)
            gh_ref[rows, :] = grad_h
            low = grad_h.astype(BF16)
            n2_ref[rows, :] = low
            n2t_ref[:, rows] = low.T
            give_att[rows, :] = dot_nt(low, wo_ref[1]).astype(BF16)

        halves_of(close_rows)
        own_rows = rows_of(head, half)
        att_copy = remote(give_att, do_ref.at[own_rows], core_send.at[steps, 0], core_recv.at[steps, 0], head=partner)
        att_copy.start()
        tick(("norm", 0))
        give_go[...] = dot(n2t_ref[...], att_ref[1]).astype(BF16)
        go_copy = remote(give_go, got_go, core_send.at[steps, 1], core_recv.at[steps, 1], head=partner)
        go_copy.start()
        do_ref[own_rows, :] = dot_nt(n2_ref[...], wo_ref[0]).astype(BF16)
        tick(("norm", 1))
        grad_o = dot(n2t_ref[...], att_ref[0]).astype(BF16)
        go_copy.wait()
        g_ref[fed - 1] = (grad_o + got_go[...]).reshape(g_ref.shape[1:])
        tick(("norm", 2))
        for kind in range(2):
            grad_copy(steps - 1, kind).wait_send()
        for copy in [hid_store] + stores:
            copy.wait()
        att_copy.wait()

    pl.run_scoped(
        feed_forward,
        pltpu.VMEM((2, half, local), BF16), pltpu.VMEM((2, local, D), BF16),
        pltpu.VMEM((steps, 2, D, D), BF16), pltpu.VMEM((steps, 2, D, D), BF16),
        pltpu.VMEM((half, D), F32), pltpu.VMEM((half, D), F32), pltpu.VMEM((half, D), F32),
        pltpu.VMEM((half, D), BF16), pltpu.VMEM((D, half), BF16),
        pltpu.VMEM((half, D), BF16), pltpu.VMEM((D, half), BF16),
        pltpu.VMEM((2, D, D), BF16), pltpu.VMEM((2, half, D), BF16), pltpu.VMEM((steps, 2, half, D), BF16),
    )

    def attention(
        all_ref, wcat_ref, nt_ref, mix_ref, late, dot_ref, qt_ref, doa_ref, kz_ref, va_ref, turned_ref,
        att_ref, q_ref, k_ref, v_ref, raw_ref, rinv_ref, terms_ref, pair_sem, terms_sem,
    ):
        def pair_loads(p, place):
            one = pl.ds(pl.multiple_of(p * LANES, LANES), LANES)
            three = pl.ds(pl.multiple_of(p * 3 * LANES, LANES), 3 * LANES)
            return [
                pltpu.make_async_copy(rinv_hbm.at[:, one], rinv_ref.at[place], pair_sem.at[place, 0]),
                pltpu.make_async_copy(att_hbm.at[:, one], att_ref.at[place], pair_sem.at[place, 1]),
                pltpu.make_async_copy(v_hbm.at[:, one], v_ref.at[place], pair_sem.at[place, 2]),
                pltpu.make_async_copy(q_hbm.at[:, one], q_ref.at[place], pair_sem.at[place, 3]),
                pltpu.make_async_copy(k_hbm.at[:, one], k_ref.at[place], pair_sem.at[place, 4]),
                pltpu.make_async_copy(raw_hbm.at[:, three], raw_ref.at[place], pair_sem.at[place, 5]),
            ]

        def terms_load(p, j):
            rows = pl.ds(j * BLOCK, slot - j * BLOCK)
            spot = lax.rem(blocks * p + j, 4)
            return pltpu.make_async_copy(
                terms_hbm.at[pl.ds(2 * p, 2), rows, pl.ds(j * BLOCK, BLOCK)],
                terms_ref.at[spot, :, rows, :],
                terms_sem.at[spot],
            )

        for copy in pair_loads(0, 0):
            copy.start()
        for j in range(2):
            terms_load(0, j).start()
        nt_load = load(nt_hbm, nt_ref)
        nt_load.start()
        for copy in late:
            copy.start()
        mix_ref[:, slot : slot + 8, :] = jnp.zeros((3, 8, LANES), F32)
        lane = lane_ids(slot)

        def at_pair(p, kind, *rest):
            for q in range(pairs):
                if plan.get((kind, q) + rest):
                    pl.when(p == q)(functools.partial(tick, (kind, q) + rest))

        def one_pair(p, _):
            place = lax.rem(p, 2)
            one = pl.ds(pl.multiple_of(p * LANES, LANES), LANES)

            @pl.when(p + 1 < pairs)
            def _():
                for copy in pair_loads(p + 1, 1 - place):
                    copy.start()

            for copy in pair_loads(p, place):
                copy.wait()
            scaled = (do_ref[:, one].astype(F32) * rinv_ref[place]).astype(BF16)
            dot_ref[...] = scaled.T
            qt_ref[...] = q_ref[place].T
            product = scaled.astype(F32) * att_ref[place].astype(F32)
            for e in range(2):
                in_head = (lane // HEAD_DIM) == e
                delta = -jnp.sum(jnp.where(in_head, product, 0.0), axis=1, keepdims=True)
                other = HEAD_DIM * (1 - e)
                ones = jnp.where((lane > other) & (lane < other + 4), 1.0, 0.0)
                doa_ref[e] = with_parts(jnp.where(in_head, scaled.astype(F32), 0.0), lane, other, delta).astype(BF16)
                va_ref[e] = jnp.where(in_head, v_ref[place].astype(F32), ones).astype(BF16)
                kz_ref[e] = jnp.where(in_head, k_ref[place].astype(F32), 0.0).astype(BF16)

            def grads_of(j, e):
                return dot_nt(doa_ref[e, j * BLOCK :, :], va_ref[e, j * BLOCK : (j + 1) * BLOCK, :])

            for j0 in range(0, blocks, 2):
                at_pair(p, "pair", j0)
                for j in (j0, j0 + 1):
                    terms_load(p, j).wait()
                    if j + 2 < blocks:
                        terms_load(p, j + 2).start()
                    else:
                        @pl.when(p + 1 < pairs)
                        def _():
                            terms_load(p + 1, j + 2 - blocks).start()
                tasks = [(j, e) for j in (j0, j0 + 1) for e in range(2)]
                coming = grads_of(*tasks[0])
                for t, (j, e) in enumerate(tasks):
                    back = coming
                    if t + 1 < len(tasks):
                        coming = grads_of(*tasks[t + 1])
                    first = j * BLOCK
                    keys = slice(first, first + BLOCK)
                    mine_rows = slice(e * HEAD_DIM, (e + 1) * HEAD_DIM)
                    terms = terms_ref[lax.rem(blocks * p + j, 4), e, first:, :]
                    grads = (terms.astype(F32) * back).astype(BF16)
                    part = dot(grads, kz_ref[e, keys, :])
                    if j == 0 and e == 0:
                        mix_ref[0, first:slot, :] = part
                    else:
                        mix_ref[0, first:slot, :] += part
                    turned_ref[0, mine_rows, keys] = dot(qt_ref[mine_rows, first:], grads)
                    turned_ref[1, mine_rows, keys] = dot(dot_ref[mine_rows, first:], terms)
            mix_ref[0, 0:slot, :] = mix_ref[0, 0:slot, :] * SCALE
            mix_ref[1, 0:slot, :] = turned_ref[0].T
            mix_ref[2, 0:slot, :] = turned_ref[1].T
            base = pl.multiple_of(p * 3 * LANES, LANES)

            @pl.when(p == 0)
            def _():
                nt_load.wait()

            for j in (2, 1, 0):
                zero = mix_ref[j, 0:slot, :]
                one_on = mix_ref[j, 1 : 1 + slot, :]
                two_on = mix_ref[j, 2 : 2 + slot, :]
                raw = raw_ref[place, :, j * LANES : (j + 1) * LANES].astype(F32)
                cols = pl.ds(pl.multiple_of(head * local + p * LANES, LANES), LANES)
                value = 0.0
                for s, moved in enumerate((zero, one_on, two_on)):
                    total = jnp.sum(moved * raw, axis=0, keepdims=True)
                    acc_ref[0, 4 + 3 * j + s : 5 + 3 * j + s, cols] = total
                    value += taps_ref[j, s : s + 1, one] * moved
                mine_cols = pl.ds(pl.multiple_of(base + j * LANES, LANES), LANES)
                all_ref[:, mine_cols] = value.astype(BF16)

                @pl.when(p == pairs - 1)
                def _():
                    grads = dot(nt_ref[...], all_ref[:, mine_cols]).astype(BF16)
                    spot = (fed + pairs - 1,) + (slice(None),) * (inner_bits + 1) + (slice(j * LANES, (j + 1) * LANES),)
                    g_ref[spot] = grads.reshape(g_ref.shape[1:-1] + (LANES,))
                    tick(("last", j))

            @pl.when(p < pairs - 1)
            def _():
                grads = dot(nt_ref[...], all_ref[:, pl.ds(base, 3 * LANES)]).astype(BF16)
                g_ref[fed + p] = grads.reshape(g_ref.shape[1:])

            at_pair(p, "taps")
            return 0

        lax.fori_loop(0, pairs, one_pair, 0)

    def tail(all_ref, wcat_ref, late, emb_ref, give_first, own_first, hid_ref, sq_ref, wr_ref):
        emb_load = load(emb_hbm, emb_ref)
        emb_load.start()
        hid_load = load(act_hbm, hid_ref)
        hid_load.start()
        ffn_loads = []
        for c in range(steps):
            for k, wr in ((1, wr_oth_hbm), (0, wr_own_hbm)):
                ffn_loads.append(load(sq_hbm.at[c, k], sq_ref.at[c, k]))
                ffn_loads.append(load(wr.at[pl.ds(c * D, D), :], wr_ref.at[c, k]))
        for copy in ffn_loads:
            copy.start()
        small_step(0)
        for copy in late:
            copy.wait()

        def other_rows(r, rows):
            there = pl.ds(pl.multiple_of(partner * half + r * two_rows, two_rows), two_rows)
            give_first[rows, :] = dot_nt(all_ref[there, :], wcat_ref[...]).astype(BF16)
            tick(("tail", r))

        halves_of(other_rows)
        first_copy = remote(
            give_first, got_first, core_send.at[steps + 1, 0], core_recv.at[steps + 1, 0], head=partner
        )
        first_copy.start()
        small_step(1)

        def own_rows(r, rows):
            here = pl.ds(pl.multiple_of(head * half + r * two_rows, two_rows), two_rows)
            own_first[rows, :] = dot_nt(all_ref[here, :], wcat_ref[...])
            tick(("tail", 2 + r))

        halves_of(own_rows)
        small_step(2)
        emb_load.wait()
        first_copy.wait()
        gain = row_of(gain_first_ref)
        late_ref[0] = jnp.zeros(late_ref.shape[1:], F32)

        def norm_rows(r, rows):
            grad_n = own_first[rows, :] + got_first[rows, :].astype(F32)
            hat, scale = normalise(emb_ref[rows, :])
            late_ref[0, 0:1, :] += jnp.sum(grad_n * hat, axis=0, keepdims=True)
            late_ref[0, 1:2, :] += jnp.sum(grad_n, axis=0, keepdims=True)
            gh_ref[rows, :] = gh_ref[rows, :] + norm_back(grad_n, hat, scale, gain)
            tick(("tail", 4 + r))

        halves_of(norm_rows)
        for copy in group_give:
            copy.start()
        got_group[seat] = late_ref[0]
        gin_store = load(gh_ref, gin_hbm)
        gin_store.start()
        small_step(3)
        hid_load.wait()
        for copy in ffn_loads:
            copy.wait()

        def ffn_rows(first, c):
            rows = slice(first, first + two_rows)
            hid_ref[rows, :] += dot(sq_ref[c, 1, rows, :], wr_ref[c, 1]) + dot(sq_ref[c, 0, rows, :], wr_ref[c, 0])

        for c in range(steps):
            ffn_rows(0, c)
            if c < 2:
                tick(("tail", 6 + c))
        for copy in group_take:
            copy.wait_recv()
        total = got_group[0]
        for k in range(1, group):
            total = total + got_group[k]
        late_ref[1] = total
        for copy in outer_give:
            copy.start()
        got_outer[line] = total
        small_step(4)
        for c in range(steps):
            ffn_rows(two_rows, c)
            if c < 2:
                tick(("tail", 8 + c))
        act_store = load(hid_ref, act_hbm)
        act_store.start()
        small_step(5)
        for copy in outer_take:
            copy.wait_recv()
        total = got_outer[0]
        for k in range(1, outer):
            total = total + got_outer[k]
        now, k = 6, 6
        while plan or k < small_steps:
            tick(("tail", now))
            if k < small_steps:
                small_step(k)
            now, k = now + 1, k + 1
        small_ref[0:2, :] = total[0:2, :]
        gin_store.wait()
        act_store.wait()
        for copy in group_give + outer_give:
            copy.wait_send()

    def backward(all_ref, wcat_ref):
        late = []
        for p in range(pairs):
            for j, w_hbm in enumerate((wq_hbm, wk_hbm, wv_hbm)):
                base = (3 * p + j) * LANES
                late.append(load(w_hbm.at[:, pl.ds(p * LANES, LANES)], wcat_ref.at[:, pl.ds(base, LANES)]))
        pl.run_scoped(
            lambda nt, mix, *rest: attention(all_ref, wcat_ref, nt, mix, late, *rest),
            pltpu.VMEM((D, slot), BF16),
            pltpu.VMEM((3, slot + 8, LANES), F32),
            pltpu.VMEM((LANES, slot), BF16),
            pltpu.VMEM((LANES, slot), BF16),
            pltpu.VMEM((2, slot, LANES), BF16),
            pltpu.VMEM((2, slot, LANES), BF16),
            pltpu.VMEM((2, slot, LANES), BF16),
            pltpu.VMEM((2, LANES, slot), F32),
            pltpu.VMEM((2, slot, LANES), BF16),
            pltpu.VMEM((2, slot, LANES), BF16),
            pltpu.VMEM((2, slot, LANES), BF16),
            pltpu.VMEM((2, slot, LANES), BF16),
            pltpu.VMEM((2, slot, 3 * LANES), BF16),
            pltpu.VMEM((2, slot, LANES), F32),
            pltpu.VMEM((4, 2, slot, BLOCK), BF16),
            pltpu.SemaphoreType.DMA((2, 6)),
            pltpu.SemaphoreType.DMA((4,)),
        )
        pl.run_scoped(
            functools.partial(tail, all_ref, wcat_ref, late),
            pltpu.VMEM((half, D), F32),
            pltpu.VMEM((half, D), BF16),
            pltpu.VMEM((half, D), F32),
            pltpu.VMEM((half, D), F32),
            pltpu.VMEM((steps, 2, half, D), BF16),
            pltpu.VMEM((steps, 2, D, D), BF16),
        )

    pl.run_scoped(backward, pltpu.VMEM((slot, 3 * local), BF16), pltpu.VMEM((D, 3 * local), BF16))
    for n in range(len(entries)):
        drain(n)
    for k in range(inner_bits + 1):
        small_copy(k).wait_send()
    for k in range(inner_bits + 1, inner_bits + 1 + line_steps):
        pl.when(line_sender(k - 1 - inner_bits))(lambda k=k: small_copy(k).wait_send())


def finish_kernel(
    split, sum_hbm, act_hbm, gin_hbm, small_ref,
    act_out, gin_out, q_out, k_out, v_out, go_out, ge_out, gr_out, taps_ref, *rest,
):
    vec_refs, (sum_ref, wide_ref, row_ref, load_sem, store_sem, row_load, row_store) = rest[:-7], rest[-7:]
    chunks, _, width = sum_hbm.shape
    pairs = q_out.shape[1] // LANES
    fed = chunks - pairs
    half = act_hbm.shape[0] // 2
    row_loads, row_stores = [], []
    for k, (src, dst) in enumerate(((act_hbm, act_out), (gin_hbm, gin_out))):
        for r in range(2):
            rows, spot = pl.ds(r * half, half), 2 * k + r
            row_loads.append(pltpu.make_async_copy(src.at[rows], row_ref.at[spot], row_load.at[spot]))
            row_stores.append(pltpu.make_async_copy(row_ref.at[spot], dst.at[rows], row_store.at[spot]))
    loads = [pltpu.make_async_copy(sum_hbm.at[c], sum_ref.at[c], load_sem.at[c]) for c in range(chunks)]
    for copy in row_loads + loads:
        copy.start()
    for j in range(3):
        taps_ref[j] = small_ref[4 + 3 * j : 7 + 3 * j, :]
    for k, ref in enumerate(vec_refs):
        ref[...] = small_ref[k, :]
    for came, go in zip(row_loads, row_stores):
        came.wait()
        go.start()
    stores = []

    def store(src, dst):
        stores.append(pltpu.make_async_copy(src, dst, store_sem.at[len(stores)]))
        stores[-1].start()

    for c in range(chunks):
        loads[c].wait()
        wide_ref[c] = sum_ref[c].astype(F32)
        if c < fed - 1:
            step, kind, k = c // (2 * split), (c // split) % 2, c % split
            store(wide_ref.at[c], (gr_out, ge_out)[kind].at[:, pl.ds((step * split + k) * width, width)])
        elif c == fed - 1:
            store(wide_ref.at[c], go_out)
        else:
            for j, out in enumerate((q_out, k_out, v_out)):
                part = wide_ref.at[c, :, pl.ds(j * LANES, LANES)]
                store(part, out.at[:, pl.ds((c - fed) * LANES, LANES)])
    for copy in stores + row_stores:
        copy.wait()


def params(vmem, **kw):
    return pltpu.CompilerParams(vmem_limit_bytes=vmem * MIB, **kw)


def body(
    token_ids, lengths, query_weight, key_weight, value_weight, output_weight,
    expand_weight, reduce_weight, dconv_taps, gain_first, bias_first,
    gain_second, bias_second, cotangent,
):
    half = token_ids.shape[1]
    slot = 2 * half
    local = query_weight.shape[1]
    units = expand_weight.shape[1]
    pairs = local // LANES
    outer = lax.axis_size("outer")
    inner = lax.axis_size("inner")
    inner_bits = inner.bit_length() - 1
    rows = D // inner
    width = 3 * LANES

    shape = jax.ShapeDtypeStruct
    smem = pl.BlockSpec(memory_space=pltpu.SMEM)
    anywhere = pl.BlockSpec(memory_space=pl.ANY)
    dma = pltpu.SemaphoreType.DMA
    vec = whole((D,))

    column = pl.BlockSpec((D, LANES), lambda p: (0, p))
    taps_spec = pl.BlockSpec((3, 3, LANES), lambda p: (0, 0, p))
    pair_rows = pl.BlockSpec((slot, LANES), lambda p: (0, p))
    raw_spec = pl.BlockSpec((slot, 3 * LANES), lambda p: (0, p))
    (
        attended, queries, key_rows, value_rows, raw, inverse, embedded, normed_t, att_oth,
        we_oth, wr_oth, wo_oth, terms,
    ) = pl.pallas_call(
        forward_kernel,
        grid=(pairs,),
        in_specs=[smem, whole((1, half)), vec, vec, column, column, column, taps_spec] + [anywhere] * 3,
        out_specs=[pair_rows] * 4 + [raw_spec, pair_rows] + [anywhere] * 7,
        out_shape=[shape((slot, local), BF16)] * 4
        + [shape((slot, 3 * local), BF16), shape((slot, local), F32), shape((half, D), F32), shape((D, slot), BF16)]
        + [shape((slot, local), BF16)]
        + [shape(w.shape, BF16) for w in (expand_weight, reduce_weight, output_weight)]
        + [shape((2 * pairs, slot, slot), BF16)],
        scratch_shapes=[
            pltpu.VMEM(output_weight.shape, BF16),
            pltpu.VMEM(expand_weight.shape, BF16),
            pltpu.VMEM(reduce_weight.shape, BF16),
            pltpu.VMEM((half, D), F32),
            pltpu.VMEM((D, slot), BF16),
            pltpu.VMEM((slot, D), BF16),
            pltpu.VMEM((2, 3, BLOCK + 8, LANES), F32),
            pltpu.VMEM((D, 3 * LANES), BF16),
            pltpu.VMEM((2, slot, LANES), BF16),
            pltpu.VMEM((2, LANES, slot), BF16),
            pltpu.VMEM((2, slot, LANES), BF16),
            pltpu.VMEM((2, slot, slot), BF16),
            pltpu.VMEM((pairs, slot, LANES), BF16),
            dma((PIECES,)), dma((PIECES,)), dma((pairs, slot // BLOCK)), dma((pairs, slot // BLOCK)), dma((3,)), dma((3,)),
            dma((slot // BLOCK,)), dma((4 + pairs,)),
        ],
        compiler_params=params(58, collective_id=0, has_side_effects=True),
        name="attention_forward",
    )(
        lengths, token_ids, gain_first, bias_first,
        query_weight, key_weight, value_weight, dconv_taps, expand_weight, reduce_weight, output_weight,
    )

    steps = units // D
    split = D // width
    fed = 2 * steps * split + 1
    chunks = fed + pairs
    twos = (2,) * inner_bits
    line_stages = inner_bits + outer
    vmem = lambda dims, kind: pltpu.VMEM(dims, kind)
    sums, small, activations, grad_input, _ = pl.pallas_call(
        functools.partial(layer_kernel, inner_bits, outer),
        in_specs=[smem, vec, vec, vec, whole((3, 3, local))] + [anywhere] * 20,
        out_specs=[whole((chunks, rows, width)), whole((16, D)), anywhere, anywhere, anywhere],
        out_shape=[
            shape((chunks, rows, width), BF16), shape((16, D), F32), shape((half, D), F32), shape((half, D), F32),
            shape((steps, 2, half, D), BF16),
        ],
        scratch_shapes=[
            vmem((half, D), F32),
            vmem((chunks,) + twos + (rows, width), BF16),
            vmem((chunks, rows, width), BF16),
            vmem((chunks, rows, width), BF16),
            vmem((slot, local), BF16),
            vmem((2, 2, D, D), BF16),
            vmem((D, local), BF16),
            vmem((half, D), BF16),
            vmem((inner_bits + 2, 16, D), F32),
            vmem((inner_bits + 3, 16, D), F32),
            vmem((2, 8, D), F32),
            vmem((2 * inner, 8, D), F32),
            vmem((outer, 8, D), F32),
            dma((12 + 10 * steps + 3 * pairs,)),
            dma((2 * chunks + 1, line_stages)), dma((2 * chunks + 1, line_stages)),
            dma((line_stages + 1,)), dma((line_stages + 1,)),
            dma((steps + 2, 2)), dma((steps + 2, 2)),
            dma((2 * inner,)), dma((2 * inner,)), dma((outer,)), dma((outer,)),
        ]
        + [vmem((chunks,) + (2,) * (inner_bits - 1 - s) + (rows, width), BF16) for s in range(inner_bits)],
        compiler_params=params(63, collective_id=1, has_side_effects=True),
        name="layer",
    )(
        lengths, gain_first, gain_second, bias_second, dconv_taps,
        att_oth, embedded, cotangent[0], output_weight, wo_oth,
        expand_weight, we_oth, reduce_weight, wr_oth, query_weight, key_weight, value_weight,
        attended, queries, key_rows, value_rows, raw, inverse, normed_t, terms,
    )
    vmem_all = pl.BlockSpec(memory_space=pltpu.VMEM)
    activations, grad_input, gq, gk, gv, go_sum, ge_sum, gr_sum, tap_sum, *vec_sums = pl.pallas_call(
        functools.partial(finish_kernel, split),
        in_specs=[anywhere] * 3 + [vmem_all],
        out_specs=[anywhere] * 8 + [vmem_all] * 5,
        out_shape=[shape((half, D), F32)] * 2
        + [shape((rows, local), F32)] * 4
        + [shape((rows, units), F32)] * 2
        + [shape((3, 3, D), F32)]
        + [shape((D,), F32)] * 4,
        scratch_shapes=[
            vmem((chunks, rows, width), BF16), vmem((chunks, rows, width), F32),
            vmem((4, half // 2, D), F32),
            dma((chunks,)), dma((fed + 3 * pairs,)), dma((4,)), dma((4,)),
        ],
        compiler_params=params(62),
        name="finish",
    )(sums, activations, grad_input, small)
    return (
        activations[None],
        grad_input[None],
        gq,
        gk,
        gv,
        go_sum.T,
        ge_sum,
        gr_sum.T,
        tap_sum,
        *vec_sums,
    )


def solution(mesh):
    return jax.shard_map(
        body,
        mesh=mesh,
        in_specs=(
            P(("outer", "inner"), "head"),
            P(("outer", "inner")),
            P(None, "head"),
            P(None, "head"),
            P(None, "head"),
            P("head", None),
            P(None, "head"),
            P("head", None),
            P(None, None, "head"),
            P(),
            P(),
            P(),
            P(),
            P(("outer", "inner"), "head", None),
        ),
        out_specs=(
            P(("outer", "inner"), "head", None),
            P(("outer", "inner"), "head", None),
            P("inner", "head"),
            P("inner", "head"),
            P("inner", "head"),
            P("head", "inner"),
            P("inner", "head"),
            P("head", "inner"),
            P(),
            P(),
            P(),
            P(),
            P(),
        ),
        check_vma=False,
    )
```

```python
import functools
import math

import jax
import jax.numpy as jnp
from jax import lax
from jax.experimental import pallas as pl
from jax.experimental.pallas import tpu as pltpu
from jax.sharding import PartitionSpec as P

HEAD_DIM = 64
D = 768
BLOCK = 256
LANES = 128
EPS = 1e-05
MODULUS = 32749
NEGATIVE = -1e30
SCALE = HEAD_DIM ** (-0.5)
F32 = jnp.float32
BF16 = jnp.bfloat16
MIB = 1024 * 1024

SINE = (
    4.442882913726386,
    -7.308248583654593,
    3.606466623722958,
    -0.8474403474577161,
    0.11605422299047748,
    -0.010267162611370253,
    0.0005523348366953617,
)


def dot(a, b):
    return lax.dot_general(a, b, (((1,), (0,)), ((), ())), preferred_element_type=F32)


def dot_nt(a, b):
    return lax.dot_general(a, b, (((1,), (1,)), ((), ())), preferred_element_type=F32)


def whole(shape):
    return pl.BlockSpec(shape, lambda *_: (0,) * len(shape))


def normalise(values):
    centre = values - jnp.mean(values, axis=-1, keepdims=True)
    spread = jnp.mean(centre * centre, axis=-1, keepdims=True)
    scale = lax.rsqrt(spread + EPS)
    return centre * scale, scale


def norm_back(grad, hat, scale, gain):
    q = grad * gain
    mean_q = jnp.mean(q, axis=-1, keepdims=True)
    mean_qh = jnp.mean(q * hat, axis=-1, keepdims=True)
    return scale * (q - mean_q - hat * mean_qh)


def lane_ids(rows):
    return lax.broadcasted_iota(jnp.int32, (rows, LANES), 1)


def split_three(column):
    high = column.astype(BF16).astype(F32)
    rest = column - high
    middle = rest.astype(BF16).astype(F32)
    return high, middle, rest - middle


def with_parts(base, lane, offset, column):
    high, middle, small = split_three(column)
    base = jnp.where(lane == offset + 1, high, base)
    base = jnp.where(lane == offset + 2, middle, base)
    return jnp.where(lane == offset + 3, small, base)


def remote(src, dst, send, recv, **place):
    return pltpu.make_async_remote_copy(
        src_ref=src, dst_ref=dst, send_sem=send, recv_sem=recv,
        device_id=place, device_id_type=pl.DeviceIdType.MESH,
    )


def greet(*places):
    barrier = pltpu.get_barrier_semaphore()
    for place in places:
        pl.semaphore_signal(barrier, inc=1, device_id=place, device_id_type=pl.DeviceIdType.MESH)
    pl.semaphore_wait(barrier, len(places))


def rows_of(which, half):
    return pl.ds(pl.multiple_of(which * half, half), half)


def remainder(product):
    turns = jnp.floor(product.astype(F32) * (1.0 / MODULUS) + 0.5)
    return (product - turns.astype(jnp.int32) * MODULUS).astype(F32)


def embed_rows(tok_ref, gain, bias, emb_ref, normed_ref, base, first):
    tokens = jnp.broadcast_to(tok_ref[:, pl.ds(first, LANES)], (LANES, LANES)).T
    column = lax.broadcasted_iota(jnp.int32, (1, LANES), 1)
    start = remainder(tokens * (column + 1) + column * column)
    stride = remainder(tokens * LANES + column * (2 * LANES))
    parts = []
    for c in range(D // LANES):
        phase = start + (stride * float(c) + float(c * c * LANES * LANES))
        u = (phase - jnp.floor(phase * (1.0 / MODULUS) + 0.5) * float(MODULUS)) * (2.0 / MODULUS)
        z = u * u
        value = jnp.full_like(u, SINE[-1])
        for coefficient in SINE[-2::-1]:
            value = value * z + coefficient
        parts.append(value * u)
    embedded = jnp.concatenate(parts, axis=1)
    emb_ref[pl.ds(first, LANES), :] = embedded
    hat, _ = normalise(embedded)
    rows = pl.ds(pl.multiple_of(base + first, LANES), LANES)
    normed_ref[rows, :] = (hat * gain + bias).astype(BF16)


PIECES = 3


def row_of(ref):
    return ref[...].reshape(1, D)


def forward_kernel(
    len_ref, tok_ref, gain_ref, bias_ref, wq_ref, wk_ref, wv_ref, taps_ref, we_hbm, wr_hbm, wo_hbm,
    att_ref, q_ref, k_ref, v_ref, raw_ref, rinv_ref,
    emb_hbm, nt_hbm, att_oth_hbm, we_oth_hbm, wr_oth_hbm, wo_oth_hbm, terms_hbm,
    wo_ref, we_ref, wr_ref, emb_ref, nt_ref, normed_ref, shift_ref, wcat_ref, qa_ref, ka_ref, va_ref, terms_ref, give_ref,
    row_send, row_recv, att_send, att_recv, weight_send, weight_recv, terms_sem, store_sem,
):
    slot = att_ref.shape[0]
    half = slot // 2
    blocks = slot // BLOCK
    step = pl.program_id(0)
    pairs = att_oth_hbm.shape[1] // LANES
    head = lax.axis_index("head")
    partner = 1 - head
    piece = half // PIECES

    def row_copy(k):
        rows = pl.ds(pl.multiple_of(head * half + k * piece, piece), piece)
        return remote(normed_ref.at[rows], normed_ref.at[rows], row_send.at[k], row_recv.at[k], head=partner)

    def att_copy(p, i):
        rows = pl.ds(i * BLOCK, BLOCK)
        land = att_oth_hbm.at[rows, pl.ds(pl.multiple_of(p * LANES, LANES), LANES)]
        return remote(give_ref.at[p, rows], land, att_send.at[p, i], att_recv.at[p, i], head=partner)

    def weight_copy(k):
        src, dst = ((wo_ref, wo_oth_hbm), (we_ref, we_oth_hbm), (wr_ref, wr_oth_hbm))[k]
        return remote(src, dst, weight_send.at[k], weight_recv.at[k], head=partner)

    def weight_load(k):
        src, dst = ((wo_hbm, wo_ref), (we_hbm, we_ref), (wr_hbm, wr_ref))[k]
        return pltpu.make_async_copy(src, dst, store_sem.at[1 + pairs + k])

    def emb_store():
        return pltpu.make_async_copy(emb_ref, emb_hbm, store_sem.at[0])

    def nt_store(p):
        part = pl.ds(pl.multiple_of(p * (D // pairs), D // pairs), D // pairs)
        return pltpu.make_async_copy(nt_ref.at[part], nt_hbm.at[part], store_sem.at[1 + p])

    def terms_copy(p, i):
        rows, cols = pl.ds(i * BLOCK, BLOCK), pl.ds(0, (i + 1) * BLOCK)
        return pltpu.make_async_copy(
            terms_ref.at[:, rows, cols], terms_hbm.at[pl.ds(2 * p, 2), rows, cols], terms_sem.at[i]
        )

    @pl.when(step == 0)
    def _():
        for k in range(3):
            weight_load(k).start()
        greet({"head": partner})
        base = head * half
        for k in range(PIECES):
            def embed_step(i, _):
                first = pl.multiple_of(k * piece + i * LANES, LANES)
                embed_rows(tok_ref, row_of(gain_ref), row_of(bias_ref), emb_ref, normed_ref, base, first)
                return 0

            lax.fori_loop(0, piece // LANES, embed_step, 0)
            row_copy(k).start()
        for k in range(3):
            weight_load(k).wait()
            weight_copy(k).start()
        emb_store().start()
        for k in range(PIECES):
            row_copy(k).wait()

    for j, w_ref in enumerate((wq_ref, wk_ref, wv_ref)):
        wcat_ref[:, j * LANES : (j + 1) * LANES] = w_ref[...]
    shift_ref[0, :, 0:8, :] = jnp.zeros((3, 8, LANES), F32)
    lane = lane_ids(BLOCK)
    features = D // pairs
    some = pl.ds(pl.multiple_of(step * features, features), features)

    def raws_of(r):
        return dot(normed_ref[r * BLOCK : (r + 1) * BLOCK, :], wcat_ref[...])

    coming = raws_of(0)
    for r in range(blocks):
        rows = slice(r * BLOCK, (r + 1) * BLOCK)
        raws = coming
        if r + 1 < blocks:
            coming = raws_of(r + 1)
        raw_ref[rows, :] = raws.astype(BF16)
        nt_ref[some, rows] = normed_ref[rows, some].T
        mixed = []
        this, after = r % 2, (r + 1) % 2
        for j in range(3):
            raw = raws[:, j * LANES : (j + 1) * LANES]
            shift_ref[this, j, 8 : 8 + BLOCK, :] = raw
            one = shift_ref[this, j, 7 : 7 + BLOCK, :]
            two = shift_ref[this, j, 6 : 6 + BLOCK, :]
            value = taps_ref[j, 0:1, :] * raw + taps_ref[j, 1:2, :] * one + taps_ref[j, 2:3, :] * two
            mixed.append(value * SCALE if j == 0 else value)
            shift_ref[after, j, 0:8, :] = raw[BLOCK - 8 :, :]
        for ref, value in zip((q_ref, k_ref, v_ref), mixed):
            ref[rows, :] = value.astype(BF16)
        row = lax.broadcasted_iota(jnp.int32, (BLOCK, 1), 0) + r * BLOCK
        key_bias = jnp.where(row < len_ref[0], 0.0, NEGATIVE)
        for e in range(2):
            mine = (lane // HEAD_DIM) == e
            other = HEAD_DIM * (1 - e)
            qa_ref[e, rows, :] = jnp.where(mine, mixed[0], jnp.where(lane == other, 1.0, 0.0)).astype(BF16)
            key = jnp.where(mine, mixed[1], jnp.where(lane == other, key_bias, 0.0)).astype(BF16)
            ka_ref[e, :, rows] = key.T
            va_ref[e, rows, :] = jnp.where(mine, mixed[2], jnp.where(lane == other, 1.0, 0.0)).astype(BF16)

    nt_store(step).start()

    @pl.when(step > 0)
    def _():
        for i in range(blocks):
            terms_copy(step - 1, i).wait()

    causal = lax.broadcasted_iota(jnp.int32, (BLOCK, BLOCK), 1) <= lax.broadcasted_iota(
        jnp.int32, (BLOCK, BLOCK), 0
    )
    tasks = [(i, e) for i in range(blocks) for e in range(2)]

    def scores_of(i, e):
        rows = slice(i * BLOCK, (i + 1) * BLOCK)
        query = qa_ref[e, rows, :]
        diagonal = jnp.where(causal, dot(query, ka_ref[e, :, rows]), NEGATIVE)
        before = dot(query, ka_ref[e, :, : i * BLOCK]) if i else None
        return diagonal, before

    coming = scores_of(*tasks[0])
    outs = []
    for t, (i, e) in enumerate(tasks):
        diagonal, before = coming
        if t + 1 < len(tasks):
            coming = scores_of(*tasks[t + 1])
        rows = slice(i * BLOCK, (i + 1) * BLOCK)
        other = HEAD_DIM * (1 - e)
        row_max = jnp.max(diagonal, axis=1, keepdims=True)
        if i:
            row_max = jnp.maximum(row_max, jnp.max(before, axis=1, keepdims=True))
        terms = jnp.exp((diagonal - row_max).astype(BF16))
        terms_ref[e, rows, rows] = terms
        out = dot(terms, va_ref[e, rows, :])
        if i:
            terms = jnp.exp((before - row_max).astype(BF16))
            terms_ref[e, rows, : i * BLOCK] = terms
            out += dot(terms, va_ref[e, : i * BLOCK, :])
        inverse = 1.0 / out[:, other : other + 1]
        outs.append((out, inverse))
        if e == 1:
            first_head = lane < HEAD_DIM
            inverse = jnp.where(first_head, outs[0][1], outs[1][1])
            attended = (jnp.where(first_head, outs[0][0], outs[1][0]) * inverse).astype(BF16)
            att_ref[rows, :] = attended
            give_ref[step, rows, :] = attended
            att_copy(step, i).start()
            rinv_ref[rows, :] = inverse
            outs = []
            terms_copy(step, i).start()

    @pl.when(step == pairs - 1)
    def _():
        for p in range(pairs):
            for i in range(blocks):
                att_copy(p, i).wait()
            nt_store(p).wait()
        emb_store().wait()
        for k in range(3):
            weight_copy(k).wait()
        for i in range(blocks):
            terms_copy(step, i).wait()


def plan_sums(entries, ready, points, tail, inner_bits, line_steps, orders, rate=0.05, hop=1.8):
    stages = inner_bits + line_steps + 1
    done, arrive, free, plan, begun = [0] * len(entries), {}, {}, {}, set()

    def step_of(n, now):
        chunk, size, kind = entries[n]
        stage = done[n]
        if stage < inner_bits:
            link, part = ("bit", orders[kind][stage]), size / 2 ** (stage + 1)
        else:
            t = stage - inner_bits
            link, part = ("line", t), size / 2**inner_bits
        if stage < stages - 1:
            free[link] = max(free.get(link, 0.0), now) + part / rate
            arrive[n] = free[link] + hop
        done[n] += 1

    at, now, late = 0, 0.0, 0
    while at < len(points) or any(d < stages for d in done):
        if at < len(points):
            place, when = points[at]
            now, slack = max(now, when), 0.3 if place[0] != "tail" else 0.0
        else:
            place, slack = ("tail", tail + late), 0.0
            late += 1
            now = max(now, min(arrive[n] for n in range(len(entries)) if done[n] < stages))
        at += 1
        for n, (chunk, _, _) in enumerate(entries):
            if ready[n] == place:
                begun.add(n)
        while True:
            able = [n for n in begun if done[n] < stages and (done[n] == 0 or arrive[n] <= now - slack)]
            if not able:
                break
            n = min(able, key=lambda m: (-done[m], m))
            plan.setdefault(place, []).append((n, done[n]))
            step_of(n, now)
    return plan


def layer_kernel(
    inner_bits, outer,
    len_ref, gain_first_ref, gain_second_ref, bias_second_ref, taps_ref,
    att_oth_hbm, emb_hbm, cot_hbm, wo_own_hbm, wo_oth_hbm,
    we_own_hbm, we_oth_hbm, wr_own_hbm, wr_oth_hbm, wq_hbm, wk_hbm, wv_hbm,
    att_hbm, q_hbm, k_hbm, v_hbm, raw_hbm, rinv_hbm, nt_hbm, terms_hbm,
    sum_ref, small_ref, act_hbm, gin_hbm, sq_hbm,
    gh_ref, g_ref, rz_ref, rc_ref, do_ref, got_ref, got_go, got_first, acc_ref, got_small, late_ref, got_group, got_outer,
    load_sem, send_sem, recv_sem, small_send, small_recv, core_send, core_recv,
    group_send, group_recv, outer_send, outer_recv, *halves,
):
    half = gh_ref.shape[0]
    slot = 2 * half
    local = att_oth_hbm.shape[1]
    units = we_own_hbm.shape[1]
    steps = units // D
    width = sum_ref.shape[2]
    split = D // width
    pairs = local // LANES
    fed = 2 * steps * split + 1
    blocks = slot // BLOCK
    head = lax.axis_index("head")
    partner = 1 - head
    mine = lax.axis_index("inner")
    line = lax.axis_index("outer")
    centre = outer // 2
    left = line < centre
    depth = jnp.where(left, centre - 1 - line, line - centre)
    inward = jnp.where(left, line + 1, line - 1)
    outward = jnp.where(left, line - 1, line + 1)
    bit = [(mine // (1 << b)) % 2 for b in range(inner_bits)]
    across = [mine + (1 << b) * (1 - 2 * bit[b]) for b in range(inner_bits)]

    def chunk_of(c, kind, k):
        return (2 * c + kind) * split + k

    entries = []
    for c in range(fed):
        entries.append((c, 0, width, c % 2))
    for c in range(fed, fed + pairs - 1):
        entries += [(c, 0, 2 * LANES, c % 2), (c, 2 * LANES, LANES, 1 - c % 2)]
    entries += [(fed + pairs - 1, j * LANES, LANES, j % 2) for j in range(3)]
    order_of = [tuple((b + first) % inner_bits for b in range(inner_bits)) for first in range(2)]
    line_steps = 2 * centre - 1
    stage_count = inner_bits + line_steps + 1

    def index_of(fixed):
        return tuple(fixed.get(b, slice(None)) for b in reversed(range(inner_bits)))

    def lanes(entry):
        return slice(entry[1], entry[1] + entry[2])

    def halving(n, s):
        c, _, _, kind = entries[n]
        order = order_of[kind]
        fixed = {b: bit[b] for b in order[:s]}
        b = order[s]
        give = g_ref.at[(c,) + index_of({**fixed, b: 1 - bit[b]}) + (slice(None), lanes(entries[n]))]
        land = halves[s].at[(c,) + (slice(None),) * (inner_bits - 1 - s) + (slice(None), lanes(entries[n]))]
        return remote(give, land, send_sem.at[n, s], recv_sem.at[n, s], inner=across[b])

    def add_half(n, s):
        c, _, _, kind = entries[n]
        order = order_of[kind]
        index = (c,) + index_of({b: bit[b] for b in order[: s + 1]}) + (slice(None), lanes(entries[n]))
        land = (c,) + (slice(None),) * (inner_bits - 1 - s) + (slice(None), lanes(entries[n]))
        g_ref[index] = g_ref[index] + halves[s][land]

    def own(n):
        return (entries[n][0],) + tuple(bit[b] for b in reversed(range(inner_bits))) + (slice(None), lanes(entries[n]))

    def flat(n):
        return (entries[n][0], slice(None), lanes(entries[n]))

    def line_sender(t):
        if t < centre - 1:
            return depth == centre - 1 - t
        if t == centre - 1:
            return depth == 0
        return depth == t - centre

    def line_copy(n, t):
        s = inner_bits + t
        sems = (send_sem.at[n, s], recv_sem.at[n, s])
        if t < centre - 1:
            return remote(g_ref.at[own(n)], rz_ref.at[flat(n)], *sems, outer=inward)
        if t == centre - 1:
            return remote(g_ref.at[own(n)], rc_ref.at[flat(n)], *sems, outer=inward)
        return remote(rc_ref.at[flat(n)], rc_ref.at[flat(n)], *sems, outer=outward)

    def line_finish(n, t):
        if t < centre - 1:
            @pl.when(depth == centre - 2 - t)
            def _():
                line_copy(n, t).wait_recv()
                g_ref[own(n)] = g_ref[own(n)] + rz_ref[flat(n)]
        elif t == centre - 1:
            @pl.when(depth == 0)
            def _():
                line_copy(n, t).wait_recv()
                rc_ref[flat(n)] = g_ref[own(n)] + rc_ref[flat(n)]
        else:
            pl.when(depth == t - centre + 1)(lambda: line_copy(n, t).wait_recv())

    def advance(n, stage):
        if 0 < stage <= inner_bits:
            halving(n, stage - 1).wait_recv()
            add_half(n, stage - 1)
        elif stage > inner_bits:
            line_finish(n, stage - inner_bits - 1)
        if stage < inner_bits:
            halving(n, stage).start()
        elif stage < stage_count - 1:
            t = stage - inner_bits
            pl.when(line_sender(t))(lambda: line_copy(n, t).start())
        else:
            sum_ref[flat(n)] = rc_ref[flat(n)]

    def drain(n):
        for s in range(inner_bits):
            halving(n, s).wait_send()
        for t in range(line_steps):
            pl.when(line_sender(t))(lambda t=t: line_copy(n, t).wait_send())

    points = []
    now = 6.0
    for c in range(steps):
        for k, spent in enumerate((2.3, 2.3, 0.3, 2.3, 2.3, 1.2)):
            now += spent
            points.append((("feed", c, k), now))
        now += 1.1
    for k in range(3):
        now += 1.2
        points.append((("norm", k), now))
    for p in range(pairs):
        now += 1.2
        for j in range(0, blocks, 2):
            points.append((("pair", p, j), now))
            now += 8.0 * (2 * (blocks - j) - 1) * 2 / (blocks * (blocks + 1))
        if p < pairs - 1:
            now += 2.8
            points.append((("taps", p), now))
    for j in (2, 1, 0):
        now += 1.3
        points.append((("last", j), now))
    for k, spent in enumerate((0.8, 0.8, 0.8, 0.8, 1.5, 1.5, 1.4, 1.4, 1.4, 1.4)):
        now += spent
        points.append((("tail", k), now))
    ready = {}
    for c in range(steps):
        for k in range(split):
            ready[chunk_of(c, 0, k)] = ("feed", c, 2)
            ready[chunk_of(c, 1, k)] = ("feed", c, 5)
    ready[fed - 1] = ("norm", 2)
    for p in range(pairs - 1):
        ready[fed + p] = ("taps", p)
    ready_at = [ready[c] if c in ready else ("last", first // LANES) for c, first, _, _ in entries]
    plan = plan_sums(
        [(c, 2e-6 * D * wide, kind) for c, _, wide, kind in entries],
        ready_at, points, 10, inner_bits, line_steps, order_of,
    )

    def tick(place):
        for n, stage in plan.pop(place, ()):
            advance(n, stage)

    def small_copy(k):
        sems = (small_send.at[k], small_recv.at[k])
        if k == 0:
            return remote(acc_ref.at[0], got_small.at[0], *sems, head=partner)
        if k <= inner_bits:
            return remote(acc_ref.at[k], got_small.at[k], *sems, inner=across[k - 1])
        t = k - 1 - inner_bits
        if t <= centre - 1:
            return remote(acc_ref.at[inner_bits + 1], got_small.at[inner_bits + 1 + (t == centre - 1)], *sems, outer=inward)
        last = got_small.at[inner_bits + 2]
        return remote(last, last, *sems, outer=outward)

    def small_step(k):
        if 0 < k <= inner_bits + 1:
            small_copy(k - 1).wait_recv()
            acc_ref[k] = acc_ref[k - 1] + got_small[k - 1]
        elif k > inner_bits + 1:
            t = k - 2 - inner_bits
            if t < centre - 1:
                @pl.when(depth == centre - 2 - t)
                def _():
                    small_copy(k - 1).wait_recv()
                    acc_ref[inner_bits + 1] = acc_ref[inner_bits + 1] + got_small[inner_bits + 1]
            elif t == centre - 1:
                @pl.when(depth == 0)
                def _():
                    small_copy(k - 1).wait_recv()
                    got_small[inner_bits + 2] = acc_ref[inner_bits + 1] + got_small[inner_bits + 2]
            else:
                pl.when(depth == t - centre + 1)(lambda: small_copy(k - 1).wait_recv())
        if k <= inner_bits:
            small_copy(k).start()
        elif k <= inner_bits + line_steps:
            pl.when(line_sender(k - 1 - inner_bits))(lambda: small_copy(k).start())
        else:
            small_ref[...] = got_small[inner_bits + 2]

    small_steps = inner_bits + line_steps + 2

    inner = 1 << inner_bits
    group = 2 * inner
    seat = mine * 2 + head

    def group_place(k, way):
        other = lax.rem(seat + group + way * k, group)
        return other, {"inner": other // 2, "head": lax.rem(other, 2)}

    def outer_place(k, way):
        other = lax.rem(line + outer + way * k, outer)
        return other, {"outer": other}

    def late_copies(places, count, me, src, land, sends, recvs):
        give = [remote(src, land.at[me], sends.at[k], recvs.at[k], **places(k, 1)[1]) for k in range(1, count)]
        take = [
            remote(src, land.at[places(k, -1)[0]], sends.at[k], recvs.at[k], **places(k, 1)[1]) for k in range(1, count)
        ]
        return give, take

    group_give, group_take = late_copies(
        group_place, group, seat, late_ref.at[0], got_group, group_send, group_recv
    )
    outer_give, outer_take = late_copies(outer_place, outer, line, late_ref.at[1], got_outer, outer_send, outer_recv)

    load_count = iter(range(load_sem.shape[0]))

    def load(src, dst):
        return pltpu.make_async_copy(src, dst, load_sem.at[next(load_count)])

    row = lax.broadcasted_iota(jnp.int32, (half, 1), 0) + head * half
    valid = row < len_ref[0]

    def greet_all():
        barrier = pltpu.get_barrier_semaphore()
        places = [group_place(k, 1)[1] for k in range(1, group)] + [outer_place(k, 1)[1] for k in range(1, outer)]
        for place in places:
            pl.semaphore_signal(barrier, inc=1, device_id=place, device_id_type=pl.DeviceIdType.MESH)
        return lambda: pl.semaphore_wait(barrier, len(places))

    two_rows = half // 2

    def halves_of(step):
        for r in range(2):
            step(r, pl.ds(r * two_rows, two_rows))

    def feed_forward(
        att_ref, wo_ref, we_ref, wr_ref, cot_ref, hid_ref, gn_ref,
        n2_ref, n2t_ref, gl_ref, glt_ref, give_ref, relu_ref, sq_ref,
    ):
        give_att = relu_ref.at[0, :, 0:local]
        give_go = relu_ref.at[1, :, 0:local]
        loads = {}
        for k, (att, wo) in enumerate(((att_hbm.at[rows_of(head, half), :], wo_own_hbm), (att_oth_hbm.at[rows_of(head, half), :], wo_oth_hbm))):
            loads["att", k] = load(att, att_ref.at[k])
            loads["wo", k] = load(wo, wo_ref.at[k])
        loads["emb"] = load(emb_hbm, hid_ref)
        loads["cot"] = load(cot_hbm, cot_ref)
        for c in range(steps):
            cols = pl.ds(c * D, D)
            for k, we in ((1, we_oth_hbm), (0, we_own_hbm)):
                loads["we", c, k] = load(we.at[:, cols], we_ref.at[c, k])
            for k, wr in ((1, wr_oth_hbm), (0, wr_own_hbm)):
                loads["wr", c, k] = load(wr.at[cols, :], wr_ref.at[c, k])
        weights = {c: [copy for key, copy in loads.items() if key[0] in ("we", "wr") and key[1] == c] for c in range(steps)}
        for key, copy in loads.items():
            if key[0] not in ("we", "wr"):
                copy.start()
        all_here = greet_all()
        for key in (("att", 0), ("wo", 0), ("att", 1), ("wo", 1), "emb", "cot"):
            loads[key].wait()
        for copy in weights[0]:
            copy.start()
        gain, bias = row_of(gain_second_ref), row_of(bias_second_ref)

        def open_rows(r, rows):
            hidden = hid_ref[rows, :] + dot(att_ref[0, rows, :], wo_ref[0]) + dot(att_ref[1, rows, :], wo_ref[1])
            hid_ref[rows, :] = hidden
            hat, _ = normalise(hidden)
            normed = (hat * gain + bias).astype(BF16)
            n2_ref[rows, :] = normed
            n2t_ref[:, rows] = normed.T
            position = lax.broadcasted_iota(jnp.int32, (two_rows, 1), 0) + head * half + r * two_rows
            grad = jnp.where(position < len_ref[0], cot_ref[rows, :], 0.0)
            cot_ref[rows, :] = grad
            gl_ref[rows, :] = grad.astype(BF16)
            glt_ref[:, rows] = grad.astype(BF16).T

        halves_of(open_rows)
        hid_store = load(hid_ref, act_hbm)
        hid_store.start()

        def grad_copy(c, kind):
            return remote(
                give_ref.at[kind], got_ref.at[c % 2, kind], core_send.at[c, kind], core_recv.at[c, kind], head=partner
            )

        def put_own(c, kind, value):
            for k in range(split):
                part = value[:, k * width : (k + 1) * width].astype(BF16)
                g_ref[chunk_of(c, kind, k)] = part.reshape(g_ref.shape[1:])

        def add_other(c, kind):
            grad_copy(c, kind).wait_recv()
            for k in range(split):
                got = got_ref[c % 2, kind, :, k * width : (k + 1) * width]
                g_ref[chunk_of(c, kind, k)] += got.reshape(g_ref.shape[1:])

        def weight_grad(c, kind, k, left_ref, right):
            grad = dot(left_ref[...], right)
            if k == 1:
                if c:
                    grad_copy(c - 1, kind).wait_send()
                elif kind == 0:
                    all_here()
                give_ref[kind] = grad.astype(BF16)
                grad_copy(c, kind).start()
            else:
                put_own(c, kind, grad)

        stores = []
        for c in range(steps):
            for k in (1, 0):
                loads["we", c, k].wait()
                relu = jnp.maximum(dot(n2_ref[...], we_ref[c, k]), 0.0)
                relu_ref[k] = relu.astype(BF16)
                sq_ref[c, k] = (relu * relu).astype(BF16)
                stores.append(load(sq_ref.at[c, k], sq_hbm.at[c, k]))
                stores[-1].start()
                weight_grad(c, 0, k, glt_ref, sq_ref[c, k])
                tick(("feed", c, 1 - k))
            if c + 1 < steps:
                for copy in weights[c + 1]:
                    copy.start()
            add_other(c, 0)
            tick(("feed", c, 2))
            for k in (1, 0):
                loads["wr", c, k].wait()
                back = dot_nt(gl_ref[...], wr_ref[c, k])
                relu_ref[k] = (back * (2.0 * relu_ref[k].astype(F32))).astype(BF16)
                weight_grad(c, 1, k, n2t_ref, relu_ref[k])
                tick(("feed", c, 4 - k))
            for k in (1, 0):
                gn = dot_nt(relu_ref[k], we_ref[c, k])
                if c == 0 and k == 1:
                    gn_ref[...] = gn
                else:
                    gn_ref[...] += gn
                if k == 1:
                    add_other(c, 1)
                    tick(("feed", c, 5))
        acc_ref[0] = jnp.zeros(acc_ref.shape[1:], F32)

        def close_rows(r, rows):
            hat, scale = normalise(hid_ref[rows, :])
            grad_n = gn_ref[rows, :]
            acc_ref[0, 2:3, :] += jnp.sum(grad_n * hat, axis=0, keepdims=True)
            acc_ref[0, 3:4, :] += jnp.sum(grad_n, axis=0, keepdims=True)
            grad_h = cot_ref[rows, :] + norm_back(grad_n, hat, scale, gain)
            gh_ref[rows, :] = grad_h
            low = grad_h.astype(BF16)
            n2_ref[rows, :] = low
            n2t_ref[:, rows] = low.T
            give_att[rows, :] = dot_nt(low, wo_ref[1]).astype(BF16)

        halves_of(close_rows)
        own_rows = rows_of(head, half)
        att_copy = remote(give_att, do_ref.at[own_rows], core_send.at[steps, 0], core_recv.at[steps, 0], head=partner)
        att_copy.start()
        tick(("norm", 0))
        give_go[...] = dot(n2t_ref[...], att_ref[1]).astype(BF16)
        go_copy = remote(give_go, got_go, core_send.at[steps, 1], core_recv.at[steps, 1], head=partner)
        go_copy.start()
        do_ref[own_rows, :] = dot_nt(n2_ref[...], wo_ref[0]).astype(BF16)
        tick(("norm", 1))
        grad_o = dot(n2t_ref[...], att_ref[0]).astype(BF16)
        go_copy.wait()
        g_ref[fed - 1] = (grad_o + got_go[...]).reshape(g_ref.shape[1:])
        tick(("norm", 2))
        for kind in range(2):
            grad_copy(steps - 1, kind).wait_send()
        for copy in [hid_store] + stores:
            copy.wait()
        att_copy.wait()

    pl.run_scoped(
        feed_forward,
        pltpu.VMEM((2, half, local), BF16), pltpu.VMEM((2, local, D), BF16),
        pltpu.VMEM((steps, 2, D, D), BF16), pltpu.VMEM((steps, 2, D, D), BF16),
        pltpu.VMEM((half, D), F32), pltpu.VMEM((half, D), F32), pltpu.VMEM((half, D), F32),
        pltpu.VMEM((half, D), BF16), pltpu.VMEM((D, half), BF16),
        pltpu.VMEM((half, D), BF16), pltpu.VMEM((D, half), BF16),
        pltpu.VMEM((2, D, D), BF16), pltpu.VMEM((2, half, D), BF16), pltpu.VMEM((steps, 2, half, D), BF16),
    )

    def attention(
        all_ref, wcat_ref, nt_ref, mix_ref, late, dot_ref, qt_ref, doa_ref, kz_ref, va_ref, turned_ref,
        att_ref, q_ref, k_ref, v_ref, raw_ref, rinv_ref, terms_ref, pair_sem, terms_sem,
    ):
        def pair_loads(p, place):
            one = pl.ds(pl.multiple_of(p * LANES, LANES), LANES)
            three = pl.ds(pl.multiple_of(p * 3 * LANES, LANES), 3 * LANES)
            return [
                pltpu.make_async_copy(rinv_hbm.at[:, one], rinv_ref.at[place], pair_sem.at[place, 0]),
                pltpu.make_async_copy(att_hbm.at[:, one], att_ref.at[place], pair_sem.at[place, 1]),
                pltpu.make_async_copy(v_hbm.at[:, one], v_ref.at[place], pair_sem.at[place, 2]),
                pltpu.make_async_copy(q_hbm.at[:, one], q_ref.at[place], pair_sem.at[place, 3]),
                pltpu.make_async_copy(k_hbm.at[:, one], k_ref.at[place], pair_sem.at[place, 4]),
                pltpu.make_async_copy(raw_hbm.at[:, three], raw_ref.at[place], pair_sem.at[place, 5]),
            ]

        def terms_load(p, j):
            rows = pl.ds(j * BLOCK, slot - j * BLOCK)
            spot = lax.rem(blocks * p + j, 4)
            return pltpu.make_async_copy(
                terms_hbm.at[pl.ds(2 * p, 2), rows, pl.ds(j * BLOCK, BLOCK)],
                terms_ref.at[spot, :, rows, :],
                terms_sem.at[spot],
            )

        for copy in pair_loads(0, 0):
            copy.start()
        for j in range(2):
            terms_load(0, j).start()
        nt_load = load(nt_hbm, nt_ref)
        nt_load.start()
        for copy in late:
            copy.start()
        mix_ref[:, slot : slot + 8, :] = jnp.zeros((3, 8, LANES), F32)
        lane = lane_ids(slot)

        def at_pair(p, kind, *rest):
            for q in range(pairs):
                if plan.get((kind, q) + rest):
                    pl.when(p == q)(functools.partial(tick, (kind, q) + rest))

        def one_pair(p, _):
            place = lax.rem(p, 2)
            one = pl.ds(pl.multiple_of(p * LANES, LANES), LANES)

            @pl.when(p + 1 < pairs)
            def _():
                for copy in pair_loads(p + 1, 1 - place):
                    copy.start()

            for copy in pair_loads(p, place):
                copy.wait()
            scaled = (do_ref[:, one].astype(F32) * rinv_ref[place]).astype(BF16)
            dot_ref[...] = scaled.T
            qt_ref[...] = q_ref[place].T
            product = scaled.astype(F32) * att_ref[place].astype(F32)
            for e in range(2):
                in_head = (lane // HEAD_DIM) == e
                delta = -jnp.sum(jnp.where(in_head, product, 0.0), axis=1, keepdims=True)
                other = HEAD_DIM * (1 - e)
                ones = jnp.where((lane > other) & (lane < other + 4), 1.0, 0.0)
                doa_ref[e] = with_parts(jnp.where(in_head, scaled.astype(F32), 0.0), lane, other, delta).astype(BF16)
                va_ref[e] = jnp.where(in_head, v_ref[place].astype(F32), ones).astype(BF16)
                kz_ref[e] = jnp.where(in_head, k_ref[place].astype(F32), 0.0).astype(BF16)

            def grads_of(j, e):
                return dot_nt(doa_ref[e, j * BLOCK :, :], va_ref[e, j * BLOCK : (j + 1) * BLOCK, :])

            for j0 in range(0, blocks, 2):
                at_pair(p, "pair", j0)
                for j in (j0, j0 + 1):
                    terms_load(p, j).wait()
                    if j + 2 < blocks:
                        terms_load(p, j + 2).start()
                    else:
                        @pl.when(p + 1 < pairs)
                        def _():
                            terms_load(p + 1, j + 2 - blocks).start()
                tasks = [(j, e) for j in (j0, j0 + 1) for e in range(2)]
                coming = grads_of(*tasks[0])
                for t, (j, e) in enumerate(tasks):
                    back = coming
                    if t + 1 < len(tasks):
                        coming = grads_of(*tasks[t + 1])
                    first = j * BLOCK
                    keys = slice(first, first + BLOCK)
                    mine_rows = slice(e * HEAD_DIM, (e + 1) * HEAD_DIM)
                    terms = terms_ref[lax.rem(blocks * p + j, 4), e, first:, :]
                    grads = terms * back.astype(BF16)
                    part = dot(grads, kz_ref[e, keys, :])
                    if j == 0 and e == 0:
                        mix_ref[0, first:slot, :] = part
                    else:
                        mix_ref[0, first:slot, :] += part
                    turned_ref[0, mine_rows, keys] = dot(qt_ref[mine_rows, first:], grads)
                    turned_ref[1, mine_rows, keys] = dot(dot_ref[mine_rows, first:], terms)
            mix_ref[0, 0:slot, :] = mix_ref[0, 0:slot, :] * SCALE
            mix_ref[1, 0:slot, :] = turned_ref[0].T
            mix_ref[2, 0:slot, :] = turned_ref[1].T
            base = pl.multiple_of(p * 3 * LANES, LANES)

            @pl.when(p == 0)
            def _():
                nt_load.wait()

            for j in (2, 1, 0):
                zero = mix_ref[j, 0:slot, :]
                one_on = mix_ref[j, 1 : 1 + slot, :]
                two_on = mix_ref[j, 2 : 2 + slot, :]
                raw = raw_ref[place, :, j * LANES : (j + 1) * LANES].astype(F32)
                cols = pl.ds(pl.multiple_of(head * local + p * LANES, LANES), LANES)
                value = 0.0
                for s, moved in enumerate((zero, one_on, two_on)):
                    total = jnp.sum(moved * raw, axis=0, keepdims=True)
                    acc_ref[0, 4 + 3 * j + s : 5 + 3 * j + s, cols] = total
                    value += taps_ref[j, s : s + 1, one] * moved
                mine_cols = pl.ds(pl.multiple_of(base + j * LANES, LANES), LANES)
                all_ref[:, mine_cols] = value.astype(BF16)

                @pl.when(p == pairs - 1)
                def _():
                    grads = dot(nt_ref[...], all_ref[:, mine_cols]).astype(BF16)
                    spot = (fed + pairs - 1,) + (slice(None),) * (inner_bits + 1) + (slice(j * LANES, (j + 1) * LANES),)
                    g_ref[spot] = grads.reshape(g_ref.shape[1:-1] + (LANES,))
                    tick(("last", j))

            @pl.when(p < pairs - 1)
            def _():
                grads = dot(nt_ref[...], all_ref[:, pl.ds(base, 3 * LANES)]).astype(BF16)
                g_ref[fed + p] = grads.reshape(g_ref.shape[1:])

            at_pair(p, "taps")
            return 0

        lax.fori_loop(0, pairs, one_pair, 0)

    def tail(all_ref, wcat_ref, late, emb_ref, give_first, own_first, hid_ref, sq_ref, wr_ref):
        emb_load = load(emb_hbm, emb_ref)
        emb_load.start()
        hid_load = load(act_hbm, hid_ref)
        hid_load.start()
        ffn_loads = []
        for c in range(steps):
            for k, wr in ((1, wr_oth_hbm), (0, wr_own_hbm)):
                ffn_loads.append(load(sq_hbm.at[c, k], sq_ref.at[c, k]))
                ffn_loads.append(load(wr.at[pl.ds(c * D, D), :], wr_ref.at[c, k]))
        for copy in ffn_loads:
            copy.start()
        small_step(0)
        for copy in late:
            copy.wait()

        def other_rows(r, rows):
            there = pl.ds(pl.multiple_of(partner * half + r * two_rows, two_rows), two_rows)
            give_first[rows, :] = dot_nt(all_ref[there, :], wcat_ref[...]).astype(BF16)
            tick(("tail", r))

        halves_of(other_rows)
        first_copy = remote(
            give_first, got_first, core_send.at[steps + 1, 0], core_recv.at[steps + 1, 0], head=partner
        )
        first_copy.start()
        small_step(1)

        def own_rows(r, rows):
            here = pl.ds(pl.multiple_of(head * half + r * two_rows, two_rows), two_rows)
            own_first[rows, :] = dot_nt(all_ref[here, :], wcat_ref[...])
            tick(("tail", 2 + r))

        halves_of(own_rows)
        small_step(2)
        emb_load.wait()
        first_copy.wait()
        gain = row_of(gain_first_ref)
        late_ref[0] = jnp.zeros(late_ref.shape[1:], F32)

        def norm_rows(r, rows):
            grad_n = own_first[rows, :] + got_first[rows, :].astype(F32)
            hat, scale = normalise(emb_ref[rows, :])
            late_ref[0, 0:1, :] += jnp.sum(grad_n * hat, axis=0, keepdims=True)
            late_ref[0, 1:2, :] += jnp.sum(grad_n, axis=0, keepdims=True)
            gh_ref[rows, :] = gh_ref[rows, :] + norm_back(grad_n, hat, scale, gain)
            tick(("tail", 4 + r))

        halves_of(norm_rows)
        for copy in group_give:
            copy.start()
        got_group[seat] = late_ref[0]
        gin_store = load(gh_ref, gin_hbm)
        gin_store.start()
        small_step(3)
        hid_load.wait()
        for copy in ffn_loads:
            copy.wait()

        def ffn_rows(first, c):
            rows = slice(first, first + two_rows)
            hid_ref[rows, :] += dot(sq_ref[c, 1, rows, :], wr_ref[c, 1]) + dot(sq_ref[c, 0, rows, :], wr_ref[c, 0])

        for c in range(steps):
            ffn_rows(0, c)
            if c < 2:
                tick(("tail", 6 + c))
        for copy in group_take:
            copy.wait_recv()
        total = got_group[0]
        for k in range(1, group):
            total = total + got_group[k]
        late_ref[1] = total
        for copy in outer_give:
            copy.start()
        got_outer[line] = total
        small_step(4)
        for c in range(steps):
            ffn_rows(two_rows, c)
            if c < 2:
                tick(("tail", 8 + c))
        act_store = load(hid_ref, act_hbm)
        act_store.start()
        small_step(5)
        for copy in outer_take:
            copy.wait_recv()
        total = got_outer[0]
        for k in range(1, outer):
            total = total + got_outer[k]
        now, k = 6, 6
        while plan or k < small_steps:
            tick(("tail", now))
            if k < small_steps:
                small_step(k)
            now, k = now + 1, k + 1
        small_ref[0:2, :] = total[0:2, :]
        gin_store.wait()
        act_store.wait()
        for copy in group_give + outer_give:
            copy.wait_send()

    def backward(all_ref, wcat_ref):
        late = []
        for p in range(pairs):
            for j, w_hbm in enumerate((wq_hbm, wk_hbm, wv_hbm)):
                base = (3 * p + j) * LANES
                late.append(load(w_hbm.at[:, pl.ds(p * LANES, LANES)], wcat_ref.at[:, pl.ds(base, LANES)]))
        pl.run_scoped(
            lambda nt, mix, *rest: attention(all_ref, wcat_ref, nt, mix, late, *rest),
            pltpu.VMEM((D, slot), BF16),
            pltpu.VMEM((3, slot + 8, LANES), F32),
            pltpu.VMEM((LANES, slot), BF16),
            pltpu.VMEM((LANES, slot), BF16),
            pltpu.VMEM((2, slot, LANES), BF16),
            pltpu.VMEM((2, slot, LANES), BF16),
            pltpu.VMEM((2, slot, LANES), BF16),
            pltpu.VMEM((2, LANES, slot), F32),
            pltpu.VMEM((2, slot, LANES), BF16),
            pltpu.VMEM((2, slot, LANES), BF16),
            pltpu.VMEM((2, slot, LANES), BF16),
            pltpu.VMEM((2, slot, LANES), BF16),
            pltpu.VMEM((2, slot, 3 * LANES), BF16),
            pltpu.VMEM((2, slot, LANES), F32),
            pltpu.VMEM((4, 2, slot, BLOCK), BF16),
            pltpu.SemaphoreType.DMA((2, 6)),
            pltpu.SemaphoreType.DMA((4,)),
        )
        pl.run_scoped(
            functools.partial(tail, all_ref, wcat_ref, late),
            pltpu.VMEM((half, D), F32),
            pltpu.VMEM((half, D), BF16),
            pltpu.VMEM((half, D), F32),
            pltpu.VMEM((half, D), F32),
            pltpu.VMEM((steps, 2, half, D), BF16),
            pltpu.VMEM((steps, 2, D, D), BF16),
        )

    pl.run_scoped(backward, pltpu.VMEM((slot, 3 * local), BF16), pltpu.VMEM((D, 3 * local), BF16))
    for n in range(len(entries)):
        drain(n)
    for k in range(inner_bits + 1):
        small_copy(k).wait_send()
    for k in range(inner_bits + 1, inner_bits + 1 + line_steps):
        pl.when(line_sender(k - 1 - inner_bits))(lambda k=k: small_copy(k).wait_send())


def finish_kernel(
    split, sum_hbm, act_hbm, gin_hbm, small_ref,
    act_out, gin_out, q_out, k_out, v_out, go_out, ge_out, gr_out, taps_ref, *rest,
):
    vec_refs, (sum_ref, wide_ref, row_ref, load_sem, store_sem, row_load, row_store) = rest[:-7], rest[-7:]
    chunks, _, width = sum_hbm.shape
    pairs = q_out.shape[1] // LANES
    fed = chunks - pairs
    half = act_hbm.shape[0] // 2
    row_loads, row_stores = [], []
    for k, (src, dst) in enumerate(((act_hbm, act_out), (gin_hbm, gin_out))):
        for r in range(2):
            rows, spot = pl.ds(r * half, half), 2 * k + r
            row_loads.append(pltpu.make_async_copy(src.at[rows], row_ref.at[spot], row_load.at[spot]))
            row_stores.append(pltpu.make_async_copy(row_ref.at[spot], dst.at[rows], row_store.at[spot]))
    loads = [pltpu.make_async_copy(sum_hbm.at[c], sum_ref.at[c], load_sem.at[c]) for c in range(chunks)]
    for copy in row_loads + loads:
        copy.start()
    for j in range(3):
        taps_ref[j] = small_ref[4 + 3 * j : 7 + 3 * j, :]
    for k, ref in enumerate(vec_refs):
        ref[...] = small_ref[k, :]
    for came, go in zip(row_loads, row_stores):
        came.wait()
        go.start()
    stores = []

    def store(src, dst):
        stores.append(pltpu.make_async_copy(src, dst, store_sem.at[len(stores)]))
        stores[-1].start()

    for c in range(chunks):
        loads[c].wait()
        wide_ref[c] = sum_ref[c].astype(F32)
        if c < fed - 1:
            step, kind, k = c // (2 * split), (c // split) % 2, c % split
            store(wide_ref.at[c], (gr_out, ge_out)[kind].at[:, pl.ds((step * split + k) * width, width)])
        elif c == fed - 1:
            store(wide_ref.at[c], go_out)
        else:
            for j, out in enumerate((q_out, k_out, v_out)):
                part = wide_ref.at[c, :, pl.ds(j * LANES, LANES)]
                store(part, out.at[:, pl.ds((c - fed) * LANES, LANES)])
    for copy in stores + row_stores:
        copy.wait()


def params(vmem, **kw):
    return pltpu.CompilerParams(vmem_limit_bytes=vmem * MIB, **kw)


def body(
    token_ids, lengths, query_weight, key_weight, value_weight, output_weight,
    expand_weight, reduce_weight, dconv_taps, gain_first, bias_first,
    gain_second, bias_second, cotangent,
):
    half = token_ids.shape[1]
    slot = 2 * half
    local = query_weight.shape[1]
    units = expand_weight.shape[1]
    pairs = local // LANES
    outer = lax.axis_size("outer")
    inner = lax.axis_size("inner")
    inner_bits = inner.bit_length() - 1
    rows = D // inner
    width = 3 * LANES

    shape = jax.ShapeDtypeStruct
    smem = pl.BlockSpec(memory_space=pltpu.SMEM)
    anywhere = pl.BlockSpec(memory_space=pl.ANY)
    dma = pltpu.SemaphoreType.DMA
    vec = whole((D,))

    column = pl.BlockSpec((D, LANES), lambda p: (0, p))
    taps_spec = pl.BlockSpec((3, 3, LANES), lambda p: (0, 0, p))
    pair_rows = pl.BlockSpec((slot, LANES), lambda p: (0, p))
    raw_spec = pl.BlockSpec((slot, 3 * LANES), lambda p: (0, p))
    (
        attended, queries, key_rows, value_rows, raw, inverse, embedded, normed_t, att_oth,
        we_oth, wr_oth, wo_oth, terms,
    ) = pl.pallas_call(
        forward_kernel,
        grid=(pairs,),
        in_specs=[smem, whole((1, half)), vec, vec, column, column, column, taps_spec] + [anywhere] * 3,
        out_specs=[pair_rows] * 4 + [raw_spec, pair_rows] + [anywhere] * 7,
        out_shape=[shape((slot, local), BF16)] * 4
        + [shape((slot, 3 * local), BF16), shape((slot, local), F32), shape((half, D), F32), shape((D, slot), BF16)]
        + [shape((slot, local), BF16)]
        + [shape(w.shape, BF16) for w in (expand_weight, reduce_weight, output_weight)]
        + [shape((2 * pairs, slot, slot), BF16)],
        scratch_shapes=[
            pltpu.VMEM(output_weight.shape, BF16),
            pltpu.VMEM(expand_weight.shape, BF16),
            pltpu.VMEM(reduce_weight.shape, BF16),
            pltpu.VMEM((half, D), F32),
            pltpu.VMEM((D, slot), BF16),
            pltpu.VMEM((slot, D), BF16),
            pltpu.VMEM((2, 3, BLOCK + 8, LANES), F32),
            pltpu.VMEM((D, 3 * LANES), BF16),
            pltpu.VMEM((2, slot, LANES), BF16),
            pltpu.VMEM((2, LANES, slot), BF16),
            pltpu.VMEM((2, slot, LANES), BF16),
            pltpu.VMEM((2, slot, slot), BF16),
            pltpu.VMEM((pairs, slot, LANES), BF16),
            dma((PIECES,)), dma((PIECES,)), dma((pairs, slot // BLOCK)), dma((pairs, slot // BLOCK)), dma((3,)), dma((3,)),
            dma((slot // BLOCK,)), dma((4 + pairs,)),
        ],
        compiler_params=params(58, collective_id=0, has_side_effects=True),
        name="attention_forward",
    )(
        lengths, token_ids, gain_first, bias_first,
        query_weight, key_weight, value_weight, dconv_taps, expand_weight, reduce_weight, output_weight,
    )

    steps = units // D
    split = D // width
    fed = 2 * steps * split + 1
    chunks = fed + pairs
    twos = (2,) * inner_bits
    line_stages = inner_bits + outer
    vmem = lambda dims, kind: pltpu.VMEM(dims, kind)
    sums, small, activations, grad_input, _ = pl.pallas_call(
        functools.partial(layer_kernel, inner_bits, outer),
        in_specs=[smem, vec, vec, vec, whole((3, 3, local))] + [anywhere] * 20,
        out_specs=[whole((chunks, rows, width)), whole((16, D)), anywhere, anywhere, anywhere],
        out_shape=[
            shape((chunks, rows, width), BF16), shape((16, D), F32), shape((half, D), F32), shape((half, D), F32),
            shape((steps, 2, half, D), BF16),
        ],
        scratch_shapes=[
            vmem((half, D), F32),
            vmem((chunks,) + twos + (rows, width), BF16),
            vmem((chunks, rows, width), BF16),
            vmem((chunks, rows, width), BF16),
            vmem((slot, local), BF16),
            vmem((2, 2, D, D), BF16),
            vmem((D, local), BF16),
            vmem((half, D), BF16),
            vmem((inner_bits + 2, 16, D), F32),
            vmem((inner_bits + 3, 16, D), F32),
            vmem((2, 8, D), F32),
            vmem((2 * inner, 8, D), F32),
            vmem((outer, 8, D), F32),
            dma((12 + 10 * steps + 3 * pairs,)),
            dma((2 * chunks + 1, line_stages)), dma((2 * chunks + 1, line_stages)),
            dma((line_stages + 1,)), dma((line_stages + 1,)),
            dma((steps + 2, 2)), dma((steps + 2, 2)),
            dma((2 * inner,)), dma((2 * inner,)), dma((outer,)), dma((outer,)),
        ]
        + [vmem((chunks,) + (2,) * (inner_bits - 1 - s) + (rows, width), BF16) for s in range(inner_bits)],
        compiler_params=params(63, collective_id=1, has_side_effects=True),
        name="layer",
    )(
        lengths, gain_first, gain_second, bias_second, dconv_taps,
        att_oth, embedded, cotangent[0], output_weight, wo_oth,
        expand_weight, we_oth, reduce_weight, wr_oth, query_weight, key_weight, value_weight,
        attended, queries, key_rows, value_rows, raw, inverse, normed_t, terms,
    )
    vmem_all = pl.BlockSpec(memory_space=pltpu.VMEM)
    activations, grad_input, gq, gk, gv, go_sum, ge_sum, gr_sum, tap_sum, *vec_sums = pl.pallas_call(
        functools.partial(finish_kernel, split),
        in_specs=[anywhere] * 3 + [vmem_all],
        out_specs=[anywhere] * 8 + [vmem_all] * 5,
        out_shape=[shape((half, D), F32)] * 2
        + [shape((rows, local), F32)] * 4
        + [shape((rows, units), F32)] * 2
        + [shape((3, 3, D), F32)]
        + [shape((D,), F32)] * 4,
        scratch_shapes=[
            vmem((chunks, rows, width), BF16), vmem((chunks, rows, width), F32),
            vmem((4, half // 2, D), F32),
            dma((chunks,)), dma((fed + 3 * pairs,)), dma((4,)), dma((4,)),
        ],
        compiler_params=params(62),
        name="finish",
    )(sums, activations, grad_input, small)
    return (
        activations[None],
        grad_input[None],
        gq,
        gk,
        gv,
        go_sum.T,
        ge_sum,
        gr_sum.T,
        tap_sum,
        *vec_sums,
    )


def solution(mesh):
    return jax.shard_map(
        body,
        mesh=mesh,
        in_specs=(
            P(("outer", "inner"), "head"),
            P(("outer", "inner")),
            P(None, "head"),
            P(None, "head"),
            P(None, "head"),
            P("head", None),
            P(None, "head"),
            P("head", None),
            P(None, None, "head"),
            P(),
            P(),
            P(),
            P(),
            P(("outer", "inner"), "head", None),
        ),
        out_specs=(
            P(("outer", "inner"), "head", None),
            P(("outer", "inner"), "head", None),
            P("inner", "head"),
            P("inner", "head"),
            P("inner", "head"),
            P("head", "inner"),
            P("inner", "head"),
            P("head", "inner"),
            P(),
            P(),
            P(),
            P(),
            P(),
        ),
        check_vma=False,
    )
```
